32 devices in a mesh: dp: 8 (over y, x, core), tensor: 4 (over z).
Axes of the slice: x: 2, y: 2, z: 4, core: 2. Of those that a mesh axis runs over, the one named last changes fastest.
Arguments:
- activations: bfloat16 [16, 256, 2560], P('dp', 'tensor'), may hold values from -6 to 6
- norm_gain: float32 [2560], replicated, may hold values from 0.5 to 1.5
- gelu_proj: bfloat16 [2560, 2560], P('dp', 'tensor'), may hold values from -0.125 to 0.125
- input_proj: bfloat16 [2560, 2560], P('dp', 'tensor'), may hold values from -0.125 to 0.125
- conv_weight: float32 [4, 2560], P(None, 'tensor'), may hold values from -3 to 3
- gate_input: bfloat16 [256, 2560], P('dp', 'tensor'), may hold values from -0.375 to 0.375
- gate_decay: bfloat16 [256, 2560], P('dp', 'tensor'), may hold values from -0.375 to 0.375
- decay_rate: float32 [2560], P('tensor'), may hold values from 0.00025 to 0.01
- out_proj: bfloat16 [2560, 2560], P('tensor', 'dp'), may hold values from -0.25 to 0.25
- mlp_gain: float32 [2560], replicated, may hold values from 0.5 to 1.5
- feed_gate: bfloat16 [2560, 7680], P('dp', 'tensor'), may hold values from -0.125 to 0.125
- feed_up: bfloat16 [2560, 7680], P('dp', 'tensor'), may hold values from -0.125 to 0.125
- feed_down: bfloat16 [7680, 2560], P('tensor', 'dp'), may hold values from -0.125 to 0.125
- cotangent: bfloat16 [16, 256, 2560], P('dp', 'tensor'), may hold values from -6 to 6
- lengths: int32 [16], replicated, may hold values from 64 to 256, as said below
- batch_of: int32 [16], replicated, may hold values from 0 to 3, as said below
Outputs:
- output: bfloat16 [16, 256, 2560], P('dp', 'tensor')
- input_grad: float32 [16, 256, 2560], P('dp', 'tensor')
- norm_gain_grad: float32 [2560], replicated
- gelu_proj_grad: float32 [2560, 2560], P('dp', 'tensor')
- input_proj_grad: float32 [2560, 2560], P('dp', 'tensor')
- conv_grad: float32 [4, 2560], P(None, 'tensor')
- gate_input_grad: float32 [256, 2560], P('dp', 'tensor')
- gate_decay_grad: float32 [256, 2560], P('dp', 'tensor')
- decay_grad: float32 [2560], P('tensor')
- out_proj_grad: float32 [2560, 2560], P('tensor', 'dp')
- mlp_gain_grad: float32 [2560], replicated
- feed_gate_grad: float32 [2560, 7680], P('dp', 'tensor')
- feed_up_grad: float32 [2560, 7680], P('dp', 'tensor')
- feed_down_grad: float32 [7680, 2560], P('tensor', 'dp')
The draws below stay inside these ranges and needn't reach their ends.
Inputs may be any that keep to these rules, and one draw needn't show every extreme that they name: `lengths`: a sequence's valid positions are its first ones; in each aligned group of 2 sequences (one index of dp) one sequence has all 256. `batch_of`: every micro-batch holds at least one sequence.
All inputs are finite; a program needn't handle non-finite values.
Results may differ from the reference program's by a relative error of at most 0.024.
Values may be sent and summed in bfloat16 or wider, within the bound.
A program may use at most 256 MiB of HBM per device.

```python
import math
import jax
import jax.numpy as jnp
from jax import lax

D = 2560
FF = 7680
BLOCK = 256
CONV = 4
MICRO = 4
SEQ_DEV = 2
L = 256
SEQS = 16


def draw_lengths(key, part):
    key = jax.random.fold_in(key, 11)
    key_base, key_pick, key_short = jax.random.split(key, 3)
    group_count = SEQS // SEQ_DEV
    base_len = jax.random.randint(key_base, (SEQS,), L // 4, L + 1)
    chosen = jax.random.randint(key_pick, (group_count,), 0, SEQ_DEV)
    places = jnp.arange(SEQS)
    full_len = places % SEQ_DEV == chosen[places // SEQ_DEV]
    result = jnp.where(full_len, L, base_len)
    short_group = jax.random.randint(key_short, (), 0, group_count)
    short_seq = short_group * SEQ_DEV + (chosen[short_group] + 1) % SEQ_DEV
    result = jnp.where(places == short_seq, L // 4, result)
    return result.astype(jnp.int32)


def draw_batch_of(key, part):
    key = jax.random.fold_in(key, 23)
    key_draw, key_order = jax.random.split(key)
    result = jax.random.randint(key_draw, (SEQS,), 0, MICRO)
    order = jax.random.permutation(key_order, SEQS)
    result = result.at[order[:MICRO]].set(jnp.arange(MICRO))
    return result.astype(jnp.int32)


def block_levels(key, shape, cuts, least, largest):
    def one(position, blocks):
        heights = jax.random.uniform(jax.random.fold_in(jax.random.fold_in(key, 6), position), (blocks,), jnp.float32, least / len(cuts), largest / len(cuts))
        return jnp.repeat(jnp.exp(heights), shape[position] // blocks).reshape((-1,) + (1,) * (len(shape) - position - 1))

    factor_of = one(*cuts[0])
    for cut in cuts[1:]:
        factor_of = factor_of * one(*cut)
    return factor_of


def gaussian(stream_key, shape, deviation, limit, cuts=(), held_as=jnp.bfloat16):
    level = block_levels(stream_key, shape, cuts, -0.22, 0.18) if cuts else 1.0
    array = jax.random.normal(stream_key, shape, jnp.float32) * deviation * level
    return jnp.minimum(jnp.maximum(array, -limit), limit).astype(held_as)


def setup_inputs(seed: int = 0) -> dict:
    splits = jax.random.split(jax.random.key(seed), 17)
    activations = gaussian(splits[0], (SEQS, L, D), 1.0, 6.0, ((0, 8), (1, 4)))
    norm_gain = jnp.clip(1.0 + 0.1 * jax.random.normal(splits[1], (D,), jnp.float32), 0.5, 1.5)
    gelu_proj = gaussian(splits[2], (D, D), D ** -0.5, 0.125, ((0, 8), (1, 4)))
    input_proj = gaussian(splits[3], (D, D), D ** -0.5, 0.125, ((0, 8), (1, 4)))
    conv_weight = gaussian(splits[4], (CONV, D), 0.5, 3.0, ((1, 4),), jnp.float32)
    gate_input = gaussian(splits[5], (BLOCK, D), BLOCK ** -0.5, 0.375, ((0, 8), (1, 4)))
    gate_decay = gaussian(splits[6], (BLOCK, D), BLOCK ** -0.5, 0.375, ((0, 8), (1, 4)))
    decay_rate = jnp.clip(jnp.exp(math.log(0.01) - 3.6888794 * jax.random.uniform(splits[7], (D,), jnp.float32) ** block_levels(splits[7], (D,), ((0, 4),), -0.2, 0.2)), 0.00025, 0.01)
    out_proj = gaussian(splits[8], (D, D), (D // 4) ** -0.5, 0.25, ((0, 4), (1, 8)))
    mlp_gain = jnp.clip(1.0 + 0.1 * jax.random.normal(splits[9], (D,), jnp.float32), 0.5, 1.5)
    feed_gate = gaussian(splits[10], (D, FF), D ** -0.5, 0.125, ((0, 8), (1, 4)))
    feed_up = gaussian(splits[11], (D, FF), D ** -0.5, 0.125, ((0, 8), (1, 4)))
    feed_down = gaussian(splits[12], (FF, D), (FF // 4) ** -0.5, 0.125, ((0, 4), (1, 8)))
    cotangent = gaussian(splits[13], (SEQS, L, D), 1.0, 6.0, ((0, 8), (1, 4)))
    lengths = draw_lengths(jax.random.fold_in(splits[16], 71), 0)
    batch_of = draw_batch_of(jax.random.fold_in(splits[16], 71), 0)
    return dict(activations=activations, norm_gain=norm_gain, gelu_proj=gelu_proj, input_proj=input_proj, conv_weight=conv_weight, gate_input=gate_input, gate_decay=gate_decay, decay_rate=decay_rate, out_proj=out_proj, mlp_gain=mlp_gain, feed_gate=feed_gate, feed_up=feed_up, feed_down=feed_down, cotangent=cotangent, lengths=lengths, batch_of=batch_of)


EPS = 1e-06
FINEST_PRECISION = lax.Precision.HIGHEST

@jax.custom_vjp
def low(v):
    return lax.optimization_barrier(v.astype(jnp.bfloat16)).astype(jnp.float32)

@jax.custom_vjp
def low_back(v):
    return v

def low_keep(v):
    return (low(v), None)

def low_pass(kept, grad):
    return (grad,)

def back_keep(v):
    return (v, None)

def back_low(kept, grad):
    return (low(grad),)
low.defvjp(low_keep, low_pass)
low_back.defvjp(back_keep, back_low)

def normalize(value_entries, scale_gain):
    return value_entries * lax.rsqrt(lax.optimization_barrier(jnp.mean(value_entries * value_entries, axis=-1, keepdims=True)) + EPS) * scale_gain

def causal_conv(value_entries, kernel):
    summed = value_entries * kernel[0]
    for offset in range(1, kernel.shape[0]):
        shifted = jnp.concatenate([jnp.zeros_like(value_entries[:, :offset]), value_entries[:, :-offset]], axis=1)
        summed = summed + shifted * kernel[offset]
    return summed

def decay_inputs(input_pre, decay_pre, conv_vals, decay_rate):
    log_decay = -8.0 * jax.nn.sigmoid(decay_pre) * decay_rate
    scaled = jnp.sqrt(-jnp.expm1(2.0 * log_decay))
    return (log_decay, scaled * jax.nn.sigmoid(input_pre) * conv_vals)

def recurrence(log_steps, inputs):

    def advance(carried, pieces):
        step_log, step_in = pieces
        carried = jnp.exp(step_log) * carried + step_in
        return (carried, carried)
    start = jnp.zeros((log_steps.shape[0], log_steps.shape[2]), jnp.float32)
    _, states = lax.scan(advance, start, (jnp.swapaxes(log_steps, 0, 1), jnp.swapaxes(inputs, 0, 1)))
    return jnp.swapaxes(states, 0, 1)

def project(value_entries, weight_matrix):
    return jnp.einsum('brf,fc->brc', value_entries, weight_matrix, precision=FINEST_PRECISION)

def block_gates(conv_bf, gate_matrix):
    seq_count, length, width = conv_bf.shape
    block_num = width // BLOCK
    tile_view = conv_bf.reshape(seq_count, length, block_num, BLOCK)
    result = jnp.einsum('slbk,kbc->slbc', tile_view, gate_matrix.reshape(BLOCK, block_num, BLOCK), precision=FINEST_PRECISION)
    return result.reshape(seq_count, length, width)

def block_forward(inputs, norm_gain, gelu_proj, input_proj, conv_weight, gate_input, gate_decay, decay_rate, out_proj, mlp_gain, feed_gate, feed_up, feed_down):
    normed = low(normalize(inputs, norm_gain))
    gelu_preactivation = low_back(project(normed, gelu_proj))
    input_pre = low_back(project(normed, input_proj))
    conv_bf = low(causal_conv(input_pre, conv_weight))
    input_gate = low_back(block_gates(conv_bf, gate_input))
    decay_gate = low_back(block_gates(conv_bf, gate_decay))
    log_decay, drive_in = decay_inputs(input_gate, decay_gate, conv_bf, decay_rate)
    states = recurrence(log_decay, drive_in)
    mixer_output = low(jax.nn.gelu(gelu_preactivation) * states)
    middle = inputs + low_back(project(mixer_output, out_proj))
    normed_two = low(normalize(middle, mlp_gain))
    gate_pre = low_back(project(normed_two, feed_gate))
    lift_pre = low_back(project(normed_two, feed_up))
    hidden_rows = low(jax.nn.gelu(gate_pre) * lift_pre)
    return middle + low_back(project(hidden_rows, feed_down))

def reference(activations, norm_gain, gelu_proj, input_proj, conv_weight, gate_input, gate_decay, decay_rate, out_proj, mlp_gain, feed_gate, feed_up, feed_down, cotangent, lengths, batch_of):
    members = (batch_of[:, None] == jnp.arange(MICRO)[None, :]).astype(jnp.float32)
    counts = lax.optimization_barrier(jnp.sum(members * lengths[:, None].astype(jnp.float32), axis=0))
    per_batch = float(SEQS * L) / (MICRO * counts)
    seq_weight = lax.optimization_barrier(jnp.sum(members * per_batch[None, :], axis=1))
    valid_mask = (jnp.arange(L)[None, :] < lengths[:, None]).astype(jnp.float32)
    scaled = cotangent.astype(jnp.float32) * (valid_mask * seq_weight[:, None])[:, :, None]
    params = tuple((item.astype(jnp.float32) for item in (norm_gain, gelu_proj, input_proj, conv_weight, gate_input, gate_decay, decay_rate, out_proj, mlp_gain, feed_gate, feed_up, feed_down)))
    group_size = math.gcd(SEQS, 8)
    group_count = SEQS // group_size
    inputs_all = activations.astype(jnp.float32).reshape(group_count, group_size, L, D)
    scaled_all = scaled.reshape(group_count, group_size, L, D)

    def accumulate(totals, pieces):
        inputs, cot_group = pieces
        result, backward = jax.vjp(block_forward, inputs, *params)
        grads = backward(cot_group)
        totals = tuple((left + right for left, right in zip(totals, grads[1:])))
        return (totals, (result.astype(jnp.bfloat16), grads[0]))
    totals, (results, input_grads) = lax.scan(accumulate, tuple((jnp.zeros_like(item) for item in params)), (inputs_all, scaled_all))
    output = results.reshape(SEQS, L, D)
    input_grad = input_grads.reshape(SEQS, L, D)
    return (output, input_grad, totals[0], totals[1], totals[2], totals[3], totals[4], totals[5], totals[6], totals[7], totals[8], totals[9], totals[10], totals[11])
```

```python
import functools

import jax
import jax.numpy as jnp
from jax import lax
from jax.experimental import pallas as pl
from jax.experimental.pallas import tpu as pltpu
from jax.sharding import PartitionSpec as P

MICRO = 4
EPS = 1e-06
MESH = pl.DeviceIdType.MESH
ANY = pl.BlockSpec(memory_space=pl.ANY)
VMEM = pl.BlockSpec(memory_space=pltpu.VMEM)
DMA = pltpu.SemaphoreType.DMA
BF16 = jnp.bfloat16
F32 = jnp.float32


def place():
    return lax.axis_index("dp"), lax.axis_index("tensor")


def greet(d, t, depth, dp_masks=(1, 2, 4), z_all=False):
    barrier = pltpu.get_barrier_semaphore()
    for mask in dp_masks:
        pl.semaphore_signal(barrier, inc=1, device_id=(d ^ mask, t), device_id_type=MESH)
    if z_all:
        for step in range(1, depth):
            pl.semaphore_signal(
                barrier, inc=1, device_id=(d, lax.rem(t + step, depth)), device_id_type=MESH
            )
        pl.semaphore_wait(barrier, len(dp_masks) + depth - 1)
        return

    @pl.when(t > 0)
    def _():
        pl.semaphore_signal(barrier, inc=1, device_id=(d, t - 1), device_id_type=MESH)

    @pl.when(t < depth - 1)
    def _():
        pl.semaphore_signal(barrier, inc=1, device_id=(d, t + 1), device_id_type=MESH)

    ends = jnp.where((t == 0) | (t == depth - 1), 1, 2)
    pl.semaphore_wait(barrier, len(dp_masks) + ends)


def add_rows(total, term, rows, step=32):
    step = min(step, rows)

    @pl.loop(0, rows, step=step)
    def _(start):
        part = pl.ds(pl.multiple_of(start, step), step)
        total[part, :] = (total[part, :].astype(F32) + term[part, :].astype(F32)).astype(BF16)


class WeightGather:
    def __init__(self, shard, out, local, send, recv, d, t):
        rows = shard.shape[0]
        half = rows // 2
        top, low = pl.ds(0, half), pl.ds(half, half)
        plan = [
            (shard.at[top], d, top, 2),
            (shard.at[low], d, low, 4),
            (shard.at[low], d, low, 2),
            (shard.at[top], d, top, 4),
            (out.at[d ^ 2, top], d ^ 2, top, 4),
            (out.at[d ^ 4, low], d ^ 4, low, 2),
            (shard.at[top], d, top, 1),
            (shard.at[low], d, low, 1),
            (out.at[d ^ 2, top], d ^ 2, top, 1),
            (out.at[d ^ 4, low], d ^ 4, low, 1),
            (out.at[d ^ 2, low], d ^ 2, low, 1),
            (out.at[d ^ 4, top], d ^ 4, top, 1),
            (out.at[d ^ 6, top], d ^ 6, top, 1),
            (out.at[d ^ 6, low], d ^ 6, low, 1),
        ]
        self.copies = [
            pltpu.make_async_remote_copy(
                src_ref=src,
                dst_ref=out.at[slot, part],
                send_sem=send.at[i],
                recv_sem=recv.at[i],
                device_id=(d ^ mask, t),
                device_id_type=MESH,
            )
            for i, (src, slot, part, mask) in enumerate(plan)
        ]
        self.own = pltpu.make_async_copy(shard, out.at[d], local)

    def start(self):
        for i in (0, 1, 2, 3):
            self.copies[i].start()
        self.own.start()

    def relay(self):
        c = self.copies
        for i in (6, 7):
            c[i].start()
        c[0].wait_recv()
        c[4].start()
        c[1].wait_recv()
        c[5].start()
        c[8].start()
        c[9].start()

    def relay_two(self):
        c = self.copies
        c[2].wait_recv()
        c[10].start()
        c[3].wait_recv()
        c[11].start()

    def relay_last(self):
        c = self.copies
        c[4].wait_recv()
        c[12].start()
        c[5].wait_recv()
        c[13].start()

    def end(self):
        for i in range(6, 14):
            self.copies[i].wait_recv()
        for i in range(14):
            self.copies[i].wait_send()
        self.own.wait()


def gather_scratch(count):
    return [DMA((count,)), DMA((count, 14)), DMA((count, 14))]


class GradScatter:
    ORDER = (6, 2, 4, 0)

    def __init__(self, grad, out, own, core, diag, last, local, send, recv, d, t):
        self.out, self.own, self.core, self.diag, self.last = out, own, core, diag, last
        self.rows = rows = grad.shape[1]
        half = rows // 2
        self.half = half
        self.top, self.low = pl.ds(0, half), pl.ds(half, half)
        self.loads = [
            pltpu.make_async_copy(grad.at[d ^ r], own.at[i], local.at[i])
            for i, r in enumerate(self.ORDER)
        ]
        top, low = self.top, self.low
        plan = [(grad.at[d ^ 1 ^ r], core.at[i], 1) for i, r in enumerate(self.ORDER)] + [
            (own.at[0, top], diag.at[0], 2),
            (own.at[0, low], diag.at[1], 4),
            (own.at[1, top], last.at[0, top], 2),
            (own.at[2, low], last.at[1, low], 4),
            (own.at[2, top], last.at[1, top], 4),
            (own.at[1, low], last.at[0, low], 2),
        ]
        self.copies = [
            pltpu.make_async_remote_copy(
                src_ref=src,
                dst_ref=dst,
                send_sem=send.at[i],
                recv_sem=recv.at[i],
                device_id=(d ^ mask, t),
                device_id_type=MESH,
            )
            for i, (src, dst, mask) in enumerate(plan)
        ]

    def start(self):
        for i in range(4):
            self.copies[i].start()
            self.loads[i].start()

    def pair(self, i):
        self.loads[i].wait()
        self.copies[i].wait_recv()
        add_rows(self.own.at[i], self.core.at[i], self.rows)

    def first(self):
        self.pair(0)
        self.copies[4].start()
        self.copies[5].start()

    def second(self):
        self.pair(1)
        self.copies[6].start()
        self.pair(2)
        self.copies[7].start()
        self.pair(3)

    def third(self):
        c = self.copies
        c[4].wait_recv()
        add_rows(self.own.at[2, self.top], self.diag.at[0], self.half)
        c[8].start()
        c[5].wait_recv()
        add_rows(self.own.at[1, self.low], self.diag.at[1], self.half)
        c[9].start()

    def end(self):
        for i in (6, 7, 8, 9):
            self.copies[i].wait_recv()
        step = 16

        @pl.loop(0, self.rows, step=step)
        def _(start):
            part = pl.ds(pl.multiple_of(start, step), step)
            self.out[part, :] = (
                self.own[3, part, :].astype(F32)
                + self.last[0, part, :].astype(F32)
                + self.last[1, part, :].astype(F32)
            )

        for i in range(10):
            self.copies[i].wait_send()


def scatter_scratch(shapes):
    own = [pltpu.VMEM((4,) + s, BF16) for s in shapes]
    core = [pltpu.VMEM((4,) + s, BF16) for s in shapes]
    diag = [pltpu.VMEM((2, s[0] // 2, s[1]), BF16) for s in shapes]
    last = [pltpu.VMEM((2,) + s, BF16) for s in shapes]
    n = len(shapes)
    return own + core + diag + last + [DMA((n, 4)), DMA((n, 10)), DMA((n, 10))]


def make_scatters(grads, outs, scratch, d, t):
    n = len(grads)
    own, core, diag, last = (scratch[i * n : (i + 1) * n] for i in range(4))
    local, send, recv = scratch[4 * n :]
    return [
        GradScatter(
            grads[i],
            outs[i],
            own[i],
            core[i],
            diag[i],
            last[i],
            local.at[i],
            send.at[i],
            recv.at[i],
            d,
            t,
        )
        for i in range(n)
    ]


class LineGather:
    def __init__(self, block, out, local, send, recv, d, t, depth):
        self.block, self.out, self.send, self.recv = block, out, send, recv
        self.d, self.t, self.depth = d, t, depth
        self.rows = block.shape[1]
        self.own = pltpu.make_async_copy(block, self.slot(t), local)

    def slot(self, j):
        return self.out.at[:, pl.ds(pl.multiple_of(j * self.rows, self.rows), self.rows)]

    def copy(self, way, step, j, to):
        return pltpu.make_async_remote_copy(
            src_ref=self.block if step == 0 else self.slot(j),
            dst_ref=self.slot(j),
            send_sem=self.send.at[way, step],
            recv_sem=self.recv.at[way, step],
            device_id=(self.d, to),
            device_id_type=MESH,
        )

    def step(self, s):
        t, depth = self.t, self.depth
        if s == 0:
            self.own.start()
        if s > 0:

            @pl.when(t - s >= 0)
            def _():
                self.copy(0, s - 1, t, t).wait_recv()

        if s < depth - 1:

            @pl.when((t - s >= 0) & (t < depth - 1))
            def _():
                self.copy(0, s, t - s, t + 1).start()

        if s > 0:

            @pl.when(t + s < depth)
            def _():
                self.copy(1, s - 1, t, t).wait_recv()

        if s < depth - 1:

            @pl.when((t + s < depth) & (t > 0))
            def _():
                self.copy(1, s, t + s, t - 1).start()

    def end(self):
        t, depth = self.t, self.depth
        for s in range(depth - 1):

            @pl.when((t - s >= 0) & (t < depth - 1))
            def _():
                self.copy(0, s, t, t).wait_send()

            @pl.when((t + s < depth) & (t > 0))
            def _():
                self.copy(1, s, t, t).wait_send()

        self.own.wait()


def line_gather_scratch(depth):
    return [DMA, DMA((2, depth - 1)), DMA((2, depth - 1))]


class LineScatter:
    def __init__(self, part, got, send, recv, d, t, depth):
        self.part, self.got, self.send, self.recv = part, got, send, recv
        self.d, self.t, self.depth = d, t, depth
        self.seqs = part.shape[0]
        self.rows = part.shape[1] // depth

    def copy(self, way, j, s, src, to):
        return pltpu.make_async_remote_copy(
            src_ref=src,
            dst_ref=self.got.at[way, j, s],
            send_sem=self.send.at[way, j, s],
            recv_sem=self.recv.at[way, j, s],
            device_id=(self.d, to),
            device_id_type=MESH,
        )

    def move(self, way, j):
        t, depth = self.t, self.depth
        rows = pl.ds(j * self.rows, self.rows)
        if way == 0:
            source, hears, sends, to = t == 0, (t > 0) & (j >= t), j > t, t + 1
        else:
            source, hears, sends, to = t == depth - 1, (t < depth - 1) & (j <= t), j < t, t - 1
        for s in range(self.seqs):
            mine = self.got.at[way, j, s]

            @pl.when(hears)
            def _():
                self.copy(way, j, s, mine, t).wait_recv()

            @pl.when(sends & source)
            def _():
                self.copy(way, j, s, self.part.at[s, rows], to).start()

            @pl.when(sends & jnp.logical_not(source))
            def _():
                add_rows(mine, self.part.at[s, rows], self.rows)
                self.copy(way, j, s, mine, to).start()

    def step(self, k):
        depth, t = self.depth, self.t
        right, left = depth - 1 - k, k

        @pl.when(t < depth // 2)
        def _():
            self.move(0, right)

        self.move(1, left)

        @pl.when(t >= depth // 2)
        def _():
            self.move(0, right)

    def total(self, out):
        t, depth = self.t, self.depth
        mine = pl.ds(pl.multiple_of(t * self.rows, self.rows), self.rows)
        out[...] = self.part[:, mine, :].astype(F32)

        @pl.when(t > 0)
        def _():
            out[...] += self.got[0, t].astype(F32)

        @pl.when(t < depth - 1)
        def _():
            out[...] += self.got[1, t].astype(F32)

    def end(self):
        t, depth = self.t, self.depth
        for j in range(depth):
            for s in range(self.seqs):
                mine = self.got.at[0, j, s]

                @pl.when((j > t) & (t < depth - 1))
                def _():
                    self.copy(0, j, s, mine, t).wait_send()

                @pl.when((j < t) & (t > 0))
                def _():
                    self.copy(1, j, s, mine, t).wait_send()


def line_scatter_scratch(seqs, rows, width, depth):
    return [
        pltpu.VMEM((2, depth, seqs, rows, width), BF16),
        DMA((2, depth, seqs)),
        DMA((2, depth, seqs)),
    ]


def call(kernel, name, number, ins, outs, scratch, args, vmem=60 * 1024 * 1024):
    return pl.pallas_call(
        kernel,
        name=name,
        out_shape=[o[0] for o in outs],
        in_specs=ins,
        out_specs=[o[1] for o in outs],
        scratch_shapes=scratch,
        compiler_params=pltpu.CompilerParams(
            collective_id=number, has_side_effects=True, vmem_limit_bytes=vmem
        ),
    )(*args)


def shaped(shape, dtype, spec):
    return (jax.ShapeDtypeStruct(shape, dtype), spec)


def gather_kernel(depth, n_weights, *refs):
    blocks = refs[:2]
    shards = refs[2 : 2 + n_weights]
    outs = refs[2 + n_weights :]
    wide, full = outs[:2], outs[2 : 2 + n_weights]
    scratch = outs[2 + n_weights :]
    d, t = place()
    greet(d, t, depth)
    local, send, recv = scratch[:3]
    lines = [
        LineGather(blocks[i], wide[i], *scratch[3 + 3 * i : 6 + 3 * i], d, t, depth)
        for i in range(2)
    ]
    gathers = [
        WeightGather(shards[i], full[i], local.at[i], send.at[i], recv.at[i], d, t)
        for i in range(n_weights)
    ]
    lines[0].step(0)
    for g in gathers:
        g.start()
    early, late = gathers[:-1], gathers[-1:]
    lines[0].step(1)
    for g in early:
        g.relay()
    lines[0].step(2)
    lines[1].step(0)
    for g in early:
        g.relay_two()
    lines[0].step(3)
    for g in early:
        g.relay_last()
    lines[1].step(1)
    for g in late:
        g.relay()
    lines[1].step(2)
    for g in late:
        g.relay_two()
    lines[1].step(3)
    for g in late:
        g.relay_last()
    for g in gathers:
        g.end()
    for line in lines:
        line.end()


def gather_first(normed, cot, weights, depth):
    seqs, rows, width = normed.shape
    n = len(weights)
    outs = [shaped((seqs, rows * depth, width), BF16, ANY)] * 2
    outs += [shaped((8,) + w.shape, BF16, ANY) for w in weights]
    scratch = gather_scratch(n) + line_gather_scratch(depth) * 2
    res = call(
        functools.partial(gather_kernel, depth, n),
        "gather_first",
        0,
        [ANY] * (2 + n),
        outs,
        scratch,
        (normed, cot) + tuple(weights),
    )
    return res[0], res[1], res[2:]


def middle_kernel(depth, part, act, gain, w0, w1, middle, wide, f0, f1, *scratch):
    local, send, recv = scratch[:3]
    got, ssem, rsem = scratch[3:6]
    block = scratch[6]
    lsem = scratch[7:10]
    d, t = place()
    greet(d, t, depth)
    gathers = [
        WeightGather(w, f, local.at[i], send.at[i], recv.at[i], d, t)
        for i, (w, f) in enumerate(((w0, f0), (w1, f1)))
    ]
    scatter = LineScatter(part, got, ssem, rsem, d, t, depth)
    scatter.step(0)
    for g in gathers:
        g.start()
    scatter.step(1)
    gathers[0].relay()
    scatter.step(2)
    gathers[0].relay_two()
    scatter.step(3)
    scatter.total(middle)
    seqs, rows, width = act.shape
    for s in range(seqs):
        value = middle[s] + act[s].astype(F32)
        middle[s] = value
        inverse = lax.rsqrt(jnp.mean(value * value, axis=-1, keepdims=True) + EPS)
        block[s] = (value * inverse * gain[...]).astype(BF16)
    line = LineGather(block, wide, *lsem, d, t, depth)
    line.step(0)
    gathers[0].relay_last()
    gathers[1].relay()
    line.step(1)
    gathers[1].relay_two()
    line.step(2)
    gathers[1].relay_last()
    line.step(3)
    for g in gathers:
        g.end()
    scatter.end()
    line.end()


def middle_phase(part, act, gain, w0, w1, depth):
    seqs, rows, width = act.shape
    outs = [
        shaped(act.shape, F32, VMEM),
        shaped((seqs, rows * depth, width), BF16, ANY),
        shaped((8,) + w0.shape, BF16, ANY),
        shaped((8,) + w1.shape, BF16, ANY),
    ]
    scratch = (
        gather_scratch(2)
        + line_scatter_scratch(seqs, rows, width, depth)
        + [pltpu.VMEM(act.shape, BF16)]
        + line_gather_scratch(depth)
    )
    return call(
        functools.partial(middle_kernel, depth),
        "middle_phase",
        1,
        [VMEM, VMEM, VMEM, ANY, ANY],
        outs,
        scratch,
        (part, act, gain.reshape(1, width), w0, w1),
    )


def norm_back(value, gain, error):
    inverse = lax.rsqrt(jnp.mean(value * value, axis=-1, keepdims=True) + EPS)
    scaled = error * gain
    mean = jnp.mean(scaled * value, axis=-1, keepdims=True)
    grad = inverse * scaled - value * (inverse * inverse * inverse * mean)
    return grad, jnp.sum(error * value * inverse, axis=0, keepdims=True)


def back_kernel(depth, part, middle, gain, cot, g0, g1, grad, wide, gain_grad, o0, o1, *scratch):
    got, ssem, rsem = scratch[:3]
    block = scratch[3]
    lsem = scratch[4:7]
    d, t = place()
    greet(d, t, depth)
    scatters = make_scatters((g0, g1), (o0, o1), scratch[7:], d, t)
    scatter = LineScatter(part, got, ssem, rsem, d, t, depth)
    scatter.step(0)
    for g in scatters:
        g.start()
    scatters[0].first()
    scatters[0].second()
    scatter.step(1)
    scatters[1].first()
    scatters[0].third()
    scatter.step(2)
    scatters[1].second()
    scatter.step(3)
    scatter.total(grad)
    seqs, rows, width = middle.shape
    for s in range(seqs):
        change, gain_part = norm_back(middle[s], gain[...], grad[s])
        change = change + cot[s]
        grad[s] = change
        block[s] = change.astype(BF16)
        if s == 0:
            gain_grad[...] = gain_part
        else:
            gain_grad[...] += gain_part
    line = LineGather(block, wide, *lsem, d, t, depth)
    line.step(0)
    scatters[1].third()
    line.step(1)
    scatters[0].end()
    line.step(2)
    line.step(3)
    scatters[1].end()
    scatter.end()
    line.end()


def back_phase(part, middle, gain, cot, g0, g1, depth):
    seqs, rows, width = middle.shape
    shapes = [g0.shape[1:], g1.shape[1:]]
    outs = [
        shaped(middle.shape, F32, VMEM),
        shaped((seqs, rows * depth, width), BF16, ANY),
        shaped((1, width), F32, VMEM),
        shaped(shapes[0], F32, VMEM),
        shaped(shapes[1], F32, VMEM),
    ]
    scratch = (
        line_scatter_scratch(seqs, rows, width, depth)
        + [pltpu.VMEM(middle.shape, BF16)]
        + line_gather_scratch(depth)
        + scatter_scratch(shapes)
    )
    return call(
        functools.partial(back_kernel, depth),
        "back_phase",
        2,
        [VMEM, VMEM, VMEM, VMEM, ANY, ANY],
        outs,
        scratch,
        (part, middle, gain.reshape(1, width), cot, g0, g1),
    )


def last_kernel(depth, n_grads, part, feed, act, gain, middle, grad_middle, mlp_part, small, *refs):
    grads = refs[:n_grads]
    refs = refs[n_grads:]
    output, input_grad, gains, smalls = refs[:4]
    outs = refs[4 : 4 + n_grads]
    scratch = refs[4 + n_grads :]
    got0, ssem0, rsem0, got1, ssem1, rsem1 = scratch[:6]
    pack, packs, small_all, line_pack, line_packs = scratch[6:11]
    psend, precv, qsend, qrecv, zsend, zrecv = scratch[11:17]
    total = scratch[17]
    d, t = place()
    greet(d, t, depth, dp_masks=(1, 2, 3, 4, 5, 6, 7), z_all=True)
    scatters = make_scatters(grads, outs, scratch[18:], d, t)
    first = LineScatter(part, got0, ssem0, rsem0, d, t, depth)
    second = LineScatter(feed, got1, ssem1, rsem1, d, t, depth)

    def dp_copies(src, dst, send, recv):
        return [
            pltpu.make_async_remote_copy(
                src_ref=src,
                dst_ref=dst.at[d],
                send_sem=send.at[mask - 1],
                recv_sem=recv.at[mask - 1],
                device_id=(d ^ mask, t),
                device_id_type=MESH,
            )
            for mask in range(1, 8)
        ]

    small_copies = dp_copies(small, small_all, qsend, qrecv)
    for c in small_copies:
        c.start()
    first.step(0)
    for g in scatters:
        g.start()
    for g in scatters[:-1]:
        g.first()
        g.second()
    first.step(1)
    for g in scatters[:-1]:
        g.third()
    scatters[-1].first()
    first.step(2)
    second.step(0)
    scatters[-1].second()
    first.step(3)
    first.total(input_grad)
    seqs = act.shape[0]
    pack[1:2, :] = mlp_part[...]
    for s in range(seqs):
        change, gain_part = norm_back(act[s].astype(F32), gain[...], input_grad[s])
        input_grad[s] = change + grad_middle[s]
        if s == 0:
            pack[0:1, :] = gain_part
        else:
            pack[0:1, :] += gain_part
    pack_copies = dp_copies(pack, packs, psend, precv)
    for c in pack_copies:
        c.start()
    scatters[-1].third()
    second.step(1)
    packs[d] = pack[...]
    small_all[d] = small[...]
    for c in pack_copies:
        c.wait_recv()
    sum_ = packs[0]
    for i in range(1, 8):
        sum_ = sum_ + packs[i]
    line_pack[...] = sum_
    z_copies = [
        pltpu.make_async_remote_copy(
            src_ref=line_pack,
            dst_ref=line_packs.at[t],
            send_sem=zsend.at[step - 1],
            recv_sem=zrecv.at[step - 1],
            device_id=(d, lax.rem(t + step, depth)),
            device_id_type=MESH,
        )
        for step in range(1, depth)
    ]
    for c in z_copies:
        c.start()
    line_packs[t] = sum_
    second.step(2)
    for g in scatters[:-1]:
        g.end()
    second.step(3)
    second.total(total)
    output[...] = (total[...] + middle[...]).astype(BF16)
    for c in small_copies:
        c.wait_recv()
    sum_ = small_all[0]
    for i in range(1, 8):
        sum_ = sum_ + small_all[i]
    smalls[...] = sum_
    for c in z_copies:
        c.wait_recv()
    sum_ = line_packs[0]
    for i in range(1, depth):
        sum_ = sum_ + line_packs[i]
    gains[...] = sum_
    scatters[-1].end()
    for c in small_copies + pack_copies + z_copies:
        c.wait_send()
    first.end()
    second.end()


def last_phase(part, feed, act, gain, middle, grad_middle, mlp_part, small, grads, depth):
    seqs, rows, width = act.shape
    n = len(grads)
    shapes = [g.shape[1:] for g in grads]
    outs = [
        shaped(act.shape, BF16, VMEM),
        shaped(act.shape, F32, VMEM),
        shaped((8, width), F32, VMEM),
        shaped(small.shape, F32, VMEM),
    ] + [shaped(s, F32, VMEM) for s in shapes]
    scratch = (
        line_scatter_scratch(seqs, rows, width, depth) * 2
        + [
            pltpu.VMEM((8, width), F32),
            pltpu.VMEM((8, 8, width), F32),
            pltpu.VMEM((8,) + small.shape, F32),
            pltpu.VMEM((8, width), F32),
            pltpu.VMEM((depth, 8, width), F32),
        ]
        + [DMA((7,))] * 4
        + [DMA((depth - 1,))] * 2
        + [pltpu.VMEM(act.shape, F32)]
        + scatter_scratch(shapes)
    )
    res = call(
        functools.partial(last_kernel, depth, n),
        "last_phase",
        3,
        [VMEM] * 8 + [ANY] * n,
        outs,
        scratch,
        (part, feed, act, gain.reshape(1, width), middle, grad_middle, mlp_part, small)
        + tuple(grads),
    )
    return res[0], res[1], res[2], res[3], res[4:]


def scan_kernel(backward, rate_ref, drive_ref, out_ref):
    seqs, length, width = rate_ref.shape
    tile = 8
    row = lax.broadcasted_iota(jnp.int32, (tile, width), 0)

    def body(i, carried):
        k = length // tile - 1 - i if backward else i
        rows = pl.ds(pl.multiple_of(k * tile, tile), tile)
        ends = []
        for s in range(seqs):
            rate = rate_ref[s, rows, :]
            drive = drive_ref[s, rows, :]
            for shift in (1, 2, 4):
                turn = tile - shift if backward else shift
                inside = row < tile - shift if backward else row >= shift
                before = jnp.where(inside, pltpu.roll(drive, turn, 0), 0.0)
                drive = drive + rate * before
                rate = rate * jnp.where(inside, pltpu.roll(rate, turn, 0), 1.0)
            states = drive + rate * carried[s]
            out_ref[s, rows, :] = states
            ends.append(states[0:1] if backward else states[tile - 1 : tile])
        return tuple(ends)

    start = tuple(jnp.zeros((1, width), F32) for _ in range(seqs))
    lax.fori_loop(0, length // tile, body, start)


def recurrence(rate, drive, backward=False):
    return pl.pallas_call(
        functools.partial(scan_kernel, backward),
        name="recurrence",
        out_shape=jax.ShapeDtypeStruct(drive.shape, F32),
        in_specs=[VMEM, VMEM],
        out_specs=VMEM,
        compiler_params=pltpu.CompilerParams(vmem_limit_bytes=32 * 1024 * 1024),
    )(rate, drive)


def swapped(block, axis):
    count = lax.axis_size(axis)
    return lax.ppermute(block, axis, [(i, i ^ 1) for i in range(count)])


def normalize(value_entries, scale_gain):
    return (
        value_entries
        * lax.rsqrt(jnp.mean(value_entries * value_entries, axis=-1, keepdims=True) + EPS)
        * scale_gain
    )


def causal_conv(value_entries, kernel):
    summed = value_entries * kernel[0]
    for offset in range(1, kernel.shape[0]):
        shifted = jnp.concatenate(
            [jnp.zeros_like(value_entries[:, :offset]), value_entries[:, :-offset]], axis=1
        )
        summed = summed + shifted * kernel[offset]
    return summed


def decay_inputs(input_pre, decay_pre, conv_vals, decay_rate):
    log_decay = -8.0 * jax.nn.sigmoid(decay_pre) * decay_rate
    scaled = jnp.sqrt(-jnp.expm1(2.0 * log_decay))
    return (log_decay, scaled * jax.nn.sigmoid(input_pre) * conv_vals)


class Fast:
    @staticmethod
    def first(normed, cot, weights, depth):
        return gather_first(normed, cot, weights, depth)

    middle = staticmethod(middle_phase)
    back = staticmethod(back_phase)
    last = staticmethod(last_phase)


class Plain:
    @staticmethod
    def wide(block):
        return lax.all_gather(block, "tensor", axis=1, tiled=True)

    @staticmethod
    def narrow(part):
        return lax.psum_scatter(part, "tensor", scatter_dimension=1, tiled=True).astype(F32)

    @staticmethod
    def full(shard):
        return lax.all_gather(shard, "dp", axis=0, tiled=False)

    @staticmethod
    def own(grad):
        return lax.psum_scatter(grad, "dp", scatter_dimension=0, tiled=False).astype(F32)

    @classmethod
    def first(cls, normed, cot, weights, depth):
        return cls.wide(normed), cls.wide(cot), [cls.full(w) for w in weights]

    @classmethod
    def middle(cls, part, act, gain, w0, w1, depth):
        middle = act.astype(F32) + cls.narrow(part)
        wide = cls.wide(normalize(middle, gain).astype(BF16))
        return middle, wide, cls.full(w0), cls.full(w1)

    @classmethod
    def back(cls, part, middle, gain, cot, g0, g1, depth):
        _, back = jax.vjp(normalize, middle, gain)
        change, gain_grad = back(cls.narrow(part))
        grad = cot + change
        return grad, cls.wide(grad.astype(BF16)), gain_grad[None], cls.own(g0), cls.own(g1)

    @classmethod
    def last(cls, part, feed, act, gain, middle, grad_middle, mlp_part, small, grads, depth):
        _, back = jax.vjp(normalize, act.astype(F32), gain)
        change, gain_grad = back(cls.narrow(part))
        output = (middle + cls.narrow(feed)).astype(BF16)
        gains = lax.psum(jnp.concatenate([gain_grad[None], mlp_part]), ("dp", "tensor"))
        small = lax.psum(small, "dp")
        return output, grad_middle + change, gains, small, [cls.own(g) for g in grads]


def dot(spec, left, right):
    return jnp.einsum(spec, left, right, preferred_element_type=F32)


def shards(
    activations,
    norm_gain,
    gelu_proj,
    input_proj,
    conv_weight,
    gate_input,
    gate_decay,
    decay_rate,
    out_proj,
    mlp_gain,
    feed_gate,
    feed_up,
    feed_down,
    cotangent,
    lengths,
    batch_of,
):
    depth = lax.axis_size("tensor")
    dp_count = lax.axis_size("dp")
    moves = Fast if dp_count == 8 and depth == 4 else Plain
    tensor_index = lax.axis_index("tensor")
    data_index = lax.axis_index("dp")
    seq_count, row_count, model_width = activations.shape
    full_length = row_count * depth
    members = (batch_of[:, None] == jnp.arange(MICRO)[None, :]).astype(F32)
    counts = jnp.sum(members * lengths[:, None].astype(F32), axis=0)
    total_seqs = lengths.shape[0]
    per_batch = float(total_seqs * full_length) / (MICRO * counts)
    weight_all = jnp.sum(members * per_batch[None, :], axis=1)
    my_weight = lax.dynamic_slice_in_dim(weight_all, data_index * seq_count, seq_count)
    my_length = lax.dynamic_slice_in_dim(lengths, data_index * seq_count, seq_count)
    places = tensor_index * row_count + jnp.arange(row_count)
    valid_mask = (places[None, :] < my_length[:, None]).astype(F32)
    scaled_cot = cotangent.astype(F32) * (valid_mask * my_weight[:, None])[:, :, None]
    normed = normalize(activations.astype(F32), norm_gain).astype(BF16)

    normed_all, cot_all, weights = moves.first(
        normed,
        scaled_cot.astype(BF16),
        (gelu_proj, input_proj, gate_input, gate_decay, out_proj.T, feed_up),
        depth,
    )
    gelu_w, input_w, gate_in_w, gate_dec_w, out_w, up_w = (
        w.reshape(-1, w.shape[-1]) for w in weights
    )
    channels = gelu_w.shape[1]
    block_size = gate_in_w.shape[0]
    half_block = block_size // 2
    window_width = channels + half_block
    window_count = window_width // block_size
    parity = tensor_index % 2

    gelu_pre = dot("kqg,ga->kqa", normed_all, gelu_w)
    input_pre = dot("kqg,ga->kqa", normed_all, input_w)
    gelu_out, gelu_back = jax.vjp(jax.nn.gelu, gelu_pre)
    conv_out, conv_back = jax.vjp(causal_conv, input_pre, conv_weight)
    conv_bf = conv_out.astype(BF16)
    rim_send = lax.dynamic_slice_in_dim(
        conv_bf, (1 - parity) * (channels - half_block), half_block, 2
    )
    rim_recv = swapped(rim_send, "tensor")
    window = jnp.zeros((seq_count, full_length, window_width), BF16)
    window = lax.dynamic_update_slice_in_dim(window, conv_bf, parity * half_block, 2)
    window = lax.dynamic_update_slice_in_dim(window, rim_recv, (1 - parity) * channels, 2)
    tile_view = window.reshape(seq_count, full_length, window_count, block_size)
    gate_pair = jnp.stack([gate_in_w, gate_dec_w])
    placed = lax.dynamic_update_slice_in_dim(
        jnp.zeros((2, block_size, window_width), BF16), gate_pair, parity * half_block, 2
    )
    placed = placed.reshape(2, block_size, window_count, block_size)
    gate_wide = dot("slbk,gkbc->gslbc", tile_view, placed)
    gate_wide = gate_wide.reshape(2, seq_count, full_length, window_width)
    gate_own = lax.dynamic_slice_in_dim(gate_wide, parity * half_block, channels, 3)
    (log_decay, drive_in), gate_back = jax.vjp(
        decay_inputs, gate_own[0], gate_own[1], conv_bf.astype(F32), decay_rate
    )
    step_decay = jnp.exp(log_decay)
    states = recurrence(step_decay, drive_in)
    mixed = (gelu_out * states).astype(BF16)
    branch_part = dot("xgq,pq->xgp", mixed, out_w).astype(BF16)

    middle, normed_two_all, gate_w, down_w = moves.middle(
        branch_part, activations, mlp_gain, feed_gate, feed_down.T, depth
    )
    gate_w = gate_w.reshape(-1, gate_w.shape[-1])
    down_w = down_w.reshape(-1, down_w.shape[-1])
    gate_pre = dot("nwo,ob->nwb", normed_two_all, gate_w)
    lift_pre = dot("nwo,ob->nwb", normed_two_all, up_w)
    gate_act, activ_back = jax.vjp(jax.nn.gelu, gate_pre)
    hidden = (gate_act * lift_pre).astype(BF16)
    grad_hidden = dot("gre,eu->gru", cot_all, down_w)
    gate_grad = activ_back(grad_hidden * lift_pre)[0].astype(BF16)
    lift_grad = (grad_hidden * gate_act).astype(BF16)
    back_two = dot("mqa,ya->mqy", gate_grad, gate_w) + dot("mqa,ya->mqy", lift_grad, up_w)

    def weight_grad(left, right):
        total = dot("pkr,pku->ru", left, right).astype(BF16)
        return total.reshape(dp_count, -1, total.shape[-1])

    grad_down_part = weight_grad(cot_all, hidden)
    grad_gate_part = weight_grad(normed_two_all, gate_grad)
    grad_lift_part = weight_grad(normed_two_all, lift_grad)
    feed_part = dot("xav,tv->xat", hidden, down_w).astype(BF16)

    grad_middle, branch_grad_all, mlp_part, grad_down, grad_gate = moves.back(
        back_two.astype(BF16), middle, mlp_gain, scaled_cot, grad_down_part, grad_gate_part, depth
    )
    grad_mixed = dot("xtz,zm->xtm", branch_grad_all, out_w)
    grad_out_part = weight_grad(branch_grad_all, mixed)
    grad_states = grad_mixed * gelu_out
    gelu_pre_grad = gelu_back(grad_mixed * states)[0].astype(BF16)
    later = jnp.concatenate([step_decay[:, 1:], jnp.zeros_like(step_decay[:, :1])], axis=1)
    grad_drive = recurrence(later, grad_states, backward=True)
    earlier = jnp.concatenate([jnp.zeros_like(states[:, :1]), states[:, :-1]], axis=1)
    grad_log = grad_drive * step_decay * earlier
    grad_in_pre, grad_dec_pre, grad_conv_val, grad_rate = gate_back((grad_log, grad_drive))
    grad_pair = jnp.stack([grad_in_pre, grad_dec_pre]).astype(BF16)
    grad_wide = lax.dynamic_update_slice_in_dim(
        jnp.zeros((2, seq_count, full_length, window_width), BF16),
        grad_pair,
        parity * half_block,
        3,
    )
    grad_wide = grad_wide.reshape(2, seq_count, full_length, window_count, block_size)
    grad_window = dot("gslbc,gkbc->slbk", grad_wide, placed)
    grad_window = grad_window.reshape(seq_count, full_length, window_width)
    grad_placed = dot("slbk,gslbc->gkbc", tile_view, grad_wide)
    grad_placed = grad_placed.reshape(2, block_size, window_width)
    grad_gates = lax.dynamic_slice_in_dim(grad_placed, parity * half_block, channels, 2)
    rim_grad = lax.dynamic_slice_in_dim(grad_window, (1 - parity) * channels, half_block, 2)
    rim_return = swapped(rim_grad.astype(BF16), "tensor").astype(F32)
    grad_conv = grad_conv_val + lax.dynamic_slice_in_dim(
        grad_window, parity * half_block, channels, 2
    )
    rim_start = (1 - parity) * (channels - half_block)
    rim_sum = lax.dynamic_slice_in_dim(grad_conv, rim_start, half_block, 2) + rim_return
    grad_conv = lax.dynamic_update_slice_in_dim(grad_conv, rim_sum, rim_start, 2)
    input_pre_grad, grad_taps = conv_back(grad_conv)
    input_pre_grad = input_pre_grad.astype(BF16)
    grad_gelu_part = weight_grad(normed_all, gelu_pre_grad)
    grad_input_part = weight_grad(normed_all, input_pre_grad)
    back_one = dot("mzf,af->mza", gelu_pre_grad, gelu_w) + dot(
        "mzf,af->mza", input_pre_grad, input_w
    )
    gate_parts = grad_gates.astype(BF16).reshape(2, dp_count, -1, channels)
    small = jnp.concatenate([grad_rate[None], grad_taps, jnp.zeros((3, channels), F32)])

    output, input_grad, gains, small, grads = moves.last(
        back_one.astype(BF16),
        feed_part,
        activations,
        norm_gain,
        middle,
        grad_middle,
        mlp_part,
        small,
        (
            grad_gelu_part,
            grad_input_part,
            grad_out_part,
            gate_parts[0],
            gate_parts[1],
            grad_lift_part,
        ),
        depth,
    )
    return (
        output,
        input_grad,
        gains[0],
        grads[0],
        grads[1],
        small[1:5],
        grads[3],
        grads[4],
        small[0],
        grads[2].T,
        gains[1],
        grad_gate,
        grads[5],
        grad_down.T,
    )


def solution(mesh):
    placed = (
        P("dp", "tensor", None),
        P(),
        P("dp", "tensor"),
        P("dp", "tensor"),
        P(None, "tensor"),
        P("dp", "tensor"),
        P("dp", "tensor"),
        P("tensor"),
        P("tensor", "dp"),
        P(),
        P("dp", "tensor"),
        P("dp", "tensor"),
        P("tensor", "dp"),
        P("dp", "tensor", None),
        P(),
        P(),
    )
    return jax.shard_map(
        shards,
        mesh=mesh,
        in_specs=placed,
        out_specs=(
            P("dp", "tensor", None),
            P("dp", "tensor", None),
            P(),
            P("dp", "tensor"),
            P("dp", "tensor"),
            P(None, "tensor"),
            P("dp", "tensor"),
            P("dp", "tensor"),
            P("tensor"),
            P("tensor", "dp"),
            P(),
            P("dp", "tensor"),
            P("dp", "tensor"),
            P("tensor", "dp"),
        ),
        check_vma=False,
    )
```

```python
import functools

import jax
import jax.numpy as jnp
from jax import lax
from jax.experimental import pallas as pl
from jax.experimental.pallas import tpu as pltpu
from jax.sharding import PartitionSpec as P

MICRO = 4
EPS = 1e-06
MESH = pl.DeviceIdType.MESH
ANY = pl.BlockSpec(memory_space=pl.ANY)
VMEM = pl.BlockSpec(memory_space=pltpu.VMEM)
DMA = pltpu.SemaphoreType.DMA
BF16 = jnp.bfloat16
F32 = jnp.float32


def place():
    return lax.axis_index("dp"), lax.axis_index("tensor")


def greet(d, t, depth, dp_masks=(1, 2, 4), z_all=False):
    barrier = pltpu.get_barrier_semaphore()
    for mask in dp_masks:
        pl.semaphore_signal(barrier, inc=1, device_id=(d ^ mask, t), device_id_type=MESH)
    if z_all:
        for step in range(1, depth):
            pl.semaphore_signal(
                barrier, inc=1, device_id=(d, lax.rem(t + step, depth)), device_id_type=MESH
            )
        pl.semaphore_wait(barrier, len(dp_masks) + depth - 1)
        return

    @pl.when(t > 0)
    def _():
        pl.semaphore_signal(barrier, inc=1, device_id=(d, t - 1), device_id_type=MESH)

    @pl.when(t < depth - 1)
    def _():
        pl.semaphore_signal(barrier, inc=1, device_id=(d, t + 1), device_id_type=MESH)

    ends = jnp.where((t == 0) | (t == depth - 1), 1, 2)
    pl.semaphore_wait(barrier, len(dp_masks) + ends)


def add_rows(total, term, rows, step=32):
    step = min(step, rows)

    @pl.loop(0, rows, step=step)
    def _(start):
        part = pl.ds(pl.multiple_of(start, step), step)
        total[part, :] = (total[part, :].astype(F32) + term[part, :].astype(F32)).astype(BF16)


class WeightGather:
    def __init__(self, shard, out, local, send, recv, d, t):
        rows = shard.shape[0]
        half = rows // 2
        top, low = pl.ds(0, half), pl.ds(half, half)
        plan = [
            (shard.at[top], d, top, 2),
            (shard.at[low], d, low, 4),
            (shard.at[low], d, low, 2),
            (shard.at[top], d, top, 4),
            (out.at[d ^ 2, top], d ^ 2, top, 4),
            (out.at[d ^ 4, low], d ^ 4, low, 2),
            (shard.at[top], d, top, 1),
            (shard.at[low], d, low, 1),
            (out.at[d ^ 2, top], d ^ 2, top, 1),
            (out.at[d ^ 4, low], d ^ 4, low, 1),
            (out.at[d ^ 2, low], d ^ 2, low, 1),
            (out.at[d ^ 4, top], d ^ 4, top, 1),
            (out.at[d ^ 6, top], d ^ 6, top, 1),
            (out.at[d ^ 6, low], d ^ 6, low, 1),
        ]
        self.copies = [
            pltpu.make_async_remote_copy(
                src_ref=src,
                dst_ref=out.at[slot, part],
                send_sem=send.at[i],
                recv_sem=recv.at[i],
                device_id=(d ^ mask, t),
                device_id_type=MESH,
            )
            for i, (src, slot, part, mask) in enumerate(plan)
        ]
        self.own = pltpu.make_async_copy(shard, out.at[d], local)

    def start(self):
        for i in (0, 1, 2, 3, 6, 7):
            self.copies[i].start()
        self.own.start()

    def relay(self):
        c = self.copies
        c[0].wait_recv()
        c[4].start()
        c[1].wait_recv()
        c[5].start()
        c[8].start()
        c[9].start()

    def relay_two(self):
        c = self.copies
        c[2].wait_recv()
        c[10].start()
        c[3].wait_recv()
        c[11].start()

    def relay_last(self):
        c = self.copies
        c[4].wait_recv()
        c[12].start()
        c[5].wait_recv()
        c[13].start()

    def end(self):
        for i in range(6, 14):
            self.copies[i].wait_recv()
        for i in range(14):
            self.copies[i].wait_send()
        self.own.wait()


def gather_scratch(count):
    return [DMA((count,)), DMA((count, 14)), DMA((count, 14))]


class GradScatter:
    ORDER = (6, 2, 4, 0)

    def __init__(self, grad, out, own, core, diag, last, local, send, recv, d, t):
        self.out, self.own, self.core, self.diag, self.last = out, own, core, diag, last
        self.rows = rows = grad.shape[1]
        half = rows // 2
        self.half = half
        self.top, self.low = pl.ds(0, half), pl.ds(half, half)
        self.loads = [
            pltpu.make_async_copy(grad.at[d ^ r], own.at[i], local.at[i])
            for i, r in enumerate(self.ORDER)
        ]
        top, low = self.top, self.low
        plan = [(grad.at[d ^ 1 ^ r], core.at[i], 1) for i, r in enumerate(self.ORDER)] + [
            (own.at[0, top], diag.at[0], 2),
            (own.at[0, low], diag.at[1], 4),
            (own.at[1, top], last.at[0, top], 2),
            (own.at[2, low], last.at[1, low], 4),
            (own.at[2, top], last.at[1, top], 4),
            (own.at[1, low], last.at[0, low], 2),
        ]
        self.copies = [
            pltpu.make_async_remote_copy(
                src_ref=src,
                dst_ref=dst,
                send_sem=send.at[i],
                recv_sem=recv.at[i],
                device_id=(d ^ mask, t),
                device_id_type=MESH,
            )
            for i, (src, dst, mask) in enumerate(plan)
        ]

    def start(self):
        for i in range(4):
            self.copies[i].start()
            self.loads[i].start()

    def pair(self, i):
        self.loads[i].wait()
        self.copies[i].wait_recv()
        add_rows(self.own.at[i], self.core.at[i], self.rows)

    def first(self):
        self.pair(0)
        self.copies[4].start()
        self.copies[5].start()

    def second(self):
        self.pair(1)
        self.copies[6].start()
        self.pair(2)
        self.copies[7].start()
        self.pair(3)

    def third(self):
        c = self.copies
        c[4].wait_recv()
        add_rows(self.own.at[2, self.top], self.diag.at[0], self.half)
        c[8].start()
        c[5].wait_recv()
        add_rows(self.own.at[1, self.low], self.diag.at[1], self.half)
        c[9].start()

    def end(self):
        for i in (6, 7, 8, 9):
            self.copies[i].wait_recv()
        step = 16

        @pl.loop(0, self.rows, step=step)
        def _(start):
            part = pl.ds(pl.multiple_of(start, step), step)
            self.out[part, :] = (
                self.own[3, part, :].astype(F32)
                + self.last[0, part, :].astype(F32)
                + self.last[1, part, :].astype(F32)
            )

        for i in range(10):
            self.copies[i].wait_send()


def scatter_scratch(shapes):
    own = [pltpu.VMEM((4,) + s, BF16) for s in shapes]
    core = [pltpu.VMEM((4,) + s, BF16) for s in shapes]
    diag = [pltpu.VMEM((2, s[0] // 2, s[1]), BF16) for s in shapes]
    last = [pltpu.VMEM((2,) + s, BF16) for s in shapes]
    n = len(shapes)
    return own + core + diag + last + [DMA((n, 4)), DMA((n, 10)), DMA((n, 10))]


def make_scatters(grads, outs, scratch, d, t):
    n = len(grads)
    own, core, diag, last = (scratch[i * n : (i + 1) * n] for i in range(4))
    local, send, recv = scratch[4 * n :]
    return [
        GradScatter(
            grads[i],
            outs[i],
            own[i],
            core[i],
            diag[i],
            last[i],
            local.at[i],
            send.at[i],
            recv.at[i],
            d,
            t,
        )
        for i in range(n)
    ]


class LineGather:
    def __init__(self, block, out, local, send, recv, d, t, depth):
        self.block, self.out, self.send, self.recv = block, out, send, recv
        self.d, self.t, self.depth = d, t, depth
        self.rows = block.shape[1]
        self.own = pltpu.make_async_copy(block, self.slot(t), local)

    def slot(self, j):
        return self.out.at[:, pl.ds(pl.multiple_of(j * self.rows, self.rows), self.rows)]

    def copy(self, way, step, j, to):
        return pltpu.make_async_remote_copy(
            src_ref=self.block if step == 0 else self.slot(j),
            dst_ref=self.slot(j),
            send_sem=self.send.at[way, step],
            recv_sem=self.recv.at[way, step],
            device_id=(self.d, to),
            device_id_type=MESH,
        )

    def step(self, s):
        t, depth = self.t, self.depth
        if s == 0:
            self.own.start()
        if s > 0:

            @pl.when(t - s >= 0)
            def _():
                self.copy(0, s - 1, t, t).wait_recv()

        if s < depth - 1:

            @pl.when((t - s >= 0) & (t < depth - 1))
            def _():
                self.copy(0, s, t - s, t + 1).start()

        if s > 0:

            @pl.when(t + s < depth)
            def _():
                self.copy(1, s - 1, t, t).wait_recv()

        if s < depth - 1:

            @pl.when((t + s < depth) & (t > 0))
            def _():
                self.copy(1, s, t + s, t - 1).start()

    def end(self):
        t, depth = self.t, self.depth
        for s in range(depth - 1):

            @pl.when((t - s >= 0) & (t < depth - 1))
            def _():
                self.copy(0, s, t, t).wait_send()

            @pl.when((t + s < depth) & (t > 0))
            def _():
                self.copy(1, s, t, t).wait_send()

        self.own.wait()


def line_gather_scratch(depth):
    return [DMA, DMA((2, depth - 1)), DMA((2, depth - 1))]


class LineScatter:
    def __init__(self, part, got, send, recv, d, t, depth):
        self.part, self.got, self.send, self.recv = part, got, send, recv
        self.d, self.t, self.depth = d, t, depth
        self.seqs = part.shape[0]
        self.rows = part.shape[1] // depth

    def copy(self, way, j, s, src, to):
        return pltpu.make_async_remote_copy(
            src_ref=src,
            dst_ref=self.got.at[way, j, s],
            send_sem=self.send.at[way, j, s],
            recv_sem=self.recv.at[way, j, s],
            device_id=(self.d, to),
            device_id_type=MESH,
        )

    def block(self, j, s):
        return self.part.at[s, pl.ds(pl.multiple_of(j * self.rows, self.rows), self.rows)]

    def start(self):
        t, depth = self.t, self.depth

        @pl.when(t == 0)
        def _():
            for j in range(depth - 1, 0, -1):
                for s in range(self.seqs):
                    self.copy(0, j, s, self.block(j, s), t + 1).start()

        @pl.when(t == depth - 1)
        def _():
            for j in range(depth - 1):
                for s in range(self.seqs):
                    self.copy(1, j, s, self.block(j, s), t - 1).start()

    def pass_on(self, way, j, to):
        for s in range(self.seqs):
            mine = self.got.at[way, j, s]
            self.copy(way, j, s, mine, self.t).wait_recv()
            add_rows(mine, self.block(j, s), self.rows)
            self.copy(way, j, s, mine, to).start()

    def step(self, k):
        t, depth = self.t, self.depth
        right = depth - 1 - k + t
        left = k - (depth - 1 - t)

        @pl.when((t > 0) & (t < right) & (right < depth))
        def _():
            self.pass_on(0, right, t + 1)

        @pl.when((left >= 0) & (left < t) & (t < depth - 1))
        def _():
            self.pass_on(1, left, t - 1)

    def total(self, out):
        t, depth = self.t, self.depth
        mine = pl.ds(pl.multiple_of(t * self.rows, self.rows), self.rows)
        out[...] = self.part[:, mine, :].astype(F32)

        @pl.when(t > 0)
        def _():
            for s in range(self.seqs):
                self.copy(0, t, s, self.got.at[0, t, s], t).wait_recv()
            out[...] += self.got[0, t].astype(F32)

        @pl.when(t < depth - 1)
        def _():
            for s in range(self.seqs):
                self.copy(1, t, s, self.got.at[1, t, s], t).wait_recv()
            out[...] += self.got[1, t].astype(F32)

    def end(self):
        t, depth = self.t, self.depth
        for j in range(depth):
            for s in range(self.seqs):
                mine = self.got.at[0, j, s]

                @pl.when((j > t) & (t < depth - 1))
                def _():
                    self.copy(0, j, s, mine, t).wait_send()

                @pl.when((j < t) & (t > 0))
                def _():
                    self.copy(1, j, s, mine, t).wait_send()


def line_scatter_scratch(seqs, rows, width, depth):
    return [
        pltpu.VMEM((2, depth, seqs, rows, width), BF16),
        DMA((2, depth, seqs)),
        DMA((2, depth, seqs)),
    ]


def call(kernel, name, number, ins, outs, scratch, args, vmem=60 * 1024 * 1024):
    return pl.pallas_call(
        kernel,
        name=name,
        out_shape=[o[0] for o in outs],
        in_specs=ins,
        out_specs=[o[1] for o in outs],
        scratch_shapes=scratch,
        compiler_params=pltpu.CompilerParams(
            collective_id=number, has_side_effects=True, vmem_limit_bytes=vmem
        ),
    )(*args)


def shaped(shape, dtype, spec):
    return (jax.ShapeDtypeStruct(shape, dtype), spec)


def gather_kernel(depth, n_weights, *refs):
    blocks = refs[:2]
    shards = refs[2 : 2 + n_weights]
    outs = refs[2 + n_weights :]
    wide, full = outs[:2], outs[2 : 2 + n_weights]
    scratch = outs[2 + n_weights :]
    d, t = place()
    greet(d, t, depth)
    local, send, recv = scratch[:3]
    lines = [
        LineGather(blocks[i], wide[i], *scratch[3 + 3 * i : 6 + 3 * i], d, t, depth)
        for i in range(2)
    ]
    gathers = [
        WeightGather(shards[i], full[i], local.at[i], send.at[i], recv.at[i], d, t)
        for i in range(n_weights)
    ]
    one, two, three = gathers[:-2], gathers[-2], gathers[-1]
    lines[0].step(0)
    for g in one:
        g.start()
    lines[1].step(0)
    for g in one:
        g.relay()
    two.start()
    lines[0].step(1)
    for g in one:
        g.relay_two()
    for g in one:
        g.relay_last()
    lines[1].step(1)
    two.relay()
    three.start()
    two.relay_two()
    two.relay_last()
    lines[0].step(2)
    three.relay()
    lines[1].step(2)
    three.relay_two()
    lines[0].step(3)
    three.relay_last()
    lines[1].step(3)
    for g in gathers:
        g.end()
    for line in lines:
        line.end()


def gather_first(normed, cot, weights, depth):
    seqs, rows, width = normed.shape
    n = len(weights)
    outs = [shaped((seqs, rows * depth, width), BF16, ANY)] * 2
    outs += [shaped((8,) + w.shape, BF16, ANY) for w in weights]
    scratch = gather_scratch(n) + line_gather_scratch(depth) * 2
    res = call(
        functools.partial(gather_kernel, depth, n),
        "gather_first",
        0,
        [VMEM] * (2 + n),
        outs,
        scratch,
        (normed, cot) + tuple(weights),
    )
    return res[0], res[1], res[2:]


def middle_kernel(depth, part, act, gain, w0, w1, middle, wide, f0, f1, *scratch):
    local, send, recv = scratch[:3]
    got, ssem, rsem = scratch[3:6]
    block = scratch[6]
    lsem = scratch[7:10]
    d, t = place()
    greet(d, t, depth)
    gathers = [
        WeightGather(w, f, local.at[i], send.at[i], recv.at[i], d, t)
        for i, (w, f) in enumerate(((w0, f0), (w1, f1)))
    ]
    scatter = LineScatter(part, got, ssem, rsem, d, t, depth)
    scatter.start()
    gathers[0].start()
    gathers[0].relay()
    gathers[1].start()
    scatter.step(1)
    gathers[0].relay_two()
    scatter.step(2)
    gathers[0].relay_last()
    scatter.total(middle)
    seqs, rows, width = act.shape
    for s in range(seqs):
        value = middle[s] + act[s].astype(F32)
        middle[s] = value
        inverse = lax.rsqrt(jnp.mean(value * value, axis=-1, keepdims=True) + EPS)
        block[s] = (value * inverse * gain[...]).astype(BF16)
    line = LineGather(block, wide, *lsem, d, t, depth)
    line.step(0)
    gathers[1].relay()
    line.step(1)
    gathers[1].relay_two()
    line.step(2)
    gathers[1].relay_last()
    line.step(3)
    for g in gathers:
        g.end()
    scatter.end()
    line.end()


def middle_phase(part, act, gain, w0, w1, depth):
    seqs, rows, width = act.shape
    outs = [
        shaped(act.shape, F32, VMEM),
        shaped((seqs, rows * depth, width), BF16, ANY),
        shaped((8,) + w0.shape, BF16, ANY),
        shaped((8,) + w1.shape, BF16, ANY),
    ]
    scratch = (
        gather_scratch(2)
        + line_scatter_scratch(seqs, rows, width, depth)
        + [pltpu.VMEM(act.shape, BF16)]
        + line_gather_scratch(depth)
    )
    return call(
        functools.partial(middle_kernel, depth),
        "middle_phase",
        1,
        [VMEM] * 5,
        outs,
        scratch,
        (part, act, gain.reshape(1, width), w0, w1),
    )


def norm_back(value, gain, error):
    inverse = lax.rsqrt(jnp.mean(value * value, axis=-1, keepdims=True) + EPS)
    scaled = error * gain
    mean = jnp.mean(scaled * value, axis=-1, keepdims=True)
    grad = inverse * scaled - value * (inverse * inverse * inverse * mean)
    return grad, jnp.sum(error * value * inverse, axis=0, keepdims=True)


def back_kernel(depth, part, middle, gain, cot, g0, g1, grad, wide, gain_grad, o0, o1, *scratch):
    got, ssem, rsem = scratch[:3]
    block = scratch[3]
    lsem = scratch[4:7]
    d, t = place()
    greet(d, t, depth)
    scatters = make_scatters((g0, g1), (o0, o1), scratch[7:], d, t)
    scatter = LineScatter(part, got, ssem, rsem, d, t, depth)
    scatter.start()
    for g in scatters:
        g.start()
    scatters[0].first()
    scatters[0].second()
    scatter.step(1)
    scatters[0].third()
    scatter.step(2)
    scatters[1].first()
    scatters[1].second()
    scatter.total(grad)
    seqs, rows, width = middle.shape
    for s in range(seqs):
        change, gain_part = norm_back(middle[s], gain[...], grad[s])
        change = change + cot[s]
        grad[s] = change
        block[s] = change.astype(BF16)
        if s == 0:
            gain_grad[...] = gain_part
        else:
            gain_grad[...] += gain_part
    line = LineGather(block, wide, *lsem, d, t, depth)
    line.step(0)
    scatters[0].end()
    line.step(1)
    scatters[1].third()
    line.step(2)
    line.step(3)
    scatters[1].end()
    scatter.end()
    line.end()


def back_phase(part, middle, gain, cot, g0, g1, depth):
    seqs, rows, width = middle.shape
    shapes = [g0.shape[1:], g1.shape[1:]]
    outs = [
        shaped(middle.shape, F32, VMEM),
        shaped((seqs, rows * depth, width), BF16, ANY),
        shaped((1, width), F32, VMEM),
        shaped(shapes[0], F32, VMEM),
        shaped(shapes[1], F32, VMEM),
    ]
    scratch = (
        line_scatter_scratch(seqs, rows, width, depth)
        + [pltpu.VMEM(middle.shape, BF16)]
        + line_gather_scratch(depth)
        + scatter_scratch(shapes)
    )
    return call(
        functools.partial(back_kernel, depth),
        "back_phase",
        2,
        [VMEM, VMEM, VMEM, VMEM, ANY, ANY],
        outs,
        scratch,
        (part, middle, gain.reshape(1, width), cot, g0, g1),
    )


def last_kernel(depth, n_grads, part, feed, act, gain, middle, grad_middle, mlp_part, small, *refs):
    grads = refs[:n_grads]
    refs = refs[n_grads:]
    output, input_grad, gains, smalls = refs[:4]
    outs = refs[4 : 4 + n_grads]
    scratch = refs[4 + n_grads :]
    got0, ssem0, rsem0, got1, ssem1, rsem1 = scratch[:6]
    pack, packs, small_all, line_pack, line_packs = scratch[6:11]
    psend, precv, qsend, qrecv, zsend, zrecv = scratch[11:17]
    total = scratch[17]
    d, t = place()
    greet(d, t, depth, dp_masks=(1, 2, 3, 4, 5, 6, 7), z_all=True)
    scatters = make_scatters(grads, outs, scratch[18:], d, t)
    first = LineScatter(part, got0, ssem0, rsem0, d, t, depth)
    second = LineScatter(feed, got1, ssem1, rsem1, d, t, depth)

    def dp_copies(src, dst, send, recv):
        return [
            pltpu.make_async_remote_copy(
                src_ref=src,
                dst_ref=dst.at[d],
                send_sem=send.at[mask - 1],
                recv_sem=recv.at[mask - 1],
                device_id=(d ^ mask, t),
                device_id_type=MESH,
            )
            for mask in range(1, 8)
        ]

    small_copies = dp_copies(small, small_all, qsend, qrecv)
    for c in small_copies:
        c.start()
    big, rest = scatters[-1], scatters[:-1]
    first.start()
    big.start()
    second.start()
    for g in rest:
        g.start()
    big.first()
    big.second()
    first.step(1)
    big.third()
    first.step(2)
    for g in rest:
        g.first()
    for g in rest:
        g.second()
    first.total(input_grad)
    seqs = act.shape[0]
    quarter = pack.shape[1]
    for i in range(4):
        pack[4 + i : 5 + i, :] = mlp_part[:, i * quarter : (i + 1) * quarter]
    for s in range(seqs):
        change, gain_part = norm_back(act[s].astype(F32), gain[...], input_grad[s])
        input_grad[s] = change + grad_middle[s]
        for i in range(4):
            piece = gain_part[:, i * quarter : (i + 1) * quarter]
            if s == 0:
                pack[i : i + 1, :] = piece
            else:
                pack[i : i + 1, :] += piece
    pack_copies = dp_copies(pack, packs, psend, precv)
    for c in pack_copies:
        c.start()
    big.end()
    packs[d] = pack[...]
    small_all[d] = small[...]
    second.step(1)
    for g in rest:
        g.third()
    for c in pack_copies:
        c.wait_recv()
    sum_ = packs[0]
    for i in range(1, 8):
        sum_ = sum_ + packs[i]
    line_pack[...] = sum_
    z_copies = [
        pltpu.make_async_remote_copy(
            src_ref=line_pack,
            dst_ref=line_packs.at[t],
            send_sem=zsend.at[step - 1],
            recv_sem=zrecv.at[step - 1],
            device_id=(d, lax.rem(t + step, depth)),
            device_id_type=MESH,
        )
        for step in range(1, depth)
    ]
    second.step(2)
    for c in z_copies:
        c.start()
    line_packs[t] = sum_
    for g in rest:
        g.end()
    second.total(total)
    output[...] = (total[...] + middle[...]).astype(BF16)
    for c in small_copies:
        c.wait_recv()
    sum_ = small_all[0]
    for i in range(1, 8):
        sum_ = sum_ + small_all[i]
    smalls[...] = sum_
    for c in z_copies:
        c.wait_recv()
    sum_ = line_packs[0]
    for i in range(1, depth):
        sum_ = sum_ + line_packs[i]
    gains[...] = sum_
    for c in small_copies + pack_copies + z_copies:
        c.wait_send()
    first.end()
    second.end()


def last_phase(part, feed, act, gain, middle, grad_middle, mlp_part, small, grads, depth):
    seqs, rows, width = act.shape
    n = len(grads)
    shapes = [g.shape[1:] for g in grads]
    outs = [
        shaped(act.shape, BF16, VMEM),
        shaped(act.shape, F32, VMEM),
        shaped((8, width // 4), F32, VMEM),
        shaped(small.shape, F32, VMEM),
    ] + [shaped(s, F32, VMEM) for s in shapes]
    scratch = (
        line_scatter_scratch(seqs, rows, width, depth) * 2
        + [
            pltpu.VMEM((8, width // 4), F32),
            pltpu.VMEM((8, 8, width // 4), F32),
            pltpu.VMEM((8,) + small.shape, F32),
            pltpu.VMEM((8, width // 4), F32),
            pltpu.VMEM((depth, 8, width // 4), F32),
        ]
        + [DMA((7,))] * 4
        + [DMA((depth - 1,))] * 2
        + [pltpu.VMEM(act.shape, F32)]
        + scatter_scratch(shapes)
    )
    res = call(
        functools.partial(last_kernel, depth, n),
        "last_phase",
        3,
        [VMEM] * 8 + [ANY] * n,
        outs,
        scratch,
        (part, feed, act, gain.reshape(1, width), middle, grad_middle, mlp_part, small)
        + tuple(grads),
    )
    return res[0], res[1], res[2].reshape(2, width), res[3], res[4:]


def scan_kernel(backward, rate_ref, drive_ref, out_ref):
    seqs, length, width = rate_ref.shape
    tile = 8
    row = lax.broadcasted_iota(jnp.int32, (tile, width), 0)

    def body(i, carried):
        k = length // tile - 1 - i if backward else i
        rows = pl.ds(pl.multiple_of(k * tile, tile), tile)
        ends = []
        for s in range(seqs):
            rate = rate_ref[s, rows, :]
            drive = drive_ref[s, rows, :]
            for shift in (1, 2, 4):
                turn = tile - shift if backward else shift
                inside = row < tile - shift if backward else row >= shift
                before = jnp.where(inside, pltpu.roll(drive, turn, 0), 0.0)
                drive = drive + rate * before
                rate = rate * jnp.where(inside, pltpu.roll(rate, turn, 0), 1.0)
            states = drive + rate * carried[s]
            out_ref[s, rows, :] = states
            ends.append(states[0:1] if backward else states[tile - 1 : tile])
        return tuple(ends)

    start = tuple(jnp.zeros((1, width), F32) for _ in range(seqs))
    lax.fori_loop(0, length // tile, body, start)


def recurrence(rate, drive, backward=False):
    return pl.pallas_call(
        functools.partial(scan_kernel, backward),
        name="recurrence",
        out_shape=jax.ShapeDtypeStruct(drive.shape, F32),
        in_specs=[VMEM, VMEM],
        out_specs=VMEM,
        compiler_params=pltpu.CompilerParams(vmem_limit_bytes=32 * 1024 * 1024),
    )(rate, drive)


def swapped(block, axis):
    count = lax.axis_size(axis)
    return lax.ppermute(block, axis, [(i, i ^ 1) for i in range(count)])


def normalize(value_entries, scale_gain):
    return (
        value_entries
        * lax.rsqrt(jnp.mean(value_entries * value_entries, axis=-1, keepdims=True) + EPS)
        * scale_gain
    )


def causal_conv(value_entries, kernel):
    summed = value_entries * kernel[0]
    for offset in range(1, kernel.shape[0]):
        shifted = jnp.concatenate(
            [jnp.zeros_like(value_entries[:, :offset]), value_entries[:, :-offset]], axis=1
        )
        summed = summed + shifted * kernel[offset]
    return summed


def decay_inputs(input_pre, decay_pre, conv_vals, decay_rate):
    log_decay = -8.0 * jax.nn.sigmoid(decay_pre) * decay_rate
    scaled = jnp.sqrt(-jnp.expm1(2.0 * log_decay))
    return (log_decay, scaled * jax.nn.sigmoid(input_pre) * conv_vals)


class Fast:
    @staticmethod
    def first(normed, cot, weights, depth):
        return gather_first(normed, cot, weights, depth)

    middle = staticmethod(middle_phase)
    back = staticmethod(back_phase)
    last = staticmethod(last_phase)


class Plain:
    @staticmethod
    def wide(block):
        return lax.all_gather(block, "tensor", axis=1, tiled=True)

    @staticmethod
    def narrow(part):
        return lax.psum_scatter(part, "tensor", scatter_dimension=1, tiled=True).astype(F32)

    @staticmethod
    def full(shard):
        return lax.all_gather(shard, "dp", axis=0, tiled=False)

    @staticmethod
    def own(grad):
        return lax.psum_scatter(grad, "dp", scatter_dimension=0, tiled=False).astype(F32)

    @classmethod
    def first(cls, normed, cot, weights, depth):
        return cls.wide(normed), cls.wide(cot), [cls.full(w) for w in weights]

    @classmethod
    def middle(cls, part, act, gain, w0, w1, depth):
        middle = act.astype(F32) + cls.narrow(part)
        wide = cls.wide(normalize(middle, gain).astype(BF16))
        return middle, wide, cls.full(w0), cls.full(w1)

    @classmethod
    def back(cls, part, middle, gain, cot, g0, g1, depth):
        _, back = jax.vjp(normalize, middle, gain)
        change, gain_grad = back(cls.narrow(part))
        grad = cot + change
        return grad, cls.wide(grad.astype(BF16)), gain_grad[None], cls.own(g0), cls.own(g1)

    @classmethod
    def last(cls, part, feed, act, gain, middle, grad_middle, mlp_part, small, grads, depth):
        _, back = jax.vjp(normalize, act.astype(F32), gain)
        change, gain_grad = back(cls.narrow(part))
        output = (middle + cls.narrow(feed)).astype(BF16)
        gains = lax.psum(jnp.concatenate([gain_grad[None], mlp_part]), ("dp", "tensor"))
        small = lax.psum(small, "dp")
        return output, grad_middle + change, gains, small, [cls.own(g) for g in grads]


def dot(spec, left, right):
    return jnp.einsum(spec, left, right, preferred_element_type=F32)


def shards(
    activations,
    norm_gain,
    gelu_proj,
    input_proj,
    conv_weight,
    gate_input,
    gate_decay,
    decay_rate,
    out_proj,
    mlp_gain,
    feed_gate,
    feed_up,
    feed_down,
    cotangent,
    lengths,
    batch_of,
):
    depth = lax.axis_size("tensor")
    dp_count = lax.axis_size("dp")
    moves = Fast if dp_count == 8 and depth == 4 else Plain
    tensor_index = lax.axis_index("tensor")
    data_index = lax.axis_index("dp")
    seq_count, row_count, model_width = activations.shape
    full_length = row_count * depth
    members = (batch_of[:, None] == jnp.arange(MICRO)[None, :]).astype(F32)
    counts = jnp.sum(members * lengths[:, None].astype(F32), axis=0)
    total_seqs = lengths.shape[0]
    per_batch = float(total_seqs * full_length) / (MICRO * counts)
    weight_all = jnp.sum(members * per_batch[None, :], axis=1)
    my_weight = lax.dynamic_slice_in_dim(weight_all, data_index * seq_count, seq_count)
    my_length = lax.dynamic_slice_in_dim(lengths, data_index * seq_count, seq_count)
    places = tensor_index * row_count + jnp.arange(row_count)
    valid_mask = (places[None, :] < my_length[:, None]).astype(F32)
    scaled_cot = cotangent.astype(F32) * (valid_mask * my_weight[:, None])[:, :, None]
    normed = normalize(activations.astype(F32), norm_gain).astype(BF16)

    normed_all, cot_all, weights = moves.first(
        normed,
        scaled_cot.astype(BF16),
        (gelu_proj, input_proj, gate_input, gate_decay, out_proj.T, feed_up),
        depth,
    )
    gelu_w, input_w, gate_in_w, gate_dec_w, out_w, up_w = (
        w.reshape(-1, w.shape[-1]) for w in weights
    )
    channels = gelu_w.shape[1]
    block_size = gate_in_w.shape[0]
    half_block = block_size // 2
    window_width = channels + half_block
    window_count = window_width // block_size
    parity = tensor_index % 2

    gelu_pre = dot("kqg,ga->kqa", normed_all, gelu_w)
    input_pre = dot("kqg,ga->kqa", normed_all, input_w)
    gelu_out, gelu_back = jax.vjp(jax.nn.gelu, gelu_pre)
    conv_out, conv_back = jax.vjp(causal_conv, input_pre, conv_weight)
    conv_bf = conv_out.astype(BF16)
    rim_send = lax.dynamic_slice_in_dim(
        conv_bf, (1 - parity) * (channels - half_block), half_block, 2
    )
    rim_recv = swapped(rim_send, "tensor")
    window = jnp.zeros((seq_count, full_length, window_width), BF16)
    window = lax.dynamic_update_slice_in_dim(window, conv_bf, parity * half_block, 2)
    window = lax.dynamic_update_slice_in_dim(window, rim_recv, (1 - parity) * channels, 2)
    tile_view = window.reshape(seq_count, full_length, window_count, block_size)
    gate_pair = jnp.stack([gate_in_w, gate_dec_w])
    placed = lax.dynamic_update_slice_in_dim(
        jnp.zeros((2, block_size, window_width), BF16), gate_pair, parity * half_block, 2
    )
    placed = placed.reshape(2, block_size, window_count, block_size)
    gate_wide = dot("slbk,gkbc->gslbc", tile_view, placed)
    gate_wide = gate_wide.reshape(2, seq_count, full_length, window_width)
    gate_own = lax.dynamic_slice_in_dim(gate_wide, parity * half_block, channels, 3)
    (log_decay, drive_in), gate_back = jax.vjp(
        decay_inputs, gate_own[0], gate_own[1], conv_bf.astype(F32), decay_rate
    )
    step_decay = jnp.exp(log_decay)
    states = recurrence(step_decay, drive_in)
    mixed = (gelu_out * states).astype(BF16)
    branch_part = dot("xgq,pq->xgp", mixed, out_w).astype(BF16)

    middle, normed_two_all, gate_w, down_w = moves.middle(
        branch_part, activations, mlp_gain, feed_gate, feed_down.T, depth
    )
    gate_w = gate_w.reshape(-1, gate_w.shape[-1])
    down_w = down_w.reshape(-1, down_w.shape[-1])
    gate_pre = dot("nwo,ob->nwb", normed_two_all, gate_w)
    lift_pre = dot("nwo,ob->nwb", normed_two_all, up_w)
    gate_act, activ_back = jax.vjp(jax.nn.gelu, gate_pre)
    hidden = (gate_act * lift_pre).astype(BF16)
    grad_hidden = dot("gre,eu->gru", cot_all, down_w)
    gate_grad = activ_back(grad_hidden * lift_pre)[0].astype(BF16)
    lift_grad = (grad_hidden * gate_act).astype(BF16)
    back_two = dot("mqa,ya->mqy", gate_grad, gate_w) + dot("mqa,ya->mqy", lift_grad, up_w)

    def weight_grad(left, right):
        total = dot("pkr,pku->ru", left, right).astype(BF16)
        return total.reshape(dp_count, -1, total.shape[-1])

    grad_down_part = weight_grad(cot_all, hidden)
    grad_gate_part = weight_grad(normed_two_all, gate_grad)
    grad_lift_part = weight_grad(normed_two_all, lift_grad)
    feed_part = dot("xav,tv->xat", hidden, down_w).astype(BF16)

    grad_middle, branch_grad_all, mlp_part, grad_down, grad_gate = moves.back(
        back_two.astype(BF16), middle, mlp_gain, scaled_cot, grad_down_part, grad_gate_part, depth
    )
    grad_mixed = dot("xtz,zm->xtm", branch_grad_all, out_w)
    grad_out_part = weight_grad(branch_grad_all, mixed)
    grad_states = grad_mixed * gelu_out
    gelu_pre_grad = gelu_back(grad_mixed * states)[0].astype(BF16)
    later = jnp.concatenate([step_decay[:, 1:], jnp.zeros_like(step_decay[:, :1])], axis=1)
    grad_drive = recurrence(later, grad_states, backward=True)
    earlier = jnp.concatenate([jnp.zeros_like(states[:, :1]), states[:, :-1]], axis=1)
    grad_log = grad_drive * step_decay * earlier
    grad_in_pre, grad_dec_pre, grad_conv_val, grad_rate = gate_back((grad_log, grad_drive))
    grad_pair = jnp.stack([grad_in_pre, grad_dec_pre]).astype(BF16)
    grad_wide = lax.dynamic_update_slice_in_dim(
        jnp.zeros((2, seq_count, full_length, window_width), BF16),
        grad_pair,
        parity * half_block,
        3,
    )
    grad_wide = grad_wide.reshape(2, seq_count, full_length, window_count, block_size)
    grad_window = dot("gslbc,gkbc->slbk", grad_wide, placed)
    grad_window = grad_window.reshape(seq_count, full_length, window_width)
    grad_placed = dot("slbk,gslbc->gkbc", tile_view, grad_wide)
    grad_placed = grad_placed.reshape(2, block_size, window_width)
    grad_gates = lax.dynamic_slice_in_dim(grad_placed, parity * half_block, channels, 2)
    rim_grad = lax.dynamic_slice_in_dim(grad_window, (1 - parity) * channels, half_block, 2)
    rim_return = swapped(rim_grad.astype(BF16), "tensor").astype(F32)
    grad_conv = grad_conv_val + lax.dynamic_slice_in_dim(
        grad_window, parity * half_block, channels, 2
    )
    rim_start = (1 - parity) * (channels - half_block)
    rim_sum = lax.dynamic_slice_in_dim(grad_conv, rim_start, half_block, 2) + rim_return
    grad_conv = lax.dynamic_update_slice_in_dim(grad_conv, rim_sum, rim_start, 2)
    input_pre_grad, grad_taps = conv_back(grad_conv)
    input_pre_grad = input_pre_grad.astype(BF16)
    grad_gelu_part = weight_grad(normed_all, gelu_pre_grad)
    grad_input_part = weight_grad(normed_all, input_pre_grad)
    back_one = dot("mzf,af->mza", gelu_pre_grad, gelu_w) + dot(
        "mzf,af->mza", input_pre_grad, input_w
    )
    gate_parts = grad_gates.astype(BF16).reshape(2, dp_count, -1, channels)
    small = jnp.concatenate([grad_rate[None], grad_taps, jnp.zeros((3, channels), F32)])

    output, input_grad, gains, small, grads = moves.last(
        back_one.astype(BF16),
        feed_part,
        activations,
        norm_gain,
        middle,
        grad_middle,
        mlp_part,
        small,
        (
            grad_gelu_part,
            grad_input_part,
            grad_out_part,
            gate_parts[0],
            gate_parts[1],
            grad_lift_part,
        ),
        depth,
    )
    return (
        output,
        input_grad,
        gains[0],
        grads[0],
        grads[1],
        small[1:5],
        grads[3],
        grads[4],
        small[0],
        grads[2].T,
        gains[1],
        grad_gate,
        grads[5],
        grad_down.T,
    )


def solution(mesh):
    placed = (
        P("dp", "tensor", None),
        P(),
        P("dp", "tensor"),
        P("dp", "tensor"),
        P(None, "tensor"),
        P("dp", "tensor"),
        P("dp", "tensor"),
        P("tensor"),
        P("tensor", "dp"),
        P(),
        P("dp", "tensor"),
        P("dp", "tensor"),
        P("tensor", "dp"),
        P("dp", "tensor", None),
        P(),
        P(),
    )
    return jax.shard_map(
        shards,
        mesh=mesh,
        in_specs=placed,
        out_specs=(
            P("dp", "tensor", None),
            P("dp", "tensor", None),
            P(),
            P("dp", "tensor"),
            P("dp", "tensor"),
            P(None, "tensor"),
            P("dp", "tensor"),
            P("dp", "tensor"),
            P("tensor"),
            P("tensor", "dp"),
            P(),
            P("dp", "tensor"),
            P("dp", "tensor"),
            P("tensor", "dp"),
        ),
        check_vma=False,
    )
```

```python
import functools

import jax
import jax.numpy as jnp
from jax import lax
from jax.experimental import pallas as pl
from jax.experimental.pallas import tpu as pltpu
from jax.sharding import PartitionSpec as P

MICRO = 4
EPS = 1e-06
MESH = pl.DeviceIdType.MESH
ANY = pl.BlockSpec(memory_space=pl.ANY)
VMEM = pl.BlockSpec(memory_space=pltpu.VMEM)
DMA = pltpu.SemaphoreType.DMA
BF16 = jnp.bfloat16
F32 = jnp.float32


def place():
    return lax.axis_index("dp"), lax.axis_index("tensor")


def greet(d, t, depth, dp_masks=(1, 2, 4), z_all=False):
    barrier = pltpu.get_barrier_semaphore()
    for mask in dp_masks:
        pl.semaphore_signal(barrier, inc=1, device_id=(d ^ mask, t), device_id_type=MESH)
    if z_all:
        for step in range(1, depth):
            pl.semaphore_signal(
                barrier, inc=1, device_id=(d, lax.rem(t + step, depth)), device_id_type=MESH
            )
        pl.semaphore_wait(barrier, len(dp_masks) + depth - 1)
        return

    @pl.when(t > 0)
    def _():
        pl.semaphore_signal(barrier, inc=1, device_id=(d, t - 1), device_id_type=MESH)

    @pl.when(t < depth - 1)
    def _():
        pl.semaphore_signal(barrier, inc=1, device_id=(d, t + 1), device_id_type=MESH)

    ends = jnp.where((t == 0) | (t == depth - 1), 1, 2)
    pl.semaphore_wait(barrier, len(dp_masks) + ends)


def add_rows(total, term, rows, step=32):
    step = min(step, rows)

    @pl.loop(0, rows, step=step)
    def _(start):
        part = pl.ds(pl.multiple_of(start, step), step)
        total[part, :] = (total[part, :].astype(F32) + term[part, :].astype(F32)).astype(BF16)


class WeightGather:
    def __init__(self, shard, out, local, send, recv, d, t):
        rows = shard.shape[0]
        half = rows // 2

        def view(slot, start, size):
            if len(out.shape) == 3:
                return out.at[slot, pl.ds(start, size)]
            return out.at[pl.ds(pl.multiple_of(slot * rows + start, 16), size)]

        top, low = (0, half), (half, half)
        plan = [
            (None, d, top, 2),
            (None, d, low, 4),
            (None, d, low, 2),
            (None, d, top, 4),
            (2, d ^ 2, top, 4),
            (4, d ^ 4, low, 2),
            (None, d, top, 1),
            (None, d, low, 1),
            (2, d ^ 2, top, 1),
            (4, d ^ 4, low, 1),
            (2, d ^ 2, low, 1),
            (4, d ^ 4, top, 1),
            (6, d ^ 6, top, 1),
            (6, d ^ 6, low, 1),
        ]
        self.copies = [
            pltpu.make_async_remote_copy(
                src_ref=shard.at[pl.ds(*part)] if came is None else view(slot, *part),
                dst_ref=view(slot, *part),
                send_sem=send.at[i],
                recv_sem=recv.at[i],
                device_id=(d ^ mask, t),
                device_id_type=MESH,
            )
            for i, (came, slot, part, mask) in enumerate(plan)
        ]
        self.own = pltpu.make_async_copy(shard, view(d, 0, rows), local)

    def start(self):
        for i in (0, 1, 2, 3, 6, 7):
            self.copies[i].start()
        self.own.start()

    def relay(self):
        c = self.copies
        c[0].wait_recv()
        c[4].start()
        c[1].wait_recv()
        c[5].start()
        c[8].start()
        c[9].start()

    def relay_two(self):
        c = self.copies
        c[2].wait_recv()
        c[10].start()
        c[3].wait_recv()
        c[11].start()

    def relay_last(self):
        c = self.copies
        c[4].wait_recv()
        c[12].start()
        c[5].wait_recv()
        c[13].start()

    def arrive(self):
        for i in range(6, 14):
            self.copies[i].wait_recv()
        self.own.wait()

    def end(self):
        for i in range(14):
            self.copies[i].wait_send()


def gather_scratch(count):
    return [DMA((count,)), DMA((count, 14)), DMA((count, 14))]


class GradScatter:
    ORDER = (6, 2, 4, 0)

    def __init__(self, grad, out, own, core, diag, last, local, send, recv, d, t):
        self.out, self.core, self.diag, self.last = out, core, diag, last
        self.rows = rows = out.shape[0]
        half = rows // 2
        self.half = half
        self.top, self.low = pl.ds(0, half), pl.ds(half, half)

        def block(slot, start=0, size=rows):
            return grad.at[pl.ds(pl.multiple_of(slot * rows + start, 16), size)]

        if own is None:
            self.loads = []
            self.mine = lambda i, start=0, size=rows: block(d ^ self.ORDER[i], start, size)
        else:
            self.loads = [
                pltpu.make_async_copy(block(d ^ r), own.at[i], local.at[i])
                for i, r in enumerate(self.ORDER)
            ]
            self.mine = lambda i, start=0, size=rows: own.at[i, pl.ds(start, size)]
        mine, top, low = self.mine, self.top, self.low
        plan = [(block(d ^ 1 ^ r), core.at[i], 1) for i, r in enumerate(self.ORDER)] + [
            (mine(0, 0, half), diag.at[0], 2),
            (mine(0, half, half), diag.at[1], 4),
            (mine(1, 0, half), last.at[0, top], 2),
            (mine(2, half, half), last.at[1, low], 4),
            (mine(2, 0, half), last.at[1, top], 4),
            (mine(1, half, half), last.at[0, low], 2),
        ]
        self.copies = [
            pltpu.make_async_remote_copy(
                src_ref=src,
                dst_ref=dst,
                send_sem=send.at[i],
                recv_sem=recv.at[i],
                device_id=(d ^ mask, t),
                device_id_type=MESH,
            )
            for i, (src, dst, mask) in enumerate(plan)
        ]

    def start(self):
        for i in range(4):
            self.copies[i].start()
        for load in self.loads:
            load.start()

    def pair(self, i):
        if self.loads:
            self.loads[i].wait()
        self.copies[i].wait_recv()
        add_rows(self.mine(i), self.core.at[i], self.rows)

    def first(self):
        self.pair(0)
        self.copies[4].start()
        self.copies[5].start()

    def second(self):
        self.pair(1)
        self.copies[6].start()
        self.pair(2)
        self.copies[7].start()
        self.pair(3)

    def third(self):
        c = self.copies
        c[4].wait_recv()
        add_rows(self.mine(2, 0, self.half), self.diag.at[0], self.half)
        c[8].start()
        c[5].wait_recv()
        add_rows(self.mine(1, self.half, self.half), self.diag.at[1], self.half)
        c[9].start()

    def end(self):
        for i in (6, 7, 8, 9):
            self.copies[i].wait_recv()
        step = 16
        own = self.mine(3)

        @pl.loop(0, self.rows, step=step)
        def _(start):
            part = pl.ds(pl.multiple_of(start, step), step)
            self.out[part, :] = (
                own[part, :].astype(F32)
                + self.last[0, part, :].astype(F32)
                + self.last[1, part, :].astype(F32)
            )

        for i in range(10):
            self.copies[i].wait_send()


def scatter_scratch(shapes, loaded):
    own = [pltpu.VMEM((4,) + s, BF16) for s, far in zip(shapes, loaded) if far]
    core = [pltpu.VMEM((4,) + s, BF16) for s in shapes]
    diag = [pltpu.VMEM((2, s[0] // 2, s[1]), BF16) for s in shapes]
    last = [pltpu.VMEM((2,) + s, BF16) for s in shapes]
    n = len(shapes)
    return own + core + diag + last + [DMA((n, 4)), DMA((n, 10)), DMA((n, 10))]


def make_scatters(grads, outs, loaded, scratch, d, t):
    n = len(grads)
    scratch = list(scratch)
    own = [scratch.pop(0) if far else None for far in loaded]
    core, diag, last = (scratch[i * n : (i + 1) * n] for i in range(3))
    local, send, recv = scratch[3 * n :]
    return [
        GradScatter(
            grads[i],
            outs[i],
            own[i],
            core[i],
            diag[i],
            last[i],
            local.at[i],
            send.at[i],
            recv.at[i],
            d,
            t,
        )
        for i in range(n)
    ]


class LineGather:
    def __init__(self, block, out, local, send, recv, d, t, depth):
        self.block, self.out, self.send, self.recv = block, out, send, recv
        self.d, self.t, self.depth = d, t, depth
        self.rows = block.shape[1]
        self.own = pltpu.make_async_copy(block, self.slot(t), local)

    def slot(self, j):
        return self.out.at[:, pl.ds(pl.multiple_of(j * self.rows, self.rows), self.rows)]

    def copy(self, way, step, j, to):
        return pltpu.make_async_remote_copy(
            src_ref=self.block if step == 0 else self.slot(j),
            dst_ref=self.slot(j),
            send_sem=self.send.at[way, step],
            recv_sem=self.recv.at[way, step],
            device_id=(self.d, to),
            device_id_type=MESH,
        )

    def step(self, s):
        t, depth = self.t, self.depth
        if s == 0:
            self.own.start()
        if s > 0:

            @pl.when(t - s >= 0)
            def _():
                self.copy(0, s - 1, t, t).wait_recv()

        if s < depth - 1:

            @pl.when((t - s >= 0) & (t < depth - 1))
            def _():
                self.copy(0, s, t - s, t + 1).start()

        if s > 0:

            @pl.when(t + s < depth)
            def _():
                self.copy(1, s - 1, t, t).wait_recv()

        if s < depth - 1:

            @pl.when((t + s < depth) & (t > 0))
            def _():
                self.copy(1, s, t + s, t - 1).start()

    def end(self):
        t, depth = self.t, self.depth
        for s in range(depth - 1):

            @pl.when((t - s >= 0) & (t < depth - 1))
            def _():
                self.copy(0, s, t, t).wait_send()

            @pl.when((t + s < depth) & (t > 0))
            def _():
                self.copy(1, s, t, t).wait_send()


def line_gather_scratch(depth):
    return [DMA, DMA((2, depth - 1)), DMA((2, depth - 1))]


class LineScatter:
    def __init__(self, part, got, send, recv, d, t, depth):
        self.part, self.got, self.send, self.recv = part, got, send, recv
        self.d, self.t, self.depth = d, t, depth
        self.seqs = part.shape[0]
        self.rows = part.shape[1] // depth

    def slot(self, way, j, s):
        return self.got.at[way, j - 1 if way == 0 else j, s]

    def copy(self, way, j, s, src, to):
        return pltpu.make_async_remote_copy(
            src_ref=src,
            dst_ref=self.slot(way, j, s),
            send_sem=self.send.at[way, j, s],
            recv_sem=self.recv.at[way, j, s],
            device_id=(self.d, to),
            device_id_type=MESH,
        )

    def block(self, j, s):
        return self.part.at[s, pl.ds(pl.multiple_of(j * self.rows, self.rows), self.rows)]

    def start(self, first=0, last=None):
        t, depth = self.t, self.depth
        steps = range(first, depth - 1 if last is None else last)

        @pl.when(t == 0)
        def _():
            for k in steps:
                for s in range(self.seqs):
                    j = depth - 1 - k
                    self.copy(0, j, s, self.block(j, s), t + 1).start()

        @pl.when(t == depth - 1)
        def _():
            for j in steps:
                for s in range(self.seqs):
                    self.copy(1, j, s, self.block(j, s), t - 1).start()

    def pass_on(self, way, j, to):
        for s in range(self.seqs):
            mine = self.slot(way, j, s)
            self.copy(way, j, s, mine, self.t).wait_recv()
            add_rows(mine, self.block(j, s), self.rows)
            self.copy(way, j, s, mine, to).start()

    def step(self, k):
        t, depth = self.t, self.depth
        right = depth - 1 - k + t
        left = k - (depth - 1 - t)

        @pl.when((t > 0) & (t < right) & (right < depth))
        def _():
            self.pass_on(0, right, t + 1)

        @pl.when((left >= 0) & (left < t) & (t < depth - 1))
        def _():
            self.pass_on(1, left, t - 1)

    def total(self, out):
        t, depth = self.t, self.depth
        mine = pl.ds(pl.multiple_of(t * self.rows, self.rows), self.rows)
        out[...] = self.part[:, mine, :].astype(F32)

        @pl.when(t > 0)
        def _():
            for s in range(self.seqs):
                self.copy(0, t, s, self.slot(0, t, s), t).wait_recv()
            out[...] += self.got[0, t - 1].astype(F32)

        @pl.when(t < depth - 1)
        def _():
            for s in range(self.seqs):
                self.copy(1, t, s, self.slot(1, t, s), t).wait_recv()
            out[...] += self.got[1, t].astype(F32)

    def end(self):
        t, depth = self.t, self.depth
        for j in range(depth):
            for s in range(self.seqs):
                if j > 0:

                    @pl.when(j > t)
                    def _():
                        self.copy(0, j, s, self.slot(0, j, s), t).wait_send()

                if j < depth - 1:

                    @pl.when(j < t)
                    def _():
                        self.copy(1, j, s, self.slot(1, j, s), t).wait_send()


def line_scatter_scratch(seqs, rows, width, depth):
    return [
        pltpu.VMEM((2, depth - 1, seqs, rows, width), BF16),
        DMA((2, depth, seqs)),
        DMA((2, depth, seqs)),
    ]


def call(kernel, name, number, ins, outs, scratch, args, vmem=60 * 1024 * 1024):
    return pl.pallas_call(
        kernel,
        name=name,
        out_shape=[o[0] for o in outs],
        in_specs=ins,
        out_specs=[o[1] for o in outs],
        scratch_shapes=scratch,
        compiler_params=pltpu.CompilerParams(
            collective_id=number, has_side_effects=True, vmem_limit_bytes=vmem
        ),
    )(*args)


def shaped(shape, dtype, spec):
    return (jax.ShapeDtypeStruct(shape, dtype), spec)


def sigmoid(x):
    return 1.0 / (1.0 + jnp.exp(-x))


def one_less_exp(y):
    series = 1.0 + y / 6.0 * (1.0 + y / 7.0)
    for k in (5.0, 4.0, 3.0, 2.0):
        series = 1.0 + y / k * series
    return jnp.where(y > -0.5, -y * series, 1.0 - jnp.exp(y))


GELU_SCALE = 0.7978845608028654
GELU_CUBE = 0.044715


def gelu(x):
    return 0.5 * x * (1.0 + jnp.tanh(GELU_SCALE * (x + GELU_CUBE * x * x * x)))


def gelu_both(x):
    square = x * x
    bent = jnp.tanh(GELU_SCALE * (x + GELU_CUBE * square * x))
    half = 0.5 * (1.0 + bent)
    slope = half + 0.5 * x * (1.0 - bent * bent) * (
        GELU_SCALE * (1.0 + 3.0 * GELU_CUBE * square)
    )
    return x * half, slope


def rows_of(index, size):
    return pl.ds(pl.multiple_of(index * size, size), size)


def contract(left, right, dims):
    return lax.dot_general(left, right, ((dims[:1], dims[1:]), ((), ())), preferred_element_type=F32)


def scan_rows(rate, out, seqs, length, base=0, backward=False):
    tile = 8
    width = out.shape[1]
    row = lax.broadcasted_iota(jnp.int32, (tile, width), 0)

    def body(i, carried):
        k = length // tile - 1 - i if backward else i
        ends = []
        for s in range(seqs):
            start = pl.multiple_of(s * length + k * tile, tile)
            rows = pl.ds(start, tile)
            if backward:
                pair = rate[pl.ds(start, 2 * tile), :]
                step = pltpu.roll(pair, 2 * tile - 1, 0)[:tile]
                step = jnp.where((row == tile - 1) & (i == 0), 0.0, step)
            else:
                step = rate[rows, :]
            held = pl.ds(pl.multiple_of(base + start, tile), tile)
            drive = out[held, :]
            for shift in (1, 2, 4):
                turn = tile - shift if backward else shift
                inside = row < tile - shift if backward else row >= shift
                before = jnp.where(inside, pltpu.roll(drive, turn, 0), 0.0)
                drive = drive + step * before
                step = step * jnp.where(inside, pltpu.roll(step, turn, 0), 1.0)
            states = drive + step * carried[s]
            out[held, :] = states
            ends.append(states[0:1] if backward else states[tile - 1 : tile])
        return tuple(ends)

    start = tuple(jnp.zeros((1, width), F32) for _ in range(seqs))
    lax.fori_loop(0, length // tile, body, start)


STRIP = 16


def gate_blocks(parity, width, block):
    half = block // 2
    shift = parity * half
    blocks = []
    for k in range((width + half) // block):
        low, high = k * block - shift, (k + 1) * block - shift
        blocks.append((k, max(low, 0), min(high, width)))
    return blocks


def first_kernel(
    depth,
    normed_block,
    cot_block,
    gelu_shard,
    input_shard,
    gate_in_shard,
    gate_dec_shard,
    out_shard,
    up_shard,
    taps,
    rate,
    normed_out,
    cot_out,
    gelu_full,
    input_full,
    gate_in_full,
    gate_dec_full,
    out_full,
    up_full,
    gelu_pre_out,
    input_pre_out,
    conv_out,
    window_out,
    gate_in_out,
    gate_dec_out,
    states_out,
    mixed_out,
    part_out,
    *scratch,
):
    normed, gelu_w, input_w, gate_in_w, gate_dec_w, out_w = scratch[:6]
    gelu_pre, input_pre, conv, window, gate_in, gate_dec, decay, states, mixed, part = scratch[6:16]
    local, send, recv = scratch[16:19]
    line_sems = scratch[19:25]
    rim_send, rim_recv, save_sem = scratch[25:28]
    d, t = place()
    parity = lax.rem(t, 2)
    even = parity == 0
    odd = parity == 1
    greet(d, t, depth)
    seqs, length, _ = normed.shape
    tokens = seqs * length
    width = conv.shape[1]
    block = gate_in_w.shape[0]
    half = block // 2
    lines = [
        LineGather(normed_block, normed, *line_sems[:3], d, t, depth),
        LineGather(cot_block, cot_out, *line_sems[3:], d, t, depth),
    ]
    pairs = (
        (gelu_shard, gelu_w),
        (input_shard, input_w),
        (gate_in_shard, gate_in_w),
        (gate_dec_shard, gate_dec_w),
        (out_shard, out_w),
        (up_shard, up_full),
    )
    gathers = [
        WeightGather(shard, full, local.at[i], send.at[i], recv.at[i], d, t)
        for i, (shard, full) in enumerate(pairs)
    ]
    saves = []

    def save(src, dst):
        copy = pltpu.make_async_copy(src, dst, save_sem.at[len(saves)])
        copy.start()
        saves.append(copy)

    one, two, three = gathers[:-2], gathers[-2], gathers[-1]
    lines[0].step(0)
    for g in one:
        g.start()
    for g in one:
        g.relay()
    two.start()
    lines[0].step(1)
    for g in one:
        g.relay_two()
    lines[0].step(2)
    for g in one:
        g.relay_last()
    two.relay()
    three.start()
    two.relay_two()
    two.relay_last()
    lines[0].step(3)
    lines[0].own.wait()
    lines[1].step(0)
    for g in one:
        g.arrive()
    save(normed, normed_out)
    save(gelu_w, gelu_full)
    save(input_w, input_full)
    save(gate_in_w, gate_in_full)
    save(gate_dec_w, gate_dec_full)

    for s in range(seqs):
        rows = pl.ds(s * length, length)
        input_pre[s, 0:8, :] = jnp.zeros((8, width), F32)
        input_pre[s, 8 : 8 + length, :] = contract(normed[s], input_w[...], (1, 0))
        gelu_pre[rows, :] = contract(normed[s], gelu_w[...], (1, 0))

    for s in range(seqs):

        @pl.loop(0, length // STRIP)
        def _(i):
            near = input_pre[s, pl.ds(pl.multiple_of(i * STRIP, STRIP), STRIP + 8), :]
            total = taps[0:1, :] * near[8:]
            for k in range(1, taps.shape[0]):
                total = total + taps[k : k + 1, :] * pltpu.roll(near, k, 0)[8:]
            rows = pl.ds(pl.multiple_of(s * length + i * STRIP, STRIP), STRIP)
            conv[rows, :] = total.astype(BF16)

    def rim(to, src, dst):
        return pltpu.make_async_remote_copy(
            src_ref=conv.at[:, pl.ds(src, half)],
            dst_ref=window.at[:, pl.ds(dst, half)],
            send_sem=rim_send,
            recv_sem=rim_recv,
            device_id=(d, to),
            device_id_type=MESH,
        )

    @pl.when(even)
    def _():
        rim(t + 1, width - half, 0).start()
        window[:, 0:width] = conv[...]

    @pl.when(odd)
    def _():
        rim(t - 1, 0, width).start()
        window[:, half : half + width] = conv[...]

    def gates(blocks):
        for k, low, high in blocks:
            near = window[:, k * block : (k + 1) * block]
            gate_in[:, low:high] = contract(near, gate_in_w[:, low:high], (1, 0))
            gate_dec[:, low:high] = contract(near, gate_dec_w[:, low:high], (1, 0))

    even_blocks, odd_blocks = gate_blocks(0, width, block), gate_blocks(1, width, block)

    @pl.when(even)
    def _():
        gates(even_blocks[:-1])

    @pl.when(odd)
    def _():
        gates(odd_blocks[1:])

    three.relay()

    @pl.when(even)
    def _():
        rim(t + 1, width - half, width).wait_recv()
        gates(even_blocks[-1:])

    @pl.when(odd)
    def _():
        rim(t - 1, 0, 0).wait_recv()
        gates(odd_blocks[:1])

    lines[1].step(1)

    @pl.loop(0, tokens // STRIP)
    def _(i):
        rows = rows_of(i, STRIP)
        log = -8.0 * sigmoid(gate_dec[rows, :]) * rate[...]
        decay[rows, :] = jnp.exp(log)
        drive = jnp.sqrt(one_less_exp(2.0 * log)) * sigmoid(gate_in[rows, :])
        held = pl.ds(pl.multiple_of(i * STRIP + 8, 8), STRIP)
        states[held, :] = drive * conv[rows, :].astype(F32)

    states[0:8, :] = jnp.zeros((8, width), F32)
    scan_rows(decay, states, seqs, length, base=8)

    @pl.loop(0, tokens // STRIP)
    def _(i):
        rows = rows_of(i, STRIP)
        held = pl.ds(pl.multiple_of(i * STRIP + 8, 8), STRIP)
        mixed[rows, :] = (gelu(gelu_pre[rows, :]) * states[held, :]).astype(BF16)

    save(gelu_pre, gelu_pre_out)
    save(input_pre, input_pre_out)
    save(conv, conv_out)
    save(window, window_out)
    save(gate_in, gate_in_out)
    save(gate_dec, gate_dec_out)
    save(states, states_out)
    save(mixed, mixed_out)
    three.relay_two()
    two.arrive()
    save(out_w, out_full)
    panel = 512

    @pl.loop(0, out_w.shape[0] // panel)
    def _(i):
        columns = rows_of(i, panel)
        value = contract(mixed[...], out_w[columns, :], (1, 1)).astype(BF16)
        for s in range(seqs):
            part[s, :, columns] = value[s * length : (s + 1) * length]

    save(part, part_out)
    lines[1].step(2)
    three.relay_last()
    lines[1].step(3)
    lines[1].own.wait()
    three.arrive()

    @pl.when(even)
    def _():
        rim(t + 1, width - half, 0).wait_send()

    @pl.when(odd)
    def _():
        rim(t - 1, 0, width).wait_send()

    for g in gathers:
        g.end()
    for line in lines:
        line.end()
    for copy in saves:
        copy.wait()


def first_phase(normed, cot, weights, taps, rate, depth):
    seqs, rows, model = normed.shape
    length = rows * depth
    tokens = seqs * length
    n = len(weights)
    block, width = weights[2].shape[0] * 8, weights[0].shape[1]
    wide = block // 2 + width
    wide_rows = (seqs, length, model)
    mixers = [(model, width), (model, width), (block, width), (block, width), (model, width)]
    saved = [
        ((tokens, width), F32),
        ((seqs, length + 8, width), F32),
        ((tokens, width), BF16),
        ((tokens, wide), BF16),
        ((tokens, width), F32),
        ((tokens, width), F32),
        ((tokens + 8, width), F32),
        ((tokens, width), BF16),
        (wide_rows, BF16),
    ]
    outs = [shaped(wide_rows, BF16, ANY)] * 2
    outs += [shaped(shape, BF16, ANY) for shape in mixers]
    outs += [shaped((8,) + weights[-1].shape, BF16, ANY)]
    outs += [shaped(shape, dtype, ANY) for shape, dtype in saved]
    saved_scratch = saved[:6] + [((tokens, width), F32)] + saved[6:]
    scratch = [pltpu.VMEM(wide_rows, BF16)]
    scratch += [pltpu.VMEM(shape, BF16) for shape in mixers]
    scratch += [pltpu.VMEM(shape, dtype) for shape, dtype in saved_scratch]
    scratch += gather_scratch(n) + line_gather_scratch(depth) * 2 + [DMA, DMA, DMA((16,))]
    res = call(
        functools.partial(first_kernel, depth),
        "first_phase",
        0,
        [VMEM] * (4 + n),
        outs,
        scratch,
        (normed, cot) + tuple(weights) + (taps, rate.reshape(1, width)),
    )
    return res[0], res[1], res[2 : 2 + n], res[2 + n : -1], res[-1]


def middle_kernel(depth, part, act, gain, w0, w1, middle, wide, f0, f1, *scratch):
    local, send, recv = scratch[:3]
    got, ssem, rsem = scratch[3:6]
    block = scratch[6]
    lsem = scratch[7:10]
    d, t = place()
    greet(d, t, depth)
    gathers = [
        WeightGather(w, f, local.at[i], send.at[i], recv.at[i], d, t)
        for i, (w, f) in enumerate(((w0, f0), (w1, f1)))
    ]
    scatter = LineScatter(part, got, ssem, rsem, d, t, depth)
    scatter.start()
    gathers[0].start()
    gathers[0].relay()
    gathers[1].start()
    scatter.step(1)
    gathers[0].relay_two()
    scatter.step(2)
    gathers[0].relay_last()
    scatter.total(middle)
    seqs, rows, width = act.shape
    for s in range(seqs):
        value = middle[s] + act[s].astype(F32)
        middle[s] = value
        inverse = lax.rsqrt(jnp.mean(value * value, axis=-1, keepdims=True) + EPS)
        block[s] = (value * inverse * gain[...]).astype(BF16)
    line = LineGather(block, wide, *lsem, d, t, depth)
    line.step(0)
    gathers[1].relay()
    line.step(1)
    gathers[1].relay_two()
    line.step(2)
    gathers[1].relay_last()
    line.step(3)
    for g in gathers:
        g.arrive()
        g.end()
    scatter.end()
    line.own.wait()
    line.end()


def middle_phase(part, act, gain, w0, w1, depth):
    seqs, rows, width = act.shape
    outs = [
        shaped(act.shape, F32, VMEM),
        shaped((seqs, rows * depth, width), BF16, ANY),
        shaped((8,) + w0.shape, BF16, ANY),
        shaped((8,) + w1.shape, BF16, ANY),
    ]
    scratch = (
        gather_scratch(2)
        + line_scatter_scratch(seqs, rows, width, depth)
        + [pltpu.VMEM(act.shape, BF16)]
        + line_gather_scratch(depth)
    )
    return call(
        functools.partial(middle_kernel, depth),
        "middle_phase",
        1,
        [VMEM] * 5,
        outs,
        scratch,
        (part, act, gain.reshape(1, width), w0, w1),
    )


def norm_back(value, gain, error):
    inverse = lax.rsqrt(jnp.mean(value * value, axis=-1, keepdims=True) + EPS)
    scaled = error * gain
    mean = jnp.mean(scaled * value, axis=-1, keepdims=True)
    grad = inverse * scaled - value * (inverse * inverse * inverse * mean)
    return grad, jnp.sum(error * value * inverse, axis=0, keepdims=True)


def back_kernel(depth, part, middle, gain, cot, g0, g1, grad, wide, gain_grad, o0, o1, *scratch):
    got, ssem, rsem = scratch[:3]
    block = scratch[3]
    lsem = scratch[4:7]
    d, t = place()
    greet(d, t, depth)
    scatters = make_scatters((g0, g1), (o0, o1), (True, True), scratch[7:], d, t)
    scatter = LineScatter(part, got, ssem, rsem, d, t, depth)
    scatter.start()
    for g in scatters:
        g.start()
    scatters[0].first()
    scatters[0].second()
    scatter.step(1)
    scatters[0].third()
    scatter.step(2)
    scatters[1].first()
    scatters[1].second()
    scatter.total(grad)
    seqs, rows, width = middle.shape
    for s in range(seqs):
        change, gain_part = norm_back(middle[s], gain[...], grad[s])
        change = change + cot[s]
        grad[s] = change
        block[s] = change.astype(BF16)
        if s == 0:
            gain_grad[...] = gain_part
        else:
            gain_grad[...] += gain_part
    line = LineGather(block, wide, *lsem, d, t, depth)
    line.step(0)
    scatters[0].end()
    line.step(1)
    scatters[1].third()
    line.step(2)
    line.step(3)
    scatters[1].end()
    scatter.end()
    line.own.wait()
    line.end()


def back_phase(part, middle, gain, cot, g0, g1, depth):
    seqs, rows, width = middle.shape
    shapes = [(g.shape[0] // 8, g.shape[1]) for g in (g0, g1)]
    outs = [
        shaped(middle.shape, F32, VMEM),
        shaped((seqs, rows * depth, width), BF16, ANY),
        shaped((1, width), F32, VMEM),
        shaped(shapes[0], F32, VMEM),
        shaped(shapes[1], F32, VMEM),
    ]
    scratch = (
        line_scatter_scratch(seqs, rows, width, depth)
        + [pltpu.VMEM(middle.shape, BF16)]
        + line_gather_scratch(depth)
        + scatter_scratch(shapes, (True, True))
    )
    return call(
        functools.partial(back_kernel, depth),
        "back_phase",
        2,
        [VMEM, VMEM, VMEM, VMEM, ANY, ANY],
        outs,
        scratch,
        (part, middle, gain.reshape(1, width), cot, g0, g1),
    )


def mixer_back_kernel(
    depth,
    branch_in,
    out_w_in,
    gelu_pre_in,
    input_pre_in,
    conv_in,
    window_in,
    gate_in_in,
    gate_dec_in,
    states_in,
    gelu_w_in,
    input_w_in,
    gate_in_w_in,
    gate_dec_w_in,
    up_in,
    feed,
    middle,
    taps,
    rate,
    part_out,
    gelu_grad_out,
    input_grad_out,
    gate_in_grad_out,
    gate_dec_grad_out,
    small,
    output,
    up_out,
    *scratch,
):
    branch, weight, input_w = scratch[:3]
    gelu_pre, input_pre, conv, window, gate_in, gate_dec, states, gate_in_w, gate_dec_w = scratch[3:12]
    grad, decay, grad_conv, gelu_grad, input_grad, grad_in, grad_dec = scratch[12:19]
    rim_out, rim_in, gate_in_grad, gate_dec_grad, part, sums, total = scratch[19:26]
    got, ssem, rsem = scratch[26:29]
    rim_send, rim_recv, load_sem, save_sem = scratch[29:33]
    d, t = place()
    parity = lax.rem(t, 2)
    even = parity == 0
    odd = parity == 1
    greet(d, t, depth)
    seqs, length, _ = branch.shape
    tokens = seqs * length
    width = conv.shape[1]
    block = gate_in_w.shape[0]
    half = block // 2
    even_blocks, odd_blocks = gate_blocks(0, width, block), gate_blocks(1, width, block)
    (scatter,) = make_scatters((up_in,), (up_out,), (True,), scratch[33:], d, t)
    line = LineScatter(feed, got, ssem, rsem, d, t, depth)
    saves = []

    def save(src, dst):
        copy = pltpu.make_async_copy(src, dst, save_sem.at[len(saves)])
        copy.start()
        saves.append(copy)

    def load(i, src, dst):
        copy = pltpu.make_async_copy(src, dst, load_sem.at[i])
        copy.start()
        return copy

    early = [load(0, branch_in, branch), load(1, out_w_in, weight)]
    next_ = [
        load(2, gelu_pre_in, gelu_pre),
        load(3, states_in, states),
        load(4, gate_dec_in, gate_dec),
    ]
    line.start(0, 1)
    scatter.start()
    then = [
        load(5, gate_in_in, gate_in),
        load(6, conv_in, conv),
        load(7, window_in, window),
        load(8, gate_in_w_in, gate_in_w),
        load(9, gate_dec_w_in, gate_dec_w),
        load(10, input_pre_in, input_pre),
        load(11, input_w_in, input_w),
    ]
    for copy in early:
        copy.wait()
    for s in range(seqs):
        rows = pl.ds(s * length, length)
        grad[rows, :] = contract(branch[s], weight[...], (1, 0))
    reload = load(0, gelu_w_in, weight)
    scatter.first()
    for copy in next_:
        copy.wait()

    @pl.loop(0, tokens // STRIP)
    def _(i):
        rows = rows_of(i, STRIP)
        held = pl.ds(pl.multiple_of(i * STRIP + 8, 8), STRIP)
        act, slope = gelu_both(gelu_pre[rows, :])
        came = grad[rows, :]
        gelu_grad[rows, :] = (came * states[held, :] * slope).astype(BF16)
        grad[rows, :] = came * act
        decay[rows, :] = jnp.exp(-8.0 * sigmoid(gate_dec[rows, :]) * rate[...])

    decay[tokens : tokens + 8, :] = jnp.zeros((8, width), F32)
    save(gelu_grad, gelu_grad_out)
    scatter.second()
    scan_rows(decay, grad, seqs, length, backward=True)
    for copy in then:
        copy.wait()
    sums[...] = jnp.zeros(sums.shape, F32)

    def fold(value):
        return value[0:8] + value[8:16]

    first_row = lax.broadcasted_iota(jnp.int32, (STRIP, width), 0) == 0
    for s in range(seqs):

        @pl.loop(0, length // STRIP)
        def _(i):
            start = pl.multiple_of(s * length + i * STRIP, STRIP)
            rows = pl.ds(start, STRIP)
            earlier = pltpu.roll(states[pl.ds(start, STRIP + 8), :], 1, 0)[8:]
            earlier = jnp.where(first_row & (i == 0), 0.0, earlier)
            came = grad[rows, :]
            open_in = sigmoid(gate_in[rows, :])
            open_dec = sigmoid(gate_dec[rows, :])
            slow = -8.0 * rate[...]
            lost = one_less_exp(2.0 * open_dec * slow)
            root = jnp.sqrt(lost)
            value = conv[rows, :].astype(F32)
            step = decay[rows, :]
            through = came * open_in
            grad_log = step * (came * earlier - through * value * step / root)
            sums[0] += fold(grad_log * (-8.0 * open_dec))
            through = through * root
            grad_conv[s, pl.ds(pl.multiple_of(i * STRIP, STRIP), STRIP), :] = through
            grad_in[rows, :] = (through * value * (1.0 - open_in)).astype(BF16)
            grad_dec[rows, :] = (grad_log * slow * open_dec * (1.0 - open_dec)).astype(BF16)

        grad_conv[s, length : length + 8, :] = jnp.zeros((8, width), F32)

    def gates_back(k, low, high):
        return contract(grad_in[:, low:high], gate_in_w[:, low:high], (1, 1)) + contract(
            grad_dec[:, low:high], gate_dec_w[:, low:high], (1, 1)
        )

    def add_conv(low, high, value):
        for s in range(seqs):
            grad_conv[s, 0:length, low:high] += value[s * length : (s + 1) * length]

    def rim(to):
        return pltpu.make_async_remote_copy(
            src_ref=rim_out,
            dst_ref=rim_in,
            send_sem=rim_send,
            recv_sem=rim_recv,
            device_id=(d, to),
            device_id_type=MESH,
        )

    @pl.when(even)
    def _():
        value = gates_back(*even_blocks[-1])
        rim_out[...] = value[:, half:].astype(BF16)
        rim(t + 1).start()
        add_conv(width - half, width, value[:, :half])

    @pl.when(odd)
    def _():
        value = gates_back(*odd_blocks[0])
        rim_out[...] = value[:, :half].astype(BF16)
        rim(t - 1).start()
        add_conv(0, half, value[:, half:])

    line.start(1)
    line.step(1)

    def inner(blocks):
        for k, low, high in blocks:
            add_conv(low, high, gates_back(k, low, high))

    def gate_grads(blocks):
        for k, low, high in blocks:
            near = window[:, k * block : (k + 1) * block]
            gate_in_grad[:, low:high] = contract(near, grad_in[:, low:high], (0, 0)).astype(BF16)
            gate_dec_grad[:, low:high] = contract(near, grad_dec[:, low:high], (0, 0)).astype(BF16)

    @pl.when(even)
    def _():
        inner(even_blocks[:-1])
        gate_grads(even_blocks)

    @pl.when(odd)
    def _():
        inner(odd_blocks[1:])
        gate_grads(odd_blocks)

    save(gate_in_grad, gate_in_grad_out)
    save(gate_dec_grad, gate_dec_grad_out)
    scatter.third()

    @pl.when(even)
    def _():
        rim(t + 1).wait()
        add_conv(width - half, width, rim_in[...].astype(F32))

    @pl.when(odd)
    def _():
        rim(t - 1).wait()
        add_conv(0, half, rim_in[...].astype(F32))

    for s in range(seqs):

        @pl.loop(0, length // STRIP)
        def _(i):
            near = pl.ds(pl.multiple_of(i * STRIP, STRIP), STRIP + 8)
            later = grad_conv[s, near, :]
            before = input_pre[s, near, :]
            here = later[:STRIP]
            value = taps[0:1, :] * here
            sums[1] += fold(here * before[8:])
            for k in range(1, taps.shape[0]):
                value = value + taps[k : k + 1, :] * pltpu.roll(later, STRIP + 8 - k, 0)[:STRIP]
                sums[1 + k] += fold(here * pltpu.roll(before, k, 0)[8:])
            rows = pl.ds(pl.multiple_of(s * length + i * STRIP, STRIP), STRIP)
            input_grad[rows, :] = value.astype(BF16)

    save(input_grad, input_grad_out)
    for k in range(sums.shape[0]):
        small[k : k + 1, :] = jnp.sum(sums[k], axis=0, keepdims=True)
    small[sums.shape[0] :, :] = jnp.zeros((8 - sums.shape[0], width), F32)
    reload.wait()
    panel = 512

    @pl.loop(0, weight.shape[0] // panel)
    def _(i):
        columns = rows_of(i, panel)
        value = contract(gelu_grad[...], weight[columns, :], (1, 1))
        value = (value + contract(input_grad[...], input_w[columns, :], (1, 1))).astype(BF16)
        for s in range(seqs):
            part[s, :, columns] = value[s * length : (s + 1) * length]

    save(part, part_out)
    line.step(2)
    scatter.end()
    line.total(total)
    output[...] = (total[...] + middle[...]).astype(BF16)
    line.end()
    for copy in saves:
        copy.wait()


def mixer_back_phase(branch, saved, weights, up, feed, middle, taps, rate, depth):
    seqs, length, model = branch.shape
    tokens = seqs * length
    gelu_w, input_w, gate_in_w, gate_dec_w, out_w = weights[:5]
    gelu_pre, input_pre, conv, window, gate_in, gate_dec, states, mixed = saved
    width = out_w.shape[1]
    block = gate_in_w.shape[0]
    half = block // 2
    up_shape = (up.shape[0] // 8, up.shape[1])
    flat = (tokens, width)
    outs = [
        shaped(branch.shape, BF16, ANY),
        shaped(flat, BF16, ANY),
        shaped(flat, BF16, ANY),
        shaped(gate_in_w.shape, BF16, ANY),
        shaped(gate_in_w.shape, BF16, ANY),
        shaped((8, width), F32, VMEM),
        shaped(middle.shape, BF16, VMEM),
        shaped(up_shape, F32, VMEM),
    ]
    scratch = [
        pltpu.VMEM(x.shape, x.dtype)
        for x in (
            branch,
            out_w,
            input_w,
            gelu_pre,
            input_pre,
            conv,
            window,
            gate_in,
            gate_dec,
            states,
            gate_in_w,
            gate_dec_w,
        )
    ]
    scratch += [
        pltpu.VMEM(flat, F32),
        pltpu.VMEM((tokens + 8, width), F32),
        pltpu.VMEM((seqs, length + 8, width), F32),
    ]
    scratch += [pltpu.VMEM(flat, BF16)] * 4
    scratch += [pltpu.VMEM((tokens, half), BF16)] * 2
    scratch += [pltpu.VMEM(gate_in_w.shape, BF16)] * 2
    scratch += [
        pltpu.VMEM(branch.shape, BF16),
        pltpu.VMEM((1 + taps.shape[0], 8, width), F32),
        pltpu.VMEM(middle.shape, F32),
    ]
    scratch += line_scatter_scratch(seqs, length // depth, model, depth)
    scratch += [DMA, DMA, DMA((12,)), DMA((8,))]
    scratch += scatter_scratch([up_shape], (True,))
    return call(
        functools.partial(mixer_back_kernel, depth),
        "mixer_back_phase",
        3,
        [ANY] * 14 + [VMEM] * 4,
        outs,
        scratch,
        (
            branch,
            out_w,
            gelu_pre,
            input_pre,
            conv,
            window,
            gate_in,
            gate_dec,
            states,
            gelu_w,
            input_w,
            gate_in_w,
            gate_dec_w,
            up,
            feed,
            middle,
            taps,
            rate.reshape(1, width),
        ),
    )


def last_kernel(
    depth,
    part,
    act,
    gain,
    grad_middle,
    mlp_part,
    small,
    branch_in,
    normed_in,
    mixed_in,
    gelu_grad_in,
    input_grad_in,
    gate_in_grad,
    gate_dec_grad,
    input_grad,
    gains,
    smalls,
    out_out,
    gelu_out,
    input_out,
    gate_in_out,
    gate_dec_out,
    *scratch,
):
    got, ssem, rsem = scratch[:3]
    pack, packs, small_all, line_pack, line_packs = scratch[3:8]
    psend, precv, qsend, qrecv, zsend, zrecv = scratch[8:14]
    branch, normed, mixed, gelu_grad, input_rows = scratch[14:19]
    out_w_grad, gelu_w_grad, input_w_grad, load_sem = scratch[19:23]
    d, t = place()
    greet(d, t, depth, dp_masks=(1, 2, 3, 4, 5, 6, 7), z_all=True)
    scatters = make_scatters(
        (out_w_grad, gelu_w_grad, input_w_grad, gate_in_grad, gate_dec_grad),
        (out_out, gelu_out, input_out, gate_in_out, gate_dec_out),
        (False, False, False, True, True),
        scratch[23:],
        d,
        t,
    )
    line = LineScatter(part, got, ssem, rsem, d, t, depth)

    def load(i, src, dst):
        copy = pltpu.make_async_copy(src, dst, load_sem.at[i])
        copy.start()
        return copy

    loads = [
        load(0, branch_in, branch),
        load(1, mixed_in, mixed),
        load(2, normed_in, normed),
        load(3, gelu_grad_in, gelu_grad),
        load(4, input_grad_in, input_rows),
    ]

    def dp_copies(src, dst, send, recv):
        return [
            pltpu.make_async_remote_copy(
                src_ref=src,
                dst_ref=dst.at[d],
                send_sem=send.at[mask - 1],
                recv_sem=recv.at[mask - 1],
                device_id=(d ^ mask, t),
                device_id_type=MESH,
            )
            for mask in range(1, 8)
        ]

    line.start()
    small_copies = dp_copies(small, small_all, qsend, qrecv)
    for c in small_copies:
        c.start()
    small_all[d] = small[...]
    for g in scatters[3:]:
        g.start()
    seqs, length, model = branch.shape
    panel = 512

    def weight_grad(left, right, out):
        @pl.loop(0, model // panel)
        def _(i):
            columns = rows_of(i, panel)
            value = contract(left[0, :, columns], right[0:length, :], (0, 0))
            for s in range(1, seqs):
                value = value + contract(
                    left[s, :, columns], right[s * length : (s + 1) * length, :], (0, 0)
                )
            out[columns, :] = value.astype(BF16)

    loads[0].wait()
    loads[1].wait()
    weight_grad(branch, mixed, out_w_grad)
    scatters[0].start()
    loads[2].wait()
    loads[3].wait()
    weight_grad(normed, gelu_grad, gelu_w_grad)
    scatters[1].start()
    scatters[0].first()
    scatters[0].second()
    loads[4].wait()
    weight_grad(normed, input_rows, input_w_grad)
    scatters[2].start()
    line.step(1)
    scatters[1].first()
    scatters[1].second()
    scatters[0].third()
    scatters[2].first()
    scatters[2].second()
    line.step(2)
    for g in scatters[3:]:
        g.first()
        g.second()
    scatters[1].third()
    scatters[0].end()
    line.total(input_grad)
    quarter = pack.shape[1]
    for i in range(4):
        pack[4 + i : 5 + i, :] = mlp_part[:, i * quarter : (i + 1) * quarter]
    for s in range(seqs):
        change, gain_part = norm_back(act[s].astype(F32), gain[...], input_grad[s])
        input_grad[s] = change + grad_middle[s]
        for i in range(4):
            piece = gain_part[:, i * quarter : (i + 1) * quarter]
            if s == 0:
                pack[i : i + 1, :] = piece
            else:
                pack[i : i + 1, :] += piece
    pack_copies = dp_copies(pack, packs, psend, precv)
    for c in pack_copies:
        c.start()
    packs[d] = pack[...]
    for g in scatters[2:]:
        g.third()
    for c in small_copies:
        c.wait_recv()
    sum_ = small_all[0]
    for i in range(1, 8):
        sum_ = sum_ + small_all[i]
    smalls[...] = sum_
    for c in pack_copies:
        c.wait_recv()
    sum_ = packs[0]
    for i in range(1, 8):
        sum_ = sum_ + packs[i]
    line_pack[...] = sum_
    z_copies = [
        pltpu.make_async_remote_copy(
            src_ref=line_pack,
            dst_ref=line_packs.at[t],
            send_sem=zsend.at[step - 1],
            recv_sem=zrecv.at[step - 1],
            device_id=(d, lax.rem(t + step, depth)),
            device_id_type=MESH,
        )
        for step in range(1, depth)
    ]
    for c in z_copies:
        c.start()
    line_packs[t] = sum_
    for g in scatters[1:]:
        g.end()
    for c in z_copies:
        c.wait_recv()
    sum_ = line_packs[0]
    for i in range(1, depth):
        sum_ = sum_ + line_packs[i]
    gains[...] = sum_
    for c in small_copies + pack_copies + z_copies:
        c.wait_send()
    line.end()


def last_phase(
    part, act, gain, grad_middle, mlp_part, small, branch, normed, mixed, gelu_grad, input_grad,
    gate_in_grad, gate_dec_grad, depth,
):
    seqs, rows, model = act.shape
    width = mixed.shape[1]
    mixer, gate = (model // 8, width), (gate_in_grad.shape[0] // 8, width)
    shapes = [mixer] * 3 + [gate] * 2
    pack = (8, model // 4)
    outs = [
        shaped(act.shape, F32, VMEM),
        shaped(pack, F32, VMEM),
        shaped(small.shape, F32, VMEM),
    ] + [shaped(s, F32, VMEM) for s in shapes]
    scratch = (
        line_scatter_scratch(seqs, rows, model, depth)
        + [
            pltpu.VMEM(pack, F32),
            pltpu.VMEM((8,) + pack, F32),
            pltpu.VMEM((8,) + small.shape, F32),
            pltpu.VMEM(pack, F32),
            pltpu.VMEM((depth,) + pack, F32),
        ]
        + [DMA((7,))] * 4
        + [DMA((depth - 1,))] * 2
        + [
            pltpu.VMEM(x.shape, BF16) for x in (branch, normed, mixed, gelu_grad, input_grad)
        ]
        + [pltpu.VMEM((model, width), BF16)] * 3
        + [DMA((5,))]
        + scatter_scratch(shapes, (False, False, False, True, True))
    )
    res = call(
        functools.partial(last_kernel, depth),
        "last_phase",
        4,
        [VMEM] * 6 + [ANY] * 7,
        outs,
        scratch,
        (
            part,
            act,
            gain.reshape(1, model),
            grad_middle,
            mlp_part,
            small,
            branch,
            normed,
            mixed,
            gelu_grad,
            input_grad,
            gate_in_grad,
            gate_dec_grad,
        ),
    )
    return res[0], res[1].reshape(2, model), res[2], res[3:]


def swapped(block, axis):
    count = lax.axis_size(axis)
    return lax.ppermute(block, axis, [(i, i ^ 1) for i in range(count)])


def normalize(value_entries, scale_gain):
    return (
        value_entries
        * lax.rsqrt(jnp.mean(value_entries * value_entries, axis=-1, keepdims=True) + EPS)
        * scale_gain
    )


def causal_conv(value_entries, kernel):
    summed = value_entries * kernel[0]
    for offset in range(1, kernel.shape[0]):
        shifted = jnp.concatenate(
            [jnp.zeros_like(value_entries[:, :offset]), value_entries[:, :-offset]], axis=1
        )
        summed = summed + shifted * kernel[offset]
    return summed


def decay_inputs(input_pre, decay_pre, conv_vals, decay_rate):
    log_decay = -8.0 * jax.nn.sigmoid(decay_pre) * decay_rate
    scaled = jnp.sqrt(-jnp.expm1(2.0 * log_decay))
    return (log_decay, scaled * jax.nn.sigmoid(input_pre) * conv_vals)


def recurrence(rate, drive):
    def join(left, right):
        return left[0] * right[0], left[1] * right[0] + right[1]

    return lax.associative_scan(join, (rate, drive), axis=1)[1]


def dot(spec, left, right):
    return jnp.einsum(spec, left, right, preferred_element_type=F32)


def weight_grad(left, right):
    return dot("pkr,pku->ru", left, right).astype(BF16)


class Fast:
    def __init__(self, depth, taps, rate):
        self.depth, self.taps, self.rate = depth, taps, rate

    def first(self, normed, cot, weights):
        normed_all, cot_all, weights, saved, part = first_phase(
            normed, cot, weights, self.taps, self.rate, self.depth
        )
        self.saved, self.weights, self.normed = saved, weights, normed_all
        return cot_all, weights[5].reshape(-1, weights[5].shape[-1]), part

    def middle(self, part, act, gain, w0, w1):
        middle, wide, w0, w1 = middle_phase(part, act, gain, w0, w1, self.depth)
        return middle, wide, w0.reshape(-1, w0.shape[-1]), w1.reshape(-1, w1.shape[-1])

    def back(self, part, middle, gain, cot, g0, g1):
        return back_phase(part, middle, gain, cot, g0, g1, self.depth)

    def last(self, branch, up, feed, act, gain, middle, grad_middle, mlp_part):
        part, gelu_grad, input_rows, gate_in, gate_dec, small, output, up = mixer_back_phase(
            branch, self.saved, self.weights, up, feed, middle, self.taps, self.rate, self.depth
        )
        input_grad, gains, small, grads = last_phase(
            part,
            act,
            gain,
            grad_middle,
            mlp_part,
            small,
            branch,
            self.normed,
            self.saved[-1],
            gelu_grad,
            input_rows,
            gate_in,
            gate_dec,
            self.depth,
        )
        return output, input_grad, gains, small, grads, up


class Plain:
    def __init__(self, depth, taps, rate):
        self.depth, self.taps, self.rate = depth, taps, rate

    @staticmethod
    def wide(block):
        return lax.all_gather(block, "tensor", axis=1, tiled=True)

    @staticmethod
    def narrow(part):
        return lax.psum_scatter(part, "tensor", scatter_dimension=1, tiled=True).astype(F32)

    @staticmethod
    def full(shard):
        return lax.all_gather(shard, "dp", axis=0, tiled=True)

    @staticmethod
    def own(grad):
        return lax.psum_scatter(grad, "dp", scatter_dimension=0, tiled=True).astype(F32)

    def first(self, normed, cot, weights):
        gelu_w, input_w, gate_in_w, gate_dec_w, out_w, up_w = (self.full(w) for w in weights)
        normed_all = self.wide(normed)
        seqs, length, _ = normed_all.shape
        channels = gelu_w.shape[1]
        block = gate_in_w.shape[0]
        half = block // 2
        width = channels + half
        parity = lax.axis_index("tensor") % 2
        gelu_pre = dot("kqg,ga->kqa", normed_all, gelu_w)
        input_pre = dot("kqg,ga->kqa", normed_all, input_w)
        gelu_out, gelu_back = jax.vjp(jax.nn.gelu, gelu_pre)
        conv_out, conv_back = jax.vjp(causal_conv, input_pre, self.taps)
        conv_bf = conv_out.astype(BF16)
        rim = lax.dynamic_slice_in_dim(conv_bf, (1 - parity) * (channels - half), half, 2)
        window = jnp.zeros((seqs, length, width), BF16)
        window = lax.dynamic_update_slice_in_dim(window, conv_bf, parity * half, 2)
        window = lax.dynamic_update_slice_in_dim(
            window, swapped(rim, "tensor"), (1 - parity) * channels, 2
        )
        tiles = window.reshape(seqs, length, width // block, block)
        placed = lax.dynamic_update_slice_in_dim(
            jnp.zeros((2, block, width), BF16), jnp.stack([gate_in_w, gate_dec_w]), parity * half, 2
        ).reshape(2, block, width // block, block)
        gates = dot("slbk,gkbc->gslbc", tiles, placed).reshape(2, seqs, length, width)
        gates = lax.dynamic_slice_in_dim(gates, parity * half, channels, 3)
        (log_decay, drive), gate_back = jax.vjp(
            decay_inputs, gates[0], gates[1], conv_bf.astype(F32), self.rate
        )
        decay = jnp.exp(log_decay)
        states = recurrence(decay, drive)
        mixed = (gelu_out * states).astype(BF16)
        self.kept = (
            normed_all, gelu_w, input_w, out_w, gelu_out, gelu_back, conv_back, tiles, placed,
            gate_back, decay, states, mixed,
        )
        part = dot("xgq,pq->xgp", mixed, out_w).astype(BF16)
        return self.wide(cot), up_w, part

    def middle(self, part, act, gain, w0, w1):
        middle = act.astype(F32) + self.narrow(part)
        wide = self.wide(normalize(middle, gain).astype(BF16))
        return middle, wide, self.full(w0), self.full(w1)

    def back(self, part, middle, gain, cot, g0, g1):
        _, back = jax.vjp(normalize, middle, gain)
        change, gain_grad = back(self.narrow(part))
        grad = cot + change
        return grad, self.wide(grad.astype(BF16)), gain_grad[None], self.own(g0), self.own(g1)

    def last(self, branch, up, feed, act, gain, middle, grad_middle, mlp_part):
        (
            normed_all, gelu_w, input_w, out_w, gelu_out, gelu_back, conv_back, tiles, placed,
            gate_back, decay, states, mixed,
        ) = self.kept
        seqs, length, channels = states.shape
        block = tiles.shape[-1]
        half = block // 2
        width = channels + half
        parity = lax.axis_index("tensor") % 2
        grad_mixed = dot("xtz,zm->xtm", branch, out_w)
        gelu_grad = gelu_back(grad_mixed * states)[0].astype(BF16)
        later = jnp.concatenate([decay[:, 1:], jnp.zeros_like(decay[:, :1])], axis=1)
        grad_drive = jnp.flip(
            recurrence(jnp.flip(later, 1), jnp.flip(grad_mixed * gelu_out, 1)), 1
        )
        earlier = jnp.concatenate([jnp.zeros_like(states[:, :1]), states[:, :-1]], axis=1)
        grad_in, grad_dec, grad_conv, grad_rate = gate_back(
            (grad_drive * decay * earlier, grad_drive)
        )
        grads = lax.dynamic_update_slice_in_dim(
            jnp.zeros((2, seqs, length, width), BF16),
            jnp.stack([grad_in, grad_dec]).astype(BF16),
            parity * half,
            3,
        ).reshape(2, seqs, length, width // block, block)
        grad_window = dot("gslbc,gkbc->slbk", grads, placed).reshape(seqs, length, width)
        grad_placed = dot("slbk,gslbc->gkbc", tiles, grads).reshape(2, block, width)
        grad_gates = lax.dynamic_slice_in_dim(grad_placed, parity * half, channels, 2)
        rim = lax.dynamic_slice_in_dim(grad_window, (1 - parity) * channels, half, 2)
        rim = swapped(rim.astype(BF16), "tensor").astype(F32)
        grad_conv = grad_conv + lax.dynamic_slice_in_dim(grad_window, parity * half, channels, 2)
        start = (1 - parity) * (channels - half)
        rim = lax.dynamic_slice_in_dim(grad_conv, start, half, 2) + rim
        grad_conv = lax.dynamic_update_slice_in_dim(grad_conv, rim, start, 2)
        input_rows, grad_taps = conv_back(grad_conv)
        input_rows = input_rows.astype(BF16)
        part = dot("mzf,af->mza", gelu_grad, gelu_w) + dot("mzf,af->mza", input_rows, input_w)
        _, back = jax.vjp(normalize, act.astype(F32), gain)
        change, gain_grad = back(self.narrow(part.astype(BF16)))
        output = (middle + self.narrow(feed)).astype(BF16)
        gains = lax.psum(jnp.concatenate([gain_grad[None], mlp_part]), ("dp", "tensor"))
        small = lax.psum(jnp.concatenate([grad_rate[None], grad_taps]), "dp")
        parts = (
            weight_grad(branch, mixed),
            weight_grad(normed_all, gelu_grad),
            weight_grad(normed_all, input_rows),
            grad_gates[0].astype(BF16),
            grad_gates[1].astype(BF16),
        )
        own = [self.own(g) for g in parts]
        return output, grad_middle + change, gains, small, own, self.own(up)


def shards(
    activations,
    norm_gain,
    gelu_proj,
    input_proj,
    conv_weight,
    gate_input,
    gate_decay,
    decay_rate,
    out_proj,
    mlp_gain,
    feed_gate,
    feed_up,
    feed_down,
    cotangent,
    lengths,
    batch_of,
):
    depth = lax.axis_size("tensor")
    fast = lax.axis_size("dp") == 8 and depth == 4
    run = (Fast if fast else Plain)(depth, conv_weight, decay_rate)
    tensor_index = lax.axis_index("tensor")
    data_index = lax.axis_index("dp")
    seq_count, row_count, _ = activations.shape
    full_length = row_count * depth
    members = (batch_of[:, None] == jnp.arange(MICRO)[None, :]).astype(F32)
    counts = jnp.sum(members * lengths[:, None].astype(F32), axis=0)
    total_seqs = lengths.shape[0]
    per_batch = float(total_seqs * full_length) / (MICRO * counts)
    weight_all = jnp.sum(members * per_batch[None, :], axis=1)
    my_weight = lax.dynamic_slice_in_dim(weight_all, data_index * seq_count, seq_count)
    my_length = lax.dynamic_slice_in_dim(lengths, data_index * seq_count, seq_count)
    places = tensor_index * row_count + jnp.arange(row_count)
    valid_mask = (places[None, :] < my_length[:, None]).astype(F32)
    scaled_cot = cotangent.astype(F32) * (valid_mask * my_weight[:, None])[:, :, None]
    normed = normalize(activations.astype(F32), norm_gain).astype(BF16)

    cot_all, up_w, branch_part = run.first(
        normed,
        scaled_cot.astype(BF16),
        (gelu_proj, input_proj, gate_input, gate_decay, out_proj.T, feed_up),
    )
    middle, normed_two_all, gate_w, down_w = run.middle(
        branch_part, activations, mlp_gain, feed_gate, feed_down.T
    )
    gate_pre = dot("nwo,ob->nwb", normed_two_all, gate_w)
    lift_pre = dot("nwo,ob->nwb", normed_two_all, up_w)
    gate_act, activ_back = jax.vjp(jax.nn.gelu, gate_pre)
    hidden = (gate_act * lift_pre).astype(BF16)
    grad_hidden = dot("gre,eu->gru", cot_all, down_w)
    gate_grad = activ_back(grad_hidden * lift_pre)[0].astype(BF16)
    lift_grad = (grad_hidden * gate_act).astype(BF16)
    back_two = dot("mqa,ya->mqy", gate_grad, gate_w) + dot("mqa,ya->mqy", lift_grad, up_w)
    grad_down_part = weight_grad(cot_all, hidden)
    grad_gate_part = weight_grad(normed_two_all, gate_grad)
    grad_lift_part = weight_grad(normed_two_all, lift_grad)
    feed_part = dot("xav,tv->xat", hidden, down_w).astype(BF16)

    grad_middle, branch_grad_all, mlp_part, grad_down, grad_gate = run.back(
        back_two.astype(BF16), middle, mlp_gain, scaled_cot, grad_down_part, grad_gate_part
    )
    output, input_grad, gains, small, grads, grad_up = run.last(
        branch_grad_all,
        grad_lift_part,
        feed_part,
        activations,
        norm_gain,
        middle,
        grad_middle,
        mlp_part,
    )
    return (
        output,
        input_grad,
        gains[0],
        grads[1],
        grads[2],
        small[1:5],
        grads[3],
        grads[4],
        small[0],
        grads[0].T,
        gains[1],
        grad_gate,
        grad_up,
        grad_down.T,
    )


def solution(mesh):
    placed = (
        P("dp", "tensor", None),
        P(),
        P("dp", "tensor"),
        P("dp", "tensor"),
        P(None, "tensor"),
        P("dp", "tensor"),
        P("dp", "tensor"),
        P("tensor"),
        P("tensor", "dp"),
        P(),
        P("dp", "tensor"),
        P("dp", "tensor"),
        P("tensor", "dp"),
        P("dp", "tensor", None),
        P(),
        P(),
    )
    return jax.shard_map(
        shards,
        mesh=mesh,
        in_specs=placed,
        out_specs=(
            P("dp", "tensor", None),
            P("dp", "tensor", None),
            P(),
            P("dp", "tensor"),
            P("dp", "tensor"),
            P(None, "tensor"),
            P("dp", "tensor"),
            P("dp", "tensor"),
            P("tensor"),
            P("tensor", "dp"),
            P(),
            P("dp", "tensor"),
            P("dp", "tensor"),
            P("tensor", "dp"),
        ),
        check_vma=False,
    )
```

```python
import functools

import jax
import jax.numpy as jnp
from jax import lax
from jax.experimental import pallas as pl
from jax.experimental.pallas import tpu as pltpu
from jax.sharding import PartitionSpec as P

MICRO = 4
EPS = 1e-06
MESH = pl.DeviceIdType.MESH
ANY = pl.BlockSpec(memory_space=pl.ANY)
VMEM = pl.BlockSpec(memory_space=pltpu.VMEM)
DMA = pltpu.SemaphoreType.DMA
BF16 = jnp.bfloat16
F32 = jnp.float32


def place():
    return lax.axis_index("dp"), lax.axis_index("tensor")


def greet(d, t, depth, dp_masks=(1, 2, 4), z_all=False):
    barrier = pltpu.get_barrier_semaphore()
    for mask in dp_masks:
        pl.semaphore_signal(barrier, inc=1, device_id=(d ^ mask, t), device_id_type=MESH)
    if z_all:
        for step in range(1, depth):
            pl.semaphore_signal(
                barrier, inc=1, device_id=(d, lax.rem(t + step, depth)), device_id_type=MESH
            )
        pl.semaphore_wait(barrier, len(dp_masks) + depth - 1)
        return

    @pl.when(t > 0)
    def _():
        pl.semaphore_signal(barrier, inc=1, device_id=(d, t - 1), device_id_type=MESH)

    @pl.when(t < depth - 1)
    def _():
        pl.semaphore_signal(barrier, inc=1, device_id=(d, t + 1), device_id_type=MESH)

    ends = jnp.where((t == 0) | (t == depth - 1), 1, 2)
    pl.semaphore_wait(barrier, len(dp_masks) + ends)


def add_rows(total, term, rows, step=32):
    step = min(step, rows)

    @pl.loop(0, rows, step=step)
    def _(start):
        part = pl.ds(pl.multiple_of(start, step), step)
        total[part, :] = (total[part, :].astype(F32) + term[part, :].astype(F32)).astype(BF16)


class WeightGather:
    def __init__(self, shard, out, local, send, recv, d, t):
        rows = shard.shape[0]
        half = rows // 2

        def view(slot, start, size):
            if len(out.shape) == 3:
                return out.at[slot, pl.ds(start, size)]
            return out.at[pl.ds(pl.multiple_of(slot * rows + start, 16), size)]

        top, low = (0, half), (half, half)
        plan = [
            (None, d, top, 2),
            (None, d, low, 4),
            (None, d, low, 2),
            (None, d, top, 4),
            (2, d ^ 2, top, 4),
            (4, d ^ 4, low, 2),
            (None, d, top, 1),
            (None, d, low, 1),
            (2, d ^ 2, top, 1),
            (4, d ^ 4, low, 1),
            (2, d ^ 2, low, 1),
            (4, d ^ 4, top, 1),
            (6, d ^ 6, top, 1),
            (6, d ^ 6, low, 1),
        ]
        self.copies = [
            pltpu.make_async_remote_copy(
                src_ref=shard.at[pl.ds(*part)] if came is None else view(slot, *part),
                dst_ref=view(slot, *part),
                send_sem=send.at[i],
                recv_sem=recv.at[i],
                device_id=(d ^ mask, t),
                device_id_type=MESH,
            )
            for i, (came, slot, part, mask) in enumerate(plan)
        ]
        self.own = pltpu.make_async_copy(shard, view(d, 0, rows), local)

    def start(self):
        for i in (0, 1, 2, 3, 6, 7):
            self.copies[i].start()
        self.own.start()

    def relay(self):
        c = self.copies
        c[0].wait_recv()
        c[4].start()
        c[1].wait_recv()
        c[5].start()
        c[8].start()
        c[9].start()

    def relay_two(self):
        c = self.copies
        c[2].wait_recv()
        c[10].start()
        c[3].wait_recv()
        c[11].start()

    def relay_last(self):
        c = self.copies
        c[4].wait_recv()
        c[12].start()
        c[5].wait_recv()
        c[13].start()

    def arrive(self):
        for i in range(6, 14):
            self.copies[i].wait_recv()
        self.own.wait()

    def end(self):
        for i in range(14):
            self.copies[i].wait_send()


def gather_scratch(count):
    return [DMA((count,)), DMA((count, 14)), DMA((count, 14))]


class GradScatter:
    ORDER = (6, 2, 4, 0)

    def __init__(self, grad, out, own, core, diag, last, local, send, recv, d, t):
        self.out, self.core, self.diag, self.last = out, core, diag, last
        self.grad, self.d, self.t = grad, d, t
        self.credit = None
        self.reused = self.again = False
        self.before = self.flush = None
        self.rows = rows = out.shape[0]
        half = rows // 2
        self.half = half
        self.top, self.low = pl.ds(0, half), pl.ds(half, half)

        def block(slot, start=0, size=rows):
            return grad.at[pl.ds(pl.multiple_of(slot * rows + start, 16), size)]

        if own is None:
            self.loads = []
            self.mine = lambda i, start=0, size=rows: block(d ^ self.ORDER[i], start, size)
        else:
            self.loads = [
                pltpu.make_async_copy(block(d ^ r), own.at[i], local.at[i])
                for i, r in enumerate(self.ORDER)
            ]
            self.mine = lambda i, start=0, size=rows: own.at[i, pl.ds(start, size)]
        mine, top, low = self.mine, self.top, self.low
        plan = [(block(d ^ 1 ^ r), core.at[i], 1) for i, r in enumerate(self.ORDER)] + [
            (mine(0, 0, half), diag.at[0], 2),
            (mine(0, half, half), diag.at[1], 4),
            (mine(1, 0, half), last.at[0, top], 2),
            (mine(2, half, half), last.at[1, low], 4),
            (mine(2, 0, half), last.at[1, top], 4),
            (mine(1, half, half), last.at[0, low], 2),
        ]
        self.copies = [
            pltpu.make_async_remote_copy(
                src_ref=src,
                dst_ref=dst,
                send_sem=send.at[i],
                recv_sem=recv.at[i],
                device_id=(d ^ mask, t),
                device_id_type=MESH,
            )
            for i, (src, dst, mask) in enumerate(plan)
        ]

    def start(self):
        if self.reused:
            pl.semaphore_wait(self.credit.at[0], 1)
        for i in range(4):
            self.copies[i].start()
        for load in self.loads:
            load.start()

    def pair(self, i):
        if self.loads:
            self.loads[i].wait()
        self.copies[i].wait_recv()
        add_rows(self.mine(i), self.core.at[i], self.rows)

    def first(self):
        self.pair(0)
        if self.reused:
            pl.semaphore_wait(self.credit.at[1], 1)
        self.copies[4].start()
        if self.reused:
            pl.semaphore_wait(self.credit.at[2], 1)
        self.copies[5].start()

    def second(self):
        self.pair(1)
        self.copies[6].start()
        self.pair(2)
        self.copies[7].start()
        self.pair(3)

    def third(self):
        c = self.copies
        c[4].wait_recv()
        add_rows(self.mine(2, 0, self.half), self.diag.at[0], self.half)
        c[8].start()
        c[5].wait_recv()
        add_rows(self.mine(1, self.half, self.half), self.diag.at[1], self.half)
        c[9].start()

    def end(self):
        for i in (6, 7, 8, 9):
            self.copies[i].wait_recv()
        step = 16
        own = self.mine(3)
        if self.before is not None:
            self.before.flush.wait()

        @pl.loop(0, self.rows, step=step)
        def _(start):
            part = pl.ds(pl.multiple_of(start, step), step)
            self.out[part, :] = (
                own[part, :].astype(F32)
                + self.last[0, part, :].astype(F32)
                + self.last[1, part, :].astype(F32)
            )

        if self.flush is not None:
            self.flush.start()
        for i in range(10):
            self.copies[i].wait_send()
        if self.again:
            for i, mask in enumerate((1, 2, 4)):
                pl.semaphore_signal(
                    self.credit.at[i], inc=1, device_id=(self.d ^ mask, self.t), device_id_type=MESH
                )


class PanelRing:
    def __init__(self, outs, scratch, d, t):
        grads, core, diag, last, stage, send, recv, credit, flush = scratch
        self.slots = slots = grads.shape[0]
        self.panels = []
        for i, out in enumerate(outs):
            q = i % slots
            panel = GradScatter(
                grads.at[q],
                stage.at[q],
                None,
                core.at[q],
                diag.at[q],
                last.at[q],
                None,
                send.at[q],
                recv.at[q],
                d,
                t,
            )
            panel.credit = credit.at[q]
            panel.reused = i >= slots
            panel.again = i + slots < len(outs)
            panel.before = self.panels[i - slots] if i >= slots else None
            panel.flush = pltpu.make_async_copy(stage.at[q], out, flush.at[q])
            self.panels.append(panel)

    def end(self):
        for panel in self.panels[-self.slots :]:
            panel.flush.wait()


def ring_scratch(slots, rows, n):
    return [
        pltpu.VMEM((slots, 8 * rows, n), BF16),
        pltpu.VMEM((slots, 4, rows, n), BF16),
        pltpu.VMEM((slots, 2, rows // 2, n), BF16),
        pltpu.VMEM((slots, 2, rows, n), BF16),
        pltpu.VMEM((slots, rows, n), F32),
        DMA((slots, 10)),
        DMA((slots, 10)),
        pltpu.SemaphoreType.REGULAR((slots, 3)),
        DMA((slots,)),
    ]


def scatter_scratch(shapes, loaded):
    own = [pltpu.VMEM((4,) + s, BF16) for s, far in zip(shapes, loaded) if far]
    core = [pltpu.VMEM((4,) + s, BF16) for s in shapes]
    diag = [pltpu.VMEM((2, s[0] // 2, s[1]), BF16) for s in shapes]
    last = [pltpu.VMEM((2,) + s, BF16) for s in shapes]
    n = len(shapes)
    return own + core + diag + last + [DMA((n, 4)), DMA((n, 10)), DMA((n, 10))]


def make_scatters(grads, outs, loaded, scratch, d, t):
    n = len(grads)
    scratch = list(scratch)
    own = [scratch.pop(0) if far else None for far in loaded]
    core, diag, last = (scratch[i * n : (i + 1) * n] for i in range(3))
    local, send, recv = scratch[3 * n :]
    return [
        GradScatter(
            grads[i],
            outs[i],
            own[i],
            core[i],
            diag[i],
            last[i],
            local.at[i],
            send.at[i],
            recv.at[i],
            d,
            t,
        )
        for i in range(n)
    ]


class LineGather:
    def __init__(self, block, out, local, send, recv, d, t, depth):
        self.block, self.out, self.send, self.recv = block, out, send, recv
        self.d, self.t, self.depth = d, t, depth
        self.rows = block.shape[-2]
        self.own = pltpu.make_async_copy(block, self.slot(t), local)

    def slot(self, j):
        rows = pl.ds(pl.multiple_of(j * self.rows, self.rows), self.rows)
        return self.out.at[:, rows] if len(self.out.shape) == 3 else self.out.at[rows]

    def copy(self, way, step, j, to):
        return pltpu.make_async_remote_copy(
            src_ref=self.block if step == 0 else self.slot(j),
            dst_ref=self.slot(j),
            send_sem=self.send.at[way, step],
            recv_sem=self.recv.at[way, step],
            device_id=(self.d, to),
            device_id_type=MESH,
        )

    def step(self, s):
        t, depth = self.t, self.depth
        if s == 0:
            self.own.start()
        if s > 0:

            @pl.when(t - s >= 0)
            def _():
                self.copy(0, s - 1, t, t).wait_recv()

        if s < depth - 1:

            @pl.when((t - s >= 0) & (t < depth - 1))
            def _():
                self.copy(0, s, t - s, t + 1).start()

        if s > 0:

            @pl.when(t + s < depth)
            def _():
                self.copy(1, s - 1, t, t).wait_recv()

        if s < depth - 1:

            @pl.when((t + s < depth) & (t > 0))
            def _():
                self.copy(1, s, t + s, t - 1).start()

    def end(self):
        t, depth = self.t, self.depth
        for s in range(depth - 1):

            @pl.when((t - s >= 0) & (t < depth - 1))
            def _():
                self.copy(0, s, t, t).wait_send()

            @pl.when((t + s < depth) & (t > 0))
            def _():
                self.copy(1, s, t, t).wait_send()


def line_gather_scratch(depth):
    return [DMA, DMA((2, depth - 1)), DMA((2, depth - 1))]


class LineScatter:
    def __init__(self, part, got, send, recv, d, t, depth, which=None):
        self.part, self.got, self.send, self.recv = part, got, send, recv
        self.d, self.t, self.depth = d, t, depth
        self.which = range(part.shape[0]) if which is None else which
        self.rows = part.shape[1] // depth

    def slot(self, way, j, s):
        return self.got.at[way, j - 1 if way == 0 else j, s]

    def copy(self, way, j, s, src, to):
        return pltpu.make_async_remote_copy(
            src_ref=src,
            dst_ref=self.slot(way, j, s),
            send_sem=self.send.at[way, j, s],
            recv_sem=self.recv.at[way, j, s],
            device_id=(self.d, to),
            device_id_type=MESH,
        )

    def block(self, j, s):
        return self.part.at[s, pl.ds(pl.multiple_of(j * self.rows, self.rows), self.rows)]

    def start(self, first=0, last=None):
        t, depth = self.t, self.depth
        steps = range(first, depth - 1 if last is None else last)

        @pl.when(t == 0)
        def _():
            for k in steps:
                for s in self.which:
                    j = depth - 1 - k
                    self.copy(0, j, s, self.block(j, s), t + 1).start()

        @pl.when(t == depth - 1)
        def _():
            for j in steps:
                for s in self.which:
                    self.copy(1, j, s, self.block(j, s), t - 1).start()

    def pass_on(self, way, j, to):
        for s in self.which:
            mine = self.slot(way, j, s)
            self.copy(way, j, s, mine, self.t).wait_recv()
            add_rows(mine, self.block(j, s), self.rows)
            self.copy(way, j, s, mine, to).start()

    def step(self, k):
        t, depth = self.t, self.depth
        right = depth - 1 - k + t
        left = k - (depth - 1 - t)

        @pl.when((t > 0) & (t < right) & (right < depth))
        def _():
            self.pass_on(0, right, t + 1)

        @pl.when((left >= 0) & (left < t) & (t < depth - 1))
        def _():
            self.pass_on(1, left, t - 1)

    def total(self, out):
        t, depth = self.t, self.depth
        mine = pl.ds(pl.multiple_of(t * self.rows, self.rows), self.rows)
        for s in self.which:
            out[s] = self.part[s, mine, :].astype(F32)

        @pl.when(t > 0)
        def _():
            for s in self.which:
                self.copy(0, t, s, self.slot(0, t, s), t).wait_recv()
                out[s] += self.got[0, t - 1, s].astype(F32)

        @pl.when(t < depth - 1)
        def _():
            for s in self.which:
                self.copy(1, t, s, self.slot(1, t, s), t).wait_recv()
                out[s] += self.got[1, t, s].astype(F32)

    def end(self):
        t, depth = self.t, self.depth
        for j in range(depth):
            for s in self.which:
                if j > 0:

                    @pl.when(j > t)
                    def _():
                        self.copy(0, j, s, self.slot(0, j, s), t).wait_send()

                if j < depth - 1:

                    @pl.when(j < t)
                    def _():
                        self.copy(1, j, s, self.slot(1, j, s), t).wait_send()


def line_scatter_scratch(seqs, rows, width, depth):
    return [
        pltpu.VMEM((2, depth - 1, seqs, rows, width), BF16),
        DMA((2, depth, seqs)),
        DMA((2, depth, seqs)),
    ]


def call(kernel, name, number, ins, outs, scratch, args, vmem=60 * 1024 * 1024):
    return pl.pallas_call(
        kernel,
        name=name,
        out_shape=[o[0] for o in outs],
        in_specs=ins,
        out_specs=[o[1] for o in outs],
        scratch_shapes=scratch,
        compiler_params=pltpu.CompilerParams(
            collective_id=number, has_side_effects=True, vmem_limit_bytes=vmem
        ),
    )(*args)


def shaped(shape, dtype, spec):
    return (jax.ShapeDtypeStruct(shape, dtype), spec)


def sigmoid(x):
    return 1.0 / (1.0 + jnp.exp(-x))


def one_less_exp(y):
    series = 1.0 + y / 6.0 * (1.0 + y / 7.0)
    for k in (5.0, 4.0, 3.0, 2.0):
        series = 1.0 + y / k * series
    return jnp.where(y > -0.5, -y * series, 1.0 - jnp.exp(y))


GELU_SCALE = 0.7978845608028654
GELU_CUBE = 0.044715


def gelu(x):
    return 0.5 * x * (1.0 + jnp.tanh(GELU_SCALE * (x + GELU_CUBE * x * x * x)))


def gelu_both(x):
    square = x * x
    bent = jnp.tanh(GELU_SCALE * (x + GELU_CUBE * square * x))
    half = 0.5 * (1.0 + bent)
    slope = half + 0.5 * x * (1.0 - bent * bent) * (
        GELU_SCALE * (1.0 + 3.0 * GELU_CUBE * square)
    )
    return x * half, slope


def rows_of(index, size):
    return pl.ds(pl.multiple_of(index * size, size), size)


def contract(left, right, dims):
    return lax.dot_general(left, right, ((dims[:1], dims[1:]), ((), ())), preferred_element_type=F32)


def scan_rows(rate, out, seqs, length, base=0, backward=False):
    tile = 8
    width = out.shape[1]
    row = lax.broadcasted_iota(jnp.int32, (tile, width), 0)

    def body(i, carried):
        k = length // tile - 1 - i if backward else i
        ends = []
        for s in range(seqs):
            start = pl.multiple_of(s * length + k * tile, tile)
            rows = pl.ds(start, tile)
            if backward:
                pair = rate[pl.ds(start, 2 * tile), :]
                step = pltpu.roll(pair, 2 * tile - 1, 0)[:tile]
                step = jnp.where((row == tile - 1) & (i == 0), 0.0, step)
            else:
                step = rate[rows, :]
            held = pl.ds(pl.multiple_of(base + start, tile), tile)
            drive = out[held, :]
            for shift in (1, 2, 4):
                turn = tile - shift if backward else shift
                inside = row < tile - shift if backward else row >= shift
                before = jnp.where(inside, pltpu.roll(drive, turn, 0), 0.0)
                drive = drive + step * before
                step = step * jnp.where(inside, pltpu.roll(step, turn, 0), 1.0)
            states = drive + step * carried[s]
            out[held, :] = states
            ends.append(states[0:1] if backward else states[tile - 1 : tile])
        return tuple(ends)

    start = tuple(jnp.zeros((1, width), F32) for _ in range(seqs))
    lax.fori_loop(0, length // tile, body, start)


STRIP = 16
PANEL = 640


def gate_blocks(parity, width, block):
    half = block // 2
    shift = parity * half
    blocks = []
    for k in range((width + half) // block):
        low, high = k * block - shift, (k + 1) * block - shift
        blocks.append((k, max(low, 0), min(high, width)))
    return blocks


def front_kernel(
    depth,
    normed_block,
    cot_block,
    gelu_shard,
    input_shard,
    gate_in_shard,
    gate_dec_shard,
    out_shard,
    down_shard,
    gate_shard,
    up_shard,
    taps,
    rate,
    act,
    gain,
    middle,
    normed_out,
    cot_out,
    normed_two_out,
    gelu_full,
    input_full,
    gate_in_full,
    gate_dec_full,
    out_full,
    down_full,
    gate_full,
    up_full,
    gelu_pre_out,
    input_pre_out,
    conv_out,
    window_out,
    gate_in_out,
    gate_dec_out,
    states_out,
    mixed_out,
    grad_hidden_out,
    gate_pre_out,
    *scratch,
):
    normed, gelu_w, input_w, gate_in_w, gate_dec_w, out_w = scratch[:6]
    gelu_pre, input_pre, conv, window, gate_in, gate_dec, decay, states, mixed, part = scratch[6:16]
    local, send, recv = scratch[16:19]
    line_sems = [scratch[19 + 3 * i : 22 + 3 * i] for i in range(5)]
    rim_send, rim_recv, save_sem = scratch[34:37]
    cot, normed_two, block_two, panel_w, product = scratch[37:42]
    panel_sem, product_sem = scratch[42:44]
    got, ssem, rsem = scratch[44:47]
    d, t = place()
    parity = lax.rem(t, 2)
    even = parity == 0
    odd = parity == 1
    greet(d, t, depth)
    seqs, length, model = normed.shape
    tokens = seqs * length
    width = conv.shape[1]
    block = gate_in_w.shape[0]
    half = block // 2
    spans = [pl.ds(s * length, length) for s in range(seqs)]
    first_line = LineGather(normed_block, normed, *line_sems[0], d, t, depth)
    cots = [
        LineGather(cot_block.at[s], cot.at[spans[s]], *line_sems[1 + s], d, t, depth)
        for s in range(seqs)
    ]
    twos = [
        LineGather(block_two.at[s], normed_two.at[spans[s]], *line_sems[3 + s], d, t, depth)
        for s in range(seqs)
    ]
    scatters = [LineScatter(part, got, ssem, rsem, d, t, depth, (s,)) for s in range(seqs)]
    pairs = (
        (gelu_shard, gelu_w),
        (input_shard, input_w),
        (gate_in_shard, gate_in_w),
        (gate_dec_shard, gate_dec_w),
        (out_shard, out_w),
        (down_shard, down_full),
        (gate_shard, gate_full),
        (up_shard, up_full),
    )
    gathers = [
        WeightGather(shard, full, local.at[i], send.at[i], recv.at[i], d, t)
        for i, (shard, full) in enumerate(pairs)
    ]
    saves = []

    def save(src, dst):
        copy = pltpu.make_async_copy(src, dst, save_sem.at[len(saves)])
        copy.start()
        saves.append(copy)

    one = gathers[:4]
    out_g, down_g, gate_g, up_g = gathers[4:]
    first_line.step(0)
    for g in one:
        g.start()
    for g in one:
        g.relay()
    out_g.start()
    first_line.step(1)
    for g in one:
        g.relay_two()
    for g in one:
        g.relay_last()
    first_line.step(2)
    out_g.relay()
    down_g.start()
    out_g.relay_two()
    out_g.relay_last()
    first_line.step(3)
    first_line.own.wait()
    cots[0].step(0)
    for g in one:
        g.arrive()
    save(normed, normed_out)
    save(gelu_w, gelu_full)
    save(input_w, input_full)
    save(gate_in_w, gate_in_full)
    save(gate_dec_w, gate_dec_full)

    for s in range(seqs):
        rows = pl.ds(s * length, length)
        input_pre[s, 0:8, :] = jnp.zeros((8, width), F32)
        input_pre[s, 8 : 8 + length, :] = contract(normed[s], input_w[...], (1, 0))
        gelu_pre[rows, :] = contract(normed[s], gelu_w[...], (1, 0))

    for s in range(seqs):

        @pl.loop(0, length // STRIP)
        def _(i):
            near = input_pre[s, pl.ds(pl.multiple_of(i * STRIP, STRIP), STRIP + 8), :]
            total = taps[0:1, :] * near[8:]
            for k in range(1, taps.shape[0]):
                total = total + taps[k : k + 1, :] * pltpu.roll(near, k, 0)[8:]
            rows = pl.ds(pl.multiple_of(s * length + i * STRIP, STRIP), STRIP)
            conv[rows, :] = total.astype(BF16)

    def rim(to, src, dst):
        return pltpu.make_async_remote_copy(
            src_ref=conv.at[:, pl.ds(src, half)],
            dst_ref=window.at[:, pl.ds(dst, half)],
            send_sem=rim_send,
            recv_sem=rim_recv,
            device_id=(d, to),
            device_id_type=MESH,
        )

    @pl.when(even)
    def _():
        rim(t + 1, width - half, 0).start()
        window[:, 0:width] = conv[...]

    @pl.when(odd)
    def _():
        rim(t - 1, 0, width).start()
        window[:, half : half + width] = conv[...]

    def gates(blocks):
        for k, low, high in blocks:
            near = window[:, k * block : (k + 1) * block]
            gate_in[:, low:high] = contract(near, gate_in_w[:, low:high], (1, 0))
            gate_dec[:, low:high] = contract(near, gate_dec_w[:, low:high], (1, 0))

    even_blocks, odd_blocks = gate_blocks(0, width, block), gate_blocks(1, width, block)

    @pl.when(even)
    def _():
        gates(even_blocks[:-1])

    @pl.when(odd)
    def _():
        gates(odd_blocks[1:])

    cots[0].step(1)
    down_g.relay()
    gate_g.start()

    @pl.when(even)
    def _():
        rim(t + 1, width - half, width).wait_recv()
        gates(even_blocks[-1:])

    @pl.when(odd)
    def _():
        rim(t - 1, 0, 0).wait_recv()
        gates(odd_blocks[:1])

    @pl.loop(0, tokens // STRIP)
    def _(i):
        rows = rows_of(i, STRIP)
        log = -8.0 * sigmoid(gate_dec[rows, :]) * rate[...]
        decay[rows, :] = jnp.exp(log)
        drive = jnp.sqrt(one_less_exp(2.0 * log)) * sigmoid(gate_in[rows, :])
        held = pl.ds(pl.multiple_of(i * STRIP + 8, 8), STRIP)
        states[held, :] = drive * conv[rows, :].astype(F32)

    states[0:8, :] = jnp.zeros((8, width), F32)
    cots[0].step(2)
    scan_rows(decay, states, seqs, length, base=8)

    @pl.loop(0, tokens // STRIP)
    def _(i):
        rows = rows_of(i, STRIP)
        held = pl.ds(pl.multiple_of(i * STRIP + 8, 8), STRIP)
        mixed[rows, :] = (gelu(gelu_pre[rows, :]) * states[held, :]).astype(BF16)

    panel = 512
    out_g.arrive()
    for s in range(seqs):

        @pl.loop(0, model // panel)
        def _(i):
            columns = rows_of(i, panel)
            part[s, :, columns] = contract(mixed[spans[s], :], out_w[columns, :], (1, 1)).astype(
                BF16
            )

        scatters[s].start()
    cots[0].step(3)
    cots[1].step(0)
    down_g.relay_two()
    scatters[0].step(1)
    save(gelu_pre, gelu_pre_out)
    save(input_pre, input_pre_out)
    save(conv, conv_out)
    save(window, window_out)
    save(gate_in, gate_in_out)
    save(gate_dec, gate_dec_out)
    save(states, states_out)
    save(mixed, mixed_out)
    save(out_w, out_full)
    scatters[0].step(2)
    down_g.relay_last()

    def norm_step(s):
        scatters[s].total(middle)
        value = middle[s] + act[s].astype(F32)
        middle[s] = value
        inverse = lax.rsqrt(jnp.mean(value * value, axis=-1, keepdims=True) + EPS)
        block_two[s] = (value * inverse * gain[...]).astype(BF16)
        twos[s].step(0)

    norm_step(0)
    gate_g.relay()
    up_g.start()
    scatters[1].step(1)
    twos[0].step(1)
    scatters[1].step(2)
    gate_g.relay_two()
    norm_step(1)
    cots[1].step(1)
    gate_g.relay_last()
    twos[0].step(2)
    cots[1].step(2)
    twos[1].step(1)
    cots[1].step(3)
    for s in range(seqs):
        cots[s].own.wait()
    save(cot, cot_out)
    up_g.relay()
    panels = down_full.shape[1] // PANEL

    def load_panel(full, i):
        columns = pl.ds(i % panels * PANEL, PANEL)
        copy = pltpu.make_async_copy(full.at[:, columns], panel_w.at[i % 2], panel_sem.at[i % 2])
        copy.start()
        return copy

    results = []

    def multiply(left, full, out, i, following):
        nonlocal loaded
        loaded.wait()
        if following is not None:
            loaded = load_panel(*following)
        if len(results) >= 2:
            results[-2].wait()
        for s in range(seqs):
            product[i % 2, spans[s], :] = contract(left[spans[s], :], panel_w[i % 2], (1, 0))
        columns = pl.ds(i % panels * PANEL, PANEL)
        copy = pltpu.make_async_copy(product.at[i % 2], out.at[:, columns], product_sem.at[i % 2])
        copy.start()
        results.append(copy)

    down_g.arrive()
    gate_g.arrive()
    loaded = load_panel(down_full, 0)
    for i in range(panels):
        multiply(
            cot,
            down_full,
            grad_hidden_out,
            i,
            (down_full, i + 1) if i < panels - 1 else (gate_full, panels),
        )
    twos[0].step(3)
    twos[1].step(2)
    up_g.relay_two()
    twos[1].step(3)
    for s in range(seqs):
        twos[s].own.wait()
    save(normed_two, normed_two_out)
    for i in range(panels, 2 * panels):
        multiply(
            normed_two,
            gate_full,
            gate_pre_out,
            i,
            (gate_full, i + 1) if i < 2 * panels - 1 else None,
        )
    up_g.relay_last()
    up_g.arrive()

    @pl.when(even)
    def _():
        rim(t + 1, width - half, 0).wait_send()

    @pl.when(odd)
    def _():
        rim(t - 1, 0, width).wait_send()

    for g in gathers:
        g.end()
    for line in [first_line] + cots + twos + scatters:
        line.end()
    for copy in saves + results[-2:]:
        copy.wait()


def front_phase(normed, cot, weights, taps, rate, act, gain, depth):
    seqs, rows, model = normed.shape
    length = rows * depth
    tokens = seqs * length
    n = len(weights)
    block, width = weights[2].shape[0] * 8, weights[0].shape[1]
    units = weights[-1].shape[1]
    wide = block // 2 + width
    wide_rows = (seqs, length, model)
    mixers = [(model, width), (model, width), (block, width), (block, width), (model, width)]
    saved = [
        ((tokens, width), F32),
        ((seqs, length + 8, width), F32),
        ((tokens, width), BF16),
        ((tokens, wide), BF16),
        ((tokens, width), F32),
        ((tokens, width), F32),
        ((tokens + 8, width), F32),
        ((tokens, width), BF16),
    ]
    outs = [shaped(act.shape, F32, VMEM)]
    outs += [shaped(wide_rows, BF16, ANY)] + [shaped((tokens, model), BF16, ANY)] * 2
    outs += [shaped(shape, BF16, ANY) for shape in mixers]
    outs += [shaped((model, units), BF16, ANY)] * 3
    outs += [shaped(shape, dtype, ANY) for shape, dtype in saved]
    outs += [shaped((tokens, units), F32, ANY)] * 2
    saved_scratch = saved[:6] + [((tokens, width), F32)] + saved[6:] + [(wide_rows, BF16)]
    scratch = [pltpu.VMEM(wide_rows, BF16)]
    scratch += [pltpu.VMEM(shape, BF16) for shape in mixers]
    scratch += [pltpu.VMEM(shape, dtype) for shape, dtype in saved_scratch]
    scratch += gather_scratch(n) + line_gather_scratch(depth) * 5 + [DMA, DMA, DMA((16,))]
    scratch += [
        pltpu.VMEM((tokens, model), BF16),
        pltpu.VMEM((tokens, model), BF16),
        pltpu.VMEM(act.shape, BF16),
        pltpu.VMEM((2, model, PANEL), BF16),
        pltpu.VMEM((2, tokens, PANEL), F32),
        DMA((2,)),
        DMA((2,)),
    ]
    scratch += line_scatter_scratch(seqs, rows, model, depth)
    res = call(
        functools.partial(front_kernel, depth),
        "front_phase",
        0,
        [VMEM] * (6 + n),
        outs,
        scratch,
        (normed, cot) + tuple(weights) + (taps, rate.reshape(1, width), act, gain.reshape(1, model)),
    )
    return res[0], res[1:4], res[4:9], res[9:12], res[12:20], res[20:]


def norm_back(value, gain, error):
    inverse = lax.rsqrt(jnp.mean(value * value, axis=-1, keepdims=True) + EPS)
    scaled = error * gain
    mean = jnp.mean(scaled * value, axis=-1, keepdims=True)
    grad = inverse * scaled - value * (inverse * inverse * inverse * mean)
    return grad, jnp.sum(error * value * inverse, axis=0, keepdims=True)


HOSTED = 5


def feed_kernel(
    depth,
    normed_in,
    cot_in,
    gate_in,
    up_in,
    down_in,
    grad_hidden_in,
    gate_pre_in,
    middle,
    gain,
    cot_own,
    grad,
    wide,
    gain_grad,
    feed_out,
    *refs,
):
    panels = gate_in.shape[1] // PANEL
    n_panels = 3 * panels
    outs, refs = refs[:n_panels], refs[n_panels:]
    normed, cot, hidden, gate_rows, lift_rows = refs[:5]
    gate_w, up_w, down_w, gate_pre, lift_pre, grad_hidden, acc, part, block, stage = refs[5:15]
    got, ssem, rsem = refs[15:18]
    load_sem, weight_sem, save_sem = refs[18:21]
    lines = refs[21:24], refs[24:27]
    d, t = place()
    greet(d, t, depth)
    seqs = middle.shape[0]
    tokens, model = normed_in.shape
    length = tokens // seqs
    tile = 512
    ring = PanelRing(outs[:HOSTED], refs[27:], d, t)
    scatters = [LineScatter(part, got, ssem, rsem, d, t, depth, (s,)) for s in range(seqs)]
    gathers = [
        LineGather(block.at[s], wide.at[s], *lines[s], d, t, depth) for s in range(seqs)
    ]

    def load(i, src, dst):
        copy = pltpu.make_async_copy(src, dst, load_sem.at[i])
        copy.start()
        return copy

    def weight(i, src, dst, p):
        copy = pltpu.make_async_copy(
            src.at[:, pl.ds(p * PANEL, PANEL)], dst, weight_sem.at[i]
        )
        copy.start()
        return copy

    def held_rows(s, p):
        rows, columns = pl.ds(s * length, length), pl.ds(p * PANEL, PANEL)
        q = (s * panels + p) % 2
        return [
            load(2 + q, gate_pre_in.at[rows, columns], gate_pre.at[q]),
            load(4 + q, grad_hidden_in.at[rows, columns], grad_hidden.at[q]),
        ]

    normed_load = load(0, normed_in, normed)
    ups = (up_w, down_w)
    up_load = weight(1, up_in, up_w, 0)
    row_loads = held_rows(0, 0)
    gate_load = weight(0, gate_in, gate_w, 0)
    cot_load = load(1, cot_in, cot)

    def forward(s, p, more):
        nonlocal gate_load, up_load, row_loads
        rows = pl.ds(s * length, length)
        columns = pl.ds(p * PANEL, PANEL)
        q = (s * panels + p) % 2
        if s == 0 and p == 0:
            normed_load.wait()
        up = ups[q]
        up_load.wait()
        if more is not None:
            up_load = weight(2 - q, up_in, ups[1 - q], more)
        lift_pre[...] = contract(normed[rows, :], up[...], (1, 0))
        for copy in row_loads:
            copy.wait()
        if more is not None:
            row_loads = held_rows(*((s, more) if more > p else (s + 1, more)))

        @pl.loop(0, length // STRIP)
        def _(i):
            strip = rows_of(i, STRIP)
            held = pl.ds(pl.multiple_of(s * length + i * STRIP, STRIP), STRIP)
            act, slope = gelu_both(gate_pre[q, strip, :])
            lift = lift_pre[strip, :]
            came = grad_hidden[q, strip, :]
            hidden[held, columns] = (act * lift).astype(BF16)
            gate_rows[held, columns] = (came * lift * slope).astype(BF16)
            lift_rows[held, columns] = (came * act).astype(BF16)

        gate_load.wait()

        @pl.loop(0, model // tile)
        def _(i):
            out = rows_of(i, tile)
            value = contract(gate_rows[rows, columns], gate_w[out, :], (1, 1))
            value = value + contract(lift_rows[rows, columns], up[out, :], (1, 1))
            if p == 0:
                acc[:, out] = value
            elif p < panels - 1:
                acc[:, out] += value
            else:
                part[s, :, out] = (acc[:, out] + value).astype(BF16)

        if more is not None:
            gate_load = weight(0, gate_in, gate_w, more)

    kinds = ((cot, hidden), (normed, gate_rows), (normed, lift_rows))

    def weight_grad(i, out):
        left, right = kinds[i // panels]
        columns = pl.ds(i % panels * PANEL, PANEL)

        @pl.loop(0, model // tile)
        def _(k):
            rows = rows_of(k, tile)
            out[rows, :] = contract(left[:, rows], right[:, columns], (0, 0)).astype(BF16)

    def begin(i):
        panel = ring.panels[i]
        weight_grad(i, panel.grad)
        panel.start()
        panel.first()
        panel.second()

    def norm_step(s):
        scatters[s].total(grad)
        change, gain_part = norm_back(middle[s], gain[...], grad[s])
        change = change + cot_own[s]
        grad[s] = change
        block[s] = change.astype(BF16)
        if s == 0:
            gain_grad[...] = gain_part
        else:
            gain_grad[...] += gain_part

    for p in range(panels):
        forward(0, p, (p + 1) % panels)
    scatters[0].start()
    forward(1, 0, 1)
    scatters[0].step(1)
    cot_load.wait()
    begin(0)
    forward(1, 1, 2)
    scatters[0].step(2)
    ring.panels[0].third()
    begin(1)
    forward(1, 2, None)
    down_loads = [weight(0, down_in, gate_w, 0), weight(1, down_in, up_w, 1)]
    down_loads.append(weight(2, down_in, down_w, 2))
    scatters[1].start()
    norm_step(0)
    gathers[0].step(0)
    ring.panels[0].end()
    ring.panels[1].third()
    begin(2)
    scatters[1].step(1)
    gathers[0].step(1)
    ring.panels[1].end()
    ring.panels[2].third()
    begin(3)
    scatters[1].step(2)
    gathers[0].step(2)
    ring.panels[2].end()
    ring.panels[3].third()
    begin(4)
    norm_step(1)
    gathers[1].step(0)
    gathers[0].step(3)
    pending = {}

    def keep(key, src, dst):
        if key in pending:
            pending[key].wait()
        pending[key] = pltpu.make_async_copy(src, dst, save_sem.at[key])
        pending[key].start()

    def feed(s):
        rows = pl.ds(s * length, length)
        if pending:
            pending.pop(0).wait()
        downs = (gate_w, up_w, down_w)

        @pl.loop(0, model // tile)
        def _(i):
            out = rows_of(i, tile)
            value = contract(hidden[rows, 0:PANEL], downs[0][out, :], (1, 1))
            for p in range(1, panels):
                columns = pl.ds(p * PANEL, PANEL)
                value = value + contract(hidden[rows, columns], downs[p][out, :], (1, 1))
            stage[:, out] = value.astype(BF16)

        keep(0, stage, feed_out.at[s])

    def store_grad(i):
        q = i % ring.slots
        if 1 + q in pending:
            pending.pop(1 + q).wait()
        weight_grad(i, ring.panels[q].grad)
        keep(1 + q, ring.panels[q].grad, outs[i])

    for copy in down_loads:
        copy.wait()
    feed(0)
    gathers[1].step(1)
    ring.panels[3].end()
    ring.panels[4].third()
    feed(1)
    gathers[1].step(2)
    store_grad(5)
    store_grad(6)
    ring.panels[4].end()
    gathers[1].step(3)
    store_grad(7)
    store_grad(8)
    ring.end()
    for copy in pending.values():
        copy.wait()
    for line in scatters:
        line.end()
    for line in gathers:
        line.own.wait()
        line.end()


def feed_phase(normed, cot, weights, held, middle, gain, cot_own, depth):
    down_w, gate_w, up_w = weights
    seqs, rows, model = middle.shape
    tokens = normed.shape[0]
    length = tokens // seqs
    wide_rows = (seqs, length, model)
    units = gate_w.shape[1]
    count = 3 * (units // PANEL)
    outs = [
        shaped(middle.shape, F32, VMEM),
        shaped(wide_rows, BF16, ANY),
        shaped((1, model), F32, VMEM),
        shaped(wide_rows, BF16, ANY),
    ]
    outs += [shaped((model // 8, PANEL), F32, ANY)] * HOSTED
    outs += [shaped((model, PANEL), BF16, ANY)] * (count - HOSTED)
    scratch = [pltpu.VMEM((tokens, model), BF16)] * 2
    scratch += [pltpu.VMEM((tokens, units), BF16)] * 3
    scratch += [pltpu.VMEM((model, PANEL), BF16)] * 3
    scratch += [pltpu.VMEM((2, length, PANEL), F32), pltpu.VMEM((length, PANEL), F32)]
    scratch += [pltpu.VMEM((2, length, PANEL), F32)]
    scratch += [
        pltpu.VMEM((length, model), F32),
        pltpu.VMEM(wide_rows, BF16),
        pltpu.VMEM(middle.shape, BF16),
        pltpu.VMEM((length, model), BF16),
    ]
    scratch += line_scatter_scratch(seqs, rows, model, depth)
    scratch += [DMA((6,)), DMA((3,)), DMA((8,))]
    scratch += line_gather_scratch(depth) * 2
    scratch += ring_scratch(3, model // 8, PANEL)
    res = call(
        functools.partial(feed_kernel, depth),
        "feed_phase",
        2,
        [ANY] * 7 + [VMEM] * 3,
        outs,
        scratch,
        (normed, cot, gate_w, up_w, down_w) + tuple(held) + (middle, gain.reshape(1, model), cot_own),
    )
    return res[0], res[1], res[2], res[3], res[4:]


def mixer_back_kernel(
    depth,
    n_panels,
    branch_in,
    normed_in,
    out_w_in,
    gelu_pre_in,
    input_pre_in,
    conv_in,
    window_in,
    gate_in_in,
    gate_dec_in,
    states_in,
    mixed_in,
    gelu_w_in,
    input_w_in,
    gate_in_w_in,
    gate_dec_w_in,
    feed,
    middle,
    taps,
    rate,
    act,
    gain,
    grad_middle,
    mlp_part,
    *refs,
):
    panels_in, refs = refs[:n_panels], refs[n_panels:]
    n_sums = n_panels + 3
    output, input_grad, gains, smalls, gate_in_out, gate_dec_out = refs[:6]
    panels_out, scratch = refs[6 : 6 + n_sums], refs[6 + n_sums :]
    branch, weight, input_w = scratch[:3]
    gelu_pre, input_pre, conv, window, gate_in, gate_dec, states, gate_in_w, gate_dec_w = scratch[3:12]
    grad, decay, grad_conv, gelu_grad, input_rows, grad_in, grad_dec, mixed = scratch[12:20]
    rim_out, rim_in, gate_in_grad, gate_dec_grad, part, sums, total = scratch[20:27]
    got, ssem, rsem = scratch[27:30]
    last_got, last_ssem, last_rsem = scratch[30:33]
    rim_send, rim_recv, load_sem, panel_sem = scratch[33:37]
    small, small_all, pack, packs, line_pack, line_packs = scratch[37:43]
    psend, precv, qsend, qrecv, zsend, zrecv = scratch[43:49]
    ring = PanelRing(panels_out, scratch[49:58], *place())
    d, t = place()
    parity = lax.rem(t, 2)
    even = parity == 0
    odd = parity == 1
    greet(d, t, depth, dp_masks=(1, 2, 3, 4, 5, 6, 7), z_all=True)
    seqs, length, model = branch_in.shape
    tokens = seqs * length
    width = conv.shape[1]
    block = gate_in_w.shape[0]
    half = block // 2
    even_blocks, odd_blocks = gate_blocks(0, width, block), gate_blocks(1, width, block)
    gate_scatters = make_scatters(
        (gate_in_grad, gate_dec_grad),
        (gate_in_out, gate_dec_out),
        (False, False),
        scratch[58:],
        d,
        t,
    )
    line = LineScatter(feed, got, ssem, rsem, d, t, depth)
    last_line = LineScatter(part, last_got, last_ssem, last_rsem, d, t, depth)

    def load(i, src, dst):
        copy = pltpu.make_async_copy(src, dst, load_sem.at[i])
        copy.start()
        return copy

    def load_wide(i, src):
        return [
            load(i + s, src.at[s], branch.at[pl.ds(s * length, length)]) for s in range(seqs)
        ]

    early = [load(0, out_w_in, weight)] + load_wide(12, branch_in)
    next_ = [
        load(2, gelu_pre_in, gelu_pre),
        load(3, states_in, states),
        load(4, gate_dec_in, gate_dec),
    ]
    line.start(0, 1)
    panel_loads = [
        pltpu.make_async_copy(src, panel.grad, panel_sem.at[i])
        for i, (src, panel) in enumerate(zip(panels_in, ring.panels))
    ]

    def weight_grad(left, right, out):
        panel = 512

        @pl.loop(0, model // panel)
        def _(i):
            columns = rows_of(i, panel)
            out[columns, :] = contract(left[:, columns], right[...], (0, 0)).astype(BF16)

    def dp_copies(src, dst, send, recv):
        return [
            pltpu.make_async_remote_copy(
                src_ref=src,
                dst_ref=dst.at[d],
                send_sem=send.at[mask - 1],
                recv_sem=recv.at[mask - 1],
                device_id=(d ^ mask, t),
                device_id_type=MESH,
            )
            for mask in range(1, 8)
        ]

    def begin(i):
        if i < n_panels:
            panel_loads[i].wait()
        ring.panels[i].start()
        ring.panels[i].first()
        ring.panels[i].second()

    def finish(i):
        ring.panels[i].end()
        if i + ring.slots < n_panels:
            panel_loads[i + ring.slots].start()

    for i in range(ring.slots):
        panel_loads[i].start()
    then = [
        load(5, gate_in_in, gate_in),
        load(6, conv_in, conv),
        load(7, window_in, window),
        load(8, gate_in_w_in, gate_in_w),
        load(9, gate_dec_w_in, gate_dec_w),
        load(10, input_pre_in, input_pre),
        load(11, input_w_in, input_w),
        load(1, mixed_in, mixed),
    ]
    for copy in early:
        copy.wait()
    for s in range(seqs):
        rows = pl.ds(s * length, length)
        grad[rows, :] = contract(branch[rows, :], weight[...], (1, 0))
    reload = load(0, gelu_w_in, weight)
    begin(0)
    for copy in next_:
        copy.wait()

    @pl.loop(0, tokens // STRIP)
    def _(i):
        rows = rows_of(i, STRIP)
        held = pl.ds(pl.multiple_of(i * STRIP + 8, 8), STRIP)
        act, slope = gelu_both(gelu_pre[rows, :])
        came = grad[rows, :]
        gelu_grad[rows, :] = (came * states[held, :] * slope).astype(BF16)
        grad[rows, :] = came * act
        decay[rows, :] = jnp.exp(-8.0 * sigmoid(gate_dec[rows, :]) * rate[...])

    decay[tokens : tokens + 8, :] = jnp.zeros((8, width), F32)
    begin(1)
    ring.panels[0].third()
    scan_rows(decay, grad, seqs, length, backward=True)
    for copy in then:
        copy.wait()
    sums[...] = jnp.zeros(sums.shape, F32)

    def fold(value):
        return value[0:8] + value[8:16]

    first_row = lax.broadcasted_iota(jnp.int32, (STRIP, width), 0) == 0
    for s in range(seqs):

        @pl.loop(0, length // STRIP)
        def _(i):
            start = pl.multiple_of(s * length + i * STRIP, STRIP)
            rows = pl.ds(start, STRIP)
            earlier = pltpu.roll(states[pl.ds(start, STRIP + 8), :], 1, 0)[8:]
            earlier = jnp.where(first_row & (i == 0), 0.0, earlier)
            came = grad[rows, :]
            open_in = sigmoid(gate_in[rows, :])
            open_dec = sigmoid(gate_dec[rows, :])
            slow = -8.0 * rate[...]
            lost = one_less_exp(2.0 * open_dec * slow)
            root = jnp.sqrt(lost)
            value = conv[rows, :].astype(F32)
            step = decay[rows, :]
            through = came * open_in
            grad_log = step * (came * earlier - through * value * step / root)
            sums[0] += fold(grad_log * (-8.0 * open_dec))
            through = through * root
            grad_conv[s, pl.ds(pl.multiple_of(i * STRIP, STRIP), STRIP), :] = through
            grad_in[rows, :] = (through * value * (1.0 - open_in)).astype(BF16)
            grad_dec[rows, :] = (grad_log * slow * open_dec * (1.0 - open_dec)).astype(BF16)

        grad_conv[s, length : length + 8, :] = jnp.zeros((8, width), F32)

    def gates_back(k, low, high):
        return contract(grad_in[:, low:high], gate_in_w[:, low:high], (1, 1)) + contract(
            grad_dec[:, low:high], gate_dec_w[:, low:high], (1, 1)
        )

    def add_conv(low, high, value):
        for s in range(seqs):
            grad_conv[s, 0:length, low:high] += value[s * length : (s + 1) * length]

    def rim(to):
        return pltpu.make_async_remote_copy(
            src_ref=rim_out,
            dst_ref=rim_in,
            send_sem=rim_send,
            recv_sem=rim_recv,
            device_id=(d, to),
            device_id_type=MESH,
        )

    @pl.when(even)
    def _():
        value = gates_back(*even_blocks[-1])
        rim_out[...] = value[:, half:].astype(BF16)
        rim(t + 1).start()
        add_conv(width - half, width, value[:, :half])

    @pl.when(odd)
    def _():
        value = gates_back(*odd_blocks[0])
        rim_out[...] = value[:, :half].astype(BF16)
        rim(t - 1).start()
        add_conv(0, half, value[:, half:])

    line.start(1)
    line.step(1)
    finish(0)
    ring.panels[1].third()

    def inner(blocks):
        for k, low, high in blocks:
            add_conv(low, high, gates_back(k, low, high))

    def gate_grads(blocks):
        for k, low, high in blocks:
            near = window[:, k * block : (k + 1) * block]
            gate_in_grad[:, low:high] = contract(near, grad_in[:, low:high], (0, 0)).astype(BF16)
            gate_dec_grad[:, low:high] = contract(near, grad_dec[:, low:high], (0, 0)).astype(BF16)

    @pl.when(even)
    def _():
        inner(even_blocks[:-1])
        gate_grads(even_blocks)

    @pl.when(odd)
    def _():
        inner(odd_blocks[1:])
        gate_grads(odd_blocks)

    for g in gate_scatters:
        g.start()
    begin(2)

    @pl.when(even)
    def _():
        rim(t + 1).wait()
        add_conv(width - half, width, rim_in[...].astype(F32))

    @pl.when(odd)
    def _():
        rim(t - 1).wait()
        add_conv(0, half, rim_in[...].astype(F32))

    for s in range(seqs):

        @pl.loop(0, length // STRIP)
        def _(i):
            near = pl.ds(pl.multiple_of(i * STRIP, STRIP), STRIP + 8)
            later = grad_conv[s, near, :]
            before = input_pre[s, near, :]
            here = later[:STRIP]
            value = taps[0:1, :] * here
            sums[1] += fold(here * before[8:])
            for k in range(1, taps.shape[0]):
                value = value + taps[k : k + 1, :] * pltpu.roll(later, STRIP + 8 - k, 0)[:STRIP]
                sums[1 + k] += fold(here * pltpu.roll(before, k, 0)[8:])
            rows = pl.ds(pl.multiple_of(s * length + i * STRIP, STRIP), STRIP)
            input_rows[rows, :] = value.astype(BF16)

    finish(1)
    ring.panels[2].third()
    for k in range(sums.shape[0]):
        small[k : k + 1, :] = jnp.sum(sums[k], axis=0, keepdims=True)
    small[sums.shape[0] :, :] = jnp.zeros((8 - sums.shape[0], width), F32)
    small_copies = dp_copies(small, small_all, qsend, qrecv)
    for c in small_copies:
        c.start()
    small_all[d] = small[...]
    reload.wait()
    panel = 512

    @pl.loop(0, weight.shape[0] // panel)
    def _(i):
        columns = rows_of(i, panel)
        value = contract(gelu_grad[...], weight[columns, :], (1, 1))
        value = (value + contract(input_rows[...], input_w[columns, :], (1, 1))).astype(BF16)
        for s in range(seqs):
            part[s, :, columns] = value[s * length : (s + 1) * length]

    last_line.start()
    begin(3)
    for g in gate_scatters:
        g.first()
        g.second()
    line.step(2)
    finish(2)
    ring.panels[3].third()
    weight_grad(branch, mixed, ring.panels[4].grad)
    wide_loads = load_wide(12, normed_in)
    begin(4)
    for g in gate_scatters:
        g.third()
    line.total(total)
    output[...] = (total[...] + middle[...]).astype(BF16)
    finish(3)
    ring.panels[4].third()
    for copy in wide_loads:
        copy.wait()
    weight_grad(branch, gelu_grad, ring.panels[5].grad)
    begin(5)
    last_line.step(1)
    finish(4)
    ring.panels[5].third()
    weight_grad(branch, input_rows, ring.panels[6].grad)
    begin(6)
    last_line.step(2)
    finish(5)
    ring.panels[6].third()
    last_line.total(input_grad)
    quarter = pack.shape[1]
    for i in range(4):
        pack[4 + i : 5 + i, :] = mlp_part[:, i * quarter : (i + 1) * quarter]
    for s in range(seqs):
        change, gain_part = norm_back(act[s].astype(F32), gain[...], input_grad[s])
        input_grad[s] = change + grad_middle[s]
        for i in range(4):
            piece = gain_part[:, i * quarter : (i + 1) * quarter]
            if s == 0:
                pack[i : i + 1, :] = piece
            else:
                pack[i : i + 1, :] += piece
    pack_copies = dp_copies(pack, packs, psend, precv)
    for c in pack_copies:
        c.start()
    packs[d] = pack[...]
    for c in small_copies:
        c.wait_recv()
    sum_ = small_all[0]
    for i in range(1, 8):
        sum_ = sum_ + small_all[i]
    smalls[...] = sum_
    for g in gate_scatters:
        g.end()
    for c in pack_copies:
        c.wait_recv()
    sum_ = packs[0]
    for i in range(1, 8):
        sum_ = sum_ + packs[i]
    line_pack[...] = sum_
    z_copies = [
        pltpu.make_async_remote_copy(
            src_ref=line_pack,
            dst_ref=line_packs.at[t],
            send_sem=zsend.at[step - 1],
            recv_sem=zrecv.at[step - 1],
            device_id=(d, lax.rem(t + step, depth)),
            device_id_type=MESH,
        )
        for step in range(1, depth)
    ]
    for c in z_copies:
        c.start()
    line_packs[t] = sum_
    finish(6)
    for c in z_copies:
        c.wait_recv()
    sum_ = line_packs[0]
    for i in range(1, depth):
        sum_ = sum_ + line_packs[i]
    gains[...] = sum_
    for c in small_copies + pack_copies + z_copies:
        c.wait_send()
    ring.end()
    line.end()
    last_line.end()


def mixer_back_phase(
    branch, normed, saved, weights, panels, feed, middle, taps, rate, act, gain, grad_middle,
    mlp_part, depth,
):
    seqs, length, model = branch.shape
    tokens = seqs * length
    gelu_w, input_w, gate_in_w, gate_dec_w, out_w = weights[:5]
    gelu_pre, input_pre, conv, window, gate_in, gate_dec, states, mixed = saved
    width = out_w.shape[1]
    block = gate_in_w.shape[0]
    half = block // 2
    n = len(panels)
    panel = (panels[0].shape[0] // 8, panels[0].shape[1])
    gate = (block // 8, width)
    pack = (8, model // 4)
    small = (8, width)
    flat = (tokens, width)
    outs = [
        shaped(middle.shape, BF16, VMEM),
        shaped(middle.shape, F32, VMEM),
        shaped(pack, F32, VMEM),
        shaped(small, F32, VMEM),
        shaped(gate, F32, VMEM),
        shaped(gate, F32, VMEM),
    ] + [shaped(panel, F32, ANY)] * (n + 3)
    scratch = [pltpu.VMEM((tokens, model), BF16)]
    scratch += [
        pltpu.VMEM(x.shape, x.dtype)
        for x in (
            out_w,
            input_w,
            gelu_pre,
            input_pre,
            conv,
            window,
            gate_in,
            gate_dec,
            states,
            gate_in_w,
            gate_dec_w,
        )
    ]
    scratch += [
        pltpu.VMEM(flat, F32),
        pltpu.VMEM((tokens + 8, width), F32),
        pltpu.VMEM((seqs, length + 8, width), F32),
    ]
    scratch += [pltpu.VMEM(flat, BF16)] * 5
    scratch += [pltpu.VMEM((tokens, half), BF16)] * 2
    scratch += [pltpu.VMEM(gate_in_w.shape, BF16)] * 2
    scratch += [
        pltpu.VMEM(branch.shape, BF16),
        pltpu.VMEM((1 + taps.shape[0], 8, width), F32),
        pltpu.VMEM(middle.shape, F32),
    ]
    scratch += line_scatter_scratch(seqs, length // depth, model, depth) * 2
    scratch += [DMA, DMA, DMA((12 + seqs,)), DMA((n,))]
    scratch += [
        pltpu.VMEM(small, F32),
        pltpu.VMEM((8,) + small, F32),
        pltpu.VMEM(pack, F32),
        pltpu.VMEM((8,) + pack, F32),
        pltpu.VMEM(pack, F32),
        pltpu.VMEM((depth,) + pack, F32),
    ]
    scratch += [DMA((7,))] * 4 + [DMA((depth - 1,))] * 2
    scratch += ring_scratch(2, *panel)
    scratch += scatter_scratch([gate] * 2, (False, False))
    res = call(
        functools.partial(mixer_back_kernel, depth, n),
        "mixer_back_phase",
        3,
        [ANY] * 15 + [VMEM] * 8 + [ANY] * n,
        outs,
        scratch,
        (
            branch,
            normed,
            out_w,
            gelu_pre,
            input_pre,
            conv,
            window,
            gate_in,
            gate_dec,
            states,
            mixed,
            gelu_w,
            input_w,
            gate_in_w,
            gate_dec_w,
            feed,
            middle,
            taps,
            rate.reshape(1, width),
            act,
            gain.reshape(1, model),
            grad_middle,
            mlp_part,
        )
        + tuple(panels),
        vmem=63 * 1024 * 1024,
    )
    return res[0], res[1], res[2].reshape(2, model), res[3], res[4:6], res[6:]


def swapped(block, axis):
    count = lax.axis_size(axis)
    return lax.ppermute(block, axis, [(i, i ^ 1) for i in range(count)])


def normalize(value_entries, scale_gain):
    return (
        value_entries
        * lax.rsqrt(jnp.mean(value_entries * value_entries, axis=-1, keepdims=True) + EPS)
        * scale_gain
    )


def causal_conv(value_entries, kernel):
    summed = value_entries * kernel[0]
    for offset in range(1, kernel.shape[0]):
        shifted = jnp.concatenate(
            [jnp.zeros_like(value_entries[:, :offset]), value_entries[:, :-offset]], axis=1
        )
        summed = summed + shifted * kernel[offset]
    return summed


def decay_inputs(input_pre, decay_pre, conv_vals, decay_rate):
    log_decay = -8.0 * jax.nn.sigmoid(decay_pre) * decay_rate
    scaled = jnp.sqrt(-jnp.expm1(2.0 * log_decay))
    return (log_decay, scaled * jax.nn.sigmoid(input_pre) * conv_vals)


def recurrence(rate, drive):
    def join(left, right):
        return left[0] * right[0], left[1] * right[0] + right[1]

    return lax.associative_scan(join, (rate, drive), axis=1)[1]


def dot(spec, left, right):
    return jnp.einsum(spec, left, right, preferred_element_type=F32)


def weight_grad(left, right):
    return dot("pkr,pku->ru", left, right).astype(BF16)


class Fast:
    def __init__(self, depth, taps, rate):
        self.depth, self.taps, self.rate = depth, taps, rate

    def front(self, normed, cot, weights, act, gain):
        middle, rows, self.weights, self.feeds, self.saved, self.held = front_phase(
            normed, cot, weights, self.taps, self.rate, act, gain, self.depth
        )
        self.normed, self.cot, self.normed_two = rows
        return middle

    def feed(self, middle, gain, cot_own):
        return feed_phase(
            self.normed_two, self.cot, self.feeds, self.held, middle, gain, cot_own, self.depth
        )

    def last(self, branch, panels, feed, act, gain, middle, grad_middle, mlp_part):
        output, input_grad, gains, small, gates, rest = mixer_back_phase(
            branch,
            self.normed,
            self.saved,
            self.weights,
            panels[HOSTED:],
            feed,
            middle,
            self.taps,
            self.rate,
            act,
            gain,
            grad_middle,
            mlp_part,
            self.depth,
        )
        grads = list(rest[-3:]) + list(gates)
        rest = rest[:-3]
        panels = list(panels[:HOSTED]) + list(rest)
        third = len(panels) // 3
        feeds = [
            jnp.concatenate(panels[i * third : (i + 1) * third], axis=1) for i in range(3)
        ]
        return output, input_grad, gains, small, grads, feeds


class Plain:
    def __init__(self, depth, taps, rate):
        self.depth, self.taps, self.rate = depth, taps, rate

    @staticmethod
    def wide(block):
        return lax.all_gather(block, "tensor", axis=1, tiled=True)

    @staticmethod
    def narrow(part):
        return lax.psum_scatter(part, "tensor", scatter_dimension=1, tiled=True).astype(F32)

    @staticmethod
    def full(shard):
        return lax.all_gather(shard, "dp", axis=0, tiled=True)

    @staticmethod
    def own(grad):
        return lax.psum_scatter(grad, "dp", scatter_dimension=0, tiled=True).astype(F32)

    def front(self, normed, cot, weights, act, gain):
        gelu_w, input_w, gate_in_w, gate_dec_w, out_w = (self.full(w) for w in weights[:5])
        self.feeds = tuple(self.full(w) for w in weights[5:])
        normed_all = self.wide(normed)
        seqs, length, _ = normed_all.shape
        channels = gelu_w.shape[1]
        block = gate_in_w.shape[0]
        half = block // 2
        width = channels + half
        parity = lax.axis_index("tensor") % 2
        gelu_pre = dot("kqg,ga->kqa", normed_all, gelu_w)
        input_pre = dot("kqg,ga->kqa", normed_all, input_w)
        gelu_out, gelu_back = jax.vjp(jax.nn.gelu, gelu_pre)
        conv_out, conv_back = jax.vjp(causal_conv, input_pre, self.taps)
        conv_bf = conv_out.astype(BF16)
        rim = lax.dynamic_slice_in_dim(conv_bf, (1 - parity) * (channels - half), half, 2)
        window = jnp.zeros((seqs, length, width), BF16)
        window = lax.dynamic_update_slice_in_dim(window, conv_bf, parity * half, 2)
        window = lax.dynamic_update_slice_in_dim(
            window, swapped(rim, "tensor"), (1 - parity) * channels, 2
        )
        tiles = window.reshape(seqs, length, width // block, block)
        placed = lax.dynamic_update_slice_in_dim(
            jnp.zeros((2, block, width), BF16), jnp.stack([gate_in_w, gate_dec_w]), parity * half, 2
        ).reshape(2, block, width // block, block)
        gates = dot("slbk,gkbc->gslbc", tiles, placed).reshape(2, seqs, length, width)
        gates = lax.dynamic_slice_in_dim(gates, parity * half, channels, 3)
        (log_decay, drive), gate_back = jax.vjp(
            decay_inputs, gates[0], gates[1], conv_bf.astype(F32), self.rate
        )
        decay = jnp.exp(log_decay)
        states = recurrence(decay, drive)
        mixed = (gelu_out * states).astype(BF16)
        self.kept = (
            normed_all, gelu_w, input_w, out_w, gelu_out, gelu_back, conv_back, tiles, placed,
            gate_back, decay, states, mixed,
        )
        part = dot("xgq,pq->xgp", mixed, out_w).astype(BF16)
        self.cot = self.wide(cot)
        middle = act.astype(F32) + self.narrow(part)
        self.normed_two = self.wide(normalize(middle, gain).astype(BF16))
        return middle

    def feed(self, middle, gain, cot_own):
        down_w, gate_w, up_w = self.feeds
        normed, cot = self.normed_two, self.cot
        gate_pre = dot("nwo,ob->nwb", normed, gate_w)
        lift_pre = dot("nwo,ob->nwb", normed, up_w)
        gate_act, activ_back = jax.vjp(jax.nn.gelu, gate_pre)
        hidden = (gate_act * lift_pre).astype(BF16)
        grad_hidden = dot("gre,eu->gru", cot, down_w)
        gate_grad = activ_back(grad_hidden * lift_pre)[0].astype(BF16)
        lift_grad = (grad_hidden * gate_act).astype(BF16)
        part = dot("mqa,ya->mqy", gate_grad, gate_w) + dot("mqa,ya->mqy", lift_grad, up_w)
        _, back = jax.vjp(normalize, middle, gain)
        change, gain_grad = back(self.narrow(part.astype(BF16)))
        grad = cot_own + change
        panels = (
            weight_grad(cot, hidden), weight_grad(normed, gate_grad), weight_grad(normed, lift_grad)
        )
        feed = dot("xav,tv->xat", hidden, down_w).astype(BF16)
        return grad, self.wide(grad.astype(BF16)), gain_grad[None], feed, panels

    def last(self, branch, panels, feed, act, gain, middle, grad_middle, mlp_part):
        (
            normed_all, gelu_w, input_w, out_w, gelu_out, gelu_back, conv_back, tiles, placed,
            gate_back, decay, states, mixed,
        ) = self.kept
        seqs, length, channels = states.shape
        block = tiles.shape[-1]
        half = block // 2
        width = channels + half
        parity = lax.axis_index("tensor") % 2
        grad_mixed = dot("xtz,zm->xtm", branch, out_w)
        gelu_grad = gelu_back(grad_mixed * states)[0].astype(BF16)
        later = jnp.concatenate([decay[:, 1:], jnp.zeros_like(decay[:, :1])], axis=1)
        grad_drive = jnp.flip(
            recurrence(jnp.flip(later, 1), jnp.flip(grad_mixed * gelu_out, 1)), 1
        )
        earlier = jnp.concatenate([jnp.zeros_like(states[:, :1]), states[:, :-1]], axis=1)
        grad_in, grad_dec, grad_conv, grad_rate = gate_back(
            (grad_drive * decay * earlier, grad_drive)
        )
        grads = lax.dynamic_update_slice_in_dim(
            jnp.zeros((2, seqs, length, width), BF16),
            jnp.stack([grad_in, grad_dec]).astype(BF16),
            parity * half,
            3,
        ).reshape(2, seqs, length, width // block, block)
        grad_window = dot("gslbc,gkbc->slbk", grads, placed).reshape(seqs, length, width)
        grad_placed = dot("slbk,gslbc->gkbc", tiles, grads).reshape(2, block, width)
        grad_gates = lax.dynamic_slice_in_dim(grad_placed, parity * half, channels, 2)
        rim = lax.dynamic_slice_in_dim(grad_window, (1 - parity) * channels, half, 2)
        rim = swapped(rim.astype(BF16), "tensor").astype(F32)
        grad_conv = grad_conv + lax.dynamic_slice_in_dim(grad_window, parity * half, channels, 2)
        start = (1 - parity) * (channels - half)
        rim = lax.dynamic_slice_in_dim(grad_conv, start, half, 2) + rim
        grad_conv = lax.dynamic_update_slice_in_dim(grad_conv, rim, start, 2)
        input_rows, grad_taps = conv_back(grad_conv)
        input_rows = input_rows.astype(BF16)
        part = dot("mzf,af->mza", gelu_grad, gelu_w) + dot("mzf,af->mza", input_rows, input_w)
        _, back = jax.vjp(normalize, act.astype(F32), gain)
        change, gain_grad = back(self.narrow(part.astype(BF16)))
        output = (middle + self.narrow(feed)).astype(BF16)
        gains = lax.psum(jnp.concatenate([gain_grad[None], mlp_part]), ("dp", "tensor"))
        small = lax.psum(jnp.concatenate([grad_rate[None], grad_taps]), "dp")
        parts = (
            weight_grad(branch, mixed),
            weight_grad(normed_all, gelu_grad),
            weight_grad(normed_all, input_rows),
            grad_gates[0].astype(BF16),
            grad_gates[1].astype(BF16),
        )
        own = [self.own(g) for g in parts]
        feeds = [self.own(g) for g in panels]
        return output, grad_middle + change, gains, small, own, feeds


def shards(
    activations,
    norm_gain,
    gelu_proj,
    input_proj,
    conv_weight,
    gate_input,
    gate_decay,
    decay_rate,
    out_proj,
    mlp_gain,
    feed_gate,
    feed_up,
    feed_down,
    cotangent,
    lengths,
    batch_of,
):
    depth = lax.axis_size("tensor")
    fast = lax.axis_size("dp") == 8 and depth == 4
    run = (Fast if fast else Plain)(depth, conv_weight, decay_rate)
    tensor_index = lax.axis_index("tensor")
    data_index = lax.axis_index("dp")
    seq_count, row_count, _ = activations.shape
    full_length = row_count * depth
    members = (batch_of[:, None] == jnp.arange(MICRO)[None, :]).astype(F32)
    counts = jnp.sum(members * lengths[:, None].astype(F32), axis=0)
    total_seqs = lengths.shape[0]
    per_batch = float(total_seqs * full_length) / (MICRO * counts)
    weight_all = jnp.sum(members * per_batch[None, :], axis=1)
    my_weight = lax.dynamic_slice_in_dim(weight_all, data_index * seq_count, seq_count)
    my_length = lax.dynamic_slice_in_dim(lengths, data_index * seq_count, seq_count)
    places = tensor_index * row_count + jnp.arange(row_count)
    valid_mask = (places[None, :] < my_length[:, None]).astype(F32)
    scaled_cot = cotangent.astype(F32) * (valid_mask * my_weight[:, None])[:, :, None]
    normed = normalize(activations.astype(F32), norm_gain).astype(BF16)

    weights = (
        gelu_proj, input_proj, gate_input, gate_decay, out_proj.T, feed_down.T, feed_gate, feed_up
    )
    middle = run.front(normed, scaled_cot.astype(BF16), weights, activations, mlp_gain)
    grad_middle, branch_grad_all, mlp_part, feed_part, panels = run.feed(
        middle, mlp_gain, scaled_cot
    )
    output, input_grad, gains, small, grads, feeds = run.last(
        branch_grad_all,
        panels,
        feed_part,
        activations,
        norm_gain,
        middle,
        grad_middle,
        mlp_part,
    )
    return (
        output,
        input_grad,
        gains[0],
        grads[1],
        grads[2],
        small[1:5],
        grads[3],
        grads[4],
        small[0],
        grads[0].T,
        gains[1],
        feeds[1],
        feeds[2],
        feeds[0].T,
    )


def solution(mesh):
    placed = (
        P("dp", "tensor", None),
        P(),
        P("dp", "tensor"),
        P("dp", "tensor"),
        P(None, "tensor"),
        P("dp", "tensor"),
        P("dp", "tensor"),
        P("tensor"),
        P("tensor", "dp"),
        P(),
        P("dp", "tensor"),
        P("dp", "tensor"),
        P("tensor", "dp"),
        P("dp", "tensor", None),
        P(),
        P(),
    )
    return jax.shard_map(
        shards,
        mesh=mesh,
        in_specs=placed,
        out_specs=(
            P("dp", "tensor", None),
            P("dp", "tensor", None),
            P(),
            P("dp", "tensor"),
            P("dp", "tensor"),
            P(None, "tensor"),
            P("dp", "tensor"),
            P("dp", "tensor"),
            P("tensor"),
            P("tensor", "dp"),
            P(),
            P("dp", "tensor"),
            P("dp", "tensor"),
            P("tensor", "dp"),
        ),
        check_vma=False,
    )
```

```python
import functools

import jax
import jax.numpy as jnp
from jax import lax
from jax.experimental import pallas as pl
from jax.experimental.pallas import tpu as pltpu
from jax.sharding import PartitionSpec as P

MICRO = 4
EPS = 1e-06
MESH = pl.DeviceIdType.MESH
ANY = pl.BlockSpec(memory_space=pl.ANY)
VMEM = pl.BlockSpec(memory_space=pltpu.VMEM)
DMA = pltpu.SemaphoreType.DMA
BF16 = jnp.bfloat16
F32 = jnp.float32


def place():
    return lax.axis_index("dp"), lax.axis_index("tensor")


def greet(d, t, depth, dp_masks=(1, 2, 4), z_all=False, meanwhile=None):
    barrier = pltpu.get_barrier_semaphore()
    for mask in dp_masks:
        pl.semaphore_signal(barrier, inc=1, device_id=(d ^ mask, t), device_id_type=MESH)
    if z_all:
        for step in range(1, depth):
            pl.semaphore_signal(
                barrier, inc=1, device_id=(d, lax.rem(t + step, depth)), device_id_type=MESH
            )
        if meanwhile is not None:
            meanwhile()
        pl.semaphore_wait(barrier, len(dp_masks) + depth - 1)
        return

    @pl.when(t > 0)
    def _():
        pl.semaphore_signal(barrier, inc=1, device_id=(d, t - 1), device_id_type=MESH)

    @pl.when(t < depth - 1)
    def _():
        pl.semaphore_signal(barrier, inc=1, device_id=(d, t + 1), device_id_type=MESH)

    if meanwhile is not None:
        meanwhile()
    ends = jnp.where((t == 0) | (t == depth - 1), 1, 2)
    pl.semaphore_wait(barrier, len(dp_masks) + ends)


def add_rows(total, term, rows, step=32):
    step = min(step, rows)

    @pl.loop(0, rows, step=step)
    def _(start):
        part = pl.ds(pl.multiple_of(start, step), step)
        total[part, :] = (total[part, :].astype(F32) + term[part, :].astype(F32)).astype(BF16)


class WeightGather:
    def __init__(self, shard, out, local, send, recv, d, t):
        rows = shard.shape[0]
        half = rows // 2

        def view(slot, start, size):
            if len(out.shape) == 3:
                return out.at[slot, pl.ds(start, size)]
            return out.at[pl.ds(pl.multiple_of(slot * rows + start, 16), size)]

        top, low = (0, half), (half, half)
        plan = [
            (None, d, top, 2),
            (None, d, low, 4),
            (None, d, low, 2),
            (None, d, top, 4),
            (2, d ^ 2, top, 4),
            (4, d ^ 4, low, 2),
            (None, d, top, 1),
            (None, d, low, 1),
            (2, d ^ 2, top, 1),
            (4, d ^ 4, low, 1),
            (2, d ^ 2, low, 1),
            (4, d ^ 4, top, 1),
            (6, d ^ 6, top, 1),
            (6, d ^ 6, low, 1),
        ]
        self.copies = [
            pltpu.make_async_remote_copy(
                src_ref=shard.at[pl.ds(*part)] if came is None else view(slot, *part),
                dst_ref=view(slot, *part),
                send_sem=send.at[i],
                recv_sem=recv.at[i],
                device_id=(d ^ mask, t),
                device_id_type=MESH,
            )
            for i, (came, slot, part, mask) in enumerate(plan)
        ]
        self.own = pltpu.make_async_copy(shard, view(d, 0, rows), local)

    def start(self):
        for i in (0, 1, 2, 3, 6, 7):
            self.copies[i].start()
        self.own.start()

    def relay(self):
        c = self.copies
        c[0].wait_recv()
        c[4].start()
        c[1].wait_recv()
        c[5].start()
        c[8].start()
        c[9].start()

    def relay_two(self):
        c = self.copies
        c[2].wait_recv()
        c[10].start()
        c[3].wait_recv()
        c[11].start()

    def relay_last(self):
        c = self.copies
        c[4].wait_recv()
        c[12].start()
        c[5].wait_recv()
        c[13].start()

    def arrive(self):
        for i in range(6, 14):
            self.copies[i].wait_recv()
        self.own.wait()

    def end(self):
        for i in range(14):
            self.copies[i].wait_send()


def gather_scratch(count):
    return [DMA((count,)), DMA((count, 14)), DMA((count, 14))]


class GradScatter:
    ORDER = (6, 2, 4, 0)

    def __init__(self, grad, out, own, core, diag, last, local, send, recv, d, t):
        self.out, self.core, self.diag, self.last = out, core, diag, last
        self.grad, self.d, self.t = grad, d, t
        self.credit = None
        self.reused = self.again = False
        self.before = self.flush = None
        self.rows = rows = out.shape[0]
        half = rows // 2
        self.half = half
        self.top, self.low = pl.ds(0, half), pl.ds(half, half)

        def block(slot, start=0, size=rows):
            return grad.at[pl.ds(pl.multiple_of(slot * rows + start, 16), size)]

        if own is None:
            self.loads = []
            self.mine = lambda i, start=0, size=rows: block(d ^ self.ORDER[i], start, size)
        else:
            self.loads = [
                pltpu.make_async_copy(block(d ^ r), own.at[i], local.at[i])
                for i, r in enumerate(self.ORDER)
            ]
            self.mine = lambda i, start=0, size=rows: own.at[i, pl.ds(start, size)]
        mine, top, low = self.mine, self.top, self.low
        plan = [(block(d ^ 1 ^ r), core.at[i], 1) for i, r in enumerate(self.ORDER)] + [
            (mine(0, 0, half), diag.at[0], 2),
            (mine(0, half, half), diag.at[1], 4),
            (mine(1, 0, half), last.at[0, top], 2),
            (mine(2, half, half), last.at[1, low], 4),
            (mine(2, 0, half), last.at[1, top], 4),
            (mine(1, half, half), last.at[0, low], 2),
        ]
        self.copies = [
            pltpu.make_async_remote_copy(
                src_ref=src,
                dst_ref=dst,
                send_sem=send.at[i],
                recv_sem=recv.at[i],
                device_id=(d ^ mask, t),
                device_id_type=MESH,
            )
            for i, (src, dst, mask) in enumerate(plan)
        ]

    def start(self):
        if self.reused:
            pl.semaphore_wait(self.credit.at[0], 1)
        for i in range(4):
            self.copies[i].start()
        for load in self.loads:
            load.start()

    def pair(self, i):
        if self.loads:
            self.loads[i].wait()
        self.copies[i].wait_recv()
        add_rows(self.mine(i), self.core.at[i], self.rows)

    def first(self):
        self.pair(0)
        if self.reused:
            pl.semaphore_wait(self.credit.at[1], 1)
        self.copies[4].start()
        if self.reused:
            pl.semaphore_wait(self.credit.at[2], 1)
        self.copies[5].start()

    def second(self):
        self.pair(1)
        self.copies[6].start()
        self.pair(2)
        self.copies[7].start()
        self.pair(3)

    def third(self):
        c = self.copies
        c[4].wait_recv()
        add_rows(self.mine(2, 0, self.half), self.diag.at[0], self.half)
        c[8].start()
        c[5].wait_recv()
        add_rows(self.mine(1, self.half, self.half), self.diag.at[1], self.half)
        c[9].start()

    def end(self):
        for i in (6, 7, 8, 9):
            self.copies[i].wait_recv()
        step = 16
        own = self.mine(3)
        if self.before is not None:
            self.before.flush.wait()

        @pl.loop(0, self.rows, step=step)
        def _(start):
            part = pl.ds(pl.multiple_of(start, step), step)
            self.out[part, :] = (
                own[part, :].astype(F32)
                + self.last[0, part, :].astype(F32)
                + self.last[1, part, :].astype(F32)
            )

        if self.flush is not None:
            self.flush.start()
        for i in range(10):
            self.copies[i].wait_send()
        if self.again:
            for i, mask in enumerate((1, 2, 4)):
                pl.semaphore_signal(
                    self.credit.at[i], inc=1, device_id=(self.d ^ mask, self.t), device_id_type=MESH
                )


class PanelRing:
    def __init__(self, outs, scratch, d, t):
        grads, core, diag, last, stage, send, recv, credit, flush = scratch
        self.slots = slots = grads.shape[0]
        self.panels = []
        for i, out in enumerate(outs):
            q = i % slots
            panel = GradScatter(
                grads.at[q],
                stage.at[q],
                None,
                core.at[q],
                diag.at[q],
                last.at[q],
                None,
                send.at[q],
                recv.at[q],
                d,
                t,
            )
            panel.credit = credit.at[q]
            panel.reused = i >= slots
            panel.again = i + slots < len(outs)
            panel.before = self.panels[i - slots] if i >= slots else None
            panel.flush = pltpu.make_async_copy(stage.at[q], out, flush.at[q])
            self.panels.append(panel)

    def end(self):
        for panel in self.panels[-self.slots :]:
            panel.flush.wait()


def ring_scratch(slots, rows, n):
    return [
        pltpu.VMEM((slots, 8 * rows, n), BF16),
        pltpu.VMEM((slots, 4, rows, n), BF16),
        pltpu.VMEM((slots, 2, rows // 2, n), BF16),
        pltpu.VMEM((slots, 2, rows, n), BF16),
        pltpu.VMEM((slots, rows, n), F32),
        DMA((slots, 10)),
        DMA((slots, 10)),
        pltpu.SemaphoreType.REGULAR((slots, 3)),
        DMA((slots,)),
    ]


def scatter_scratch(shapes, loaded):
    own = [pltpu.VMEM((4,) + s, BF16) for s, far in zip(shapes, loaded) if far]
    core = [pltpu.VMEM((4,) + s, BF16) for s in shapes]
    diag = [pltpu.VMEM((2, s[0] // 2, s[1]), BF16) for s in shapes]
    last = [pltpu.VMEM((2,) + s, BF16) for s in shapes]
    n = len(shapes)
    return own + core + diag + last + [DMA((n, 4)), DMA((n, 10)), DMA((n, 10))]


def make_scatters(grads, outs, loaded, scratch, d, t):
    n = len(grads)
    scratch = list(scratch)
    own = [scratch.pop(0) if far else None for far in loaded]
    core, diag, last = (scratch[i * n : (i + 1) * n] for i in range(3))
    local, send, recv = scratch[3 * n :]
    return [
        GradScatter(
            grads[i],
            outs[i],
            own[i],
            core[i],
            diag[i],
            last[i],
            local.at[i],
            send.at[i],
            recv.at[i],
            d,
            t,
        )
        for i in range(n)
    ]


class LineGather:
    def __init__(self, block, out, local, send, recv, d, t, depth):
        self.block, self.out, self.send, self.recv = block, out, send, recv
        self.d, self.t, self.depth = d, t, depth
        self.rows = block.shape[-2]
        self.own = pltpu.make_async_copy(block, self.slot(t), local)

    def slot(self, j):
        rows = pl.ds(pl.multiple_of(j * self.rows, self.rows), self.rows)
        return self.out.at[:, rows] if len(self.out.shape) == 3 else self.out.at[rows]

    def copy(self, way, step, j, to):
        return pltpu.make_async_remote_copy(
            src_ref=self.block if step == 0 else self.slot(j),
            dst_ref=self.slot(j),
            send_sem=self.send.at[way, step],
            recv_sem=self.recv.at[way, step],
            device_id=(self.d, to),
            device_id_type=MESH,
        )

    def open(self, k):
        t, depth = self.t, self.depth
        if k == 0:
            self.own.start()

        @pl.when(t == k)
        def _():
            self.copy(0, 0, t, t + 1).start()

        @pl.when(t == depth - 1 - k)
        def _():
            self.copy(1, 0, t, t - 1).start()

    def step(self, s):
        t, depth = self.t, self.depth
        if s == 0:
            for k in range(depth - 1):
                self.open(k)
            return

        @pl.when((t - s >= 0) & (t < depth - 1))
        def _():
            self.copy(0, s - 1, t, t).wait_recv()
            self.copy(0, s, t - s, t + 1).start()

        @pl.when((t + s < depth) & (t > 0))
        def _():
            self.copy(1, s - 1, t, t).wait_recv()
            self.copy(1, s, t + s, t - 1).start()

    def finish(self):
        t, depth = self.t, self.depth
        self.own.wait()
        for s in range(depth - 1):

            @pl.when(t == depth - 1)
            def _():
                self.copy(0, s, t, t).wait_recv()

            @pl.when(t == 0)
            def _():
                self.copy(1, s, t, t).wait_recv()

    def end(self):
        t, depth = self.t, self.depth
        for s in range(depth - 1):

            @pl.when((t - s >= 0) & (t < depth - 1))
            def _():
                self.copy(0, s, t, t).wait_send()

            @pl.when((t + s < depth) & (t > 0))
            def _():
                self.copy(1, s, t, t).wait_send()


def line_gather_scratch(depth):
    return [DMA, DMA((2, depth - 1)), DMA((2, depth - 1))]


class LineScatter:
    def __init__(self, part, got, send, recv, d, t, depth, which=None, first_row=None):
        self.part, self.got, self.send, self.recv = part, got, send, recv
        self.d, self.t, self.depth = d, t, depth
        self.which = range(part.shape[0]) if which is None else which
        self.first_row = first_row
        self.rows = got.shape[3]

    def slot(self, way, j, s):
        return self.got.at[way, j - 1 if way == 0 else j, s]

    def copy(self, way, j, s, src, to):
        return pltpu.make_async_remote_copy(
            src_ref=src,
            dst_ref=self.slot(way, j, s),
            send_sem=self.send.at[way, j, s],
            recv_sem=self.recv.at[way, j, s],
            device_id=(self.d, to),
            device_id_type=MESH,
        )

    def block(self, j, s):
        start = j * self.rows
        if self.first_row is not None:
            start = pl.multiple_of(self.first_row + start, self.rows)
            return self.part.at[pl.ds(start, self.rows)]
        return self.part.at[s, pl.ds(pl.multiple_of(start, self.rows), self.rows)]

    def start(self, first=0, last=None):
        t, depth = self.t, self.depth
        steps = range(first, depth - 1 if last is None else last)

        @pl.when(t == 0)
        def _():
            for k in steps:
                for s in self.which:
                    j = depth - 1 - k
                    self.copy(0, j, s, self.block(j, s), t + 1).start()

        @pl.when(t == depth - 1)
        def _():
            for j in steps:
                for s in self.which:
                    self.copy(1, j, s, self.block(j, s), t - 1).start()

    def pass_on(self, way, j, to):
        for s in self.which:
            mine = self.slot(way, j, s)
            self.copy(way, j, s, mine, self.t).wait_recv()
            add_rows(mine, self.block(j, s), self.rows)
            self.copy(way, j, s, mine, to).start()

    def step(self, k):
        t, depth = self.t, self.depth
        right = depth - 1 - k + t
        left = k - (depth - 1 - t)

        @pl.when((t > 0) & (t < right) & (right < depth))
        def _():
            self.pass_on(0, right, t + 1)

        @pl.when((left >= 0) & (left < t) & (t < depth - 1))
        def _():
            self.pass_on(1, left, t - 1)

    def total(self, out):
        t, depth = self.t, self.depth
        for s in self.which:
            out[s][...] = self.block(t, s)[...].astype(F32)

        @pl.when(t > 0)
        def _():
            for s in self.which:
                self.copy(0, t, s, self.slot(0, t, s), t).wait_recv()
                out[s][...] += self.got[0, t - 1, s].astype(F32)

        @pl.when(t < depth - 1)
        def _():
            for s in self.which:
                self.copy(1, t, s, self.slot(1, t, s), t).wait_recv()
                out[s][...] += self.got[1, t, s].astype(F32)

    def end(self):
        t, depth = self.t, self.depth
        for j in range(depth):
            for s in self.which:
                if j > 0:

                    @pl.when(j > t)
                    def _():
                        self.copy(0, j, s, self.slot(0, j, s), t).wait_send()

                if j < depth - 1:

                    @pl.when(j < t)
                    def _():
                        self.copy(1, j, s, self.slot(1, j, s), t).wait_send()


def line_scatter_scratch(seqs, rows, width, depth):
    return [
        pltpu.VMEM((2, depth - 1, seqs, rows, width), BF16),
        DMA((2, depth, seqs)),
        DMA((2, depth, seqs)),
    ]


def call(kernel, name, number, ins, outs, scratch, args, vmem=60 * 1024 * 1024):
    return pl.pallas_call(
        kernel,
        name=name,
        out_shape=[o[0] for o in outs],
        in_specs=ins,
        out_specs=[o[1] for o in outs],
        scratch_shapes=scratch,
        compiler_params=pltpu.CompilerParams(
            collective_id=number, has_side_effects=True, vmem_limit_bytes=vmem
        ),
    )(*args)


def shaped(shape, dtype, spec):
    return (jax.ShapeDtypeStruct(shape, dtype), spec)


def sigmoid(x):
    return 1.0 / (1.0 + jnp.exp(-x))


def one_less_exp(y):
    series = 1.0 + y / 6.0 * (1.0 + y / 7.0)
    for k in (5.0, 4.0, 3.0, 2.0):
        series = 1.0 + y / k * series
    return jnp.where(y > -0.5, -y * series, 1.0 - jnp.exp(y))


GELU_SCALE = 0.7978845608028654
GELU_CUBE = 0.044715


def gelu(x):
    return 0.5 * x * (1.0 + jnp.tanh(GELU_SCALE * (x + GELU_CUBE * x * x * x)))


def gelu_both(x):
    square = x * x
    bent = jnp.tanh(GELU_SCALE * (x + GELU_CUBE * square * x))
    half = 0.5 * (1.0 + bent)
    slope = half + 0.5 * x * (1.0 - bent * bent) * (
        GELU_SCALE * (1.0 + 3.0 * GELU_CUBE * square)
    )
    return x * half, slope


def rows_of(index, size):
    return pl.ds(pl.multiple_of(index * size, size), size)


def contract(left, right, dims):
    return lax.dot_general(left, right, ((dims[:1], dims[1:]), ((), ())), preferred_element_type=F32)


def scan_rows(rate, out, which, length, base=0, backward=False):
    tile = 8
    width = out.shape[1]
    row = lax.broadcasted_iota(jnp.int32, (tile, width), 0)

    def body(i, carried):
        k = length // tile - 1 - i if backward else i
        ends = []
        for at, s in enumerate(which):
            start = pl.multiple_of(s * length + k * tile, tile)
            rows = pl.ds(start, tile)
            if backward:
                pair = rate[pl.ds(start, 2 * tile), :]
                step = pltpu.roll(pair, 2 * tile - 1, 0)[:tile]
                step = jnp.where((row == tile - 1) & (i == 0), 0.0, step)
            else:
                step = rate[rows, :]
            held = pl.ds(pl.multiple_of(base + start, tile), tile)
            drive = out[held, :]
            for shift in (1, 2, 4):
                turn = tile - shift if backward else shift
                inside = row < tile - shift if backward else row >= shift
                before = jnp.where(inside, pltpu.roll(drive, turn, 0), 0.0)
                drive = drive + step * before
                step = step * jnp.where(inside, pltpu.roll(step, turn, 0), 1.0)
            states = drive + step * carried[at]
            out[held, :] = states
            ends.append(states[0:1] if backward else states[tile - 1 : tile])
        return tuple(ends)

    start = tuple(jnp.zeros((1, width), F32) for _ in which)
    lax.fori_loop(0, length // tile, body, start, unroll=2)


STRIP = 16
PANEL = 640


def gate_blocks(parity, width, block):
    half = block // 2
    shift = parity * half
    blocks = []
    for k in range((width + half) // block):
        low, high = k * block - shift, (k + 1) * block - shift
        blocks.append((k, max(low, 0), min(high, width)))
    return blocks


def front_kernel(
    depth,
    cotangent,
    token_weight,
    gelu_shard,
    input_shard,
    gate_in_shard,
    gate_dec_shard,
    out_shard,
    down_shard,
    gate_shard,
    up_shard,
    taps,
    rate,
    act,
    gain,
    first_gain,
    middle,
    normed_out,
    cot_out,
    normed_two_out,
    gelu_full,
    input_full,
    gate_in_full,
    gate_dec_full,
    out_full,
    down_full,
    gate_full,
    up_full,
    gelu_pre_out,
    input_pre_out,
    conv_out,
    window_out,
    gate_in_out,
    gate_dec_out,
    states_out,
    mixed_out,
    grad_hidden_out,
    gate_pre_out,
    *scratch,
):
    normed, gelu_w, input_w, gate_in_w, gate_dec_w, out_w = scratch[:6]
    gelu_pre, input_pre, conv, window, gate_in, gate_dec, decay, states, mixed, part = scratch[6:16]
    local, send, recv = scratch[16:19]
    line_sems = [scratch[19 + 3 * i : 22 + 3 * i] for i in range(6)]
    rim_send, rim_recv, save_sem = scratch[37:40]
    cot, normed_two, block_two, panel_w, product = scratch[40:45]
    panel_sem, product_sem = scratch[45:47]
    got, ssem, rsem = scratch[47:50]
    normed_block, cot_block = scratch[50:52]
    d, t = place()
    parity = lax.rem(t, 2)
    even = parity == 0
    odd = parity == 1

    def prepare():
        for s in range(act.shape[0]):
            value = act[s].astype(F32)
            inverse = lax.rsqrt(jnp.mean(value * value, axis=-1, keepdims=True) + EPS)
            normed_block[s] = (value * inverse * first_gain[...]).astype(BF16)
            cot_block[s] = (cotangent[s].astype(F32) * token_weight[s]).astype(BF16)

    greet(d, t, depth, meanwhile=prepare)
    seqs, length, model = normed.shape
    tokens = seqs * length
    width = conv.shape[1]
    block = gate_in_w.shape[0]
    half = block // 2
    spans = [pl.ds(s * length, length) for s in range(seqs)]
    firsts = [
        LineGather(normed_block.at[s], normed.at[s], *line_sems[5 * s], d, t, depth)
        for s in range(seqs)
    ]
    cots = [
        LineGather(cot_block.at[s], cot.at[spans[s]], *line_sems[1 + s], d, t, depth)
        for s in range(seqs)
    ]
    twos = [
        LineGather(block_two.at[s], normed_two.at[spans[s]], *line_sems[3 + s], d, t, depth)
        for s in range(seqs)
    ]
    scatters = [LineScatter(part, got, ssem, rsem, d, t, depth, (s,)) for s in range(seqs)]
    pairs = (
        (gelu_shard, gelu_w),
        (input_shard, input_w),
        (gate_in_shard, gate_in_w),
        (gate_dec_shard, gate_dec_w),
        (out_shard, out_w),
        (down_shard, down_full),
        (gate_shard, gate_full),
        (up_shard, up_full),
    )
    gathers = [
        WeightGather(shard, full, local.at[i], send.at[i], recv.at[i], d, t)
        for i, (shard, full) in enumerate(pairs)
    ]
    saves = []

    def save(src, dst):
        copy = pltpu.make_async_copy(src, dst, save_sem.at[len(saves)])
        copy.start()
        saves.append(copy)

    one = [gathers[1], gathers[0], gathers[2], gathers[3]]
    out_g, down_g, gate_g, up_g = gathers[4:]
    even_blocks, odd_blocks = gate_blocks(0, width, block), gate_blocks(1, width, block)

    def rim(s, to, src, dst):
        return pltpu.make_async_remote_copy(
            src_ref=conv.at[spans[s], pl.ds(src, half)],
            dst_ref=window.at[spans[s], pl.ds(dst, half)],
            send_sem=rim_send.at[s],
            recv_sem=rim_recv.at[s],
            device_id=(d, to),
            device_id_type=MESH,
        )

    def convolve(s):
        input_pre[s, 0:8, :] = jnp.zeros((8, width), F32)
        input_pre[s, 8 : 8 + length, :] = contract(normed[s], input_w[...], (1, 0))

        @pl.loop(0, length // STRIP)
        def _(i):
            near = input_pre[s, pl.ds(pl.multiple_of(i * STRIP, STRIP), STRIP + 8), :]
            total = taps[0:1, :] * near[8:]
            for k in range(1, taps.shape[0]):
                total = total + taps[k : k + 1, :] * pltpu.roll(near, k, 0)[8:]
            rows = pl.ds(pl.multiple_of(s * length + i * STRIP, STRIP), STRIP)
            conv[rows, :] = total.astype(BF16)

        @pl.when(even)
        def _():
            rim(s, t + 1, width - half, 0).start()
            window[spans[s], 0:width] = conv[spans[s], :]

        @pl.when(odd)
        def _():
            rim(s, t - 1, 0, width).start()
            window[spans[s], half : half + width] = conv[spans[s], :]

    def gates(s, blocks):
        for k, low, high in blocks:
            near = window[spans[s], k * block : (k + 1) * block]
            gate_in[spans[s], low:high] = contract(near, gate_in_w[:, low:high], (1, 0))
            gate_dec[spans[s], low:high] = contract(near, gate_dec_w[:, low:high], (1, 0))

    def inner_gates(s):
        gelu_pre[spans[s], :] = contract(normed[s], gelu_w[...], (1, 0))

        @pl.when(even)
        def _():
            gates(s, even_blocks[:-1])

        @pl.when(odd)
        def _():
            gates(s, odd_blocks[1:])

    def recur(s):
        @pl.when(even)
        def _():
            rim(s, t + 1, width - half, width).wait_recv()
            gates(s, even_blocks[-1:])

        @pl.when(odd)
        def _():
            rim(s, t - 1, 0, 0).wait_recv()
            gates(s, odd_blocks[:1])

        @pl.loop(0, length // STRIP)
        def _(i):
            start = pl.multiple_of(s * length + i * STRIP, STRIP)
            rows = pl.ds(start, STRIP)
            log = -8.0 * sigmoid(gate_dec[rows, :]) * rate[...]
            decay[rows, :] = jnp.exp(log)
            drive = jnp.sqrt(one_less_exp(2.0 * log)) * sigmoid(gate_in[rows, :])
            held = pl.ds(pl.multiple_of(start + 8, 8), STRIP)
            states[held, :] = drive * conv[rows, :].astype(F32)

        scan_rows(decay, states, (s,), length, base=8)

    def mix(s):
        @pl.loop(0, length // STRIP)
        def _(i):
            start = pl.multiple_of(s * length + i * STRIP, STRIP)
            rows, held = pl.ds(start, STRIP), pl.ds(pl.multiple_of(start + 8, 8), STRIP)
            mixed[rows, :] = (gelu(gelu_pre[rows, :]) * states[held, :]).astype(BF16)

        panel = 512

        @pl.loop(0, model // panel)
        def _(i):
            columns = rows_of(i, panel)
            part[s, :, columns] = contract(mixed[spans[s], :], out_w[columns, :], (1, 1)).astype(
                BF16
            )

    def norm_step(s):
        scatters[s].total([middle.at[i] for i in range(seqs)])
        value = middle[s] + act[s].astype(F32)
        middle[s] = value
        inverse = lax.rsqrt(jnp.mean(value * value, axis=-1, keepdims=True) + EPS)
        block_two[s] = (value * inverse * gain[...]).astype(BF16)
        twos[s].step(0)

    firsts[0].step(0)
    for g in one:
        g.start()
    firsts[0].step(1)
    firsts[1].step(0)
    for g in one:
        g.relay()
    out_g.start()
    firsts[0].step(2)
    for line in cots:
        line.open(0)
    for g in one:
        g.relay_two()
    firsts[1].step(1)
    for g in one:
        g.relay_last()
    firsts[0].finish()
    for line in cots:
        line.open(1)
    one[0].arrive()
    states[0:8, :] = jnp.zeros((8, width), F32)
    convolve(0)
    out_g.relay()
    down_g.start()
    gate_g.start()
    for g in one[1:]:
        g.arrive()
    inner_gates(0)
    out_g.relay_two()
    firsts[1].step(2)
    recur(0)
    out_g.relay_last()
    out_g.arrive()
    mix(0)
    firsts[1].finish()
    scatters[0].start(0, 1)
    for line in cots:
        line.open(2)
    convolve(1)
    scatters[0].start(1)
    for line in cots:
        line.step(1)
    inner_gates(1)
    scatters[0].step(1)
    down_g.relay()
    recur(1)
    scatters[0].step(2)
    mix(1)
    scatters[1].start()
    for line in cots:
        line.step(2)
    save(normed, normed_out)
    save(gelu_w, gelu_full)
    save(input_w, input_full)
    save(gate_in_w, gate_in_full)
    save(gate_dec_w, gate_dec_full)
    save(out_w, out_full)
    save(gelu_pre, gelu_pre_out)
    save(input_pre, input_pre_out)
    save(conv, conv_out)
    save(window, window_out)
    save(gate_in, gate_in_out)
    save(gate_dec, gate_dec_out)
    save(states, states_out)
    save(mixed, mixed_out)
    down_g.relay_two()
    scatters[1].step(1)
    norm_step(0)
    gate_g.relay()
    up_g.start()
    scatters[1].step(2)
    gate_g.relay_two()
    twos[0].step(1)
    norm_step(1)
    twos[0].step(2)
    down_g.relay_last()
    twos[1].step(1)
    twos[1].step(2)
    gate_g.relay_last()
    for line in cots:
        line.finish()
    save(cot, cot_out)
    up_g.relay()
    for line in twos:
        line.finish()
    save(normed_two, normed_two_out)
    panels = down_full.shape[1] // PANEL

    def load_panel(full, i):
        columns = pl.ds(i % panels * PANEL, PANEL)
        copy = pltpu.make_async_copy(full.at[:, columns], panel_w.at[i % 2], panel_sem.at[i % 2])
        copy.start()
        return copy

    results = []

    def multiply(left, full, out, i, following):
        nonlocal loaded
        loaded.wait()
        if following is not None:
            loaded = load_panel(*following)
        if len(results) >= 2:
            results[-2].wait()
        for s in range(seqs):
            product[i % 2, spans[s], :] = contract(left[spans[s], :], panel_w[i % 2], (1, 0))
        columns = pl.ds(i % panels * PANEL, PANEL)
        copy = pltpu.make_async_copy(product.at[i % 2], out.at[:, columns], product_sem.at[i % 2])
        copy.start()
        results.append(copy)

    down_g.arrive()
    gate_g.arrive()
    loaded = load_panel(down_full, 0)
    for i in range(panels):
        multiply(
            cot,
            down_full,
            grad_hidden_out,
            i,
            (down_full, i + 1) if i < panels - 1 else (gate_full, panels),
        )
    up_g.relay_two()
    for i in range(panels, 2 * panels):
        multiply(
            normed_two,
            gate_full,
            gate_pre_out,
            i,
            (gate_full, i + 1) if i < 2 * panels - 1 else None,
        )
    up_g.relay_last()
    up_g.arrive()

    for s in range(seqs):

        @pl.when(even)
        def _():
            rim(s, t + 1, width - half, 0).wait_send()

        @pl.when(odd)
        def _():
            rim(s, t - 1, 0, width).wait_send()

    for g in gathers:
        g.end()
    for line in firsts + cots + twos + scatters:
        line.end()
    for copy in saves + results[-2:]:
        copy.wait()


def front_phase(cotangent, token_weight, weights, taps, rate, act, gain, first_gain, depth):
    seqs, rows, model = act.shape
    length = rows * depth
    tokens = seqs * length
    n = len(weights)
    block, width = weights[2].shape[0] * 8, weights[0].shape[1]
    units = weights[-1].shape[1]
    wide = block // 2 + width
    wide_rows = (seqs, length, model)
    mixers = [(model, width), (model, width), (block, width), (block, width), (model, width)]
    saved = [
        ((tokens, width), F32),
        ((seqs, length + 8, width), F32),
        ((tokens, width), BF16),
        ((tokens, wide), BF16),
        ((tokens, width), F32),
        ((tokens, width), F32),
        ((tokens + 8, width), F32),
        ((tokens, width), BF16),
    ]
    outs = [shaped(act.shape, F32, VMEM)]
    outs += [shaped(wide_rows, BF16, ANY)] + [shaped((tokens, model), BF16, ANY)] * 2
    outs += [shaped(shape, BF16, ANY) for shape in mixers]
    outs += [shaped((model, units), BF16, ANY)] * 3
    outs += [shaped(shape, dtype, ANY) for shape, dtype in saved]
    outs += [shaped((tokens, units), F32, ANY)] * 2
    saved_scratch = saved[:6] + [((tokens, width), F32)] + saved[6:] + [(wide_rows, BF16)]
    scratch = [pltpu.VMEM(wide_rows, BF16)]
    scratch += [pltpu.VMEM(shape, BF16) for shape in mixers]
    scratch += [pltpu.VMEM(shape, dtype) for shape, dtype in saved_scratch]
    scratch += gather_scratch(n) + line_gather_scratch(depth) * 6 + [DMA((seqs,)), DMA((seqs,)), DMA((16,))]
    scratch += [
        pltpu.VMEM((tokens, model), BF16),
        pltpu.VMEM((tokens, model), BF16),
        pltpu.VMEM(act.shape, BF16),
        pltpu.VMEM((2, model, PANEL), BF16),
        pltpu.VMEM((2, tokens, PANEL), F32),
        DMA((2,)),
        DMA((2,)),
    ]
    scratch += line_scatter_scratch(seqs, rows, model, depth)
    scratch += [pltpu.VMEM(act.shape, BF16)] * 2
    res = call(
        functools.partial(front_kernel, depth),
        "front_phase",
        0,
        [VMEM] * (7 + n),
        outs,
        scratch,
        (cotangent, token_weight)
        + tuple(weights)
        + (taps, rate.reshape(1, width), act, gain.reshape(1, model), first_gain.reshape(1, model)),
    )
    return res[0], res[1:4], res[4:9], res[9:12], res[12:20], res[20:]


def norm_back(value, gain, error):
    inverse = lax.rsqrt(jnp.mean(value * value, axis=-1, keepdims=True) + EPS)
    scaled = error * gain
    mean = jnp.mean(scaled * value, axis=-1, keepdims=True)
    grad = inverse * scaled - value * (inverse * inverse * inverse * mean)
    return grad, jnp.sum(error * value * inverse, axis=0, keepdims=True)


HOSTED = 6


def feed_kernel(
    depth,
    normed_in,
    cot_in,
    gate_in,
    up_in,
    down_in,
    grad_hidden_in,
    gate_pre_in,
    middle,
    gain,
    cotangent,
    token_weight,
    grad,
    wide,
    gain_grad,
    output,
    *refs,
):
    panels = gate_in.shape[1] // PANEL
    n_panels = 3 * panels
    outs, refs = refs[:n_panels], refs[n_panels:]
    normed, cot, hidden, gate_rows, lift_rows = refs[:5]
    gate_w, up_w, down_w, gate_pre, lift_pre, grad_hidden, acc, part, block = refs[5:14]
    got, ssem, rsem = refs[14:17]
    feed_got, feed_ssem, feed_rsem = refs[17:20]
    load_sem, weight_sem, save_sem = refs[20:23]
    lines = refs[23:26], refs[26:29]
    d, t = place()
    greet(d, t, depth)
    seqs = middle.shape[0]
    tokens, model = normed_in.shape
    length = tokens // seqs
    tile = 512
    ring = PanelRing(outs[:HOSTED], refs[29:], d, t)
    scatters = [LineScatter(part, got, ssem, rsem, d, t, depth, (s,)) for s in range(seqs)]
    feeds = [
        LineScatter(cot, feed_got, feed_ssem, feed_rsem, d, t, depth, (s,), s * length)
        for s in range(seqs)
    ]
    own_rows = middle.shape[1]
    gathers = [
        LineGather(block.at[s], wide.at[s], *lines[s], d, t, depth) for s in range(seqs)
    ]

    def load(i, src, dst):
        copy = pltpu.make_async_copy(src, dst, load_sem.at[i])
        copy.start()
        return copy

    def weight(i, src, dst, p):
        copy = pltpu.make_async_copy(
            src.at[:, pl.ds(p * PANEL, PANEL)], dst, weight_sem.at[i]
        )
        copy.start()
        return copy

    def held_rows(s, p):
        rows, columns = pl.ds(s * length, length), pl.ds(p * PANEL, PANEL)
        q = (s * panels + p) % 2
        return [
            load(2 + q, gate_pre_in.at[rows, columns], gate_pre.at[q]),
            load(4 + q, grad_hidden_in.at[rows, columns], grad_hidden.at[q]),
        ]

    normed_load = load(0, normed_in, normed)
    ups = (up_w, down_w)
    up_load = weight(1, up_in, up_w, 0)
    row_loads = held_rows(0, 0)
    gate_load = weight(0, gate_in, gate_w, 0)
    cot_load = load(1, cot_in, cot)

    def forward(s, p, more):
        nonlocal gate_load, up_load, row_loads
        rows = pl.ds(s * length, length)
        columns = pl.ds(p * PANEL, PANEL)
        q = (s * panels + p) % 2
        if s == 0 and p == 0:
            normed_load.wait()
        up = ups[q]
        up_load.wait()
        if more is not None:
            up_load = weight(2 - q, up_in, ups[1 - q], more)
        lift_pre[...] = contract(normed[rows, :], up[...], (1, 0))
        for copy in row_loads:
            copy.wait()
        if more is not None:
            row_loads = held_rows(*((s, more) if more > p else (s + 1, more)))

        @pl.loop(0, length // STRIP)
        def _(i):
            strip = rows_of(i, STRIP)
            held = pl.ds(pl.multiple_of(s * length + i * STRIP, STRIP), STRIP)
            act, slope = gelu_both(gate_pre[q, strip, :])
            lift = lift_pre[strip, :]
            came = grad_hidden[q, strip, :]
            hidden[held, columns] = (act * lift).astype(BF16)
            gate_rows[held, columns] = (came * lift * slope).astype(BF16)
            lift_rows[held, columns] = (came * act).astype(BF16)

        gate_load.wait()

        @pl.loop(0, model // tile)
        def _(i):
            out = rows_of(i, tile)
            value = contract(gate_rows[rows, columns], gate_w[out, :], (1, 1))
            value = value + contract(lift_rows[rows, columns], up[out, :], (1, 1))
            if p == 0:
                acc[:, out] = value
            elif p < panels - 1:
                acc[:, out] += value
            else:
                part[s, :, out] = (acc[:, out] + value).astype(BF16)

        if more is not None:
            gate_load = weight(0, gate_in, gate_w, more)

    kinds = ((cot, hidden), (normed, gate_rows), (normed, lift_rows))

    def weight_grad(i, out):
        left, right = kinds[i // panels]
        columns = pl.ds(i % panels * PANEL, PANEL)

        @pl.loop(0, model // tile)
        def _(k):
            rows = rows_of(k, tile)
            out[rows, :] = contract(left[:, rows], right[:, columns], (0, 0)).astype(BF16)

    def begin(i):
        panel = ring.panels[i]
        weight_grad(i, panel.grad)
        panel.start()

    def push(i):
        ring.panels[i].first()
        ring.panels[i].second()

    def norm_step(s):
        scatters[s].total([grad.at[i] for i in range(seqs)])
        change, gain_part = norm_back(middle[s], gain[...], grad[s])
        change = change + cotangent[s].astype(F32) * token_weight[s]
        grad[s] = change
        block[s] = change.astype(BF16)
        if s == 0:
            gain_grad[...] = gain_part
        else:
            gain_grad[...] += gain_part

    def feed(s):
        rows = pl.ds(s * length, length)
        downs = (gate_w, up_w, down_w)

        @pl.loop(0, model // tile)
        def _(i):
            out = rows_of(i, tile)
            value = contract(hidden[rows, 0:PANEL], downs[0][out, :], (1, 1))
            for p in range(1, panels):
                columns = pl.ds(p * PANEL, PANEL)
                value = value + contract(hidden[rows, columns], downs[p][out, :], (1, 1))
            cot[rows, out] = value.astype(BF16)

        feeds[s].start()

    def feed_end(s):
        total = acc.at[pl.ds(s * own_rows, own_rows)]
        feeds[s].total([total] * seqs)
        output[s] = (total[...] + middle[s]).astype(BF16)

    pending = {}

    def store_grad(i):
        q = i % ring.slots
        if q in pending:
            pending.pop(q).wait()
        weight_grad(i, ring.panels[q].grad)
        pending[q] = pltpu.make_async_copy(ring.panels[q].grad, outs[i], save_sem.at[q])
        pending[q].start()

    for p in range(panels):
        forward(0, p, (p + 1) % panels)
    scatters[0].start()
    forward(1, 0, 1)
    scatters[0].step(1)
    cot_load.wait()
    begin(0)
    forward(1, 1, 2)
    scatters[0].step(2)
    push(0)
    begin(1)
    forward(1, 2, None)
    down_loads = [weight(0, down_in, gate_w, 0), weight(1, down_in, up_w, 1)]
    down_loads.append(weight(2, down_in, down_w, 2))
    scatters[1].start()
    ring.panels[0].third()
    norm_step(0)
    gathers[0].step(0)
    push(1)
    begin(2)
    scatters[1].step(1)
    gathers[0].step(1)
    ring.panels[0].end()
    ring.panels[1].third()
    push(2)
    scatters[1].step(2)
    gathers[0].step(2)
    for copy in down_loads:
        copy.wait()
    feed(0)
    begin(3)
    ring.panels[1].end()
    ring.panels[2].third()
    norm_step(1)
    gathers[1].step(0)
    feed(1)
    push(3)
    begin(4)
    feeds[0].step(1)
    gathers[1].step(1)
    ring.panels[2].end()
    ring.panels[3].third()
    push(4)
    begin(5)
    feeds[0].step(2)
    gathers[1].step(2)
    ring.panels[3].end()
    ring.panels[4].third()
    push(5)
    store_grad(6)
    feeds[1].step(1)
    ring.panels[4].end()
    ring.panels[5].third()
    store_grad(7)
    feeds[1].step(2)
    feed_end(0)
    ring.panels[5].end()
    store_grad(8)
    feed_end(1)
    for line in gathers:
        line.finish()
    ring.end()
    for copy in pending.values():
        copy.wait()
    for line in scatters + feeds + gathers:
        line.end()


def feed_phase(normed, cot, weights, held, middle, gain, cotangent, token_weight, depth):
    down_w, gate_w, up_w = weights
    seqs, rows, model = middle.shape
    tokens = normed.shape[0]
    length = tokens // seqs
    wide_rows = (seqs, length, model)
    units = gate_w.shape[1]
    count = 3 * (units // PANEL)
    outs = [
        shaped(middle.shape, F32, VMEM),
        shaped(wide_rows, BF16, ANY),
        shaped((1, model), F32, VMEM),
        shaped(middle.shape, BF16, VMEM),
    ]
    outs += [shaped((model // 8, PANEL), F32, ANY)] * HOSTED
    outs += [shaped((model, PANEL), BF16, ANY)] * (count - HOSTED)
    scratch = [pltpu.VMEM((tokens, model), BF16)] * 2
    scratch += [pltpu.VMEM((tokens, units), BF16)] * 3
    scratch += [pltpu.VMEM((model, PANEL), BF16)] * 3
    scratch += [pltpu.VMEM((2, length, PANEL), F32), pltpu.VMEM((length, PANEL), F32)]
    scratch += [pltpu.VMEM((2, length, PANEL), F32)]
    scratch += [
        pltpu.VMEM((length, model), F32),
        pltpu.VMEM(wide_rows, BF16),
        pltpu.VMEM(middle.shape, BF16),
    ]
    scratch += line_scatter_scratch(seqs, rows, model, depth) * 2
    scratch += [DMA((6,)), DMA((3,)), DMA((3,))]
    scratch += line_gather_scratch(depth) * 2
    scratch += ring_scratch(3, model // 8, PANEL)
    res = call(
        functools.partial(feed_kernel, depth),
        "feed_phase",
        2,
        [ANY] * 7 + [VMEM] * 4,
        outs,
        scratch,
        (normed, cot, gate_w, up_w, down_w) + tuple(held) + (middle, gain.reshape(1, model), cotangent, token_weight),
        vmem=63 * 1024 * 1024,
    )
    return res[0], res[1], res[2], res[3], res[4:]


def mixer_back_kernel(
    depth,
    n_panels,
    branch_in,
    normed_in,
    out_w_in,
    gelu_pre_in,
    input_pre_in,
    conv_in,
    window_in,
    gate_in_in,
    gate_dec_in,
    states_in,
    mixed_in,
    gelu_w_in,
    input_w_in,
    gate_in_w_in,
    gate_dec_w_in,
    taps,
    rate,
    act,
    gain,
    grad_middle,
    mlp_part,
    *refs,
):
    panels_in, refs = refs[:n_panels], refs[n_panels:]
    n_sums = n_panels + 3
    input_grad, gains, smalls, gate_in_out, gate_dec_out = refs[:5]
    panels_out, scratch = refs[5 : 5 + n_sums], refs[5 + n_sums :]
    branch, weight, input_w = scratch[:3]
    gelu_pre, input_pre, conv, window, gate_in, gate_dec, states, gate_in_w, gate_dec_w = scratch[3:12]
    grad, decay, grad_conv, gelu_grad, input_rows, grad_in, grad_dec, mixed = scratch[12:20]
    rim_out, rim_in, gate_in_grad, gate_dec_grad, part, sums = scratch[20:26]
    got, ssem, rsem = scratch[26:29]
    rim_send, rim_recv, load_sem, panel_sem = scratch[29:33]
    small, small_all, pack, packs, line_pack, line_packs = scratch[33:39]
    psend, precv, qsend, qrecv, zsend, zrecv = scratch[39:45]
    d, t = place()
    ring = PanelRing(panels_out, scratch[45:54], d, t)
    parity = lax.rem(t, 2)
    even = parity == 0
    odd = parity == 1
    greet(d, t, depth, dp_masks=(1, 2, 3, 4, 5, 6, 7), z_all=True)
    seqs, length, model = branch_in.shape
    tokens = seqs * length
    width = conv.shape[1]
    block = gate_in_w.shape[0]
    half = block // 2
    even_blocks, odd_blocks = gate_blocks(0, width, block), gate_blocks(1, width, block)
    gate_scatters = make_scatters(
        (gate_in_grad, gate_dec_grad),
        (gate_in_out, gate_dec_out),
        (False, False),
        scratch[54:],
        d,
        t,
    )
    lines = [LineScatter(part, got, ssem, rsem, d, t, depth, (s,)) for s in range(seqs)]

    def load(i, src, dst):
        copy = pltpu.make_async_copy(src, dst, load_sem.at[i])
        copy.start()
        return copy

    def load_wide(i, src):
        return [
            load(i + s, src.at[s], branch.at[pl.ds(s * length, length)]) for s in range(seqs)
        ]

    early = [load(0, out_w_in, weight)] + load_wide(12, branch_in)
    next_ = [
        load(2, gelu_pre_in, gelu_pre),
        load(3, states_in, states),
        load(4, gate_dec_in, gate_dec),
    ]
    panel_loads = [
        pltpu.make_async_copy(src, panel.grad, panel_sem.at[i])
        for i, (src, panel) in enumerate(zip(panels_in, ring.panels))
    ]

    def weight_grad(left, right, out):
        panel = 512

        @pl.loop(0, model // panel)
        def _(i):
            columns = rows_of(i, panel)
            out[columns, :] = contract(left[:, columns], right[...], (0, 0)).astype(BF16)

    def dp_copies(src, dst, send, recv):
        return [
            pltpu.make_async_remote_copy(
                src_ref=src,
                dst_ref=dst.at[d],
                send_sem=send.at[mask - 1],
                recv_sem=recv.at[mask - 1],
                device_id=(d ^ mask, t),
                device_id_type=MESH,
            )
            for mask in range(1, 8)
        ]

    def begin(i):
        if i < n_panels:
            panel_loads[i].wait()
        ring.panels[i].start()

    def push(i):
        ring.panels[i].first()
        ring.panels[i].second()

    for copy in panel_loads:
        copy.start()
    then = [
        load(5, gate_in_in, gate_in),
        load(6, conv_in, conv),
        load(7, window_in, window),
        load(8, gate_in_w_in, gate_in_w),
        load(9, gate_dec_w_in, gate_dec_w),
        load(10, input_pre_in, input_pre),
        load(11, input_w_in, input_w),
        load(1, mixed_in, mixed),
    ]
    for i in range(n_panels):
        begin(i)
    for copy in early:
        copy.wait()
    for s in range(seqs):
        rows = pl.ds(s * length, length)
        grad[rows, :] = contract(branch[rows, :], weight[...], (1, 0))
    reload = load(0, gelu_w_in, weight)
    push(0)
    for copy in next_:
        copy.wait()

    @pl.loop(0, tokens // STRIP)
    def _(i):
        rows = rows_of(i, STRIP)
        held = pl.ds(pl.multiple_of(i * STRIP + 8, 8), STRIP)
        act, slope = gelu_both(gelu_pre[rows, :])
        came = grad[rows, :]
        gelu_grad[rows, :] = (came * states[held, :] * slope).astype(BF16)
        grad[rows, :] = came * act
        decay[rows, :] = jnp.exp(-8.0 * sigmoid(gate_dec[rows, :]) * rate[...])

    decay[tokens : tokens + 8, :] = jnp.zeros((8, width), F32)
    push(1)
    ring.panels[0].third()
    scan_rows(decay, grad, range(seqs), length, backward=True)
    for copy in then:
        copy.wait()
    sums[...] = jnp.zeros(sums.shape, F32)

    def fold(value):
        return value[0:8] + value[8:16]

    first_row = lax.broadcasted_iota(jnp.int32, (STRIP, width), 0) == 0
    for s in range(seqs):

        @pl.loop(0, length // STRIP)
        def _(i):
            start = pl.multiple_of(s * length + i * STRIP, STRIP)
            rows = pl.ds(start, STRIP)
            earlier = pltpu.roll(states[pl.ds(start, STRIP + 8), :], 1, 0)[8:]
            earlier = jnp.where(first_row & (i == 0), 0.0, earlier)
            came = grad[rows, :]
            open_in = sigmoid(gate_in[rows, :])
            open_dec = sigmoid(gate_dec[rows, :])
            slow = -8.0 * rate[...]
            lost = one_less_exp(2.0 * open_dec * slow)
            root = jnp.sqrt(lost)
            value = conv[rows, :].astype(F32)
            step = decay[rows, :]
            through = came * open_in
            grad_log = step * (came * earlier - through * value * step / root)
            sums[0] += fold(grad_log * (-8.0 * open_dec))
            through = through * root
            grad_conv[s, pl.ds(pl.multiple_of(i * STRIP, STRIP), STRIP), :] = through
            grad_in[rows, :] = (through * value * (1.0 - open_in)).astype(BF16)
            grad_dec[rows, :] = (grad_log * slow * open_dec * (1.0 - open_dec)).astype(BF16)

        grad_conv[s, length : length + 8, :] = jnp.zeros((8, width), F32)

    def gates_back(k, low, high):
        return contract(grad_in[:, low:high], gate_in_w[:, low:high], (1, 1)) + contract(
            grad_dec[:, low:high], gate_dec_w[:, low:high], (1, 1)
        )

    def add_conv(low, high, value):
        for s in range(seqs):
            grad_conv[s, 0:length, low:high] += value[s * length : (s + 1) * length]

    def rim(to):
        return pltpu.make_async_remote_copy(
            src_ref=rim_out,
            dst_ref=rim_in,
            send_sem=rim_send,
            recv_sem=rim_recv,
            device_id=(d, to),
            device_id_type=MESH,
        )

    @pl.when(even)
    def _():
        value = gates_back(*even_blocks[-1])
        rim_out[...] = value[:, half:].astype(BF16)
        rim(t + 1).start()
        add_conv(width - half, width, value[:, :half])

    @pl.when(odd)
    def _():
        value = gates_back(*odd_blocks[0])
        rim_out[...] = value[:, :half].astype(BF16)
        rim(t - 1).start()
        add_conv(0, half, value[:, half:])

    ring.panels[0].end()
    ring.panels[1].third()
    push(2)

    def inner(blocks):
        for k, low, high in blocks:
            add_conv(low, high, gates_back(k, low, high))

    def gate_grads(blocks):
        for k, low, high in blocks:
            near = window[:, k * block : (k + 1) * block]
            gate_in_grad[:, low:high] = contract(near, grad_in[:, low:high], (0, 0)).astype(BF16)
            gate_dec_grad[:, low:high] = contract(near, grad_dec[:, low:high], (0, 0)).astype(BF16)

    @pl.when(even)
    def _():
        inner(even_blocks[:-1])
        gate_grads(even_blocks)

    @pl.when(odd)
    def _():
        inner(odd_blocks[1:])
        gate_grads(odd_blocks)

    for g in gate_scatters:
        g.start()
    weight_grad(branch, mixed, ring.panels[3].grad)
    begin(3)
    wide_loads = load_wide(12, normed_in)

    @pl.when(even)
    def _():
        rim(t + 1).wait()
        add_conv(width - half, width, rim_in[...].astype(F32))

    @pl.when(odd)
    def _():
        rim(t - 1).wait()
        add_conv(0, half, rim_in[...].astype(F32))

    for s in range(seqs):

        @pl.loop(0, length // STRIP)
        def _(i):
            near = pl.ds(pl.multiple_of(i * STRIP, STRIP), STRIP + 8)
            later = grad_conv[s, near, :]
            before = input_pre[s, near, :]
            here = later[:STRIP]
            value = taps[0:1, :] * here
            sums[1] += fold(here * before[8:])
            for k in range(1, taps.shape[0]):
                value = value + taps[k : k + 1, :] * pltpu.roll(later, STRIP + 8 - k, 0)[:STRIP]
                sums[1 + k] += fold(here * pltpu.roll(before, k, 0)[8:])
            rows = pl.ds(pl.multiple_of(s * length + i * STRIP, STRIP), STRIP)
            input_rows[rows, :] = value.astype(BF16)

    ring.panels[1].end()
    ring.panels[2].third()
    push(3)
    for k in range(sums.shape[0]):
        small[k : k + 1, :] = jnp.sum(sums[k], axis=0, keepdims=True)
    small[sums.shape[0] :, :] = jnp.zeros((8 - sums.shape[0], width), F32)
    small_copies = dp_copies(small, small_all, qsend, qrecv)
    for c in small_copies:
        c.start()
    small_all[d] = small[...]
    reload.wait()
    panel = 512

    @pl.loop(0, weight.shape[0] // panel)
    def _(i):
        columns = rows_of(i, panel)
        value = contract(gelu_grad[...], weight[columns, :], (1, 1))
        value = (value + contract(input_rows[...], input_w[columns, :], (1, 1))).astype(BF16)
        for s in range(seqs):
            part[s, :, columns] = value[s * length : (s + 1) * length]

    for line in lines:
        line.start()
    for copy in wide_loads:
        copy.wait()
    weight_grad(branch, gelu_grad, ring.panels[4].grad)
    begin(4)
    for g in gate_scatters:
        g.first()
        g.second()
    ring.panels[2].end()
    ring.panels[3].third()
    push(4)
    lines[0].step(1)
    weight_grad(branch, input_rows, ring.panels[5].grad)
    begin(5)
    for g in gate_scatters:
        g.third()
    lines[0].step(2)
    ring.panels[3].end()
    ring.panels[4].third()
    push(5)
    lines[1].step(1)
    lines[1].step(2)
    for g in gate_scatters:
        g.end()
    ring.panels[4].end()
    ring.panels[5].third()
    for s in range(seqs):
        lines[s].total([input_grad.at[i] for i in range(seqs)])
    quarter = pack.shape[1]
    for i in range(4):
        pack[4 + i : 5 + i, :] = mlp_part[:, i * quarter : (i + 1) * quarter]
    for s in range(seqs):
        change, gain_part = norm_back(act[s].astype(F32), gain[...], input_grad[s])
        input_grad[s] = change + grad_middle[s]
        for i in range(4):
            piece = gain_part[:, i * quarter : (i + 1) * quarter]
            if s == 0:
                pack[i : i + 1, :] = piece
            else:
                pack[i : i + 1, :] += piece
    pack_copies = dp_copies(pack, packs, psend, precv)
    for c in pack_copies:
        c.start()
    packs[d] = pack[...]
    for c in small_copies:
        c.wait_recv()
    sum_ = small_all[0]
    for i in range(1, 8):
        sum_ = sum_ + small_all[i]
    smalls[...] = sum_
    for c in pack_copies:
        c.wait_recv()
    sum_ = packs[0]
    for i in range(1, 8):
        sum_ = sum_ + packs[i]
    line_pack[...] = sum_
    z_copies = [
        pltpu.make_async_remote_copy(
            src_ref=line_pack,
            dst_ref=line_packs.at[t],
            send_sem=zsend.at[step - 1],
            recv_sem=zrecv.at[step - 1],
            device_id=(d, lax.rem(t + step, depth)),
            device_id_type=MESH,
        )
        for step in range(1, depth)
    ]
    for c in z_copies:
        c.start()
    line_packs[t] = sum_
    ring.panels[5].end()
    for c in z_copies:
        c.wait_recv()
    sum_ = line_packs[0]
    for i in range(1, depth):
        sum_ = sum_ + line_packs[i]
    gains[...] = sum_
    for c in small_copies + pack_copies + z_copies:
        c.wait_send()
    ring.end()
    for line in lines:
        line.end()


def mixer_back_phase(
    branch, normed, saved, weights, panels, taps, rate, act, gain, grad_middle, mlp_part, depth,
):
    seqs, length, model = branch.shape
    tokens = seqs * length
    gelu_w, input_w, gate_in_w, gate_dec_w, out_w = weights[:5]
    gelu_pre, input_pre, conv, window, gate_in, gate_dec, states, mixed = saved
    width = out_w.shape[1]
    block = gate_in_w.shape[0]
    half = block // 2
    n = len(panels)
    panel = (panels[0].shape[0] // 8, panels[0].shape[1])
    gate = (block // 8, width)
    pack = (8, model // 4)
    small = (8, width)
    flat = (tokens, width)
    outs = [
        shaped(act.shape, F32, VMEM),
        shaped(pack, F32, VMEM),
        shaped(small, F32, VMEM),
        shaped(gate, F32, VMEM),
        shaped(gate, F32, VMEM),
    ] + [shaped(panel, F32, ANY)] * (n + 3)
    scratch = [pltpu.VMEM((tokens, model), BF16)]
    scratch += [
        pltpu.VMEM(x.shape, x.dtype)
        for x in (
            out_w,
            input_w,
            gelu_pre,
            input_pre,
            conv,
            window,
            gate_in,
            gate_dec,
            states,
            gate_in_w,
            gate_dec_w,
        )
    ]
    scratch += [
        pltpu.VMEM(flat, F32),
        pltpu.VMEM((tokens + 8, width), F32),
        pltpu.VMEM((seqs, length + 8, width), F32),
    ]
    scratch += [pltpu.VMEM(flat, BF16)] * 5
    scratch += [pltpu.VMEM((tokens, half), BF16)] * 2
    scratch += [pltpu.VMEM(gate_in_w.shape, BF16)] * 2
    scratch += [
        pltpu.VMEM(branch.shape, BF16),
        pltpu.VMEM((1 + taps.shape[0], 8, width), F32),
    ]
    scratch += line_scatter_scratch(seqs, length // depth, model, depth)
    scratch += [DMA, DMA, DMA((12 + seqs,)), DMA((n,))]
    scratch += [
        pltpu.VMEM(small, F32),
        pltpu.VMEM((8,) + small, F32),
        pltpu.VMEM(pack, F32),
        pltpu.VMEM((8,) + pack, F32),
        pltpu.VMEM(pack, F32),
        pltpu.VMEM((depth,) + pack, F32),
    ]
    scratch += [DMA((7,))] * 4 + [DMA((depth - 1,))] * 2
    scratch += ring_scratch(3, *panel)
    scratch += scatter_scratch([gate] * 2, (False, False))
    res = call(
        functools.partial(mixer_back_kernel, depth, n),
        "mixer_back_phase",
        3,
        [ANY] * 15 + [VMEM] * 6 + [ANY] * n,
        outs,
        scratch,
        (
            branch,
            normed,
            out_w,
            gelu_pre,
            input_pre,
            conv,
            window,
            gate_in,
            gate_dec,
            states,
            mixed,
            gelu_w,
            input_w,
            gate_in_w,
            gate_dec_w,
            taps,
            rate.reshape(1, width),
            act,
            gain.reshape(1, model),
            grad_middle,
            mlp_part,
        )
        + tuple(panels),
        vmem=63 * 1024 * 1024,
    )
    return res[0], res[1].reshape(2, model), res[2], res[3:5], res[5:]


def swapped(block, axis):
    count = lax.axis_size(axis)
    return lax.ppermute(block, axis, [(i, i ^ 1) for i in range(count)])


def normalize(value_entries, scale_gain):
    return (
        value_entries
        * lax.rsqrt(jnp.mean(value_entries * value_entries, axis=-1, keepdims=True) + EPS)
        * scale_gain
    )


def causal_conv(value_entries, kernel):
    summed = value_entries * kernel[0]
    for offset in range(1, kernel.shape[0]):
        shifted = jnp.concatenate(
            [jnp.zeros_like(value_entries[:, :offset]), value_entries[:, :-offset]], axis=1
        )
        summed = summed + shifted * kernel[offset]
    return summed


def decay_inputs(input_pre, decay_pre, conv_vals, decay_rate):
    log_decay = -8.0 * jax.nn.sigmoid(decay_pre) * decay_rate
    scaled = jnp.sqrt(-jnp.expm1(2.0 * log_decay))
    return (log_decay, scaled * jax.nn.sigmoid(input_pre) * conv_vals)


def recurrence(rate, drive):
    def join(left, right):
        return left[0] * right[0], left[1] * right[0] + right[1]

    return lax.associative_scan(join, (rate, drive), axis=1)[1]


def dot(spec, left, right):
    return jnp.einsum(spec, left, right, preferred_element_type=F32)


def weight_grad(left, right):
    return dot("pkr,pku->ru", left, right).astype(BF16)


class Fast:
    def __init__(self, depth, taps, rate):
        self.depth, self.taps, self.rate = depth, taps, rate

    def front(self, cotangent, token_weight, weights, act, gain, first_gain):
        middle, rows, self.weights, self.feeds, self.saved, self.held = front_phase(
            cotangent, token_weight, weights, self.taps, self.rate, act, gain, first_gain,
            self.depth,
        )
        self.normed, self.cot, self.normed_two = rows
        return middle

    def feed(self, middle, gain, cotangent, token_weight):
        return feed_phase(
            self.normed_two, self.cot, self.feeds, self.held, middle, gain, cotangent,
            token_weight, self.depth,
        )

    def last(self, branch, panels, act, gain, grad_middle, mlp_part):
        input_grad, gains, small, gates, rest = mixer_back_phase(
            branch,
            self.normed,
            self.saved,
            self.weights,
            panels[HOSTED:],
            self.taps,
            self.rate,
            act,
            gain,
            grad_middle,
            mlp_part,
            self.depth,
        )
        grads = list(rest[-3:]) + list(gates)
        rest = rest[:-3]
        panels = list(panels[:HOSTED]) + list(rest)
        third = len(panels) // 3
        feeds = [
            jnp.concatenate(panels[i * third : (i + 1) * third], axis=1) for i in range(3)
        ]
        return input_grad, gains, small, grads, feeds


class Plain:
    def __init__(self, depth, taps, rate):
        self.depth, self.taps, self.rate = depth, taps, rate

    @staticmethod
    def wide(block):
        return lax.all_gather(block, "tensor", axis=1, tiled=True)

    @staticmethod
    def narrow(part):
        return lax.psum_scatter(part, "tensor", scatter_dimension=1, tiled=True).astype(F32)

    @staticmethod
    def full(shard):
        return lax.all_gather(shard, "dp", axis=0, tiled=True)

    @staticmethod
    def own(grad):
        return lax.psum_scatter(grad, "dp", scatter_dimension=0, tiled=True).astype(F32)

    def front(self, cotangent, token_weight, weights, act, gain, first_gain):
        cot = (cotangent.astype(F32) * token_weight).astype(BF16)
        normed = normalize(act.astype(F32), first_gain).astype(BF16)
        gelu_w, input_w, gate_in_w, gate_dec_w, out_w = (self.full(w) for w in weights[:5])
        self.feeds = tuple(self.full(w) for w in weights[5:])
        normed_all = self.wide(normed)
        seqs, length, _ = normed_all.shape
        channels = gelu_w.shape[1]
        block = gate_in_w.shape[0]
        half = block // 2
        width = channels + half
        parity = lax.axis_index("tensor") % 2
        gelu_pre = dot("kqg,ga->kqa", normed_all, gelu_w)
        input_pre = dot("kqg,ga->kqa", normed_all, input_w)
        gelu_out, gelu_back = jax.vjp(jax.nn.gelu, gelu_pre)
        conv_out, conv_back = jax.vjp(causal_conv, input_pre, self.taps)
        conv_bf = conv_out.astype(BF16)
        rim = lax.dynamic_slice_in_dim(conv_bf, (1 - parity) * (channels - half), half, 2)
        window = jnp.zeros((seqs, length, width), BF16)
        window = lax.dynamic_update_slice_in_dim(window, conv_bf, parity * half, 2)
        window = lax.dynamic_update_slice_in_dim(
            window, swapped(rim, "tensor"), (1 - parity) * channels, 2
        )
        tiles = window.reshape(seqs, length, width // block, block)
        placed = lax.dynamic_update_slice_in_dim(
            jnp.zeros((2, block, width), BF16), jnp.stack([gate_in_w, gate_dec_w]), parity * half, 2
        ).reshape(2, block, width // block, block)
        gates = dot("slbk,gkbc->gslbc", tiles, placed).reshape(2, seqs, length, width)
        gates = lax.dynamic_slice_in_dim(gates, parity * half, channels, 3)
        (log_decay, drive), gate_back = jax.vjp(
            decay_inputs, gates[0], gates[1], conv_bf.astype(F32), self.rate
        )
        decay = jnp.exp(log_decay)
        states = recurrence(decay, drive)
        mixed = (gelu_out * states).astype(BF16)
        self.kept = (
            normed_all, gelu_w, input_w, out_w, gelu_out, gelu_back, conv_back, tiles, placed,
            gate_back, decay, states, mixed,
        )
        part = dot("xgq,pq->xgp", mixed, out_w).astype(BF16)
        self.cot = self.wide(cot)
        middle = act.astype(F32) + self.narrow(part)
        self.normed_two = self.wide(normalize(middle, gain).astype(BF16))
        return middle

    def feed(self, middle, gain, cotangent, token_weight):
        cot_own = cotangent.astype(F32) * token_weight
        down_w, gate_w, up_w = self.feeds
        normed, cot = self.normed_two, self.cot
        gate_pre = dot("nwo,ob->nwb", normed, gate_w)
        lift_pre = dot("nwo,ob->nwb", normed, up_w)
        gate_act, activ_back = jax.vjp(jax.nn.gelu, gate_pre)
        hidden = (gate_act * lift_pre).astype(BF16)
        grad_hidden = dot("gre,eu->gru", cot, down_w)
        gate_grad = activ_back(grad_hidden * lift_pre)[0].astype(BF16)
        lift_grad = (grad_hidden * gate_act).astype(BF16)
        part = dot("mqa,ya->mqy", gate_grad, gate_w) + dot("mqa,ya->mqy", lift_grad, up_w)
        _, back = jax.vjp(normalize, middle, gain)
        change, gain_grad = back(self.narrow(part.astype(BF16)))
        grad = cot_own + change
        panels = (
            weight_grad(cot, hidden), weight_grad(normed, gate_grad), weight_grad(normed, lift_grad)
        )
        feed = dot("xav,tv->xat", hidden, down_w).astype(BF16)
        output = (middle + self.narrow(feed)).astype(BF16)
        return grad, self.wide(grad.astype(BF16)), gain_grad[None], output, panels

    def last(self, branch, panels, act, gain, grad_middle, mlp_part):
        (
            normed_all, gelu_w, input_w, out_w, gelu_out, gelu_back, conv_back, tiles, placed,
            gate_back, decay, states, mixed,
        ) = self.kept
        seqs, length, channels = states.shape
        block = tiles.shape[-1]
        half = block // 2
        width = channels + half
        parity = lax.axis_index("tensor") % 2
        grad_mixed = dot("xtz,zm->xtm", branch, out_w)
        gelu_grad = gelu_back(grad_mixed * states)[0].astype(BF16)
        later = jnp.concatenate([decay[:, 1:], jnp.zeros_like(decay[:, :1])], axis=1)
        grad_drive = jnp.flip(
            recurrence(jnp.flip(later, 1), jnp.flip(grad_mixed * gelu_out, 1)), 1
        )
        earlier = jnp.concatenate([jnp.zeros_like(states[:, :1]), states[:, :-1]], axis=1)
        grad_in, grad_dec, grad_conv, grad_rate = gate_back(
            (grad_drive * decay * earlier, grad_drive)
        )
        grads = lax.dynamic_update_slice_in_dim(
            jnp.zeros((2, seqs, length, width), BF16),
            jnp.stack([grad_in, grad_dec]).astype(BF16),
            parity * half,
            3,
        ).reshape(2, seqs, length, width // block, block)
        grad_window = dot("gslbc,gkbc->slbk", grads, placed).reshape(seqs, length, width)
        grad_placed = dot("slbk,gslbc->gkbc", tiles, grads).reshape(2, block, width)
        grad_gates = lax.dynamic_slice_in_dim(grad_placed, parity * half, channels, 2)
        rim = lax.dynamic_slice_in_dim(grad_window, (1 - parity) * channels, half, 2)
        rim = swapped(rim.astype(BF16), "tensor").astype(F32)
        grad_conv = grad_conv + lax.dynamic_slice_in_dim(grad_window, parity * half, channels, 2)
        start = (1 - parity) * (channels - half)
        rim = lax.dynamic_slice_in_dim(grad_conv, start, half, 2) + rim
        grad_conv = lax.dynamic_update_slice_in_dim(grad_conv, rim, start, 2)
        input_rows, grad_taps = conv_back(grad_conv)
        input_rows = input_rows.astype(BF16)
        part = dot("mzf,af->mza", gelu_grad, gelu_w) + dot("mzf,af->mza", input_rows, input_w)
        _, back = jax.vjp(normalize, act.astype(F32), gain)
        change, gain_grad = back(self.narrow(part.astype(BF16)))
        gains = lax.psum(jnp.concatenate([gain_grad[None], mlp_part]), ("dp", "tensor"))
        small = lax.psum(jnp.concatenate([grad_rate[None], grad_taps]), "dp")
        parts = (
            weight_grad(branch, mixed),
            weight_grad(normed_all, gelu_grad),
            weight_grad(normed_all, input_rows),
            grad_gates[0].astype(BF16),
            grad_gates[1].astype(BF16),
        )
        own = [self.own(g) for g in parts]
        feeds = [self.own(g) for g in panels]
        return grad_middle + change, gains, small, own, feeds


def shards(
    activations,
    norm_gain,
    gelu_proj,
    input_proj,
    conv_weight,
    gate_input,
    gate_decay,
    decay_rate,
    out_proj,
    mlp_gain,
    feed_gate,
    feed_up,
    feed_down,
    cotangent,
    lengths,
    batch_of,
):
    depth = lax.axis_size("tensor")
    fast = lax.axis_size("dp") == 8 and depth == 4
    run = (Fast if fast else Plain)(depth, conv_weight, decay_rate)
    tensor_index = lax.axis_index("tensor")
    data_index = lax.axis_index("dp")
    seq_count, row_count, _ = activations.shape
    full_length = row_count * depth
    members = (batch_of[:, None] == jnp.arange(MICRO)[None, :]).astype(F32)
    counts = jnp.sum(members * lengths[:, None].astype(F32), axis=0)
    total_seqs = lengths.shape[0]
    per_batch = float(total_seqs * full_length) / (MICRO * counts)
    weight_all = jnp.sum(members * per_batch[None, :], axis=1)
    my_weight = lax.dynamic_slice_in_dim(weight_all, data_index * seq_count, seq_count)
    my_length = lax.dynamic_slice_in_dim(lengths, data_index * seq_count, seq_count)
    places = tensor_index * row_count + jnp.arange(row_count)
    valid_mask = (places[None, :] < my_length[:, None]).astype(F32)
    token_weight = (valid_mask * my_weight[:, None])[:, :, None]

    weights = (
        gelu_proj, input_proj, gate_input, gate_decay, out_proj.T, feed_down.T, feed_gate, feed_up
    )
    middle = run.front(cotangent, token_weight, weights, activations, mlp_gain, norm_gain)
    grad_middle, branch_grad_all, mlp_part, output, panels = run.feed(
        middle, mlp_gain, cotangent, token_weight
    )
    input_grad, gains, small, grads, feeds = run.last(
        branch_grad_all, panels, activations, norm_gain, grad_middle, mlp_part
    )
    return (
        output,
        input_grad,
        gains[0],
        grads[1],
        grads[2],
        small[1:5],
        grads[3],
        grads[4],
        small[0],
        grads[0].T,
        gains[1],
        feeds[1],
        feeds[2],
        feeds[0].T,
    )


def solution(mesh):
    placed = (
        P("dp", "tensor", None),
        P(),
        P("dp", "tensor"),
        P("dp", "tensor"),
        P(None, "tensor"),
        P("dp", "tensor"),
        P("dp", "tensor"),
        P("tensor"),
        P("tensor", "dp"),
        P(),
        P("dp", "tensor"),
        P("dp", "tensor"),
        P("tensor", "dp"),
        P("dp", "tensor", None),
        P(),
        P(),
    )
    return jax.shard_map(
        shards,
        mesh=mesh,
        in_specs=placed,
        out_specs=(
            P("dp", "tensor", None),
            P("dp", "tensor", None),
            P(),
            P("dp", "tensor"),
            P("dp", "tensor"),
            P(None, "tensor"),
            P("dp", "tensor"),
            P("dp", "tensor"),
            P("tensor"),
            P("tensor", "dp"),
            P(),
            P("dp", "tensor"),
            P("dp", "tensor"),
            P("tensor", "dp"),
        ),
        check_vma=False,
    )
```

```python
import functools

import jax
import jax.numpy as jnp
from jax import lax
from jax.experimental import pallas as pl
from jax.experimental.pallas import tpu as pltpu
from jax.sharding import PartitionSpec as P

MICRO = 4
EPS = 1e-06
MESH = pl.DeviceIdType.MESH
ANY = pl.BlockSpec(memory_space=pl.ANY)
VMEM = pl.BlockSpec(memory_space=pltpu.VMEM)
DMA = pltpu.SemaphoreType.DMA
BF16 = jnp.bfloat16
F32 = jnp.float32


def place():
    return lax.axis_index("dp"), lax.axis_index("tensor")


def greet(d, t, depth, dp_masks=(1, 2, 4), z_all=False, meanwhile=None):
    barrier = pltpu.get_barrier_semaphore()
    for mask in dp_masks:
        pl.semaphore_signal(barrier, inc=1, device_id=(d ^ mask, t), device_id_type=MESH)
    if z_all:
        for step in range(1, depth):
            pl.semaphore_signal(
                barrier, inc=1, device_id=(d, lax.rem(t + step, depth)), device_id_type=MESH
            )
        if meanwhile is not None:
            meanwhile()
        pl.semaphore_wait(barrier, len(dp_masks) + depth - 1)
        return

    @pl.when(t > 0)
    def _():
        pl.semaphore_signal(barrier, inc=1, device_id=(d, t - 1), device_id_type=MESH)

    @pl.when(t < depth - 1)
    def _():
        pl.semaphore_signal(barrier, inc=1, device_id=(d, t + 1), device_id_type=MESH)

    if meanwhile is not None:
        meanwhile()
    ends = jnp.where((t == 0) | (t == depth - 1), 1, 2)
    pl.semaphore_wait(barrier, len(dp_masks) + ends)


def add_rows(total, *terms, rows, step=32):
    step = min(step, rows)

    @pl.loop(0, rows, step=step)
    def _(start):
        part = pl.ds(pl.multiple_of(start, step), step)
        value = total[part, :].astype(F32)
        for term in terms:
            value = value + term[part, :].astype(F32)
        total[part, :] = value.astype(BF16)


class WeightGather:
    def __init__(self, shard, out, local, send, recv, d, t):
        rows = shard.shape[0]
        half = rows // 2

        def view(slot, start, size):
            if len(out.shape) == 3:
                return out.at[slot, pl.ds(start, size)]
            return out.at[pl.ds(pl.multiple_of(slot * rows + start, 16), size)]

        top, low = (0, half), (half, half)
        plan = [
            (None, d, top, 2),
            (None, d, low, 4),
            (None, d, low, 2),
            (None, d, top, 4),
            (2, d ^ 2, top, 4),
            (4, d ^ 4, low, 2),
            (None, d, top, 1),
            (None, d, low, 1),
            (2, d ^ 2, top, 1),
            (4, d ^ 4, low, 1),
            (2, d ^ 2, low, 1),
            (4, d ^ 4, top, 1),
            (6, d ^ 6, top, 1),
            (6, d ^ 6, low, 1),
        ]
        self.copies = [
            pltpu.make_async_remote_copy(
                src_ref=shard.at[pl.ds(*part)] if came is None else view(slot, *part),
                dst_ref=view(slot, *part),
                send_sem=send.at[i],
                recv_sem=recv.at[i],
                device_id=(d ^ mask, t),
                device_id_type=MESH,
            )
            for i, (came, slot, part, mask) in enumerate(plan)
        ]
        self.own = pltpu.make_async_copy(shard, view(d, 0, rows), local)

    def start(self):
        for i in (0, 1, 2, 3, 6, 7):
            self.copies[i].start()
        self.own.start()

    def relay(self):
        c = self.copies
        c[0].wait_recv()
        c[4].start()
        c[1].wait_recv()
        c[5].start()
        c[8].start()
        c[9].start()

    def relay_two(self):
        c = self.copies
        c[2].wait_recv()
        c[10].start()
        c[3].wait_recv()
        c[11].start()

    def relay_last(self):
        c = self.copies
        c[4].wait_recv()
        c[12].start()
        c[5].wait_recv()
        c[13].start()

    def arrive(self):
        for i in range(6, 14):
            self.copies[i].wait_recv()
        self.own.wait()

    def end(self):
        for i in range(14):
            self.copies[i].wait_send()


def gather_scratch(count):
    return [DMA((count,)), DMA((count, 14)), DMA((count, 14))]


class GradScatter:
    ORDER = (6, 2, 4, 0)

    def __init__(self, grad, out, own, core, diag, last, local, send, recv, d, t):
        self.out, self.core, self.diag, self.last = out, core, diag, last
        self.grad, self.d, self.t = grad, d, t
        self.credit = None
        self.reused = self.again = False
        self.before = self.flush = None
        self.rows = rows = out.shape[0]
        half = rows // 2
        self.half = half
        self.top, self.low = pl.ds(0, half), pl.ds(half, half)

        def block(slot, start=0, size=rows):
            return grad.at[pl.ds(pl.multiple_of(slot * rows + start, 16), size)]

        if own is None:
            self.loads = []
            self.mine = lambda i, start=0, size=rows: block(d ^ self.ORDER[i], start, size)
        else:
            self.loads = [
                pltpu.make_async_copy(block(d ^ r), own.at[i], local.at[i])
                for i, r in enumerate(self.ORDER)
            ]
            self.mine = lambda i, start=0, size=rows: own.at[i, pl.ds(start, size)]
        mine, top, low = self.mine, self.top, self.low
        plan = [(block(d ^ 1 ^ r), core.at[i], 1) for i, r in enumerate(self.ORDER)] + [
            (mine(0, 0, half), diag.at[0], 2),
            (mine(0, half, half), diag.at[1], 4),
            (mine(1, 0, half), last.at[0, top], 2),
            (mine(2, half, half), last.at[1, low], 4),
            (mine(2, 0, half), last.at[1, top], 4),
            (mine(1, half, half), last.at[0, low], 2),
        ]
        self.copies = [
            pltpu.make_async_remote_copy(
                src_ref=src,
                dst_ref=dst,
                send_sem=send.at[i],
                recv_sem=recv.at[i],
                device_id=(d ^ mask, t),
                device_id_type=MESH,
            )
            for i, (src, dst, mask) in enumerate(plan)
        ]

    def start(self):
        if self.reused:
            pl.semaphore_wait(self.credit.at[0], 1)
        for i in range(4):
            self.copies[i].start()
        for load in self.loads:
            load.start()

    def arrive(self, i):
        if self.loads:
            self.loads[i].wait()
        self.copies[i].wait_recv()

    def add(self, i, start, *terms):
        half = pl.ds(start, self.half)
        add_rows(self.mine(i, start, self.half), self.core.at[i, half], *terms, rows=self.half)

    def first(self):
        self.arrive(0)
        for i, start in enumerate((0, self.half)):
            self.add(0, start)
            if self.reused:
                pl.semaphore_wait(self.credit.at[1 + i], 1)
            self.copies[4 + i].start()

    def second(self):
        self.arrive(1)
        self.add(1, 0)
        self.copies[6].start()
        self.arrive(2)
        self.add(2, self.half)
        self.copies[7].start()

    def third(self):
        c = self.copies
        c[4].wait_recv()
        self.add(2, 0, self.diag.at[0])
        c[8].start()
        c[5].wait_recv()
        self.add(1, self.half, self.diag.at[1])
        c[9].start()

    def end(self):
        self.arrive(3)
        for i in (6, 7, 8, 9):
            self.copies[i].wait_recv()
        step = 16
        own = self.mine(3)
        if self.before is not None:
            self.before.flush.wait()

        @pl.loop(0, self.rows, step=step)
        def _(start):
            part = pl.ds(pl.multiple_of(start, step), step)
            self.out[part, :] = (
                own[part, :].astype(F32)
                + self.core[3, part, :].astype(F32)
                + self.last[0, part, :].astype(F32)
                + self.last[1, part, :].astype(F32)
            )

        if self.flush is not None:
            self.flush.start()
        for i in range(10):
            self.copies[i].wait_send()
        if self.again:
            for i, mask in enumerate((1, 2, 4)):
                pl.semaphore_signal(
                    self.credit.at[i], inc=1, device_id=(self.d ^ mask, self.t), device_id_type=MESH
                )


class PanelRing:
    def __init__(self, outs, scratch, d, t):
        grads, core, diag, last, stage, send, recv, credit, flush = scratch
        self.slots = slots = grads.shape[0]
        self.panels = []
        for i, out in enumerate(outs):
            q = i % slots
            panel = GradScatter(
                grads.at[q],
                stage.at[q],
                None,
                core.at[q],
                diag.at[q],
                last.at[q],
                None,
                send.at[q],
                recv.at[q],
                d,
                t,
            )
            panel.credit = credit.at[q]
            panel.reused = i >= slots
            panel.again = i + slots < len(outs)
            panel.before = self.panels[i - slots] if i >= slots else None
            panel.flush = pltpu.make_async_copy(stage.at[q], out, flush.at[q])
            self.panels.append(panel)

    def end(self):
        for panel in self.panels[-self.slots :]:
            panel.flush.wait()


def ring_scratch(slots, rows, n):
    return [
        pltpu.VMEM((slots, 8 * rows, n), BF16),
        pltpu.VMEM((slots, 4, rows, n), BF16),
        pltpu.VMEM((slots, 2, rows // 2, n), BF16),
        pltpu.VMEM((slots, 2, rows, n), BF16),
        pltpu.VMEM((slots, rows, n), F32),
        DMA((slots, 10)),
        DMA((slots, 10)),
        pltpu.SemaphoreType.REGULAR((slots, 3)),
        DMA((slots,)),
    ]


def scatter_scratch(shapes, loaded):
    own = [pltpu.VMEM((4,) + s, BF16) for s, far in zip(shapes, loaded) if far]
    core = [pltpu.VMEM((4,) + s, BF16) for s in shapes]
    diag = [pltpu.VMEM((2, s[0] // 2, s[1]), BF16) for s in shapes]
    last = [pltpu.VMEM((2,) + s, BF16) for s in shapes]
    n = len(shapes)
    return own + core + diag + last + [DMA((n, 4)), DMA((n, 10)), DMA((n, 10))]


def make_scatters(grads, outs, loaded, scratch, d, t):
    n = len(grads)
    scratch = list(scratch)
    own = [scratch.pop(0) if far else None for far in loaded]
    core, diag, last = (scratch[i * n : (i + 1) * n] for i in range(3))
    local, send, recv = scratch[3 * n :]
    return [
        GradScatter(
            grads[i],
            outs[i],
            own[i],
            core[i],
            diag[i],
            last[i],
            local.at[i],
            send.at[i],
            recv.at[i],
            d,
            t,
        )
        for i in range(n)
    ]


class LineGather:
    def __init__(self, block, out, local, send, recv, d, t, depth):
        self.block, self.out, self.send, self.recv = block, out, send, recv
        self.d, self.t, self.depth = d, t, depth
        self.rows = block.shape[-2]
        self.own = pltpu.make_async_copy(block, self.slot(t), local)

    def slot(self, j):
        rows = pl.ds(pl.multiple_of(j * self.rows, self.rows), self.rows)
        return self.out.at[:, rows] if len(self.out.shape) == 3 else self.out.at[rows]

    def copy(self, way, step, j, to):
        return pltpu.make_async_remote_copy(
            src_ref=self.block if step == 0 else self.slot(j),
            dst_ref=self.slot(j),
            send_sem=self.send.at[way, step],
            recv_sem=self.recv.at[way, step],
            device_id=(self.d, to),
            device_id_type=MESH,
        )

    def open(self, k):
        t, depth = self.t, self.depth
        if k == 0:
            self.own.start()

        @pl.when(t == k)
        def _():
            self.copy(0, 0, t, t + 1).start()

        @pl.when(t == depth - 1 - k)
        def _():
            self.copy(1, 0, t, t - 1).start()

    def step(self, s):
        t, depth = self.t, self.depth
        if s == 0:
            for k in range(depth - 1):
                self.open(k)
            return

        @pl.when((t - s >= 0) & (t < depth - 1))
        def _():
            self.copy(0, s - 1, t, t).wait_recv()
            self.copy(0, s, t - s, t + 1).start()

        @pl.when((t + s < depth) & (t > 0))
        def _():
            self.copy(1, s - 1, t, t).wait_recv()
            self.copy(1, s, t + s, t - 1).start()

    def finish(self):
        t, depth = self.t, self.depth
        self.own.wait()
        for s in range(depth - 1):

            @pl.when(t == depth - 1)
            def _():
                self.copy(0, s, t, t).wait_recv()

            @pl.when(t == 0)
            def _():
                self.copy(1, s, t, t).wait_recv()

    def end(self):
        t, depth = self.t, self.depth
        for s in range(depth - 1):

            @pl.when((t - s >= 0) & (t < depth - 1))
            def _():
                self.copy(0, s, t, t).wait_send()

            @pl.when((t + s < depth) & (t > 0))
            def _():
                self.copy(1, s, t, t).wait_send()


def line_gather_scratch(depth):
    return [DMA, DMA((2, depth - 1)), DMA((2, depth - 1))]


class LineScatter:
    def __init__(self, part, got, send, recv, d, t, depth, which=None, first_row=None):
        self.part, self.got, self.send, self.recv = part, got, send, recv
        self.d, self.t, self.depth = d, t, depth
        self.which = range(part.shape[0]) if which is None else which
        self.first_row = first_row
        self.rows = got.shape[3]

    def slot(self, way, j, s):
        return self.got.at[way, j - 1 if way == 0 else j, s]

    def copy(self, way, j, s, src, to):
        return pltpu.make_async_remote_copy(
            src_ref=src,
            dst_ref=self.slot(way, j, s),
            send_sem=self.send.at[way, j, s],
            recv_sem=self.recv.at[way, j, s],
            device_id=(self.d, to),
            device_id_type=MESH,
        )

    def block(self, j, s):
        start = j * self.rows
        if self.first_row is not None:
            start = pl.multiple_of(self.first_row + start, self.rows)
            return self.part.at[pl.ds(start, self.rows)]
        return self.part.at[s, pl.ds(pl.multiple_of(start, self.rows), self.rows)]

    def start(self, first=0, last=None):
        t, depth = self.t, self.depth
        steps = range(first, depth - 1 if last is None else last)

        @pl.when(t == 0)
        def _():
            for k in steps:
                for s in self.which:
                    j = depth - 1 - k
                    self.copy(0, j, s, self.block(j, s), t + 1).start()

        @pl.when(t == depth - 1)
        def _():
            for j in steps:
                for s in self.which:
                    self.copy(1, j, s, self.block(j, s), t - 1).start()

    def pass_on(self, way, j, to):
        for s in self.which:
            mine = self.slot(way, j, s)
            self.copy(way, j, s, mine, self.t).wait_recv()
            add_rows(mine, self.block(j, s), rows=self.rows)
            self.copy(way, j, s, mine, to).start()

    def step(self, k):
        t, depth = self.t, self.depth
        right = depth - 1 - k + t
        left = k - (depth - 1 - t)

        @pl.when((t > 0) & (t < right) & (right < depth))
        def _():
            self.pass_on(0, right, t + 1)

        @pl.when((left >= 0) & (left < t) & (t < depth - 1))
        def _():
            self.pass_on(1, left, t - 1)

    def total(self, out, more=False):
        t, depth = self.t, self.depth
        for s in self.which:
            own = self.block(t, s)[...].astype(F32)
            out[s][...] = out[s][...] + own if more else own

        @pl.when(t > 0)
        def _():
            for s in self.which:
                self.copy(0, t, s, self.slot(0, t, s), t).wait_recv()
                out[s][...] += self.got[0, t - 1, s].astype(F32)

        @pl.when(t < depth - 1)
        def _():
            for s in self.which:
                self.copy(1, t, s, self.slot(1, t, s), t).wait_recv()
                out[s][...] += self.got[1, t, s].astype(F32)

    def end(self):
        t, depth = self.t, self.depth
        for j in range(depth):
            for s in self.which:
                if j > 0:

                    @pl.when(j > t)
                    def _():
                        self.copy(0, j, s, self.slot(0, j, s), t).wait_send()

                if j < depth - 1:

                    @pl.when(j < t)
                    def _():
                        self.copy(1, j, s, self.slot(1, j, s), t).wait_send()


def line_scatter_scratch(seqs, rows, width, depth):
    return [
        pltpu.VMEM((2, depth - 1, seqs, rows, width), BF16),
        DMA((2, depth, seqs)),
        DMA((2, depth, seqs)),
    ]


def call(kernel, name, number, ins, outs, scratch, args, vmem=60 * 1024 * 1024):
    return pl.pallas_call(
        kernel,
        name=name,
        out_shape=[o[0] for o in outs],
        in_specs=ins,
        out_specs=[o[1] for o in outs],
        scratch_shapes=scratch,
        compiler_params=pltpu.CompilerParams(
            collective_id=number, has_side_effects=True, vmem_limit_bytes=vmem
        ),
    )(*args)


def shaped(shape, dtype, spec):
    return (jax.ShapeDtypeStruct(shape, dtype), spec)


def sigmoid(x):
    return 1.0 / (1.0 + jnp.exp(-x))


def one_less_exp(y):
    series = 1.0 + y / 6.0 * (1.0 + y / 7.0)
    for k in (5.0, 4.0, 3.0, 2.0):
        series = 1.0 + y / k * series
    return jnp.where(y > -0.5, -y * series, 1.0 - jnp.exp(y))


GELU_SCALE = 0.7978845608028654
GELU_CUBE = 0.044715


def gelu(x):
    return 0.5 * x * (1.0 + jnp.tanh(GELU_SCALE * (x + GELU_CUBE * x * x * x)))


def gelu_both(x):
    square = x * x
    bent = jnp.tanh(GELU_SCALE * (x + GELU_CUBE * square * x))
    half = 0.5 * (1.0 + bent)
    slope = half + 0.5 * x * (1.0 - bent * bent) * (
        GELU_SCALE * (1.0 + 3.0 * GELU_CUBE * square)
    )
    return x * half, slope


def rows_of(index, size):
    return pl.ds(pl.multiple_of(index * size, size), size)


def contract(left, right, dims):
    return lax.dot_general(left, right, ((dims[:1], dims[1:]), ((), ())), preferred_element_type=F32)


def scan_rows(rate, out, which, length, base=0, backward=False):
    tile = 8
    width = out.shape[1]
    row = lax.broadcasted_iota(jnp.int32, (tile, width), 0)

    def body(i, carried):
        k = length // tile - 1 - i if backward else i
        ends = []
        for at, s in enumerate(which):
            start = pl.multiple_of(s * length + k * tile, tile)
            rows = pl.ds(start, tile)
            if backward:
                pair = rate[pl.ds(start, 2 * tile), :]
                step = pltpu.roll(pair, 2 * tile - 1, 0)[:tile]
                step = jnp.where((row == tile - 1) & (i == 0), 0.0, step)
            else:
                step = rate[rows, :]
            held = pl.ds(pl.multiple_of(base + start, tile), tile)
            drive = out[held, :]
            for shift in (1, 2, 4):
                turn = tile - shift if backward else shift
                inside = row < tile - shift if backward else row >= shift
                before = jnp.where(inside, pltpu.roll(drive, turn, 0), 0.0)
                drive = drive + step * before
                step = step * jnp.where(inside, pltpu.roll(step, turn, 0), 1.0)
            states = drive + step * carried[at]
            out[held, :] = states
            ends.append(states[0:1] if backward else states[tile - 1 : tile])
        return tuple(ends)

    start = tuple(jnp.zeros((1, width), F32) for _ in which)
    lax.fori_loop(0, length // tile, body, start, unroll=2)


STRIP = 16
PANEL = 640


def gate_blocks(parity, width, block):
    half = block // 2
    shift = parity * half
    blocks = []
    for k in range((width + half) // block):
        low, high = k * block - shift, (k + 1) * block - shift
        blocks.append((k, max(low, 0), min(high, width)))
    return blocks


def front_kernel(
    depth,
    cotangent,
    token_weight,
    gelu_shard,
    input_shard,
    gate_in_shard,
    gate_dec_shard,
    out_shard,
    gate_shard,
    up_shard,
    down_shard,
    taps,
    rate,
    act,
    gain,
    first_gain,
    middle,
    normed_out,
    cot_out,
    normed_two_out,
    gelu_full,
    input_full,
    gate_in_full,
    gate_dec_full,
    out_full,
    gate_full,
    up_full,
    down_full,
    gelu_pre_out,
    input_pre_out,
    window_out,
    gate_in_out,
    gate_dec_out,
    states_out,
    mixed_out,
    gate_pre_out,
    lift_pre_out,
    hidden_out,
    *scratch,
):
    normed, gelu_w, input_w, gate_in_w, gate_dec_w, out_w = scratch[:6]
    gelu_pre, input_pre, conv, window, gate_in, gate_dec, decay, states, mixed, part = scratch[6:16]
    local, send, recv = scratch[16:19]
    line_sems = [scratch[19 + 3 * i : 22 + 3 * i] for i in range(6)]
    rim_send, rim_recv, save_sem = scratch[37:40]
    cot, normed_two, block_two, panel_w, product = scratch[40:45]
    panel_sem, product_sem = scratch[45:47]
    got, ssem, rsem = scratch[47:50]
    normed_block, cot_block, hidden = scratch[50:53]
    d, t = place()
    parity = lax.rem(t, 2)
    even = parity == 0
    odd = parity == 1

    def prepare():
        for s in range(act.shape[0]):
            value = act[s].astype(F32)
            inverse = lax.rsqrt(jnp.mean(value * value, axis=-1, keepdims=True) + EPS)
            normed_block[s] = (value * inverse * first_gain[...][None]).astype(BF16)
            cot_block[s] = (cotangent[s].astype(F32) * token_weight[s]).astype(BF16)

    greet(d, t, depth, meanwhile=prepare)
    seqs, length, model = normed.shape
    tokens = seqs * length
    width = conv.shape[1]
    block = gate_in_w.shape[0]
    half = block // 2
    spans = [pl.ds(s * length, length) for s in range(seqs)]
    firsts = [
        LineGather(normed_block.at[s], normed.at[s], *line_sems[5 * s], d, t, depth)
        for s in range(seqs)
    ]
    cots = [
        LineGather(cot_block.at[s], cot.at[spans[s]], *line_sems[1 + s], d, t, depth)
        for s in range(seqs)
    ]
    twos = [
        LineGather(block_two.at[s], normed_two.at[spans[s]], *line_sems[3 + s], d, t, depth)
        for s in range(seqs)
    ]
    scatters = [LineScatter(part, got, ssem, rsem, d, t, depth, (s,)) for s in range(seqs)]
    pairs = (
        (gelu_shard, gelu_w),
        (input_shard, input_w),
        (gate_in_shard, gate_in_w),
        (gate_dec_shard, gate_dec_w),
        (out_shard, out_w),
        (gate_shard, gate_full),
        (up_shard, up_full),
        (down_shard, down_full),
    )
    gathers = [
        WeightGather(shard, full, local.at[i], send.at[i], recv.at[i], d, t)
        for i, (shard, full) in enumerate(pairs)
    ]
    saves = []

    def save(src, dst):
        copy = pltpu.make_async_copy(src, dst, save_sem.at[len(saves)])
        copy.start()
        saves.append(copy)

    one = [gathers[1], gathers[0], gathers[2], gathers[3]]
    out_g, gate_g, up_g, down_g = gathers[4:]
    even_blocks, odd_blocks = gate_blocks(0, width, block), gate_blocks(1, width, block)

    def rim(s, to, src, dst):
        return pltpu.make_async_remote_copy(
            src_ref=conv.at[spans[s], pl.ds(src, half)],
            dst_ref=window.at[spans[s], pl.ds(dst, half)],
            send_sem=rim_send.at[s],
            recv_sem=rim_recv.at[s],
            device_id=(d, to),
            device_id_type=MESH,
        )

    def convolve(s):
        input_pre[s, 0:8, :] = jnp.zeros((8, width), F32)
        input_pre[s, 8 : 8 + length, :] = contract(normed[s], input_w[...], (1, 0))

        @pl.loop(0, length // STRIP)
        def _(i):
            near = input_pre[s, pl.ds(pl.multiple_of(i * STRIP, STRIP), STRIP + 8), :]
            total = taps[0:1, :] * near[8:]
            for k in range(1, taps.shape[0]):
                total = total + taps[k : k + 1, :] * pltpu.roll(near, k, 0)[8:]
            rows = pl.ds(pl.multiple_of(s * length + i * STRIP, STRIP), STRIP)
            conv[rows, :] = total.astype(BF16)

        @pl.when(even)
        def _():
            rim(s, t + 1, width - half, 0).start()
            window[spans[s], 0:width] = conv[spans[s], :]

        @pl.when(odd)
        def _():
            rim(s, t - 1, 0, width).start()
            window[spans[s], half : half + width] = conv[spans[s], :]

    def gates(s, blocks):
        for k, low, high in blocks:
            near = window[spans[s], k * block : (k + 1) * block]
            gate_in[spans[s], low:high] = contract(near, gate_in_w[:, low:high], (1, 0))
            gate_dec[spans[s], low:high] = contract(near, gate_dec_w[:, low:high], (1, 0))

    def inner_gates(s):
        gelu_pre[spans[s], :] = contract(normed[s], gelu_w[...], (1, 0))

        @pl.when(even)
        def _():
            gates(s, even_blocks[:-1])

        @pl.when(odd)
        def _():
            gates(s, odd_blocks[1:])

    def recur(s):
        @pl.when(even)
        def _():
            rim(s, t + 1, width - half, width).wait_recv()
            gates(s, even_blocks[-1:])

        @pl.when(odd)
        def _():
            rim(s, t - 1, 0, 0).wait_recv()
            gates(s, odd_blocks[:1])

        @pl.loop(0, length // STRIP)
        def _(i):
            start = pl.multiple_of(s * length + i * STRIP, STRIP)
            rows = pl.ds(start, STRIP)
            log = -8.0 * sigmoid(gate_dec[rows, :]) * rate[...][None]
            decay[rows, :] = jnp.exp(log)
            drive = jnp.sqrt(one_less_exp(2.0 * log)) * sigmoid(gate_in[rows, :])
            held = pl.ds(pl.multiple_of(start + 8, 8), STRIP)
            states[held, :] = drive * conv[rows, :].astype(F32)

        scan_rows(decay, states, (s,), length, base=8)

    def mix(s):
        @pl.loop(0, length // STRIP)
        def _(i):
            start = pl.multiple_of(s * length + i * STRIP, STRIP)
            rows, held = pl.ds(start, STRIP), pl.ds(pl.multiple_of(start + 8, 8), STRIP)
            mixed[rows, :] = (gelu(gelu_pre[rows, :]) * states[held, :]).astype(BF16)

        panel = 512

        @pl.loop(0, model // panel)
        def _(i):
            columns = rows_of(i, panel)
            part[s, :, columns] = contract(mixed[spans[s], :], out_w[columns, :], (1, 1)).astype(
                BF16
            )

    def norm_step(s):
        scatters[s].total([middle.at[i] for i in range(seqs)])
        value = middle[s] + act[s].astype(F32)
        middle[s] = value
        inverse = lax.rsqrt(jnp.mean(value * value, axis=-1, keepdims=True) + EPS)
        block_two[s] = (value * inverse * gain[...][None]).astype(BF16)
        twos[s].step(0)

    firsts[0].step(0)
    for g in one:
        g.start()
    firsts[0].step(1)
    firsts[1].step(0)
    for g in one:
        g.relay()
    out_g.start()
    firsts[0].step(2)
    for line in cots:
        line.open(0)
    for g in one:
        g.relay_two()
    firsts[1].step(1)
    for g in one:
        g.relay_last()
    firsts[0].finish()
    for line in cots:
        line.open(1)
    one[0].arrive()
    states[0:8, :] = jnp.zeros((8, width), F32)
    convolve(0)
    out_g.relay()
    gate_g.start()
    up_g.start()
    for g in one[1:]:
        g.arrive()
    inner_gates(0)
    out_g.relay_two()
    firsts[1].step(2)
    recur(0)
    out_g.relay_last()
    out_g.arrive()
    mix(0)
    firsts[1].finish()
    scatters[0].start(0, 1)
    for line in cots:
        line.open(2)
    convolve(1)
    scatters[0].start(1)
    inner_gates(1)
    scatters[0].step(1)
    gate_g.relay()
    recur(1)
    scatters[0].step(2)
    mix(1)
    scatters[1].start()
    save(normed, normed_out)
    save(gelu_w, gelu_full)
    save(input_w, input_full)
    save(gate_in_w, gate_in_full)
    save(gate_dec_w, gate_dec_full)
    save(out_w, out_full)
    save(gelu_pre, gelu_pre_out)
    save(input_pre, input_pre_out)
    save(window, window_out)
    save(gate_in, gate_in_out)
    save(gate_dec, gate_dec_out)
    save(states, states_out)
    save(mixed, mixed_out)
    gate_g.relay_two()
    scatters[1].step(1)
    norm_step(0)
    up_g.relay()
    down_g.start()
    scatters[1].step(2)
    up_g.relay_two()
    twos[0].step(1)
    norm_step(1)
    twos[0].step(2)
    gate_g.relay_last()
    twos[1].step(1)
    for line in cots:
        line.step(1)
    twos[1].step(2)
    for line in cots:
        line.step(2)
    up_g.relay_last()
    panels = down_full.shape[1] // PANEL

    kinds = ((gate_full, gate_pre_out), (up_full, lift_pre_out))
    order = [(s, p, i) for s in range(seqs) for p in range(panels) for i in range(2)]

    def load_panel(at):
        _, p, i = order[at]
        columns = pl.ds(p * PANEL, PANEL)
        copy = pltpu.make_async_copy(
            kinds[i][0].at[:, columns], panel_w.at[at % 2], panel_sem.at[at % 2]
        )
        copy.start()
        return copy

    results = [[], []]

    def store(src, out, s, p, i):
        columns = pl.ds(p * PANEL, PANEL)
        copy = pltpu.make_async_copy(src, out.at[spans[s], columns], product_sem.at[3 * s + i])
        copy.start()
        results[s].append(copy)

    def multiply(s, p):
        nonlocal loaded
        while results[s]:
            results[s].pop().wait()
        for i, (_, out) in enumerate(kinds):
            at = (s * panels + p) * 2 + i
            loaded.wait()
            if at + 1 < len(order):
                loaded = load_panel(at + 1)
            product[i, spans[s], :] = contract(normed_two[spans[s], :], panel_w[at % 2], (1, 0))
            store(product.at[i, spans[s]], out, s, p, i)

        @pl.loop(0, length // STRIP)
        def _(k):
            rows = pl.ds(pl.multiple_of(s * length + k * STRIP, STRIP), STRIP)
            hidden[rows, :] = (gelu(product[0, rows, :]) * product[1, rows, :]).astype(BF16)

        store(hidden.at[spans[s]], hidden_out, s, p, 2)

    gate_g.arrive()
    loaded = load_panel(0)
    up_g.arrive()
    twos[0].finish()
    multiply(0, 0)
    down_g.relay()
    multiply(0, 1)
    multiply(0, 2)
    down_g.relay_two()
    twos[1].finish()
    multiply(1, 0)
    multiply(1, 1)
    multiply(1, 2)
    save(normed_two, normed_two_out)
    for line in cots:
        line.finish()
    save(cot, cot_out)
    down_g.relay_last()
    down_g.arrive()

    for s in range(seqs):

        @pl.when(even)
        def _():
            rim(s, t + 1, width - half, 0).wait_send()

        @pl.when(odd)
        def _():
            rim(s, t - 1, 0, width).wait_send()

    for g in gathers:
        g.end()
    for line in firsts + cots + twos + scatters:
        line.end()
    for copy in saves + results[0] + results[1]:
        copy.wait()


def front_phase(cotangent, token_weight, weights, taps, rate, act, gain, first_gain, depth):
    seqs, rows, model = act.shape
    length = rows * depth
    tokens = seqs * length
    n = len(weights)
    block, width = weights[2].shape[0] * 8, weights[0].shape[1]
    units = weights[-1].shape[1]
    wide = block // 2 + width
    wide_rows = (seqs, length, model)
    mixers = [(model, width), (model, width), (block, width), (block, width), (model, width)]
    saved = [
        ((tokens, width), F32),
        ((seqs, length + 8, width), F32),
        ((tokens, wide), BF16),
        ((tokens, width), F32),
        ((tokens, width), F32),
        ((tokens + 8, width), F32),
        ((tokens, width), BF16),
    ]
    outs = [shaped(act.shape, F32, VMEM)]
    outs += [shaped(wide_rows, BF16, ANY)] + [shaped((tokens, model), BF16, ANY)] * 2
    outs += [shaped(shape, BF16, ANY) for shape in mixers]
    outs += [shaped((model, units), BF16, ANY)] * 3
    outs += [shaped(shape, dtype, ANY) for shape, dtype in saved]
    outs += [shaped((tokens, units), F32, ANY)] * 2 + [shaped((tokens, units), BF16, ANY)]
    saved_scratch = saved[:2] + [((tokens, width), BF16)] + saved[2:5] + [((tokens, width), F32)]
    saved_scratch += saved[5:] + [(wide_rows, BF16)]
    scratch = [pltpu.VMEM(wide_rows, BF16)]
    scratch += [pltpu.VMEM(shape, BF16) for shape in mixers]
    scratch += [pltpu.VMEM(shape, dtype) for shape, dtype in saved_scratch]
    scratch += gather_scratch(n) + line_gather_scratch(depth) * 6 + [DMA((seqs,)), DMA((seqs,)), DMA((16,))]
    scratch += [
        pltpu.VMEM((tokens, model), BF16),
        pltpu.VMEM((tokens, model), BF16),
        pltpu.VMEM(act.shape, BF16),
        pltpu.VMEM((2, model, PANEL), BF16),
        pltpu.VMEM((2, tokens, PANEL), F32),
        DMA((2,)),
        DMA((6,)),
    ]
    scratch += line_scatter_scratch(seqs, rows, model, depth)
    scratch += [pltpu.VMEM(act.shape, BF16)] * 2 + [pltpu.VMEM((tokens, PANEL), BF16)]
    res = call(
        functools.partial(front_kernel, depth),
        "front_phase",
        0,
        [VMEM] * (7 + n),
        outs,
        scratch,
        (cotangent, token_weight)
        + tuple(weights)
        + (taps, rate, act, gain, first_gain),
    )
    return res[0], res[1:4], res[4:9], res[9:12], res[12:19], res[19:]


def norm_back(value, gain, error):
    inverse = lax.rsqrt(jnp.mean(value * value, axis=-1, keepdims=True) + EPS)
    scaled = error * gain
    mean = jnp.mean(scaled * value, axis=-1, keepdims=True)
    grad = inverse * scaled - value * (inverse * inverse * inverse * mean)
    return grad, jnp.sum(error * value * inverse, axis=0, keepdims=True)


def feed_kernel(
    depth,
    normed_in,
    cot_in,
    gate_in,
    up_in,
    down_in,
    gate_pre_in,
    lift_pre_in,
    hidden_in,
    middle,
    gain,
    cotangent,
    token_weight,
    grad,
    wide,
    gain_grad,
    feed_out,
    lift_rows_out,
    output_first,
    down_out,
    gate_out,
    *refs,
):
    panels = gate_in.shape[1] // PANEL
    outs = [
        out.at[:, pl.ds(p * PANEL, PANEL)] for out in (down_out, gate_out) for p in range(panels)
    ]
    normed, cot, hidden, gate_rows, lift_rows = refs[:5]
    gate_w, up_w, down_w, gate_pre, lift_pre, grad_hidden, acc, part, block, feed_part = refs[5:15]
    got, ssem, rsem = refs[15:18]
    load_sem, weight_sem, save_sem = refs[18:21]
    lines = refs[21:24], refs[24:27]
    feed_got, feed_ssem, feed_rsem = refs[27:30]
    d, t = place()
    greet(d, t, depth)
    seqs = middle.shape[0]
    tokens, model = normed_in.shape
    length = tokens // seqs
    tile = 512
    ring = PanelRing(outs, refs[30:], d, t)
    scatters = [LineScatter(part, got, ssem, rsem, d, t, depth, (s,)) for s in range(seqs)]
    early_feed = LineScatter(feed_part, feed_got, feed_ssem, feed_rsem, d, t, depth, (0,), 0)
    gathers = [
        LineGather(block.at[s], wide.at[s], *lines[s], d, t, depth) for s in range(seqs)
    ]

    def load(i, src, dst):
        copy = pltpu.make_async_copy(src, dst, load_sem.at[i])
        copy.start()
        return copy

    def weight(i, src, dst, p):
        copy = pltpu.make_async_copy(
            src.at[:, pl.ds(p * PANEL, PANEL)], dst, weight_sem.at[i]
        )
        copy.start()
        return copy

    def held_rows(s, p):
        rows, columns = pl.ds(s * length, length), pl.ds(p * PANEL, PANEL)
        q = (s * panels + p) % 2
        return [
            load(2 + q, gate_pre_in.at[rows, columns], gate_pre.at[q]),
            load(4 + q, lift_pre_in.at[rows, columns], lift_pre.at[q]),
        ]

    hidden_load = load(6, hidden_in, hidden)
    cot_load = load(1, cot_in, cot)
    down_loads = [weight(p, down_in, w, p) for p, w in enumerate((gate_w, up_w, down_w))]
    row_loads = held_rows(0, 0)
    normed_load = load(0, normed_in, normed)

    def forward(s, p, more):
        nonlocal down_load, gate_load, up_load, row_loads
        rows = pl.ds(s * length, length)
        columns = pl.ds(p * PANEL, PANEL)
        q = (s * panels + p) % 2
        down_load.wait()
        grad_hidden[...] = contract(cot[rows, :], down_w[...], (1, 0))
        for copy in row_loads:
            copy.wait()
        if more is not None:
            down_load = weight(2, down_in, down_w, more)
            row_loads = held_rows(*((s, more) if more > p else (s + 1, more)))

        @pl.loop(0, length // STRIP)
        def _(i):
            strip = rows_of(i, STRIP)
            held = pl.ds(pl.multiple_of(s * length + i * STRIP, STRIP), STRIP)
            act, slope = gelu_both(gate_pre[q, strip, :])
            lift = lift_pre[q, strip, :]
            came = grad_hidden[strip, :]
            gate_rows[held, columns] = (came * lift * slope).astype(BF16)
            lift_rows[held, columns] = (came * act).astype(BF16)

        gate_load.wait()
        up_load.wait()

        @pl.loop(0, model // tile)
        def _(i):
            out = rows_of(i, tile)
            value = contract(gate_rows[rows, columns], gate_w[out, :], (1, 1))
            value = value + contract(lift_rows[rows, columns], up_w[out, :], (1, 1))
            if p == 0:
                acc[:, out] = value
            elif p < panels - 1:
                acc[:, out] += value
            else:
                part[s, :, out] = (acc[:, out] + value).astype(BF16)

        if more is not None:
            gate_load = weight(0, gate_in, gate_w, more)
            up_load = weight(1, up_in, up_w, more)

    kinds = ((cot, hidden), (normed, gate_rows), (normed, lift_rows))

    def weight_grad(i, out):
        left, right = kinds[i // panels]
        columns = pl.ds(i % panels * PANEL, PANEL)

        @pl.loop(0, model // tile)
        def _(k):
            rows = rows_of(k, tile)
            out[rows, :] = contract(left[:, rows], right[:, columns], (0, 0)).astype(BF16)

    def begin(i):
        panel = ring.panels[i]
        weight_grad(i, panel.grad)
        panel.start()

    def push(i):
        ring.panels[i].first()
        ring.panels[i].second()

    def norm_step(s):
        scatters[s].total([grad.at[i] for i in range(seqs)])
        change, gain_part = norm_back(middle[s], gain[...][None], grad[s])
        change = change + cotangent[s].astype(F32) * token_weight[s]
        grad[s] = change
        block[s] = change.astype(BF16)
        if s == 0:
            gain_grad[...] = gain_part
        else:
            gain_grad[...] += gain_part

    def feed(s, out):
        rows = pl.ds(s * length, length)
        downs = (gate_w, up_w, down_w)

        @pl.loop(0, model // tile)
        def _(i):
            columns = rows_of(i, tile)
            value = contract(hidden[rows, 0:PANEL], downs[0][columns, :], (1, 1))
            for p in range(1, panels):
                units = pl.ds(p * PANEL, PANEL)
                value = value + contract(hidden[rows, units], downs[p][columns, :], (1, 1))
            out[:, columns] = value.astype(BF16)

    saves = []

    def save(i, src, dst):
        copy = pltpu.make_async_copy(src, dst, save_sem.at[i])
        copy.start()
        saves.append(copy)

    hidden_load.wait()
    cot_load.wait()
    begin(0)
    for copy in down_loads:
        copy.wait()
    feed(0, feed_part)
    early_feed.start()
    down_load = weight(2, down_in, down_w, 0)
    gate_load = weight(0, gate_in, gate_w, 0)
    up_load = weight(1, up_in, up_w, 0)
    push(0)
    forward(0, 0, 1)
    begin(1)
    early_feed.step(1)
    forward(0, 1, 2)
    early_feed.step(2)
    ring.panels[0].third()
    push(1)
    forward(0, 2, 0)
    scatters[0].start()
    forward(1, 0, 1)
    scatters[0].step(1)
    ring.panels[0].end()
    ring.panels[1].third()
    begin(2)
    scatters[0].step(2)
    forward(1, 1, 2)
    push(2)
    norm_step(0)
    gathers[0].step(0)
    forward(1, 2, None)
    down_loads = [weight(0, down_in, gate_w, 0), weight(1, down_in, up_w, 1)]
    down_loads.append(weight(2, down_in, down_w, 2))
    scatters[1].start()
    save(2, lift_rows, lift_rows_out)
    gathers[0].step(1)
    ring.panels[1].end()
    ring.panels[2].third()
    normed_load.wait()
    begin(3)
    scatters[1].step(1)
    gathers[0].step(2)
    push(3)
    begin(4)
    scatters[1].step(2)
    ring.panels[2].end()
    ring.panels[3].third()
    for copy in down_loads:
        copy.wait()
    feed(1, cot.at[pl.ds(length, length)])
    save(1, cot.at[pl.ds(length, length)], feed_out)
    push(4)
    norm_step(1)
    gathers[1].step(0)
    ring.panels[3].end()
    begin(5)
    ring.panels[4].third()
    total = acc.at[pl.ds(0, middle.shape[1])]
    early_feed.total([total])
    output_first[...] = (total[...] + middle[0]).astype(BF16)
    gathers[1].step(1)
    push(5)
    ring.panels[4].end()
    gathers[1].step(2)
    ring.panels[5].third()
    for line in gathers:
        line.finish()
    ring.panels[5].end()
    ring.end()
    for copy in saves:
        copy.wait()
    for line in scatters + gathers + [early_feed]:
        line.end()


def feed_phase(normed, cot, weights, held, middle, gain, cotangent, token_weight, depth):
    gate_w, up_w, down_w = weights
    seqs, rows, model = middle.shape
    tokens = normed.shape[0]
    length = tokens // seqs
    wide_rows = (seqs, length, model)
    units = gate_w.shape[1]
    outs = [
        shaped(middle.shape, F32, VMEM),
        shaped(wide_rows, BF16, ANY),
        shaped((1, model), F32, VMEM),
        shaped((length, model), BF16, ANY),
        shaped((tokens, units), BF16, ANY),
        shaped(middle.shape[1:], BF16, VMEM),
    ] + [shaped((model // 8, units), F32, ANY)] * 2
    scratch = [pltpu.VMEM((tokens, model), BF16)] * 2
    scratch += [pltpu.VMEM((tokens, units), BF16)] * 3
    scratch += [pltpu.VMEM((model, PANEL), BF16)] * 3
    scratch += [pltpu.VMEM((2, length, PANEL), F32)] * 2 + [pltpu.VMEM((length, PANEL), F32)]
    scratch += [
        pltpu.VMEM((length, model), F32),
        pltpu.VMEM(wide_rows, BF16),
        pltpu.VMEM(middle.shape, BF16),
        pltpu.VMEM((length, model), BF16),
    ]
    scratch += line_scatter_scratch(seqs, rows, model, depth)
    scratch += [DMA((7,)), DMA((3,)), DMA((3,))]
    scratch += line_gather_scratch(depth) * 2
    scratch += line_scatter_scratch(1, rows, model, depth)
    scratch += ring_scratch(3, model // 8, PANEL)
    return call(
        functools.partial(feed_kernel, depth),
        "feed_phase",
        2,
        [ANY] * 8 + [VMEM] * 4,
        outs,
        scratch,
        (normed, cot, gate_w, up_w, down_w) + tuple(held) + (middle, gain, cotangent, token_weight),
        vmem=63 * 1024 * 1024,
    )


def mixer_back_kernel(
    depth,
    branch_in,
    normed_in,
    out_w_in,
    gelu_pre_in,
    input_pre_in,
    window_in,
    gate_in_in,
    gate_dec_in,
    states_in,
    mixed_in,
    gelu_w_in,
    input_w_in,
    gate_in_w_in,
    gate_dec_w_in,
    normed_two_in,
    lift_rows_in,
    feed_in,
    middle_in,
    taps,
    rate,
    act,
    gain,
    grad_middle,
    mlp_part,
    output_first,
    *refs,
):
    output, input_grad, norm_grad, mlp_grad, rate_grad, taps_grad = refs[:6]
    gate_in_out, gate_dec_out, out_out, gelu_out, input_out, up_out = refs[6:12]
    scratch = refs[12:]
    panels = up_out.shape[1] // PANEL
    ups = [up_out.at[:, pl.ds(p * PANEL, PANEL)] for p in range(panels)]
    branch, weight, input_w = scratch[:3]
    gelu_pre, input_pre, window, gate_in, gate_dec, states, gate_in_w, gate_dec_w = scratch[3:11]
    grad, decay, gelu_grad, grad_in, grad_dec = scratch[11:16]
    input_rows = grad_in
    grad_conv = [decay.at[pl.ds(s * (decay.shape[0] // 2), decay.shape[0] // 2)] for s in range(2)]
    rim_out, rim_in, gate_in_grad, gate_dec_grad, part, sums = scratch[16 : 22]
    panel_sem = scratch[22]
    got, ssem, rsem = scratch[23 : 26]
    rim_send, rim_recv, load_sem, feed_sem = scratch[26 : 30]
    small, small_all, pack, packs, line_pack, line_packs = scratch[30 : 36]
    psend, precv, qsend, qrecv, zsend, zrecv = scratch[36 : 42]
    d, t = place()
    ring = PanelRing([out_out] + ups + [gelu_out, input_out], scratch[42 : 51], d, t)
    feed, lift_rows, feed_got, feed_ssem, feed_rsem = scratch[51 : 56]
    parity = lax.rem(t, 2)
    even = parity == 0
    odd = parity == 1
    greet(d, t, depth, dp_masks=(1, 2, 3, 4, 5, 6, 7), z_all=True)
    seqs, length, model = branch_in.shape
    tokens = seqs * length
    width = gate_in.shape[1]
    block = gate_in_w.shape[0]
    half = block // 2
    even_blocks, odd_blocks = gate_blocks(0, width, block), gate_blocks(1, width, block)
    gate_scatters = make_scatters(
        (gate_in_grad, gate_dec_grad),
        (gate_in_out, gate_dec_out),
        (False, False),
        scratch[56:],
        d,
        t,
    )
    feed_line = LineScatter(feed, feed_got, feed_ssem, feed_rsem, d, t, depth, (0,), 0)
    lines = [
        LineScatter(part, got, ssem, rsem, d, t, depth, (s,), s * length) for s in range(seqs)
    ]

    def load(i, src, dst):
        copy = pltpu.make_async_copy(src, dst, load_sem.at[i])
        copy.start()
        return copy

    def load_wide(i, src, dst):
        spans = [pl.ds(s * length, length) for s in range(seqs)]
        return [
            load(i + s, src.at[s] if len(src.shape) == 3 else src.at[rows], dst.at[rows])
            for s, rows in enumerate(spans)
        ]

    early = [load(0, out_w_in, weight)] + load_wide(12, branch_in, branch)
    next_ = [
        load(2, gelu_pre_in, gelu_pre),
        load(3, states_in, states),
        load(4, gate_dec_in, gate_dec),
    ]
    feed_load = pltpu.make_async_copy(feed_in, feed, feed_sem)
    feed_load.start()

    def dp_copies(src, dst, send, recv):
        return [
            pltpu.make_async_remote_copy(
                src_ref=src,
                dst_ref=dst.at[d],
                send_sem=send.at[mask - 1],
                recv_sem=recv.at[mask - 1],
                device_id=(d ^ mask, t),
                device_id_type=MESH,
            )
            for mask in range(1, 8)
        ]

    def weight_grad(left, right, out):
        panel = 512

        @pl.loop(0, model // panel)
        def _(i):
            columns = rows_of(i, panel)
            out[columns, :] = contract(left[:, columns], right[...], (0, 0)).astype(BF16)

    def begin(i, left, right):
        weight_grad(left, right, ring.panels[i].grad)
        ring.panels[i].start()

    def push(i):
        ring.panels[i].first()
        ring.panels[i].second()

    def load_lift(p):
        copy = pltpu.make_async_copy(
            lift_rows_in.at[:, pl.ds(p * PANEL, PANEL)], lift_rows, panel_sem
        )
        copy.start()
        return copy

    mixed_load = load(1, mixed_in, lift_rows)
    two_loads = load_wide(12 + seqs, normed_two_in, part)
    then = [
        load(5, gate_in_in, gate_in),
        load(7, window_in, window),
        load(8, gate_in_w_in, gate_in_w),
        load(9, gate_dec_w_in, gate_dec_w),
        load(10, input_pre_in, input_pre),
        load(11, input_w_in, input_w),
    ]
    for copy in early:
        copy.wait()
    feed_load.wait()
    feed_line.start()
    mixed_load.wait()
    begin(0, branch, lift_rows)
    lift_load = load_lift(0)
    for s in range(seqs):
        rows = pl.ds(s * length, length)
        grad[rows, :] = contract(branch[rows, :], weight[...], (1, 0))
    reload = load(0, gelu_w_in, weight)
    wide_loads = load_wide(12, normed_in, branch)
    push(0)
    for copy in two_loads:
        copy.wait()
    lift_load.wait()
    begin(1, part, lift_rows)
    lift_load = load_lift(1)
    for copy in next_:
        copy.wait()

    @pl.loop(0, tokens // STRIP)
    def _(i):
        rows = rows_of(i, STRIP)
        held = pl.ds(pl.multiple_of(i * STRIP + 8, 8), STRIP)
        act, slope = gelu_both(gelu_pre[rows, :])
        came = grad[rows, :]
        gelu_grad[rows, :] = (came * states[held, :] * slope).astype(BF16)
        grad[rows, :] = came * act
        decay[rows, :] = jnp.exp(-8.0 * sigmoid(gate_dec[rows, :]) * rate[...][None])

    decay[tokens : tokens + 8, :] = jnp.zeros((8, width), F32)
    push(1)
    ring.panels[0].third()
    feed_line.step(1)
    lift_load.wait()
    begin(2, part, lift_rows)
    lift_load = load_lift(2)
    scan_rows(decay, grad, range(seqs), length, backward=True)
    feed_line.step(2)
    push(2)
    for copy in then:
        copy.wait()
    sums[...] = jnp.zeros(sums.shape, F32)

    def fold(value):
        return value[0:8] + value[8:16]

    own_columns = pl.ds(pl.multiple_of(parity * half, half), width)
    first_row = lax.broadcasted_iota(jnp.int32, (STRIP, width), 0) == 0
    for s in range(seqs):

        @pl.loop(0, length // STRIP)
        def _(i):
            start = pl.multiple_of(s * length + i * STRIP, STRIP)
            rows = pl.ds(start, STRIP)
            earlier = pltpu.roll(states[pl.ds(start, STRIP + 8), :], 1, 0)[8:]
            earlier = jnp.where(first_row & (i == 0), 0.0, earlier)
            came = grad[rows, :]
            open_in = sigmoid(gate_in[rows, :])
            open_dec = sigmoid(gate_dec[rows, :])
            slow = -8.0 * rate[...][None]
            lost = one_less_exp(2.0 * open_dec * slow)
            root = jnp.sqrt(lost)
            value = window[rows, own_columns].astype(F32)
            step = jnp.exp(open_dec * slow)
            through = came * open_in
            grad_log = step * (came * earlier - through * value * step / root)
            sums[0] += fold(grad_log * (-8.0 * open_dec))
            through = through * root
            grad_conv[s][pl.ds(pl.multiple_of(i * STRIP, STRIP), STRIP), :] = through
            grad_in[rows, :] = (through * value * (1.0 - open_in)).astype(BF16)
            grad_dec[rows, :] = (grad_log * slow * open_dec * (1.0 - open_dec)).astype(BF16)

        grad_conv[s][length : length + 8, :] = jnp.zeros((8, width), F32)

    ring.panels[0].end()
    ring.panels[1].third()

    def gates_back(k, low, high):
        return contract(grad_in[:, low:high], gate_in_w[:, low:high], (1, 1)) + contract(
            grad_dec[:, low:high], gate_dec_w[:, low:high], (1, 1)
        )

    def add_conv(low, high, value):
        for s in range(seqs):
            grad_conv[s][0:length, low:high] += value[s * length : (s + 1) * length]

    def rim(to):
        return pltpu.make_async_remote_copy(
            src_ref=rim_out,
            dst_ref=rim_in,
            send_sem=rim_send,
            recv_sem=rim_recv,
            device_id=(d, to),
            device_id_type=MESH,
        )

    @pl.when(even)
    def _():
        value = gates_back(*even_blocks[-1])
        rim_out[...] = value[:, half:].astype(BF16)
        rim(t + 1).start()
        add_conv(width - half, width, value[:, :half])

    @pl.when(odd)
    def _():
        value = gates_back(*odd_blocks[0])
        rim_out[...] = value[:, :half].astype(BF16)
        rim(t - 1).start()
        add_conv(0, half, value[:, half:])

    lift_load.wait()
    begin(3, part, lift_rows)

    def inner(blocks):
        for k, low, high in blocks:
            add_conv(low, high, gates_back(k, low, high))

    def gate_grads(blocks):
        for k, low, high in blocks:
            near = window[:, k * block : (k + 1) * block]
            gate_in_grad[:, low:high] = contract(near, grad_in[:, low:high], (0, 0)).astype(BF16)
            gate_dec_grad[:, low:high] = contract(near, grad_dec[:, low:high], (0, 0)).astype(BF16)

    @pl.when(even)
    def _():
        inner(even_blocks[:-1])
        gate_grads(even_blocks)

    @pl.when(odd)
    def _():
        inner(odd_blocks[1:])
        gate_grads(odd_blocks)

    for g in gate_scatters:
        g.start()
    ring.panels[1].end()
    ring.panels[2].third()
    push(3)

    @pl.when(even)
    def _():
        rim(t + 1).wait()
        add_conv(width - half, width, rim_in[...].astype(F32))

    @pl.when(odd)
    def _():
        rim(t - 1).wait()
        add_conv(0, half, rim_in[...].astype(F32))

    for s in range(seqs):

        @pl.loop(0, length // STRIP)
        def _(i):
            near = pl.ds(pl.multiple_of(i * STRIP, STRIP), STRIP + 8)
            later = grad_conv[s][near, :]
            before = input_pre[s, near, :]
            here = later[:STRIP]
            value = taps[0:1, :] * here
            sums[1] += fold(here * before[8:])
            for k in range(1, taps.shape[0]):
                value = value + taps[k : k + 1, :] * pltpu.roll(later, STRIP + 8 - k, 0)[:STRIP]
                sums[1 + k] += fold(here * pltpu.roll(before, k, 0)[8:])
            rows = pl.ds(pl.multiple_of(s * length + i * STRIP, STRIP), STRIP)
            input_rows[rows, :] = value.astype(BF16)

    for k in range(sums.shape[0]):
        small[k : k + 1, :] = jnp.sum(sums[k], axis=0, keepdims=True)
    small[sums.shape[0] :, :] = jnp.zeros((8 - sums.shape[0], width), F32)
    small_copies = dp_copies(small, small_all, qsend, qrecv)
    for c in small_copies:
        c.start()
    small_all[d] = small[...]
    reload.wait()
    panel = 512
    for s in range(seqs):
        rows = pl.ds(s * length, length)

        @pl.loop(0, weight.shape[0] // panel)
        def _(i):
            columns = rows_of(i, panel)
            value = contract(gelu_grad[rows, :], weight[columns, :], (1, 1))
            value = value + contract(input_rows[rows, :], input_w[columns, :], (1, 1))
            part[rows, columns] = value.astype(BF16)

        lines[s].start()

    middle_load = load(0, middle_in.at[1], input_grad.at[1])
    ring.panels[2].end()
    ring.panels[3].third()
    for copy in wide_loads:
        copy.wait()
    begin(4, branch, gelu_grad)
    for g in gate_scatters:
        g.first()
        g.second()
    push(4)
    lines[0].step(1)
    begin(5, branch, input_rows)
    lines[0].step(2)
    ring.panels[3].end()
    ring.panels[4].third()
    push(5)
    for g in gate_scatters:
        g.third()
    middle_load.wait()
    feed_line.total([input_grad.at[1]], more=True)
    output[0] = output_first[...]
    output[1] = input_grad[1].astype(BF16)
    lines[1].step(1)
    ring.panels[4].end()
    ring.panels[5].third()
    lines[1].step(2)
    for g in gate_scatters:
        g.end()
    quarter = pack.shape[1]
    for i in range(4):
        pack[4 + i : 5 + i, :] = mlp_part[:, i * quarter : (i + 1) * quarter]
    for s in range(seqs):
        lines[s].total([input_grad.at[i] for i in range(seqs)])
        change, gain_part = norm_back(act[s].astype(F32), gain[...][None], input_grad[s])
        input_grad[s] = change + grad_middle[s]
        for i in range(4):
            piece = gain_part[:, i * quarter : (i + 1) * quarter]
            if s == 0:
                pack[i : i + 1, :] = piece
            else:
                pack[i : i + 1, :] += piece
    pack_copies = dp_copies(pack, packs, psend, precv)
    for c in pack_copies:
        c.start()
    packs[d] = pack[...]
    for c in small_copies:
        c.wait_recv()
    sum_ = small_all[0]
    for i in range(1, 8):
        sum_ = sum_ + small_all[i]
    rate_grad[...] = sum_[0]
    taps_grad[...] = sum_[1:5]
    for c in pack_copies:
        c.wait_recv()
    sum_ = packs[0]
    for i in range(1, 8):
        sum_ = sum_ + packs[i]
    line_pack[...] = sum_
    z_copies = [
        pltpu.make_async_remote_copy(
            src_ref=line_pack,
            dst_ref=line_packs.at[t],
            send_sem=zsend.at[step - 1],
            recv_sem=zrecv.at[step - 1],
            device_id=(d, lax.rem(t + step, depth)),
            device_id_type=MESH,
        )
        for step in range(1, depth)
    ]
    for c in z_copies:
        c.start()
    line_packs[t] = sum_
    ring.panels[5].end()
    for c in z_copies:
        c.wait_recv()
    sum_ = line_packs[0]
    for i in range(1, depth):
        sum_ = sum_ + line_packs[i]
    for i in range(4):
        norm_grad[i * quarter : (i + 1) * quarter] = sum_[i]
        mlp_grad[i * quarter : (i + 1) * quarter] = sum_[4 + i]
    for c in small_copies + pack_copies + z_copies:
        c.wait_send()
    ring.end()
    for line in lines + [feed_line]:
        line.end()


def mixer_back_phase(
    branch, normed, saved, weights, normed_two, lift_rows, feed, middle, taps, rate, act, gain,
    grad_middle, mlp_part, output_first, depth,
):
    seqs, length, model = branch.shape
    tokens = seqs * length
    units = lift_rows.shape[1]
    gelu_w, input_w, gate_in_w, gate_dec_w, out_w = weights[:5]
    gelu_pre, input_pre, window, gate_in, gate_dec, states, mixed = saved
    width = out_w.shape[1]
    block = gate_in_w.shape[0]
    half = block // 2
    panel = (model // 8, PANEL)
    gate = (block // 8, width)
    pack = (8, model // 4)
    small = (8, width)
    flat = (tokens, width)
    outs = [
        shaped(act.shape, BF16, VMEM),
        shaped(act.shape, F32, VMEM),
        shaped((model,), F32, VMEM),
        shaped((model,), F32, VMEM),
        shaped((width,), F32, VMEM),
        shaped(taps.shape, F32, VMEM),
        shaped(gate, F32, VMEM),
        shaped(gate, F32, VMEM),
    ]
    outs += [shaped(panel, F32, ANY)] * 3 + [shaped((model // 8, units), F32, ANY)]
    scratch = [pltpu.VMEM((tokens, model), BF16)]
    scratch += [
        pltpu.VMEM(x.shape, x.dtype)
        for x in (
            out_w,
            input_w,
            gelu_pre,
            input_pre,
            window,
            gate_in,
            gate_dec,
            states,
            gate_in_w,
            gate_dec_w,
        )
    ]
    scratch += [pltpu.VMEM(flat, F32), pltpu.VMEM((seqs * (length + 8), width), F32)]
    scratch += [pltpu.VMEM(flat, BF16)] * 3
    scratch += [pltpu.VMEM((tokens, half), BF16)] * 2
    scratch += [pltpu.VMEM(gate_in_w.shape, BF16)] * 2
    scratch += [
        pltpu.VMEM((tokens, model), BF16),
        pltpu.VMEM((1 + taps.shape[0], 8, width), F32),
        DMA,
    ]
    scratch += line_scatter_scratch(seqs, length // depth, model, depth)
    scratch += [DMA, DMA, DMA((12 + 2 * seqs,)), DMA]
    scratch += [
        pltpu.VMEM(small, F32),
        pltpu.VMEM((8,) + small, F32),
        pltpu.VMEM(pack, F32),
        pltpu.VMEM((8,) + pack, F32),
        pltpu.VMEM(pack, F32),
        pltpu.VMEM((depth,) + pack, F32),
    ]
    scratch += [DMA((7,))] * 4 + [DMA((depth - 1,))] * 2
    scratch += ring_scratch(3, *panel)
    scratch += [pltpu.VMEM((length, model), BF16), pltpu.VMEM((tokens, PANEL), BF16)]
    scratch += line_scatter_scratch(1, length // depth, model, depth)
    scratch += scatter_scratch([gate] * 2, (False, False))
    return call(
        functools.partial(mixer_back_kernel, depth),
        "mixer_back_phase",
        3,
        [ANY] * 18 + [VMEM] * 7,
        outs,
        scratch,
        (
            branch,
            normed,
            out_w,
            gelu_pre,
            input_pre,
            window,
            gate_in,
            gate_dec,
            states,
            mixed,
            gelu_w,
            input_w,
            gate_in_w,
            gate_dec_w,
            normed_two,
            lift_rows,
            feed,
            middle,
            taps,
            rate,
            act,
            gain,
            grad_middle,
            mlp_part,
            output_first,
        ),
        vmem=63 * 1024 * 1024,
    )


def finish_kernel(*refs):
    n = (len(refs) - 2) // 3
    ins, outs, held = refs[:n], refs[n : 2 * n], refs[2 * n : 3 * n]
    load_sem, save_sem = refs[3 * n :]
    loads = [pltpu.make_async_copy(ins[i], held[i], load_sem.at[i]) for i in range(n)]
    saves = [pltpu.make_async_copy(held[i], outs[i], save_sem.at[i]) for i in range(n)]
    for copy in loads:
        copy.start()
    for load, save in zip(loads, saves):
        load.wait()
        save.start()
    for save in saves:
        save.wait()


def finish(arrays):
    n = len(arrays)
    return pl.pallas_call(
        finish_kernel,
        name="finish",
        out_shape=[jax.ShapeDtypeStruct(x.shape, x.dtype) for x in arrays],
        in_specs=[ANY] * n,
        out_specs=[ANY] * n,
        scratch_shapes=[pltpu.VMEM(x.shape, x.dtype) for x in arrays] + [DMA((n,))] * 2,
        compiler_params=pltpu.CompilerParams(vmem_limit_bytes=62 * 1024 * 1024),
    )(*arrays)


def swapped(block, axis):
    count = lax.axis_size(axis)
    return lax.ppermute(block, axis, [(i, i ^ 1) for i in range(count)])


def normalize(value_entries, scale_gain):
    return (
        value_entries
        * lax.rsqrt(jnp.mean(value_entries * value_entries, axis=-1, keepdims=True) + EPS)
        * scale_gain
    )


def causal_conv(value_entries, kernel):
    summed = value_entries * kernel[0]
    for offset in range(1, kernel.shape[0]):
        shifted = jnp.concatenate(
            [jnp.zeros_like(value_entries[:, :offset]), value_entries[:, :-offset]], axis=1
        )
        summed = summed + shifted * kernel[offset]
    return summed


def decay_inputs(input_pre, decay_pre, conv_vals, decay_rate):
    log_decay = -8.0 * jax.nn.sigmoid(decay_pre) * decay_rate
    scaled = jnp.sqrt(-jnp.expm1(2.0 * log_decay))
    return (log_decay, scaled * jax.nn.sigmoid(input_pre) * conv_vals)


def recurrence(rate, drive):
    def join(left, right):
        return left[0] * right[0], left[1] * right[0] + right[1]

    return lax.associative_scan(join, (rate, drive), axis=1)[1]


def dot(spec, left, right):
    return jnp.einsum(spec, left, right, preferred_element_type=F32)


def weight_grad(left, right):
    return dot("pkr,pku->ru", left, right).astype(BF16)


class Fast:
    def __init__(self, depth, taps, rate):
        self.depth, self.taps, self.rate = depth, taps, rate

    def front(self, cotangent, token_weight, weights, act, gain, first_gain):
        middle, rows, self.weights, self.feeds, self.saved, self.held = front_phase(
            cotangent, token_weight, weights, self.taps, self.rate, act, gain, first_gain,
            self.depth,
        )
        self.normed, self.cot, self.normed_two = rows
        return middle

    def back(self, middle, gain, cotangent, token_weight, act, first_gain):
        grad_middle, branch, mlp_part, feed, lift_rows, output, down_grad, gate_grad = feed_phase(
            self.normed_two, self.cot, self.feeds, self.held, middle, gain, cotangent,
            token_weight, self.depth,
        )
        res = mixer_back_phase(
            branch, self.normed, self.saved, self.weights, self.normed_two, lift_rows, feed,
            middle, self.taps, self.rate, act, first_gain, grad_middle, mlp_part,
            output, self.depth,
        )
        output, input_grad, norm_grad, mlp_grad, rate_grad, taps_grad = res[:6]
        gate_in, gate_dec, out_grad, gelu_grad, input_w_grad, up_grad = res[6:]
        results = (
            output, input_grad, norm_grad, mlp_grad, rate_grad, taps_grad, gelu_grad, input_w_grad,
            gate_in, gate_dec, out_grad, gate_grad, up_grad, down_grad,
        )
        results = finish(results)
        return tuple(results[:6]) + (tuple(results[6:]),)


class Plain:
    def __init__(self, depth, taps, rate):
        self.depth, self.taps, self.rate = depth, taps, rate

    @staticmethod
    def wide(block):
        return lax.all_gather(block, "tensor", axis=1, tiled=True)

    @staticmethod
    def narrow(part):
        return lax.psum_scatter(part, "tensor", scatter_dimension=1, tiled=True).astype(F32)

    @staticmethod
    def full(shard):
        return lax.all_gather(shard, "dp", axis=0, tiled=True)

    @staticmethod
    def own(grad):
        return lax.psum_scatter(grad, "dp", scatter_dimension=0, tiled=True).astype(F32)

    def front(self, cotangent, token_weight, weights, act, gain, first_gain):
        cot = (cotangent.astype(F32) * token_weight).astype(BF16)
        normed = normalize(act.astype(F32), first_gain).astype(BF16)
        gelu_w, input_w, gate_in_w, gate_dec_w, out_w = (self.full(w) for w in weights[:5])
        self.feeds = tuple(self.full(w) for w in weights[5:])
        normed_all = self.wide(normed)
        seqs, length, _ = normed_all.shape
        channels = gelu_w.shape[1]
        block = gate_in_w.shape[0]
        half = block // 2
        width = channels + half
        parity = lax.axis_index("tensor") % 2
        gelu_pre = dot("kqg,ga->kqa", normed_all, gelu_w)
        input_pre = dot("kqg,ga->kqa", normed_all, input_w)
        gelu_out, gelu_back = jax.vjp(jax.nn.gelu, gelu_pre)
        conv_out, conv_back = jax.vjp(causal_conv, input_pre, self.taps)
        conv_bf = conv_out.astype(BF16)
        rim = lax.dynamic_slice_in_dim(conv_bf, (1 - parity) * (channels - half), half, 2)
        window = jnp.zeros((seqs, length, width), BF16)
        window = lax.dynamic_update_slice_in_dim(window, conv_bf, parity * half, 2)
        window = lax.dynamic_update_slice_in_dim(
            window, swapped(rim, "tensor"), (1 - parity) * channels, 2
        )
        tiles = window.reshape(seqs, length, width // block, block)
        placed = lax.dynamic_update_slice_in_dim(
            jnp.zeros((2, block, width), BF16), jnp.stack([gate_in_w, gate_dec_w]), parity * half, 2
        ).reshape(2, block, width // block, block)
        gates = dot("slbk,gkbc->gslbc", tiles, placed).reshape(2, seqs, length, width)
        gates = lax.dynamic_slice_in_dim(gates, parity * half, channels, 3)
        (log_decay, drive), gate_back = jax.vjp(
            decay_inputs, gates[0], gates[1], conv_bf.astype(F32), self.rate
        )
        decay = jnp.exp(log_decay)
        states = recurrence(decay, drive)
        mixed = (gelu_out * states).astype(BF16)
        self.kept = (
            normed_all, gelu_w, input_w, out_w, gelu_out, gelu_back, conv_back, tiles, placed,
            gate_back, decay, states, mixed,
        )
        part = dot("xgq,pq->xgp", mixed, out_w).astype(BF16)
        self.cot = self.wide(cot)
        middle = act.astype(F32) + self.narrow(part)
        self.normed_two = self.wide(normalize(middle, gain).astype(BF16))
        return middle

    def back(self, middle, gain, cotangent, token_weight, act, first_gain):
        cot_own = cotangent.astype(F32) * token_weight
        gate_w, up_w, down_w = self.feeds
        normed, cot = self.normed_two, self.cot
        gate_pre = dot("nwo,ob->nwb", normed, gate_w)
        lift_pre = dot("nwo,ob->nwb", normed, up_w)
        gate_act, activ_back = jax.vjp(jax.nn.gelu, gate_pre)
        hidden = (gate_act * lift_pre).astype(BF16)
        grad_hidden = dot("gre,eu->gru", cot, down_w)
        gate_grad = activ_back(grad_hidden * lift_pre)[0].astype(BF16)
        lift_grad = (grad_hidden * gate_act).astype(BF16)
        part = dot("mqa,ya->mqy", gate_grad, gate_w) + dot("mqa,ya->mqy", lift_grad, up_w)
        _, back = jax.vjp(normalize, middle, gain)
        change, gain_grad = back(self.narrow(part.astype(BF16)))
        grad = cot_own + change
        panels = (
            weight_grad(cot, hidden), weight_grad(normed, gate_grad), weight_grad(normed, lift_grad)
        )
        feed = dot("xav,tv->xat", hidden, down_w).astype(BF16)
        output = (middle + self.narrow(feed)).astype(BF16)
        branch = self.wide(grad.astype(BF16))
        (
            normed_all, gelu_w, input_w, out_w, gelu_out, gelu_back, conv_back, tiles, placed,
            gate_back, decay, states, mixed,
        ) = self.kept
        seqs, length, channels = states.shape
        block = tiles.shape[-1]
        half = block // 2
        width = channels + half
        parity = lax.axis_index("tensor") % 2
        grad_mixed = dot("xtz,zm->xtm", branch, out_w)
        gelu_grad = gelu_back(grad_mixed * states)[0].astype(BF16)
        later = jnp.concatenate([decay[:, 1:], jnp.zeros_like(decay[:, :1])], axis=1)
        grad_drive = jnp.flip(
            recurrence(jnp.flip(later, 1), jnp.flip(grad_mixed * gelu_out, 1)), 1
        )
        earlier = jnp.concatenate([jnp.zeros_like(states[:, :1]), states[:, :-1]], axis=1)
        grad_in, grad_dec, grad_conv, grad_rate = gate_back(
            (grad_drive * decay * earlier, grad_drive)
        )
        grads = lax.dynamic_update_slice_in_dim(
            jnp.zeros((2, seqs, length, width), BF16),
            jnp.stack([grad_in, grad_dec]).astype(BF16),
            parity * half,
            3,
        ).reshape(2, seqs, length, width // block, block)
        grad_window = dot("gslbc,gkbc->slbk", grads, placed).reshape(seqs, length, width)
        grad_placed = dot("slbk,gslbc->gkbc", tiles, grads).reshape(2, block, width)
        grad_gates = lax.dynamic_slice_in_dim(grad_placed, parity * half, channels, 2)
        rim = lax.dynamic_slice_in_dim(grad_window, (1 - parity) * channels, half, 2)
        rim = swapped(rim.astype(BF16), "tensor").astype(F32)
        grad_conv = grad_conv + lax.dynamic_slice_in_dim(grad_window, parity * half, channels, 2)
        start = (1 - parity) * (channels - half)
        rim = lax.dynamic_slice_in_dim(grad_conv, start, half, 2) + rim
        grad_conv = lax.dynamic_update_slice_in_dim(grad_conv, rim, start, 2)
        input_rows, grad_taps = conv_back(grad_conv)
        input_rows = input_rows.astype(BF16)
        part = dot("mzf,af->mza", gelu_grad, gelu_w) + dot("mzf,af->mza", input_rows, input_w)
        _, back = jax.vjp(normalize, act.astype(F32), first_gain)
        change, norm_grad = back(self.narrow(part.astype(BF16)))
        gains = lax.psum((norm_grad, gain_grad), ("dp", "tensor"))
        small = lax.psum((grad_rate, grad_taps), "dp")
        parts = (
            weight_grad(normed_all, gelu_grad),
            weight_grad(normed_all, input_rows),
            grad_gates[0].astype(BF16),
            grad_gates[1].astype(BF16),
            weight_grad(branch, mixed),
            panels[1],
            panels[2],
            panels[0],
        )
        own = [self.own(g) for g in parts]
        return (output, grad + change) + gains + small + (tuple(own),)


def shards(
    activations,
    norm_gain,
    gelu_proj,
    input_proj,
    conv_weight,
    gate_input,
    gate_decay,
    decay_rate,
    out_proj,
    mlp_gain,
    feed_gate,
    feed_up,
    feed_down,
    cotangent,
    lengths,
    batch_of,
):
    depth = lax.axis_size("tensor")
    fast = lax.axis_size("dp") == 8 and depth == 4
    run = (Fast if fast else Plain)(depth, conv_weight, decay_rate)
    tensor_index = lax.axis_index("tensor")
    data_index = lax.axis_index("dp")
    seq_count, row_count, _ = activations.shape
    full_length = row_count * depth
    members = (batch_of[:, None] == jnp.arange(MICRO)[None, :]).astype(F32)
    counts = jnp.sum(members * lengths[:, None].astype(F32), axis=0)
    total_seqs = lengths.shape[0]
    per_batch = float(total_seqs * full_length) / (MICRO * counts)
    weight_all = jnp.sum(members * per_batch[None, :], axis=1)
    my_weight = lax.dynamic_slice_in_dim(weight_all, data_index * seq_count, seq_count)
    my_length = lax.dynamic_slice_in_dim(lengths, data_index * seq_count, seq_count)
    places = tensor_index * row_count + jnp.arange(row_count)
    valid_mask = (places[None, :] < my_length[:, None]).astype(F32)
    token_weight = (valid_mask * my_weight[:, None])[:, :, None]

    weights = (
        gelu_proj, input_proj, gate_input, gate_decay, out_proj.T, feed_gate, feed_up, feed_down.T
    )
    middle = run.front(cotangent, token_weight, weights, activations, mlp_gain, norm_gain)
    output, input_grad, norm_grad, mlp_grad, rate_grad, taps_grad, grads = run.back(
        middle, mlp_gain, cotangent, token_weight, activations, norm_gain
    )
    return (
        output,
        input_grad,
        norm_grad,
        grads[0],
        grads[1],
        taps_grad,
        grads[2],
        grads[3],
        rate_grad,
        grads[4].T,
        mlp_grad,
        grads[5],
        grads[6],
        grads[7].T,
    )


def solution(mesh):
    placed = (
        P("dp", "tensor", None),
        P(),
        P("dp", "tensor"),
        P("dp", "tensor"),
        P(None, "tensor"),
        P("dp", "tensor"),
        P("dp", "tensor"),
        P("tensor"),
        P("tensor", "dp"),
        P(),
        P("dp", "tensor"),
        P("dp", "tensor"),
        P("tensor", "dp"),
        P("dp", "tensor", None),
        P(),
        P(),
    )
    return jax.shard_map(
        shards,
        mesh=mesh,
        in_specs=placed,
        out_specs=(
            P("dp", "tensor", None),
            P("dp", "tensor", None),
            P(),
            P("dp", "tensor"),
            P("dp", "tensor"),
            P(None, "tensor"),
            P("dp", "tensor"),
            P("dp", "tensor"),
            P("tensor"),
            P("tensor", "dp"),
            P(),
            P("dp", "tensor"),
            P("dp", "tensor"),
            P("tensor", "dp"),
        ),
        check_vma=False,
    )
```

```python
import functools

import jax
import jax.numpy as jnp
from jax import lax
from jax.experimental import pallas as pl
from jax.experimental.pallas import tpu as pltpu
from jax.sharding import PartitionSpec as P

MICRO = 4
EPS = 1e-06
MESH = pl.DeviceIdType.MESH
ANY = pl.BlockSpec(memory_space=pl.ANY)
VMEM = pl.BlockSpec(memory_space=pltpu.VMEM)
DMA = pltpu.SemaphoreType.DMA
BF16 = jnp.bfloat16
F32 = jnp.float32


def place():
    return lax.axis_index("dp"), lax.axis_index("tensor")


def greet(d, t, depth, dp_masks=(1, 2, 4), z_all=False, meanwhile=None):
    barrier = pltpu.get_barrier_semaphore()
    for mask in dp_masks:
        pl.semaphore_signal(barrier, inc=1, device_id=(d ^ mask, t), device_id_type=MESH)
    if z_all:
        for step in range(1, depth):
            pl.semaphore_signal(
                barrier, inc=1, device_id=(d, lax.rem(t + step, depth)), device_id_type=MESH
            )
        if meanwhile is not None:
            meanwhile()
        pl.semaphore_wait(barrier, len(dp_masks) + depth - 1)
        return

    @pl.when(t > 0)
    def _():
        pl.semaphore_signal(barrier, inc=1, device_id=(d, t - 1), device_id_type=MESH)

    @pl.when(t < depth - 1)
    def _():
        pl.semaphore_signal(barrier, inc=1, device_id=(d, t + 1), device_id_type=MESH)

    if meanwhile is not None:
        meanwhile()
    ends = jnp.where((t == 0) | (t == depth - 1), 1, 2)
    pl.semaphore_wait(barrier, len(dp_masks) + ends)


def add_rows(total, *terms, rows, step=32):
    step = min(step, rows)

    @pl.loop(0, rows, step=step)
    def _(start):
        part = pl.ds(pl.multiple_of(start, step), step)
        value = total[part, :].astype(F32)
        for term in terms:
            value = value + term[part, :].astype(F32)
        total[part, :] = value.astype(BF16)


class WeightGather:
    def __init__(self, shard, out, local, send, recv, d, t):
        rows = shard.shape[0]
        half = rows // 2

        def view(slot, start, size):
            if len(out.shape) == 3:
                return out.at[slot, pl.ds(start, size)]
            return out.at[pl.ds(pl.multiple_of(slot * rows + start, 16), size)]

        top, low = (0, half), (half, half)
        plan = [
            (None, d, top, 2),
            (None, d, low, 4),
            (None, d, low, 2),
            (None, d, top, 4),
            (2, d ^ 2, top, 4),
            (4, d ^ 4, low, 2),
            (None, d, top, 1),
            (None, d, low, 1),
            (2, d ^ 2, top, 1),
            (4, d ^ 4, low, 1),
            (2, d ^ 2, low, 1),
            (4, d ^ 4, top, 1),
            (6, d ^ 6, top, 1),
            (6, d ^ 6, low, 1),
        ]
        self.copies = [
            pltpu.make_async_remote_copy(
                src_ref=shard.at[pl.ds(*part)] if came is None else view(slot, *part),
                dst_ref=view(slot, *part),
                send_sem=send.at[i],
                recv_sem=recv.at[i],
                device_id=(d ^ mask, t),
                device_id_type=MESH,
            )
            for i, (came, slot, part, mask) in enumerate(plan)
        ]
        self.own = pltpu.make_async_copy(shard, view(d, 0, rows), local)

    def start(self):
        for i in (0, 1, 2, 3, 6, 7):
            self.copies[i].start()
        self.own.start()

    def relay(self):
        c = self.copies
        c[0].wait_recv()
        c[4].start()
        c[1].wait_recv()
        c[5].start()
        c[8].start()
        c[9].start()

    def relay_two(self):
        c = self.copies
        c[2].wait_recv()
        c[10].start()
        c[3].wait_recv()
        c[11].start()

    def relay_last(self):
        c = self.copies
        c[4].wait_recv()
        c[12].start()
        c[5].wait_recv()
        c[13].start()

    def arrive(self):
        for i in range(6, 14):
            self.copies[i].wait_recv()
        self.own.wait()

    def end(self):
        for i in range(14):
            self.copies[i].wait_send()


def gather_scratch(count):
    return [DMA((count,)), DMA((count, 14)), DMA((count, 14))]


class GradScatter:
    ORDER = (6, 2, 4, 0)

    def __init__(self, grad, out, own, core, diag, last, local, send, recv, d, t):
        self.out, self.core, self.diag, self.last = out, core, diag, last
        self.grad, self.d, self.t = grad, d, t
        self.credit = None
        self.reused = self.again = False
        self.before = self.flush = None
        self.rows = rows = out.shape[0]
        half = rows // 2
        self.half = half
        self.top, self.low = pl.ds(0, half), pl.ds(half, half)

        def block(slot, start=0, size=rows):
            return grad.at[pl.ds(pl.multiple_of(slot * rows + start, 16), size)]

        if own is None:
            self.loads = []
            self.mine = lambda i, start=0, size=rows: block(d ^ self.ORDER[i], start, size)
        else:
            self.loads = [
                pltpu.make_async_copy(block(d ^ r), own.at[i], local.at[i])
                for i, r in enumerate(self.ORDER)
            ]
            self.mine = lambda i, start=0, size=rows: own.at[i, pl.ds(start, size)]
        mine, top, low = self.mine, self.top, self.low
        plan = [(block(d ^ 1 ^ r), core.at[i], 1) for i, r in enumerate(self.ORDER)] + [
            (mine(0, 0, half), diag.at[0], 2),
            (mine(0, half, half), diag.at[1], 4),
            (mine(1, 0, half), last.at[0, top], 2),
            (mine(2, half, half), last.at[1, low], 4),
            (mine(2, 0, half), last.at[1, top], 4),
            (mine(1, half, half), last.at[0, low], 2),
        ]
        self.copies = [
            pltpu.make_async_remote_copy(
                src_ref=src,
                dst_ref=dst,
                send_sem=send.at[i],
                recv_sem=recv.at[i],
                device_id=(d ^ mask, t),
                device_id_type=MESH,
            )
            for i, (src, dst, mask) in enumerate(plan)
        ]

    def start(self):
        if self.reused:
            pl.semaphore_wait(self.credit.at[0], 1)
        for i in range(4):
            self.copies[i].start()
        for load in self.loads:
            load.start()

    def arrive(self, i):
        if self.loads:
            self.loads[i].wait()
        self.copies[i].wait_recv()

    def add(self, i, start, *terms):
        half = pl.ds(start, self.half)
        add_rows(self.mine(i, start, self.half), self.core.at[i, half], *terms, rows=self.half)

    def first(self):
        self.arrive(0)
        for i, start in enumerate((0, self.half)):
            self.add(0, start)
            if self.reused:
                pl.semaphore_wait(self.credit.at[1 + i], 1)
            self.copies[4 + i].start()

    def second(self):
        self.arrive(1)
        self.add(1, 0)
        self.copies[6].start()
        self.arrive(2)
        self.add(2, self.half)
        self.copies[7].start()

    def third(self):
        c = self.copies
        c[4].wait_recv()
        self.add(2, 0, self.diag.at[0])
        c[8].start()
        c[5].wait_recv()
        self.add(1, self.half, self.diag.at[1])
        c[9].start()

    def end(self):
        self.arrive(3)
        for i in (6, 7, 8, 9):
            self.copies[i].wait_recv()
        step = 16
        own = self.mine(3)
        if self.before is not None:
            self.before.flush.wait()

        @pl.loop(0, self.rows, step=step)
        def _(start):
            part = pl.ds(pl.multiple_of(start, step), step)
            self.out[part, :] = (
                own[part, :].astype(F32)
                + self.core[3, part, :].astype(F32)
                + self.last[0, part, :].astype(F32)
                + self.last[1, part, :].astype(F32)
            )

        if self.flush is not None:
            self.flush.start()
        for i in range(10):
            self.copies[i].wait_send()
        if self.again:
            for i, mask in enumerate((1, 2, 4)):
                pl.semaphore_signal(
                    self.credit.at[i], inc=1, device_id=(self.d ^ mask, self.t), device_id_type=MESH
                )


class PanelRing:
    def __init__(self, outs, scratch, d, t):
        grads, core, diag, last, stage, send, recv, credit, flush = scratch
        self.slots = slots = grads.shape[0]
        self.panels = []
        for i, out in enumerate(outs):
            q = i % slots
            panel = GradScatter(
                grads.at[q],
                stage.at[q],
                None,
                core.at[q],
                diag.at[q],
                last.at[q],
                None,
                send.at[q],
                recv.at[q],
                d,
                t,
            )
            panel.credit = credit.at[q]
            panel.reused = i >= slots
            panel.again = i + slots < len(outs)
            panel.before = self.panels[i - slots] if i >= slots else None
            panel.flush = pltpu.make_async_copy(stage.at[q], out, flush.at[q])
            self.panels.append(panel)

    def end(self):
        for panel in self.panels[-self.slots :]:
            panel.flush.wait()


def ring_scratch(slots, rows, n):
    return [
        pltpu.VMEM((slots, 8 * rows, n), BF16),
        pltpu.VMEM((slots, 4, rows, n), BF16),
        pltpu.VMEM((slots, 2, rows // 2, n), BF16),
        pltpu.VMEM((slots, 2, rows, n), BF16),
        pltpu.VMEM((slots, rows, n), F32),
        DMA((slots, 10)),
        DMA((slots, 10)),
        pltpu.SemaphoreType.REGULAR((slots, 3)),
        DMA((slots,)),
    ]


def scatter_scratch(shapes, loaded):
    own = [pltpu.VMEM((4,) + s, BF16) for s, far in zip(shapes, loaded) if far]
    core = [pltpu.VMEM((4,) + s, BF16) for s in shapes]
    diag = [pltpu.VMEM((2, s[0] // 2, s[1]), BF16) for s in shapes]
    last = [pltpu.VMEM((2,) + s, BF16) for s in shapes]
    n = len(shapes)
    return own + core + diag + last + [DMA((n, 4)), DMA((n, 10)), DMA((n, 10))]


def make_scatters(grads, outs, loaded, scratch, d, t):
    n = len(grads)
    scratch = list(scratch)
    own = [scratch.pop(0) if far else None for far in loaded]
    core, diag, last = (scratch[i * n : (i + 1) * n] for i in range(3))
    local, send, recv = scratch[3 * n :]
    return [
        GradScatter(
            grads[i],
            outs[i],
            own[i],
            core[i],
            diag[i],
            last[i],
            local.at[i],
            send.at[i],
            recv.at[i],
            d,
            t,
        )
        for i in range(n)
    ]


class LineGather:
    def __init__(self, block, out, local, send, recv, d, t, depth):
        self.block, self.out, self.send, self.recv = block, out, send, recv
        self.d, self.t, self.depth = d, t, depth
        self.rows = block.shape[-2]
        self.own = pltpu.make_async_copy(block, self.slot(t), local)

    def slot(self, j):
        rows = pl.ds(pl.multiple_of(j * self.rows, self.rows), self.rows)
        return self.out.at[:, rows] if len(self.out.shape) == 3 else self.out.at[rows]

    def copy(self, way, step, j, to):
        return pltpu.make_async_remote_copy(
            src_ref=self.block if step == 0 else self.slot(j),
            dst_ref=self.slot(j),
            send_sem=self.send.at[way, step],
            recv_sem=self.recv.at[way, step],
            device_id=(self.d, to),
            device_id_type=MESH,
        )

    def open(self, k):
        t, depth = self.t, self.depth
        if k == 0:
            self.own.start()

        @pl.when(t == k)
        def _():
            self.copy(0, 0, t, t + 1).start()

        @pl.when(t == depth - 1 - k)
        def _():
            self.copy(1, 0, t, t - 1).start()

    def step(self, s):
        t, depth = self.t, self.depth
        if s == 0:
            for k in range(depth - 1):
                self.open(k)
            return

        @pl.when((t - s >= 0) & (t < depth - 1))
        def _():
            self.copy(0, s - 1, t, t).wait_recv()
            self.copy(0, s, t - s, t + 1).start()

        @pl.when((t + s < depth) & (t > 0))
        def _():
            self.copy(1, s - 1, t, t).wait_recv()
            self.copy(1, s, t + s, t - 1).start()

    def finish(self):
        t, depth = self.t, self.depth
        self.own.wait()
        for s in range(depth - 1):

            @pl.when(t == depth - 1)
            def _():
                self.copy(0, s, t, t).wait_recv()

            @pl.when(t == 0)
            def _():
                self.copy(1, s, t, t).wait_recv()

    def end(self):
        t, depth = self.t, self.depth
        for s in range(depth - 1):

            @pl.when((t - s >= 0) & (t < depth - 1))
            def _():
                self.copy(0, s, t, t).wait_send()

            @pl.when((t + s < depth) & (t > 0))
            def _():
                self.copy(1, s, t, t).wait_send()


def line_gather_scratch(depth):
    return [DMA, DMA((2, depth - 1)), DMA((2, depth - 1))]


class LineScatter:
    def __init__(self, part, got, send, recv, d, t, depth, which=None, first_row=None):
        self.part, self.got, self.send, self.recv = part, got, send, recv
        self.d, self.t, self.depth = d, t, depth
        self.which = range(part.shape[0]) if which is None else which
        self.first_row = first_row
        self.rows = got.shape[3]

    def slot(self, way, j, s):
        return self.got.at[way, j - 1 if way == 0 else j, s]

    def copy(self, way, j, s, src, to):
        return pltpu.make_async_remote_copy(
            src_ref=src,
            dst_ref=self.slot(way, j, s),
            send_sem=self.send.at[way, j, s],
            recv_sem=self.recv.at[way, j, s],
            device_id=(self.d, to),
            device_id_type=MESH,
        )

    def block(self, j, s):
        start = j * self.rows
        if self.first_row is not None:
            start = pl.multiple_of(self.first_row + start, self.rows)
            return self.part.at[pl.ds(start, self.rows)]
        return self.part.at[s, pl.ds(pl.multiple_of(start, self.rows), self.rows)]

    def start(self, first=0, last=None):
        t, depth = self.t, self.depth
        steps = range(first, depth - 1 if last is None else last)

        @pl.when(t == 0)
        def _():
            for k in steps:
                for s in self.which:
                    j = depth - 1 - k
                    self.copy(0, j, s, self.block(j, s), t + 1).start()

        @pl.when(t == depth - 1)
        def _():
            for j in steps:
                for s in self.which:
                    self.copy(1, j, s, self.block(j, s), t - 1).start()

    def pass_on(self, way, j, to):
        for s in self.which:
            mine = self.slot(way, j, s)
            self.copy(way, j, s, mine, self.t).wait_recv()
            add_rows(mine, self.block(j, s), rows=self.rows)
            self.copy(way, j, s, mine, to).start()

    def step(self, k):
        t, depth = self.t, self.depth
        right = depth - 1 - k + t
        left = k - (depth - 1 - t)

        @pl.when((t > 0) & (t < right) & (right < depth))
        def _():
            self.pass_on(0, right, t + 1)

        @pl.when((left >= 0) & (left < t) & (t < depth - 1))
        def _():
            self.pass_on(1, left, t - 1)

    def total(self, out, more=False):
        t, depth = self.t, self.depth
        for s in self.which:
            own = self.block(t, s)[...].astype(F32)
            out[s][...] = out[s][...] + own if more else own

        @pl.when(t > 0)
        def _():
            for s in self.which:
                self.copy(0, t, s, self.slot(0, t, s), t).wait_recv()
                out[s][...] += self.got[0, t - 1, s].astype(F32)

        @pl.when(t < depth - 1)
        def _():
            for s in self.which:
                self.copy(1, t, s, self.slot(1, t, s), t).wait_recv()
                out[s][...] += self.got[1, t, s].astype(F32)

    def end(self):
        t, depth = self.t, self.depth
        for j in range(depth):
            for s in self.which:
                if j > 0:

                    @pl.when(j > t)
                    def _():
                        self.copy(0, j, s, self.slot(0, j, s), t).wait_send()

                if j < depth - 1:

                    @pl.when(j < t)
                    def _():
                        self.copy(1, j, s, self.slot(1, j, s), t).wait_send()


def line_scatter_scratch(seqs, rows, width, depth):
    return [
        pltpu.VMEM((2, depth - 1, seqs, rows, width), BF16),
        DMA((2, depth, seqs)),
        DMA((2, depth, seqs)),
    ]


def call(kernel, name, number, ins, outs, scratch, args, vmem=60 * 1024 * 1024):
    return pl.pallas_call(
        kernel,
        name=name,
        out_shape=[o[0] for o in outs],
        in_specs=ins,
        out_specs=[o[1] for o in outs],
        scratch_shapes=scratch,
        compiler_params=pltpu.CompilerParams(
            collective_id=number, has_side_effects=True, vmem_limit_bytes=vmem
        ),
    )(*args)


def shaped(shape, dtype, spec):
    return (jax.ShapeDtypeStruct(shape, dtype), spec)


def sigmoid(x):
    return 1.0 / (1.0 + jnp.exp(-x))


def one_less_exp(y):
    series = 1.0 + y / 6.0 * (1.0 + y / 7.0)
    for k in (5.0, 4.0, 3.0, 2.0):
        series = 1.0 + y / k * series
    return jnp.where(y > -0.5, -y * series, 1.0 - jnp.exp(y))


GELU_SCALE = 0.7978845608028654
GELU_CUBE = 0.044715


def gelu(x):
    return 0.5 * x * (1.0 + jnp.tanh(GELU_SCALE * (x + GELU_CUBE * x * x * x)))


def gelu_both(x):
    square = x * x
    bent = jnp.tanh(GELU_SCALE * (x + GELU_CUBE * square * x))
    half = 0.5 * (1.0 + bent)
    slope = half + 0.5 * x * (1.0 - bent * bent) * (
        GELU_SCALE * (1.0 + 3.0 * GELU_CUBE * square)
    )
    return x * half, slope


def rows_of(index, size):
    return pl.ds(pl.multiple_of(index * size, size), size)


def contract(left, right, dims):
    return lax.dot_general(left, right, ((dims[:1], dims[1:]), ((), ())), preferred_element_type=F32)


def scan_rows(rate, out, which, length, base=0, backward=False):
    tile = 8
    width = out.shape[1]
    row = lax.broadcasted_iota(jnp.int32, (tile, width), 0)

    def body(i, carried):
        k = length // tile - 1 - i if backward else i
        ends = []
        for at, s in enumerate(which):
            start = pl.multiple_of(s * length + k * tile, tile)
            rows = pl.ds(start, tile)
            if backward:
                pair = rate[pl.ds(start, 2 * tile), :]
                step = pltpu.roll(pair, 2 * tile - 1, 0)[:tile]
                step = jnp.where((row == tile - 1) & (i == 0), 0.0, step)
            else:
                step = rate[rows, :]
            held = pl.ds(pl.multiple_of(base + start, tile), tile)
            drive = out[held, :]
            for shift in (1, 2, 4):
                turn = tile - shift if backward else shift
                inside = row < tile - shift if backward else row >= shift
                before = jnp.where(inside, pltpu.roll(drive, turn, 0), 0.0)
                drive = drive + step * before
                step = step * jnp.where(inside, pltpu.roll(step, turn, 0), 1.0)
            states = drive + step * carried[at]
            out[held, :] = states
            ends.append(states[0:1] if backward else states[tile - 1 : tile])
        return tuple(ends)

    start = tuple(jnp.zeros((1, width), F32) for _ in which)
    lax.fori_loop(0, length // tile, body, start, unroll=2)


STRIP = 16
PANEL = 640


def gate_blocks(parity, width, block):
    half = block // 2
    shift = parity * half
    blocks = []
    for k in range((width + half) // block):
        low, high = k * block - shift, (k + 1) * block - shift
        blocks.append((k, max(low, 0), min(high, width)))
    return blocks


def front_kernel(
    depth,
    cotangent,
    token_weight,
    gelu_shard,
    input_shard,
    gate_in_shard,
    gate_dec_shard,
    out_shard,
    gate_shard,
    up_shard,
    down_shard,
    taps,
    rate,
    act,
    gain,
    first_gain,
    middle,
    normed_out,
    cot_out,
    normed_two_out,
    gelu_full,
    input_full,
    gate_in_full,
    gate_dec_full,
    out_full,
    gate_full,
    up_full,
    down_full,
    gelu_pre_out,
    input_pre_out,
    window_out,
    gate_in_out,
    gate_dec_out,
    states_out,
    mixed_out,
    gate_pre_out,
    lift_pre_out,
    hidden_out,
    *scratch,
):
    normed, gelu_w, input_w, gate_in_w, gate_dec_w, out_w = scratch[:6]
    gelu_pre, input_pre, conv, window, gate_in, gate_dec, decay, states, mixed, part = scratch[6:16]
    local, send, recv = scratch[16:19]
    line_sems = [scratch[19 + 3 * i : 22 + 3 * i] for i in range(6)]
    rim_send, rim_recv, save_sem = scratch[37:40]
    cot, normed_two, block_two, panel_w, product = scratch[40:45]
    panel_sem, product_sem = scratch[45:47]
    got, ssem, rsem = scratch[47:50]
    normed_block, cot_block, hidden = scratch[50:53]
    d, t = place()
    parity = lax.rem(t, 2)
    even = parity == 0
    odd = parity == 1

    def prepare():
        for s in range(act.shape[0]):
            value = act[s].astype(F32)
            inverse = lax.rsqrt(jnp.mean(value * value, axis=-1, keepdims=True) + EPS)
            normed_block[s] = (value * inverse * first_gain[...][None]).astype(BF16)
            cot_block[s] = (cotangent[s].astype(F32) * token_weight[s]).astype(BF16)

    greet(d, t, depth, meanwhile=prepare)
    seqs, length, model = normed.shape
    tokens = seqs * length
    width = conv.shape[1]
    block = gate_in_w.shape[0]
    half = block // 2
    spans = [pl.ds(s * length, length) for s in range(seqs)]
    firsts = [
        LineGather(normed_block.at[s], normed.at[s], *line_sems[5 * s], d, t, depth)
        for s in range(seqs)
    ]
    cots = [
        LineGather(cot_block.at[s], cot.at[spans[s]], *line_sems[1 + s], d, t, depth)
        for s in range(seqs)
    ]
    twos = [
        LineGather(block_two.at[s], normed_two.at[spans[s]], *line_sems[3 + s], d, t, depth)
        for s in range(seqs)
    ]
    scatters = [LineScatter(part, got, ssem, rsem, d, t, depth, (s,)) for s in range(seqs)]
    pairs = (
        (gelu_shard, gelu_w),
        (input_shard, input_w),
        (gate_in_shard, gate_in_w),
        (gate_dec_shard, gate_dec_w),
        (out_shard, out_w),
        (gate_shard, gate_full),
        (up_shard, up_full),
        (down_shard, down_full),
    )
    gathers = [
        WeightGather(shard, full, local.at[i], send.at[i], recv.at[i], d, t)
        for i, (shard, full) in enumerate(pairs)
    ]
    saves = []

    def save(src, dst):
        copy = pltpu.make_async_copy(src, dst, save_sem.at[len(saves)])
        copy.start()
        saves.append(copy)

    one = [gathers[1], gathers[0], gathers[2], gathers[3]]
    out_g, gate_g, up_g, down_g = gathers[4:]
    even_blocks, odd_blocks = gate_blocks(0, width, block), gate_blocks(1, width, block)

    def rim(s, to, src, dst):
        return pltpu.make_async_remote_copy(
            src_ref=conv.at[spans[s], pl.ds(src, half)],
            dst_ref=window.at[spans[s], pl.ds(dst, half)],
            send_sem=rim_send.at[s],
            recv_sem=rim_recv.at[s],
            device_id=(d, to),
            device_id_type=MESH,
        )

    def convolve(s):
        input_pre[s, 0:8, :] = jnp.zeros((8, width), F32)
        input_pre[s, 8 : 8 + length, :] = contract(normed[s], input_w[...], (1, 0))

        @pl.loop(0, length // STRIP)
        def _(i):
            near = input_pre[s, pl.ds(pl.multiple_of(i * STRIP, STRIP), STRIP + 8), :]
            total = taps[0:1, :] * near[8:]
            for k in range(1, taps.shape[0]):
                total = total + taps[k : k + 1, :] * pltpu.roll(near, k, 0)[8:]
            rows = pl.ds(pl.multiple_of(s * length + i * STRIP, STRIP), STRIP)
            conv[rows, :] = total.astype(BF16)

        @pl.when(even)
        def _():
            rim(s, t + 1, width - half, 0).start()
            window[spans[s], 0:width] = conv[spans[s], :]

        @pl.when(odd)
        def _():
            rim(s, t - 1, 0, width).start()
            window[spans[s], half : half + width] = conv[spans[s], :]

    def gates(s, blocks):
        for k, low, high in blocks:
            near = window[spans[s], k * block : (k + 1) * block]
            gate_in[spans[s], low:high] = contract(near, gate_in_w[:, low:high], (1, 0))
            gate_dec[spans[s], low:high] = contract(near, gate_dec_w[:, low:high], (1, 0))

    def inner_gates(s):
        gelu_pre[spans[s], :] = contract(normed[s], gelu_w[...], (1, 0))

        @pl.when(even)
        def _():
            gates(s, even_blocks[:-1])

        @pl.when(odd)
        def _():
            gates(s, odd_blocks[1:])

    def recur(s):
        @pl.when(even)
        def _():
            rim(s, t + 1, width - half, width).wait_recv()
            gates(s, even_blocks[-1:])

        @pl.when(odd)
        def _():
            rim(s, t - 1, 0, 0).wait_recv()
            gates(s, odd_blocks[:1])

        @pl.loop(0, length // STRIP)
        def _(i):
            start = pl.multiple_of(s * length + i * STRIP, STRIP)
            rows = pl.ds(start, STRIP)
            log = -8.0 * sigmoid(gate_dec[rows, :]) * rate[...][None]
            decay[rows, :] = jnp.exp(log)
            drive = jnp.sqrt(one_less_exp(2.0 * log)) * sigmoid(gate_in[rows, :])
            held = pl.ds(pl.multiple_of(start + 8, 8), STRIP)
            states[held, :] = drive * conv[rows, :].astype(F32)

        scan_rows(decay, states, (s,), length, base=8)

    def mix(s):
        @pl.loop(0, length // STRIP)
        def _(i):
            start = pl.multiple_of(s * length + i * STRIP, STRIP)
            rows, held = pl.ds(start, STRIP), pl.ds(pl.multiple_of(start + 8, 8), STRIP)
            mixed[rows, :] = (gelu(gelu_pre[rows, :]) * states[held, :]).astype(BF16)

        panel = 512

        @pl.loop(0, model // panel)
        def _(i):
            columns = rows_of(i, panel)
            part[s, :, columns] = contract(mixed[spans[s], :], out_w[columns, :], (1, 1)).astype(
                BF16
            )

    def norm_step(s):
        scatters[s].total([middle.at[i] for i in range(seqs)])
        value = middle[s] + act[s].astype(F32)
        middle[s] = value
        inverse = lax.rsqrt(jnp.mean(value * value, axis=-1, keepdims=True) + EPS)
        block_two[s] = (value * inverse * gain[...][None]).astype(BF16)
        twos[s].step(0)

    firsts[0].step(0)
    for g in one:
        g.start()
    firsts[0].step(1)
    firsts[1].step(0)
    for g in one:
        g.relay()
    out_g.start()
    firsts[0].step(2)
    for line in cots:
        line.open(0)
    for g in one:
        g.relay_two()
    firsts[1].step(1)
    for g in one:
        g.relay_last()
    firsts[0].finish()
    for line in cots:
        line.open(1)
    one[0].arrive()
    states[0:8, :] = jnp.zeros((8, width), F32)
    convolve(0)
    out_g.relay()
    gate_g.start()
    up_g.start()
    for g in one[1:]:
        g.arrive()
    inner_gates(0)
    out_g.relay_two()
    firsts[1].step(2)
    recur(0)
    out_g.relay_last()
    out_g.arrive()
    mix(0)
    firsts[1].finish()
    scatters[0].start(0, 1)
    for line in cots:
        line.open(2)
    convolve(1)
    scatters[0].start(1)
    inner_gates(1)
    scatters[0].step(1)
    gate_g.relay()
    recur(1)
    scatters[0].step(2)
    mix(1)
    scatters[1].start()
    save(normed, normed_out)
    save(gelu_w, gelu_full)
    save(input_w, input_full)
    save(gate_in_w, gate_in_full)
    save(gate_dec_w, gate_dec_full)
    save(out_w, out_full)
    save(gelu_pre, gelu_pre_out)
    save(input_pre, input_pre_out)
    save(window, window_out)
    save(gate_in, gate_in_out)
    save(gate_dec, gate_dec_out)
    save(states, states_out)
    save(mixed, mixed_out)
    gate_g.relay_two()
    scatters[1].step(1)
    norm_step(0)
    up_g.relay()
    down_g.start()
    scatters[1].step(2)
    up_g.relay_two()
    twos[0].step(1)
    norm_step(1)
    twos[0].step(2)
    gate_g.relay_last()
    twos[1].step(1)
    for line in cots:
        line.step(1)
    twos[1].step(2)
    for line in cots:
        line.step(2)
    up_g.relay_last()
    panels = down_full.shape[1] // PANEL

    kinds = ((gate_full, gate_pre_out), (up_full, lift_pre_out))
    order = [(s, p, i) for s in range(seqs) for p in range(panels) for i in range(2)]

    def load_panel(at):
        _, p, i = order[at]
        columns = pl.ds(p * PANEL, PANEL)
        copy = pltpu.make_async_copy(
            kinds[i][0].at[:, columns], panel_w.at[at % 2], panel_sem.at[at % 2]
        )
        copy.start()
        return copy

    results = [[], []]

    def store(src, out, s, p, i):
        columns = pl.ds(p * PANEL, PANEL)
        copy = pltpu.make_async_copy(src, out.at[spans[s], columns], product_sem.at[3 * s + i])
        copy.start()
        results[s].append(copy)

    def multiply(s, p):
        nonlocal loaded
        while results[s]:
            results[s].pop().wait()
        for i, (_, out) in enumerate(kinds):
            at = (s * panels + p) * 2 + i
            loaded.wait()
            if at + 1 < len(order):
                loaded = load_panel(at + 1)
            product[i, spans[s], :] = contract(normed_two[spans[s], :], panel_w[at % 2], (1, 0))
            store(product.at[i, spans[s]], out, s, p, i)

        @pl.loop(0, length // STRIP)
        def _(k):
            rows = pl.ds(pl.multiple_of(s * length + k * STRIP, STRIP), STRIP)
            hidden[rows, :] = (gelu(product[0, rows, :]) * product[1, rows, :]).astype(BF16)

        store(hidden.at[spans[s]], hidden_out, s, p, 2)

    gate_g.arrive()
    loaded = load_panel(0)
    up_g.arrive()
    twos[0].finish()
    multiply(0, 0)
    down_g.relay()
    multiply(0, 1)
    multiply(0, 2)
    down_g.relay_two()
    twos[1].finish()
    multiply(1, 0)
    multiply(1, 1)
    multiply(1, 2)
    save(normed_two, normed_two_out)
    for line in cots:
        line.finish()
    save(cot, cot_out)
    down_g.relay_last()
    down_g.arrive()

    for s in range(seqs):

        @pl.when(even)
        def _():
            rim(s, t + 1, width - half, 0).wait_send()

        @pl.when(odd)
        def _():
            rim(s, t - 1, 0, width).wait_send()

    for g in gathers:
        g.end()
    for line in firsts + cots + twos + scatters:
        line.end()
    for copy in saves + results[0] + results[1]:
        copy.wait()


def front_phase(cotangent, token_weight, weights, taps, rate, act, gain, first_gain, depth):
    seqs, rows, model = act.shape
    length = rows * depth
    tokens = seqs * length
    n = len(weights)
    block, width = weights[2].shape[0] * 8, weights[0].shape[1]
    units = weights[-1].shape[1]
    wide = block // 2 + width
    wide_rows = (seqs, length, model)
    mixers = [(model, width), (model, width), (block, width), (block, width), (model, width)]
    saved = [
        ((tokens, width), F32),
        ((seqs, length + 8, width), F32),
        ((tokens, wide), BF16),
        ((tokens, width), F32),
        ((tokens, width), F32),
        ((tokens + 8, width), F32),
        ((tokens, width), BF16),
    ]
    outs = [shaped(act.shape, F32, VMEM)]
    outs += [shaped(wide_rows, BF16, ANY)] + [shaped((tokens, model), BF16, ANY)] * 2
    outs += [shaped(shape, BF16, ANY) for shape in mixers]
    outs += [shaped((model, units), BF16, ANY)] * 3
    outs += [shaped(shape, dtype, ANY) for shape, dtype in saved]
    outs += [shaped((tokens, units), F32, ANY)] * 2 + [shaped((tokens, units), BF16, ANY)]
    saved_scratch = saved[:2] + [((tokens, width), BF16)] + saved[2:5] + [((tokens, width), F32)]
    saved_scratch += saved[5:] + [(wide_rows, BF16)]
    scratch = [pltpu.VMEM(wide_rows, BF16)]
    scratch += [pltpu.VMEM(shape, BF16) for shape in mixers]
    scratch += [pltpu.VMEM(shape, dtype) for shape, dtype in saved_scratch]
    scratch += gather_scratch(n) + line_gather_scratch(depth) * 6 + [DMA((seqs,)), DMA((seqs,)), DMA((16,))]
    scratch += [
        pltpu.VMEM((tokens, model), BF16),
        pltpu.VMEM((tokens, model), BF16),
        pltpu.VMEM(act.shape, BF16),
        pltpu.VMEM((2, model, PANEL), BF16),
        pltpu.VMEM((2, tokens, PANEL), F32),
        DMA((2,)),
        DMA((6,)),
    ]
    scratch += line_scatter_scratch(seqs, rows, model, depth)
    scratch += [pltpu.VMEM(act.shape, BF16)] * 2 + [pltpu.VMEM((tokens, PANEL), BF16)]
    res = call(
        functools.partial(front_kernel, depth),
        "front_phase",
        0,
        [VMEM] * (7 + n),
        outs,
        scratch,
        (cotangent, token_weight)
        + tuple(weights)
        + (taps, rate, act, gain, first_gain),
    )
    return res[0], res[1:4], res[4:9], res[9:12], res[12:19], res[19:]


def norm_back(value, gain, error):
    inverse = lax.rsqrt(jnp.mean(value * value, axis=-1, keepdims=True) + EPS)
    scaled = error * gain
    mean = jnp.mean(scaled * value, axis=-1, keepdims=True)
    grad = inverse * scaled - value * (inverse * inverse * inverse * mean)
    return grad, jnp.sum(error * value * inverse, axis=0, keepdims=True)


def feed_kernel(
    depth,
    normed_in,
    cot_in,
    gate_in,
    up_in,
    down_in,
    gate_pre_in,
    lift_pre_in,
    hidden_in,
    middle,
    gain,
    cotangent,
    token_weight,
    grad,
    wide,
    gain_grad,
    feed_out,
    lift_rows_out,
    output_first,
    down_out,
    gate_out,
    *refs,
):
    panels = gate_in.shape[1] // PANEL
    outs = [
        out.at[:, pl.ds(p * PANEL, PANEL)] for out in (down_out, gate_out) for p in range(panels)
    ]
    normed, cot, hidden, gate_rows, lift_rows = refs[:5]
    gate_w, up_w, down_w, gate_pre, lift_pre, grad_hidden, acc, part, block, feed_part = refs[5:15]
    got, ssem, rsem = refs[15:18]
    load_sem, weight_sem, save_sem = refs[18:21]
    lines = refs[21:24], refs[24:27]
    feed_got, feed_ssem, feed_rsem = refs[27:30]
    d, t = place()
    greet(d, t, depth)
    seqs = middle.shape[0]
    tokens, model = normed_in.shape
    length = tokens // seqs
    tile = 512
    ring = PanelRing(outs, refs[30:], d, t)
    scatters = [LineScatter(part, got, ssem, rsem, d, t, depth, (s,)) for s in range(seqs)]
    early_feed = LineScatter(feed_part, feed_got, feed_ssem, feed_rsem, d, t, depth, (0,), 0)
    gathers = [
        LineGather(block.at[s], wide.at[s], *lines[s], d, t, depth) for s in range(seqs)
    ]

    def load(i, src, dst):
        copy = pltpu.make_async_copy(src, dst, load_sem.at[i])
        copy.start()
        return copy

    def weight(i, src, dst, p):
        copy = pltpu.make_async_copy(
            src.at[:, pl.ds(p * PANEL, PANEL)], dst, weight_sem.at[i]
        )
        copy.start()
        return copy

    def held_rows(s, p):
        rows, columns = pl.ds(s * length, length), pl.ds(p * PANEL, PANEL)
        q = (s * panels + p) % 2
        return [
            load(2 + q, gate_pre_in.at[rows, columns], gate_pre.at[q]),
            load(4 + q, lift_pre_in.at[rows, columns], lift_pre.at[q]),
        ]

    hidden_load = load(6, hidden_in, hidden)
    cot_load = load(1, cot_in, cot)
    down_loads = [weight(p, down_in, w, p) for p, w in enumerate((gate_w, up_w, down_w))]
    row_loads = held_rows(0, 0)
    normed_load = load(0, normed_in, normed)

    def forward(s, p, more):
        nonlocal down_load, gate_load, up_load, row_loads
        rows = pl.ds(s * length, length)
        columns = pl.ds(p * PANEL, PANEL)
        q = (s * panels + p) % 2
        down_load.wait()
        grad_hidden[...] = contract(cot[rows, :], down_w[...], (1, 0))
        for copy in row_loads:
            copy.wait()
        if more is not None:
            down_load = weight(2, down_in, down_w, more)
            row_loads = held_rows(*((s, more) if more > p else (s + 1, more)))

        @pl.loop(0, length // STRIP)
        def _(i):
            strip = rows_of(i, STRIP)
            held = pl.ds(pl.multiple_of(s * length + i * STRIP, STRIP), STRIP)
            act, slope = gelu_both(gate_pre[q, strip, :])
            lift = lift_pre[q, strip, :]
            came = grad_hidden[strip, :]
            gate_rows[held, columns] = (came * lift * slope).astype(BF16)
            lift_rows[held, columns] = (came * act).astype(BF16)

        gate_load.wait()
        up_load.wait()

        @pl.loop(0, model // tile)
        def _(i):
            out = rows_of(i, tile)
            value = contract(gate_rows[rows, columns], gate_w[out, :], (1, 1))
            value = value + contract(lift_rows[rows, columns], up_w[out, :], (1, 1))
            if p == 0:
                acc[:, out] = value
            elif p < panels - 1:
                acc[:, out] += value
            else:
                part[s, :, out] = (acc[:, out] + value).astype(BF16)

        if more is not None:
            gate_load = weight(0, gate_in, gate_w, more)
            up_load = weight(1, up_in, up_w, more)

    kinds = ((cot, hidden), (normed, gate_rows), (normed, lift_rows))

    def weight_grad(i, out):
        left, right = kinds[i // panels]
        columns = pl.ds(i % panels * PANEL, PANEL)

        @pl.loop(0, model // tile)
        def _(k):
            rows = rows_of(k, tile)
            out[rows, :] = contract(left[:, rows], right[:, columns], (0, 0)).astype(BF16)

    def begin(i):
        panel = ring.panels[i]
        weight_grad(i, panel.grad)
        panel.start()

    def push(i):
        ring.panels[i].first()
        ring.panels[i].second()

    def norm_step(s):
        scatters[s].total([grad.at[i] for i in range(seqs)])
        change, gain_part = norm_back(middle[s], gain[...][None], grad[s])
        change = change + cotangent[s].astype(F32) * token_weight[s]
        grad[s] = change
        block[s] = change.astype(BF16)
        if s == 0:
            gain_grad[...] = gain_part
        else:
            gain_grad[...] += gain_part

    def feed(s, out):
        rows = pl.ds(s * length, length)
        downs = (gate_w, up_w, down_w)

        @pl.loop(0, model // tile)
        def _(i):
            columns = rows_of(i, tile)
            value = contract(hidden[rows, 0:PANEL], downs[0][columns, :], (1, 1))
            for p in range(1, panels):
                units = pl.ds(p * PANEL, PANEL)
                value = value + contract(hidden[rows, units], downs[p][columns, :], (1, 1))
            out[:, columns] = value.astype(BF16)

    saves = []

    def save(i, src, dst):
        copy = pltpu.make_async_copy(src, dst, save_sem.at[i])
        copy.start()
        saves.append(copy)

    hidden_load.wait()
    cot_load.wait()
    begin(0)
    for copy in down_loads:
        copy.wait()
    feed(0, feed_part)
    early_feed.start()
    down_load = weight(2, down_in, down_w, 0)
    gate_load = weight(0, gate_in, gate_w, 0)
    up_load = weight(1, up_in, up_w, 0)
    push(0)
    forward(0, 0, 1)
    begin(1)
    early_feed.step(1)
    forward(0, 1, 2)
    early_feed.step(2)
    ring.panels[0].third()
    push(1)
    forward(0, 2, 0)
    scatters[0].start()
    forward(1, 0, 1)
    scatters[0].step(1)
    ring.panels[0].end()
    ring.panels[1].third()
    begin(2)
    scatters[0].step(2)
    forward(1, 1, 2)
    push(2)
    norm_step(0)
    gathers[0].step(0)
    forward(1, 2, None)
    down_loads = [weight(0, down_in, gate_w, 0), weight(1, down_in, up_w, 1)]
    down_loads.append(weight(2, down_in, down_w, 2))
    scatters[1].start()
    save(2, lift_rows, lift_rows_out)
    gathers[0].step(1)
    ring.panels[1].end()
    ring.panels[2].third()
    normed_load.wait()
    begin(3)
    scatters[1].step(1)
    gathers[0].step(2)
    push(3)
    begin(4)
    scatters[1].step(2)
    ring.panels[2].end()
    ring.panels[3].third()
    for copy in down_loads:
        copy.wait()
    feed(1, cot.at[pl.ds(length, length)])
    save(1, cot.at[pl.ds(length, length)], feed_out)
    push(4)
    norm_step(1)
    gathers[1].step(0)
    ring.panels[3].end()
    begin(5)
    ring.panels[4].third()
    total = acc.at[pl.ds(0, middle.shape[1])]
    early_feed.total([total])
    output_first[...] = (total[...] + middle[0]).astype(BF16)
    gathers[1].step(1)
    push(5)
    ring.panels[4].end()
    gathers[1].step(2)
    ring.panels[5].third()
    for line in gathers:
        line.finish()
    ring.panels[5].end()
    ring.end()
    for copy in saves:
        copy.wait()
    for line in scatters + gathers + [early_feed]:
        line.end()


def feed_phase(normed, cot, weights, held, middle, gain, cotangent, token_weight, depth):
    gate_w, up_w, down_w = weights
    seqs, rows, model = middle.shape
    tokens = normed.shape[0]
    length = tokens // seqs
    wide_rows = (seqs, length, model)
    units = gate_w.shape[1]
    outs = [
        shaped(middle.shape, F32, VMEM),
        shaped(wide_rows, BF16, ANY),
        shaped((1, model), F32, VMEM),
        shaped((length, model), BF16, ANY),
        shaped((tokens, units), BF16, ANY),
        shaped(middle.shape[1:], BF16, VMEM),
    ] + [shaped((model // 8, units), F32, ANY)] * 2
    scratch = [pltpu.VMEM((tokens, model), BF16)] * 2
    scratch += [pltpu.VMEM((tokens, units), BF16)] * 3
    scratch += [pltpu.VMEM((model, PANEL), BF16)] * 3
    scratch += [pltpu.VMEM((2, length, PANEL), F32)] * 2 + [pltpu.VMEM((length, PANEL), F32)]
    scratch += [
        pltpu.VMEM((length, model), F32),
        pltpu.VMEM(wide_rows, BF16),
        pltpu.VMEM(middle.shape, BF16),
        pltpu.VMEM((length, model), BF16),
    ]
    scratch += line_scatter_scratch(seqs, rows, model, depth)
    scratch += [DMA((7,)), DMA((3,)), DMA((3,))]
    scratch += line_gather_scratch(depth) * 2
    scratch += line_scatter_scratch(1, rows, model, depth)
    scratch += ring_scratch(3, model // 8, PANEL)
    return call(
        functools.partial(feed_kernel, depth),
        "feed_phase",
        2,
        [ANY] * 8 + [VMEM] * 4,
        outs,
        scratch,
        (normed, cot, gate_w, up_w, down_w) + tuple(held) + (middle, gain, cotangent, token_weight),
        vmem=63 * 1024 * 1024,
    )


def mixer_back_kernel(
    depth,
    branch_in,
    normed_in,
    out_w_in,
    gelu_pre_in,
    input_pre_in,
    window_in,
    gate_in_in,
    gate_dec_in,
    states_in,
    mixed_in,
    gelu_w_in,
    input_w_in,
    gate_in_w_in,
    gate_dec_w_in,
    normed_two_in,
    lift_rows_in,
    feed_in,
    middle_in,
    taps,
    rate,
    act,
    gain,
    grad_middle,
    mlp_part,
    output_first,
    *refs,
):
    output, input_grad, norm_grad, mlp_grad, rate_grad, taps_grad = refs[:6]
    gate_in_out, gate_dec_out, out_out, gelu_out, input_out, up_out = refs[6:12]
    scratch = refs[12:]
    panels = up_out.shape[1] // PANEL
    ups = [up_out.at[:, pl.ds(p * PANEL, PANEL)] for p in range(panels)]
    branch, weight, input_w = scratch[:3]
    gelu_pre, input_pre, window, gate_in, gate_dec, states, gate_in_w, gate_dec_w = scratch[3:11]
    grad, decay, gelu_grad, grad_in, grad_dec = scratch[11:16]
    input_rows = scratch[-1]
    grad_conv = [decay.at[pl.ds(s * (decay.shape[0] // 2), decay.shape[0] // 2)] for s in range(2)]
    rim_out, rim_in, gate_in_grad, gate_dec_grad, part, sums = scratch[16 : 22]
    panel_sem = scratch[22]
    got, ssem, rsem = scratch[23 : 26]
    rim_send, rim_recv, load_sem, feed_sem = scratch[26 : 30]
    small, small_all, pack, packs, line_pack, line_packs = scratch[30 : 36]
    psend, precv, qsend, qrecv, zsend, zrecv = scratch[36 : 42]
    d, t = place()
    ring = PanelRing([out_out] + ups + [gelu_out, input_out], scratch[42 : 51], d, t)
    feed, lift_rows, feed_got, feed_ssem, feed_rsem = scratch[51 : 56]
    parity = lax.rem(t, 2)
    even = parity == 0
    odd = parity == 1
    greet(d, t, depth, dp_masks=(1, 2, 3, 4, 5, 6, 7), z_all=True)
    seqs, length, model = branch_in.shape
    tokens = seqs * length
    width = gate_in.shape[1]
    block = gate_in_w.shape[0]
    half = block // 2
    even_blocks, odd_blocks = gate_blocks(0, width, block), gate_blocks(1, width, block)
    gate_scatters = make_scatters(
        (gate_in_grad, gate_dec_grad),
        (gate_in_out, gate_dec_out),
        (False, False),
        scratch[56:-1],
        d,
        t,
    )
    feed_line = LineScatter(feed, feed_got, feed_ssem, feed_rsem, d, t, depth, (0,), 0)
    lines = [
        LineScatter(part, got, ssem, rsem, d, t, depth, (s,), s * length) for s in range(seqs)
    ]

    def load(i, src, dst):
        copy = pltpu.make_async_copy(src, dst, load_sem.at[i])
        copy.start()
        return copy

    def load_wide(i, src, dst):
        spans = [pl.ds(s * length, length) for s in range(seqs)]
        return [
            load(i + s, src.at[s] if len(src.shape) == 3 else src.at[rows], dst.at[rows])
            for s, rows in enumerate(spans)
        ]

    early = [load(0, out_w_in, weight)] + load_wide(12, branch_in, branch)
    next_ = [
        load(2, gelu_pre_in, gelu_pre),
        load(3, states_in, states),
        load(4, gate_dec_in, gate_dec),
    ]
    feed_load = pltpu.make_async_copy(feed_in, feed, feed_sem)
    feed_load.start()

    def dp_copies(src, dst, send, recv):
        return [
            pltpu.make_async_remote_copy(
                src_ref=src,
                dst_ref=dst.at[d],
                send_sem=send.at[mask - 1],
                recv_sem=recv.at[mask - 1],
                device_id=(d ^ mask, t),
                device_id_type=MESH,
            )
            for mask in range(1, 8)
        ]

    def weight_grad(left, right, out):
        panel = 512

        @pl.loop(0, model // panel)
        def _(i):
            columns = rows_of(i, panel)
            out[columns, :] = contract(left[:, columns], right[...], (0, 0)).astype(BF16)

    def begin(i, left, right):
        weight_grad(left, right, ring.panels[i].grad)
        ring.panels[i].start()

    def push(i):
        ring.panels[i].first()
        ring.panels[i].second()

    def load_lift(p):
        copy = pltpu.make_async_copy(
            lift_rows_in.at[:, pl.ds(p * PANEL, PANEL)], lift_rows, panel_sem
        )
        copy.start()
        return copy

    mixed_load = load(1, mixed_in, lift_rows)
    two_loads = load_wide(12 + seqs, normed_two_in, part)
    then = [
        load(5, gate_in_in, gate_in),
        load(7, window_in, window),
        load(8, gate_in_w_in, gate_in_w),
        load(9, gate_dec_w_in, gate_dec_w),
        load(10, input_pre_in, input_pre),
        load(11, input_w_in, input_w),
    ]
    for copy in early:
        copy.wait()
    feed_load.wait()
    feed_line.start()
    mixed_load.wait()
    begin(0, branch, lift_rows)
    lift_load = load_lift(0)
    for s in range(seqs):
        rows = pl.ds(s * length, length)
        grad[rows, :] = contract(branch[rows, :], weight[...], (1, 0))
    reload = load(0, gelu_w_in, weight)
    wide_loads = load_wide(12, normed_in, branch)
    push(0)
    for copy in two_loads:
        copy.wait()
    lift_load.wait()
    begin(1, part, lift_rows)
    lift_load = load_lift(1)
    for copy in next_:
        copy.wait()
    spans = [pl.ds(s * length, length) for s in range(seqs)]
    sums[...] = jnp.zeros(sums.shape, F32)

    def fold(value):
        return value[0:8] + value[8:16]

    own_columns = pl.ds(pl.multiple_of(parity * half, half), width)
    first_row = lax.broadcasted_iota(jnp.int32, (STRIP, width), 0) == 0

    def states_back(s):
        @pl.loop(0, length // STRIP)
        def _(i):
            start = pl.multiple_of(s * length + i * STRIP, STRIP)
            rows, held = pl.ds(start, STRIP), pl.ds(pl.multiple_of(start + 8, 8), STRIP)
            act, slope = gelu_both(gelu_pre[rows, :])
            came = grad[rows, :]
            gelu_grad[rows, :] = (came * states[held, :] * slope).astype(BF16)
            grad[rows, :] = came * act
            decay[rows, :] = jnp.exp(-8.0 * sigmoid(gate_dec[rows, :]) * rate[...][None])

        end = (s + 1) * length
        decay[end : end + 8, :] = jnp.zeros((8, width), F32)
        scan_rows(decay, grad, (s,), length, backward=True)

    def drive_back(s):
        @pl.loop(0, length // STRIP)
        def _(i):
            start = pl.multiple_of(s * length + i * STRIP, STRIP)
            rows = pl.ds(start, STRIP)
            earlier = pltpu.roll(states[pl.ds(start, STRIP + 8), :], 1, 0)[8:]
            earlier = jnp.where(first_row & (i == 0), 0.0, earlier)
            came = grad[rows, :]
            open_in = sigmoid(gate_in[rows, :])
            open_dec = sigmoid(gate_dec[rows, :])
            slow = -8.0 * rate[...][None]
            lost = one_less_exp(2.0 * open_dec * slow)
            root = jnp.sqrt(lost)
            value = window[rows, own_columns].astype(F32)
            step = jnp.exp(open_dec * slow)
            through = came * open_in
            grad_log = step * (came * earlier - through * value * step / root)
            sums[0] += fold(grad_log * (-8.0 * open_dec))
            through = through * root
            grad_conv[s][pl.ds(pl.multiple_of(i * STRIP, STRIP), STRIP), :] = through
            grad_in[rows, :] = (through * value * (1.0 - open_in)).astype(BF16)
            grad_dec[rows, :] = (grad_log * slow * open_dec * (1.0 - open_dec)).astype(BF16)

        grad_conv[s][length : length + 8, :] = jnp.zeros((8, width), F32)

    def gates_back(s, k, low, high):
        rows = spans[s]
        return contract(grad_in[rows, low:high], gate_in_w[:, low:high], (1, 1)) + contract(
            grad_dec[rows, low:high], gate_dec_w[:, low:high], (1, 1)
        )

    def add_conv(s, low, high, value):
        grad_conv[s][0:length, low:high] += value

    def rim(s, to):
        return pltpu.make_async_remote_copy(
            src_ref=rim_out.at[spans[s]],
            dst_ref=rim_in.at[spans[s]],
            send_sem=rim_send.at[s],
            recv_sem=rim_recv.at[s],
            device_id=(d, to),
            device_id_type=MESH,
        )

    def rim_start(s):
        @pl.when(even)
        def _():
            value = gates_back(s, *even_blocks[-1])
            rim_out[spans[s], :] = value[:, half:].astype(BF16)
            rim(s, t + 1).start()
            add_conv(s, width - half, width, value[:, :half])

        @pl.when(odd)
        def _():
            value = gates_back(s, *odd_blocks[0])
            rim_out[spans[s], :] = value[:, :half].astype(BF16)
            rim(s, t - 1).start()
            add_conv(s, 0, half, value[:, half:])

    def inner(s):
        @pl.when(even)
        def _():
            for k, low, high in even_blocks[:-1]:
                add_conv(s, low, high, gates_back(s, k, low, high))

        @pl.when(odd)
        def _():
            for k, low, high in odd_blocks[1:]:
                add_conv(s, low, high, gates_back(s, k, low, high))

    def conv_back(s):
        @pl.when(even)
        def _():
            rim(s, t + 1).wait()
            add_conv(s, width - half, width, rim_in[spans[s], :].astype(F32))

        @pl.when(odd)
        def _():
            rim(s, t - 1).wait()
            add_conv(s, 0, half, rim_in[spans[s], :].astype(F32))

        @pl.loop(0, length // STRIP)
        def _(i):
            near = pl.ds(pl.multiple_of(i * STRIP, STRIP), STRIP + 8)
            later = grad_conv[s][near, :]
            before = input_pre[s, near, :]
            here = later[:STRIP]
            value = taps[0:1, :] * here
            sums[1] += fold(here * before[8:])
            for k in range(1, taps.shape[0]):
                value = value + taps[k : k + 1, :] * pltpu.roll(later, STRIP + 8 - k, 0)[:STRIP]
                sums[1 + k] += fold(here * pltpu.roll(before, k, 0)[8:])
            rows = pl.ds(pl.multiple_of(s * length + i * STRIP, STRIP), STRIP)
            input_rows[rows, :] = value.astype(BF16)

    def project_back(s):
        rows, panel = spans[s], 512

        @pl.loop(0, weight.shape[0] // panel)
        def _(i):
            columns = rows_of(i, panel)
            value = contract(gelu_grad[rows, :], weight[columns, :], (1, 1))
            value = value + contract(input_rows[rows, :], input_w[columns, :], (1, 1))
            part[rows, columns] = value.astype(BF16)

    def gate_grads(blocks):
        for k, low, high in blocks:
            near = window[:, k * block : (k + 1) * block]
            gate_in_grad[:, low:high] = contract(near, grad_in[:, low:high], (0, 0)).astype(BF16)
            gate_dec_grad[:, low:high] = contract(near, grad_dec[:, low:high], (0, 0)).astype(BF16)

    states_back(0)
    feed_line.step(1)
    push(1)
    ring.panels[0].third()
    for copy in then:
        copy.wait()
    drive_back(0)
    rim_start(0)
    feed_line.step(2)
    inner(0)
    lift_load.wait()
    begin(2, part, lift_rows)
    lift_load = load_lift(2)
    conv_back(0)
    push(2)
    ring.panels[1].third()
    ring.panels[0].end()
    lift_load.wait()
    begin(3, part, lift_rows)
    reload.wait()
    project_back(0)
    lines[0].start(0, 1)
    states_back(1)
    ring.panels[2].third()
    push(3)
    drive_back(1)
    rim_start(1)
    lines[0].start(1)
    lines[0].step(1)
    inner(1)

    @pl.when(even)
    def _():
        gate_grads(even_blocks)

    @pl.when(odd)
    def _():
        gate_grads(odd_blocks)

    for g in gate_scatters:
        g.start()
    conv_back(1)
    lines[0].step(2)
    project_back(1)
    lines[1].start()
    middle_load = load(0, middle_in.at[1], input_grad.at[1])
    ring.panels[3].third()
    for k in range(sums.shape[0]):
        small[k : k + 1, :] = jnp.sum(sums[k], axis=0, keepdims=True)
    small[sums.shape[0] :, :] = jnp.zeros((8 - sums.shape[0], width), F32)
    small_copies = dp_copies(small, small_all, qsend, qrecv)
    for c in small_copies:
        c.start()
    small_all[d] = small[...]
    for copy in wide_loads:
        copy.wait()
    ring.panels[1].end()
    begin(4, branch, gelu_grad)
    for g in gate_scatters:
        g.first()
        g.second()
    push(4)
    lines[1].step(1)
    ring.panels[2].end()
    begin(5, branch, input_rows)
    ring.panels[4].third()
    lines[1].step(2)
    push(5)
    ring.panels[3].end()
    for g in gate_scatters:
        g.third()
    middle_load.wait()
    feed_line.total([input_grad.at[1]], more=True)
    output[0] = output_first[...]
    output[1] = input_grad[1].astype(BF16)
    quarter = pack.shape[1]
    for i in range(4):
        pack[4 + i : 5 + i, :] = mlp_part[:, i * quarter : (i + 1) * quarter]
    for s in range(seqs):
        lines[s].total([input_grad.at[i] for i in range(seqs)])
        change, gain_part = norm_back(act[s].astype(F32), gain[...][None], input_grad[s])
        input_grad[s] = change + grad_middle[s]
        for i in range(4):
            piece = gain_part[:, i * quarter : (i + 1) * quarter]
            if s == 0:
                pack[i : i + 1, :] = piece
            else:
                pack[i : i + 1, :] += piece
    pack_copies = dp_copies(pack, packs, psend, precv)
    for c in pack_copies:
        c.start()
    ring.panels[5].third()
    ring.panels[4].end()
    for g in gate_scatters:
        g.end()
    packs[d] = pack[...]
    for c in small_copies:
        c.wait_recv()
    sum_ = small_all[0]
    for i in range(1, 8):
        sum_ = sum_ + small_all[i]
    rate_grad[...] = sum_[0]
    taps_grad[...] = sum_[1:5]
    for c in pack_copies:
        c.wait_recv()
    sum_ = packs[0]
    for i in range(1, 8):
        sum_ = sum_ + packs[i]
    line_pack[...] = sum_
    z_copies = [
        pltpu.make_async_remote_copy(
            src_ref=line_pack,
            dst_ref=line_packs.at[t],
            send_sem=zsend.at[step - 1],
            recv_sem=zrecv.at[step - 1],
            device_id=(d, lax.rem(t + step, depth)),
            device_id_type=MESH,
        )
        for step in range(1, depth)
    ]
    for c in z_copies:
        c.start()
    line_packs[t] = sum_
    ring.panels[5].end()
    for c in z_copies:
        c.wait_recv()
    sum_ = line_packs[0]
    for i in range(1, depth):
        sum_ = sum_ + line_packs[i]
    for i in range(4):
        norm_grad[i * quarter : (i + 1) * quarter] = sum_[i]
        mlp_grad[i * quarter : (i + 1) * quarter] = sum_[4 + i]
    for c in small_copies + pack_copies + z_copies:
        c.wait_send()
    ring.end()
    for line in lines + [feed_line]:
        line.end()


def mixer_back_phase(
    branch, normed, saved, weights, normed_two, lift_rows, feed, middle, taps, rate, act, gain,
    grad_middle, mlp_part, output_first, depth,
):
    seqs, length, model = branch.shape
    tokens = seqs * length
    units = lift_rows.shape[1]
    gelu_w, input_w, gate_in_w, gate_dec_w, out_w = weights[:5]
    gelu_pre, input_pre, window, gate_in, gate_dec, states, mixed = saved
    width = out_w.shape[1]
    block = gate_in_w.shape[0]
    half = block // 2
    panel = (model // 8, PANEL)
    gate = (block // 8, width)
    pack = (8, model // 4)
    small = (8, width)
    flat = (tokens, width)
    outs = [
        shaped(act.shape, BF16, VMEM),
        shaped(act.shape, F32, VMEM),
        shaped((model,), F32, VMEM),
        shaped((model,), F32, VMEM),
        shaped((width,), F32, VMEM),
        shaped(taps.shape, F32, VMEM),
        shaped(gate, F32, VMEM),
        shaped(gate, F32, VMEM),
    ]
    outs += [shaped(panel, F32, ANY)] * 3 + [shaped((model // 8, units), F32, ANY)]
    scratch = [pltpu.VMEM((tokens, model), BF16)]
    scratch += [
        pltpu.VMEM(x.shape, x.dtype)
        for x in (
            out_w,
            input_w,
            gelu_pre,
            input_pre,
            window,
            gate_in,
            gate_dec,
            states,
            gate_in_w,
            gate_dec_w,
        )
    ]
    scratch += [pltpu.VMEM(flat, F32), pltpu.VMEM((seqs * (length + 8), width), F32)]
    scratch += [pltpu.VMEM(flat, BF16)] * 3
    scratch += [pltpu.VMEM((tokens, half), BF16)] * 2
    scratch += [pltpu.VMEM(gate_in_w.shape, BF16)] * 2
    scratch += [
        pltpu.VMEM((tokens, model), BF16),
        pltpu.VMEM((1 + taps.shape[0], 8, width), F32),
        DMA,
    ]
    scratch += line_scatter_scratch(seqs, length // depth, model, depth)
    scratch += [DMA((seqs,)), DMA((seqs,)), DMA((12 + 2 * seqs,)), DMA]
    scratch += [
        pltpu.VMEM(small, F32),
        pltpu.VMEM((8,) + small, F32),
        pltpu.VMEM(pack, F32),
        pltpu.VMEM((8,) + pack, F32),
        pltpu.VMEM(pack, F32),
        pltpu.VMEM((depth,) + pack, F32),
    ]
    scratch += [DMA((7,))] * 4 + [DMA((depth - 1,))] * 2
    scratch += ring_scratch(3, *panel)
    scratch += [pltpu.VMEM((length, model), BF16), pltpu.VMEM((tokens, PANEL), BF16)]
    scratch += line_scatter_scratch(1, length // depth, model, depth)
    scratch += scatter_scratch([gate] * 2, (False, False))
    scratch += [pltpu.VMEM(flat, BF16)]
    return call(
        functools.partial(mixer_back_kernel, depth),
        "mixer_back_phase",
        3,
        [ANY] * 18 + [VMEM] * 7,
        outs,
        scratch,
        (
            branch,
            normed,
            out_w,
            gelu_pre,
            input_pre,
            window,
            gate_in,
            gate_dec,
            states,
            mixed,
            gelu_w,
            input_w,
            gate_in_w,
            gate_dec_w,
            normed_two,
            lift_rows,
            feed,
            middle,
            taps,
            rate,
            act,
            gain,
            grad_middle,
            mlp_part,
            output_first,
        ),
        vmem=63 * 1024 * 1024,
    )


def finish_kernel(*refs):
    n = (len(refs) - 2) // 3
    ins, outs, held = refs[:n], refs[n : 2 * n], refs[2 * n : 3 * n]
    load_sem, save_sem = refs[3 * n :]
    loads = [pltpu.make_async_copy(ins[i], held[i], load_sem.at[i]) for i in range(n)]
    saves = [pltpu.make_async_copy(held[i], outs[i], save_sem.at[i]) for i in range(n)]
    for copy in loads:
        copy.start()
    for load, save in zip(loads, saves):
        load.wait()
        save.start()
    for save in saves:
        save.wait()


def finish(arrays):
    n = len(arrays)
    return pl.pallas_call(
        finish_kernel,
        name="finish",
        out_shape=[jax.ShapeDtypeStruct(x.shape, x.dtype) for x in arrays],
        in_specs=[ANY] * n,
        out_specs=[ANY] * n,
        scratch_shapes=[pltpu.VMEM(x.shape, x.dtype) for x in arrays] + [DMA((n,))] * 2,
        compiler_params=pltpu.CompilerParams(vmem_limit_bytes=62 * 1024 * 1024),
    )(*arrays)


def swapped(block, axis):
    count = lax.axis_size(axis)
    return lax.ppermute(block, axis, [(i, i ^ 1) for i in range(count)])


def normalize(value_entries, scale_gain):
    return (
        value_entries
        * lax.rsqrt(jnp.mean(value_entries * value_entries, axis=-1, keepdims=True) + EPS)
        * scale_gain
    )


def causal_conv(value_entries, kernel):
    summed = value_entries * kernel[0]
    for offset in range(1, kernel.shape[0]):
        shifted = jnp.concatenate(
            [jnp.zeros_like(value_entries[:, :offset]), value_entries[:, :-offset]], axis=1
        )
        summed = summed + shifted * kernel[offset]
    return summed


def decay_inputs(input_pre, decay_pre, conv_vals, decay_rate):
    log_decay = -8.0 * jax.nn.sigmoid(decay_pre) * decay_rate
    scaled = jnp.sqrt(-jnp.expm1(2.0 * log_decay))
    return (log_decay, scaled * jax.nn.sigmoid(input_pre) * conv_vals)


def recurrence(rate, drive):
    def join(left, right):
        return left[0] * right[0], left[1] * right[0] + right[1]

    return lax.associative_scan(join, (rate, drive), axis=1)[1]


def dot(spec, left, right):
    return jnp.einsum(spec, left, right, preferred_element_type=F32)


def weight_grad(left, right):
    return dot("pkr,pku->ru", left, right).astype(BF16)


class Fast:
    def __init__(self, depth, taps, rate):
        self.depth, self.taps, self.rate = depth, taps, rate

    def front(self, cotangent, token_weight, weights, act, gain, first_gain):
        middle, rows, self.weights, self.feeds, self.saved, self.held = front_phase(
            cotangent, token_weight, weights, self.taps, self.rate, act, gain, first_gain,
            self.depth,
        )
        self.normed, self.cot, self.normed_two = rows
        return middle

    def back(self, middle, gain, cotangent, token_weight, act, first_gain):
        grad_middle, branch, mlp_part, feed, lift_rows, output, down_grad, gate_grad = feed_phase(
            self.normed_two, self.cot, self.feeds, self.held, middle, gain, cotangent,
            token_weight, self.depth,
        )
        res = mixer_back_phase(
            branch, self.normed, self.saved, self.weights, self.normed_two, lift_rows, feed,
            middle, self.taps, self.rate, act, first_gain, grad_middle, mlp_part,
            output, self.depth,
        )
        output, input_grad, norm_grad, mlp_grad, rate_grad, taps_grad = res[:6]
        gate_in, gate_dec, out_grad, gelu_grad, input_w_grad, up_grad = res[6:]
        results = (
            output, input_grad, norm_grad, mlp_grad, rate_grad, taps_grad, gelu_grad, input_w_grad,
            gate_in, gate_dec, out_grad, gate_grad, up_grad, down_grad,
        )
        results = finish(results)
        return tuple(results[:6]) + (tuple(results[6:]),)


class Plain:
    def __init__(self, depth, taps, rate):
        self.depth, self.taps, self.rate = depth, taps, rate

    @staticmethod
    def wide(block):
        return lax.all_gather(block, "tensor", axis=1, tiled=True)

    @staticmethod
    def narrow(part):
        return lax.psum_scatter(part, "tensor", scatter_dimension=1, tiled=True).astype(F32)

    @staticmethod
    def full(shard):
        return lax.all_gather(shard, "dp", axis=0, tiled=True)

    @staticmethod
    def own(grad):
        return lax.psum_scatter(grad, "dp", scatter_dimension=0, tiled=True).astype(F32)

    def front(self, cotangent, token_weight, weights, act, gain, first_gain):
        cot = (cotangent.astype(F32) * token_weight).astype(BF16)
        normed = normalize(act.astype(F32), first_gain).astype(BF16)
        gelu_w, input_w, gate_in_w, gate_dec_w, out_w = (self.full(w) for w in weights[:5])
        self.feeds = tuple(self.full(w) for w in weights[5:])
        normed_all = self.wide(normed)
        seqs, length, _ = normed_all.shape
        channels = gelu_w.shape[1]
        block = gate_in_w.shape[0]
        half = block // 2
        width = channels + half
        parity = lax.axis_index("tensor") % 2
        gelu_pre = dot("kqg,ga->kqa", normed_all, gelu_w)
        input_pre = dot("kqg,ga->kqa", normed_all, input_w)
        gelu_out, gelu_back = jax.vjp(jax.nn.gelu, gelu_pre)
        conv_out, conv_back = jax.vjp(causal_conv, input_pre, self.taps)
        conv_bf = conv_out.astype(BF16)
        rim = lax.dynamic_slice_in_dim(conv_bf, (1 - parity) * (channels - half), half, 2)
        window = jnp.zeros((seqs, length, width), BF16)
        window = lax.dynamic_update_slice_in_dim(window, conv_bf, parity * half, 2)
        window = lax.dynamic_update_slice_in_dim(
            window, swapped(rim, "tensor"), (1 - parity) * channels, 2
        )
        tiles = window.reshape(seqs, length, width // block, block)
        placed = lax.dynamic_update_slice_in_dim(
            jnp.zeros((2, block, width), BF16), jnp.stack([gate_in_w, gate_dec_w]), parity * half, 2
        ).reshape(2, block, width // block, block)
        gates = dot("slbk,gkbc->gslbc", tiles, placed).reshape(2, seqs, length, width)
        gates = lax.dynamic_slice_in_dim(gates, parity * half, channels, 3)
        (log_decay, drive), gate_back = jax.vjp(
            decay_inputs, gates[0], gates[1], conv_bf.astype(F32), self.rate
        )
        decay = jnp.exp(log_decay)
        states = recurrence(decay, drive)
        mixed = (gelu_out * states).astype(BF16)
        self.kept = (
            normed_all, gelu_w, input_w, out_w, gelu_out, gelu_back, conv_back, tiles, placed,
            gate_back, decay, states, mixed,
        )
        part = dot("xgq,pq->xgp", mixed, out_w).astype(BF16)
        self.cot = self.wide(cot)
        middle = act.astype(F32) + self.narrow(part)
        self.normed_two = self.wide(normalize(middle, gain).astype(BF16))
        return middle

    def back(self, middle, gain, cotangent, token_weight, act, first_gain):
        cot_own = cotangent.astype(F32) * token_weight
        gate_w, up_w, down_w = self.feeds
        normed, cot = self.normed_two, self.cot
        gate_pre = dot("nwo,ob->nwb", normed, gate_w)
        lift_pre = dot("nwo,ob->nwb", normed, up_w)
        gate_act, activ_back = jax.vjp(jax.nn.gelu, gate_pre)
        hidden = (gate_act * lift_pre).astype(BF16)
        grad_hidden = dot("gre,eu->gru", cot, down_w)
        gate_grad = activ_back(grad_hidden * lift_pre)[0].astype(BF16)
        lift_grad = (grad_hidden * gate_act).astype(BF16)
        part = dot("mqa,ya->mqy", gate_grad, gate_w) + dot("mqa,ya->mqy", lift_grad, up_w)
        _, back = jax.vjp(normalize, middle, gain)
        change, gain_grad = back(self.narrow(part.astype(BF16)))
        grad = cot_own + change
        panels = (
            weight_grad(cot, hidden), weight_grad(normed, gate_grad), weight_grad(normed, lift_grad)
        )
        feed = dot("xav,tv->xat", hidden, down_w).astype(BF16)
        output = (middle + self.narrow(feed)).astype(BF16)
        branch = self.wide(grad.astype(BF16))
        (
            normed_all, gelu_w, input_w, out_w, gelu_out, gelu_back, conv_back, tiles, placed,
            gate_back, decay, states, mixed,
        ) = self.kept
        seqs, length, channels = states.shape
        block = tiles.shape[-1]
        half = block // 2
        width = channels + half
        parity = lax.axis_index("tensor") % 2
        grad_mixed = dot("xtz,zm->xtm", branch, out_w)
        gelu_grad = gelu_back(grad_mixed * states)[0].astype(BF16)
        later = jnp.concatenate([decay[:, 1:], jnp.zeros_like(decay[:, :1])], axis=1)
        grad_drive = jnp.flip(
            recurrence(jnp.flip(later, 1), jnp.flip(grad_mixed * gelu_out, 1)), 1
        )
        earlier = jnp.concatenate([jnp.zeros_like(states[:, :1]), states[:, :-1]], axis=1)
        grad_in, grad_dec, grad_conv, grad_rate = gate_back(
            (grad_drive * decay * earlier, grad_drive)
        )
        grads = lax.dynamic_update_slice_in_dim(
            jnp.zeros((2, seqs, length, width), BF16),
            jnp.stack([grad_in, grad_dec]).astype(BF16),
            parity * half,
            3,
        ).reshape(2, seqs, length, width // block, block)
        grad_window = dot("gslbc,gkbc->slbk", grads, placed).reshape(seqs, length, width)
        grad_placed = dot("slbk,gslbc->gkbc", tiles, grads).reshape(2, block, width)
        grad_gates = lax.dynamic_slice_in_dim(grad_placed, parity * half, channels, 2)
        rim = lax.dynamic_slice_in_dim(grad_window, (1 - parity) * channels, half, 2)
        rim = swapped(rim.astype(BF16), "tensor").astype(F32)
        grad_conv = grad_conv + lax.dynamic_slice_in_dim(grad_window, parity * half, channels, 2)
        start = (1 - parity) * (channels - half)
        rim = lax.dynamic_slice_in_dim(grad_conv, start, half, 2) + rim
        grad_conv = lax.dynamic_update_slice_in_dim(grad_conv, rim, start, 2)
        input_rows, grad_taps = conv_back(grad_conv)
        input_rows = input_rows.astype(BF16)
        part = dot("mzf,af->mza", gelu_grad, gelu_w) + dot("mzf,af->mza", input_rows, input_w)
        _, back = jax.vjp(normalize, act.astype(F32), first_gain)
        change, norm_grad = back(self.narrow(part.astype(BF16)))
        gains = lax.psum((norm_grad, gain_grad), ("dp", "tensor"))
        small = lax.psum((grad_rate, grad_taps), "dp")
        parts = (
            weight_grad(normed_all, gelu_grad),
            weight_grad(normed_all, input_rows),
            grad_gates[0].astype(BF16),
            grad_gates[1].astype(BF16),
            weight_grad(branch, mixed),
            panels[1],
            panels[2],
            panels[0],
        )
        own = [self.own(g) for g in parts]
        return (output, grad + change) + gains + small + (tuple(own),)


def shards(
    activations,
    norm_gain,
    gelu_proj,
    input_proj,
    conv_weight,
    gate_input,
    gate_decay,
    decay_rate,
    out_proj,
    mlp_gain,
    feed_gate,
    feed_up,
    feed_down,
    cotangent,
    lengths,
    batch_of,
):
    depth = lax.axis_size("tensor")
    fast = lax.axis_size("dp") == 8 and depth == 4
    run = (Fast if fast else Plain)(depth, conv_weight, decay_rate)
    tensor_index = lax.axis_index("tensor")
    data_index = lax.axis_index("dp")
    seq_count, row_count, _ = activations.shape
    full_length = row_count * depth
    members = (batch_of[:, None] == jnp.arange(MICRO)[None, :]).astype(F32)
    counts = jnp.sum(members * lengths[:, None].astype(F32), axis=0)
    total_seqs = lengths.shape[0]
    per_batch = float(total_seqs * full_length) / (MICRO * counts)
    weight_all = jnp.sum(members * per_batch[None, :], axis=1)
    my_weight = lax.dynamic_slice_in_dim(weight_all, data_index * seq_count, seq_count)
    my_length = lax.dynamic_slice_in_dim(lengths, data_index * seq_count, seq_count)
    places = tensor_index * row_count + jnp.arange(row_count)
    valid_mask = (places[None, :] < my_length[:, None]).astype(F32)
    token_weight = (valid_mask * my_weight[:, None])[:, :, None]

    weights = (
        gelu_proj, input_proj, gate_input, gate_decay, out_proj.T, feed_gate, feed_up, feed_down.T
    )
    middle = run.front(cotangent, token_weight, weights, activations, mlp_gain, norm_gain)
    output, input_grad, norm_grad, mlp_grad, rate_grad, taps_grad, grads = run.back(
        middle, mlp_gain, cotangent, token_weight, activations, norm_gain
    )
    return (
        output,
        input_grad,
        norm_grad,
        grads[0],
        grads[1],
        taps_grad,
        grads[2],
        grads[3],
        rate_grad,
        grads[4].T,
        mlp_grad,
        grads[5],
        grads[6],
        grads[7].T,
    )


def solution(mesh):
    placed = (
        P("dp", "tensor", None),
        P(),
        P("dp", "tensor"),
        P("dp", "tensor"),
        P(None, "tensor"),
        P("dp", "tensor"),
        P("dp", "tensor"),
        P("tensor"),
        P("tensor", "dp"),
        P(),
        P("dp", "tensor"),
        P("dp", "tensor"),
        P("tensor", "dp"),
        P("dp", "tensor", None),
        P(),
        P(),
    )
    return jax.shard_map(
        shards,
        mesh=mesh,
        in_specs=placed,
        out_specs=(
            P("dp", "tensor", None),
            P("dp", "tensor", None),
            P(),
            P("dp", "tensor"),
            P("dp", "tensor"),
            P(None, "tensor"),
            P("dp", "tensor"),
            P("dp", "tensor"),
            P("tensor"),
            P("tensor", "dp"),
            P(),
            P("dp", "tensor"),
            P("dp", "tensor"),
            P("tensor", "dp"),
        ),
        check_vma=False,
    )
```

```python
import functools

import jax
import jax.numpy as jnp
from jax import lax
from jax.experimental import pallas as pl
from jax.experimental.pallas import tpu as pltpu
from jax.sharding import PartitionSpec as P

MICRO = 4
EPS = 1e-06
MESH = pl.DeviceIdType.MESH
ANY = pl.BlockSpec(memory_space=pl.ANY)
VMEM = pl.BlockSpec(memory_space=pltpu.VMEM)
DMA = pltpu.SemaphoreType.DMA
BF16 = jnp.bfloat16
F32 = jnp.float32


def place():
    return lax.axis_index("dp"), lax.axis_index("tensor")


def greet(d, t, depth, dp_masks=(1, 2, 4), z_all=False, meanwhile=None):
    barrier = pltpu.get_barrier_semaphore()
    for mask in dp_masks:
        pl.semaphore_signal(barrier, inc=1, device_id=(d ^ mask, t), device_id_type=MESH)
    if z_all:
        for step in range(1, depth):
            pl.semaphore_signal(
                barrier, inc=1, device_id=(d, lax.rem(t + step, depth)), device_id_type=MESH
            )
        if meanwhile is not None:
            meanwhile()
        pl.semaphore_wait(barrier, len(dp_masks) + depth - 1)
        return

    @pl.when(t > 0)
    def _():
        pl.semaphore_signal(barrier, inc=1, device_id=(d, t - 1), device_id_type=MESH)

    @pl.when(t < depth - 1)
    def _():
        pl.semaphore_signal(barrier, inc=1, device_id=(d, t + 1), device_id_type=MESH)

    if meanwhile is not None:
        meanwhile()
    ends = jnp.where((t == 0) | (t == depth - 1), 1, 2)
    pl.semaphore_wait(barrier, len(dp_masks) + ends)


def add_rows(total, *terms, rows, step=32):
    step = min(step, rows)

    @pl.loop(0, rows, step=step)
    def _(start):
        part = pl.ds(pl.multiple_of(start, step), step)
        value = total[part, :]
        for term in terms:
            value = value + term[part, :]
        total[part, :] = value


class WeightGather:
    def __init__(self, shard, out, local, send, recv, d, t):
        rows = shard.shape[0]
        half = rows // 2

        def view(slot, start, size):
            if len(out.shape) == 3:
                return out.at[slot, pl.ds(start, size)]
            return out.at[pl.ds(pl.multiple_of(slot * rows + start, 16), size)]

        top, low = (0, half), (half, half)
        plan = [
            (None, d, top, 2),
            (None, d, low, 4),
            (None, d, low, 2),
            (None, d, top, 4),
            (2, d ^ 2, top, 4),
            (4, d ^ 4, low, 2),
            (None, d, top, 1),
            (None, d, low, 1),
            (2, d ^ 2, top, 1),
            (4, d ^ 4, low, 1),
            (2, d ^ 2, low, 1),
            (4, d ^ 4, top, 1),
            (6, d ^ 6, top, 1),
            (6, d ^ 6, low, 1),
        ]
        self.copies = [
            pltpu.make_async_remote_copy(
                src_ref=shard.at[pl.ds(*part)] if came is None else view(slot, *part),
                dst_ref=view(slot, *part),
                send_sem=send.at[i],
                recv_sem=recv.at[i],
                device_id=(d ^ mask, t),
                device_id_type=MESH,
            )
            for i, (came, slot, part, mask) in enumerate(plan)
        ]
        self.own = pltpu.make_async_copy(shard, view(d, 0, rows), local)

    def start(self):
        for i in (0, 1, 2, 3, 6, 7):
            self.copies[i].start()
        self.own.start()

    def relay(self):
        c = self.copies
        c[0].wait_recv()
        c[4].start()
        c[1].wait_recv()
        c[5].start()
        c[8].start()
        c[9].start()

    def relay_two(self):
        c = self.copies
        c[2].wait_recv()
        c[10].start()
        c[3].wait_recv()
        c[11].start()

    def relay_last(self):
        c = self.copies
        c[4].wait_recv()
        c[12].start()
        c[5].wait_recv()
        c[13].start()

    def arrive(self):
        for i in range(6, 14):
            self.copies[i].wait_recv()
        self.own.wait()

    def end(self):
        for i in range(14):
            self.copies[i].wait_send()


def gather_scratch(count):
    return [DMA((count,)), DMA((count, 14)), DMA((count, 14))]


class GradScatter:
    ORDER = (6, 2, 4, 0)

    def __init__(self, grad, out, own, core, diag, last, local, send, recv, d, t):
        self.out, self.core, self.diag, self.last = out, core, diag, last
        self.grad, self.d, self.t = grad, d, t
        self.credit = None
        self.reused = self.again = False
        self.before = self.flush = None
        self.rows = rows = out.shape[0]
        half = rows // 2
        self.half = half
        self.top, self.low = pl.ds(0, half), pl.ds(half, half)

        def block(slot, start=0, size=rows):
            return grad.at[pl.ds(pl.multiple_of(slot * rows + start, 16), size)]

        if own is None:
            self.loads = []
            self.mine = lambda i, start=0, size=rows: block(d ^ self.ORDER[i], start, size)
        else:
            self.loads = [
                pltpu.make_async_copy(block(d ^ r), own.at[i], local.at[i])
                for i, r in enumerate(self.ORDER)
            ]
            self.mine = lambda i, start=0, size=rows: own.at[i, pl.ds(start, size)]
        mine, top, low = self.mine, self.top, self.low
        plan = [(block(d ^ 1 ^ r), core.at[i], 1) for i, r in enumerate(self.ORDER)] + [
            (mine(0, 0, half), diag.at[0], 2),
            (mine(0, half, half), diag.at[1], 4),
            (mine(1, 0, half), last.at[0, top], 2),
            (mine(2, half, half), last.at[1, low], 4),
            (mine(2, 0, half), last.at[1, top], 4),
            (mine(1, half, half), last.at[0, low], 2),
        ]
        self.copies = [
            pltpu.make_async_remote_copy(
                src_ref=src,
                dst_ref=dst,
                send_sem=send.at[i],
                recv_sem=recv.at[i],
                device_id=(d ^ mask, t),
                device_id_type=MESH,
            )
            for i, (src, dst, mask) in enumerate(plan)
        ]

    def start(self):
        if self.reused:
            pl.semaphore_wait(self.credit.at[0], 1)
        for i in range(4):
            self.copies[i].start()
        for load in self.loads:
            load.start()

    def arrive(self, i):
        if self.loads:
            self.loads[i].wait()
        self.copies[i].wait_recv()

    def add(self, i, start, *terms):
        half = pl.ds(start, self.half)
        add_rows(self.mine(i, start, self.half), self.core.at[i, half], *terms, rows=self.half)

    def first(self):
        self.arrive(0)
        for i, start in enumerate((0, self.half)):
            self.add(0, start)
            if self.reused:
                pl.semaphore_wait(self.credit.at[1 + i], 1)
            self.copies[4 + i].start()

    def second(self):
        self.arrive(1)
        self.add(1, 0)
        self.copies[6].start()
        self.arrive(2)
        self.add(2, self.half)
        self.copies[7].start()

    def third(self):
        c = self.copies
        c[4].wait_recv()
        self.add(2, 0, self.diag.at[0])
        c[8].start()
        c[5].wait_recv()
        self.add(1, self.half, self.diag.at[1])
        c[9].start()

    def end(self):
        self.arrive(3)
        for i in (6, 7, 8, 9):
            self.copies[i].wait_recv()
        step = 16
        own = self.mine(3)
        if self.before is not None:
            self.before.flush.wait()

        @pl.loop(0, self.rows, step=step)
        def _(start):
            part = pl.ds(pl.multiple_of(start, step), step)
            self.out[part, :] = (
                own[part, :].astype(F32)
                + self.core[3, part, :].astype(F32)
                + self.last[0, part, :].astype(F32)
                + self.last[1, part, :].astype(F32)
            )

        if self.flush is not None:
            self.flush.start()
        for i in range(10):
            self.copies[i].wait_send()
        if self.again:
            for i, mask in enumerate((1, 2, 4)):
                pl.semaphore_signal(
                    self.credit.at[i], inc=1, device_id=(self.d ^ mask, self.t), device_id_type=MESH
                )


class PanelRing:
    def __init__(self, outs, scratch, d, t):
        grads, core, diag, last, stage, send, recv, credit, flush = scratch
        self.slots = slots = grads.shape[0]
        self.panels = []
        for i, out in enumerate(outs):
            q = i % slots
            panel = GradScatter(
                grads.at[q],
                stage.at[q],
                None,
                core.at[q],
                diag.at[q],
                last.at[q],
                None,
                send.at[q],
                recv.at[q],
                d,
                t,
            )
            panel.credit = credit.at[q]
            panel.reused = i >= slots
            panel.again = i + slots < len(outs)
            panel.before = self.panels[i - slots] if i >= slots else None
            panel.flush = pltpu.make_async_copy(stage.at[q], out, flush.at[q])
            self.panels.append(panel)

    def end(self):
        for panel in self.panels[-self.slots :]:
            panel.flush.wait()


def ring_scratch(slots, rows, n):
    return [
        pltpu.VMEM((slots, 8 * rows, n), BF16),
        pltpu.VMEM((slots, 4, rows, n), BF16),
        pltpu.VMEM((slots, 2, rows // 2, n), BF16),
        pltpu.VMEM((slots, 2, rows, n), BF16),
        pltpu.VMEM((slots, rows, n), F32),
        DMA((slots, 10)),
        DMA((slots, 10)),
        pltpu.SemaphoreType.REGULAR((slots, 3)),
        DMA((slots,)),
    ]


def scatter_scratch(shapes, loaded):
    own = [pltpu.VMEM((4,) + s, BF16) for s, far in zip(shapes, loaded) if far]
    core = [pltpu.VMEM((4,) + s, BF16) for s in shapes]
    diag = [pltpu.VMEM((2, s[0] // 2, s[1]), BF16) for s in shapes]
    last = [pltpu.VMEM((2,) + s, BF16) for s in shapes]
    n = len(shapes)
    return own + core + diag + last + [DMA((n, 4)), DMA((n, 10)), DMA((n, 10))]


def make_scatters(grads, outs, loaded, scratch, d, t):
    n = len(grads)
    scratch = list(scratch)
    own = [scratch.pop(0) if far else None for far in loaded]
    core, diag, last = (scratch[i * n : (i + 1) * n] for i in range(3))
    local, send, recv = scratch[3 * n :]
    return [
        GradScatter(
            grads[i],
            outs[i],
            own[i],
            core[i],
            diag[i],
            last[i],
            local.at[i],
            send.at[i],
            recv.at[i],
            d,
            t,
        )
        for i in range(n)
    ]


class LineGather:
    def __init__(self, block, out, local, send, recv, d, t, depth):
        self.block, self.out, self.send, self.recv = block, out, send, recv
        self.d, self.t, self.depth = d, t, depth
        self.rows = block.shape[-2]
        self.own = pltpu.make_async_copy(block, self.slot(t), local)

    def slot(self, j):
        rows = pl.ds(pl.multiple_of(j * self.rows, self.rows), self.rows)
        return self.out.at[:, rows] if len(self.out.shape) == 3 else self.out.at[rows]

    def copy(self, way, step, j, to):
        return pltpu.make_async_remote_copy(
            src_ref=self.block if step == 0 else self.slot(j),
            dst_ref=self.slot(j),
            send_sem=self.send.at[way, step],
            recv_sem=self.recv.at[way, step],
            device_id=(self.d, to),
            device_id_type=MESH,
        )

    def open(self, k):
        t, depth = self.t, self.depth
        if k == 0:
            self.own.start()

        @pl.when(t == k)
        def _():
            self.copy(0, 0, t, t + 1).start()

        @pl.when(t == depth - 1 - k)
        def _():
            self.copy(1, 0, t, t - 1).start()

    def step(self, s):
        t, depth = self.t, self.depth
        if s == 0:
            for k in range(depth - 1):
                self.open(k)
            return

        @pl.when((t - s >= 0) & (t < depth - 1))
        def _():
            self.copy(0, s - 1, t, t).wait_recv()
            self.copy(0, s, t - s, t + 1).start()

        @pl.when((t + s < depth) & (t > 0))
        def _():
            self.copy(1, s - 1, t, t).wait_recv()
            self.copy(1, s, t + s, t - 1).start()

    def finish(self):
        t, depth = self.t, self.depth
        self.own.wait()
        for s in range(depth - 1):

            @pl.when(t == depth - 1)
            def _():
                self.copy(0, s, t, t).wait_recv()

            @pl.when(t == 0)
            def _():
                self.copy(1, s, t, t).wait_recv()

    def end(self):
        t, depth = self.t, self.depth
        for s in range(depth - 1):

            @pl.when((t - s >= 0) & (t < depth - 1))
            def _():
                self.copy(0, s, t, t).wait_send()

            @pl.when((t + s < depth) & (t > 0))
            def _():
                self.copy(1, s, t, t).wait_send()


def line_gather_scratch(depth):
    return [DMA, DMA((2, depth - 1)), DMA((2, depth - 1))]


class LineScatter:
    def __init__(self, part, got, send, recv, d, t, depth, which=None, first_row=None):
        self.part, self.got, self.send, self.recv = part, got, send, recv
        self.d, self.t, self.depth = d, t, depth
        self.which = range(part.shape[0]) if which is None else which
        self.first_row = first_row
        self.rows = got.shape[3]

    def slot(self, way, j, s):
        return self.got.at[way, j - 1 if way == 0 else j, s]

    def copy(self, way, j, s, src, to):
        return pltpu.make_async_remote_copy(
            src_ref=src,
            dst_ref=self.slot(way, j, s),
            send_sem=self.send.at[way, j, s],
            recv_sem=self.recv.at[way, j, s],
            device_id=(self.d, to),
            device_id_type=MESH,
        )

    def block(self, j, s):
        start = j * self.rows
        if self.first_row is not None:
            start = pl.multiple_of(self.first_row + start, self.rows)
            return self.part.at[pl.ds(start, self.rows)]
        return self.part.at[s, pl.ds(pl.multiple_of(start, self.rows), self.rows)]

    def start(self, first=0, last=None):
        t, depth = self.t, self.depth
        steps = range(first, depth - 1 if last is None else last)

        @pl.when(t == 0)
        def _():
            for k in steps:
                for s in self.which:
                    j = depth - 1 - k
                    self.copy(0, j, s, self.block(j, s), t + 1).start()

        @pl.when(t == depth - 1)
        def _():
            for j in steps:
                for s in self.which:
                    self.copy(1, j, s, self.block(j, s), t - 1).start()

    def pass_on(self, way, j, to):
        for s in self.which:
            mine = self.slot(way, j, s)
            self.copy(way, j, s, mine, self.t).wait_recv()
            add_rows(mine, self.block(j, s), rows=self.rows)
            self.copy(way, j, s, mine, to).start()

    def step(self, k):
        t, depth = self.t, self.depth
        right = depth - 1 - k + t
        left = k - (depth - 1 - t)

        @pl.when((t > 0) & (t < right) & (right < depth))
        def _():
            self.pass_on(0, right, t + 1)

        @pl.when((left >= 0) & (left < t) & (t < depth - 1))
        def _():
            self.pass_on(1, left, t - 1)

    def total(self, out, more=False):
        t, depth = self.t, self.depth
        for s in self.which:
            own = self.block(t, s)[...].astype(F32)
            out[s][...] = out[s][...] + own if more else own

        @pl.when(t > 0)
        def _():
            for s in self.which:
                self.copy(0, t, s, self.slot(0, t, s), t).wait_recv()
                out[s][...] += self.got[0, t - 1, s].astype(F32)

        @pl.when(t < depth - 1)
        def _():
            for s in self.which:
                self.copy(1, t, s, self.slot(1, t, s), t).wait_recv()
                out[s][...] += self.got[1, t, s].astype(F32)

    def end(self):
        t, depth = self.t, self.depth
        for j in range(depth):
            for s in self.which:
                if j > 0:

                    @pl.when(j > t)
                    def _():
                        self.copy(0, j, s, self.slot(0, j, s), t).wait_send()

                if j < depth - 1:

                    @pl.when(j < t)
                    def _():
                        self.copy(1, j, s, self.slot(1, j, s), t).wait_send()


def line_scatter_scratch(seqs, rows, width, depth):
    return [
        pltpu.VMEM((2, depth - 1, seqs, rows, width), BF16),
        DMA((2, depth, seqs)),
        DMA((2, depth, seqs)),
    ]


def call(kernel, name, number, ins, outs, scratch, args, vmem=60 * 1024 * 1024):
    return pl.pallas_call(
        kernel,
        name=name,
        out_shape=[o[0] for o in outs],
        in_specs=ins,
        out_specs=[o[1] for o in outs],
        scratch_shapes=scratch,
        compiler_params=pltpu.CompilerParams(
            collective_id=number, has_side_effects=True, vmem_limit_bytes=vmem
        ),
    )(*args)


def shaped(shape, dtype, spec):
    return (jax.ShapeDtypeStruct(shape, dtype), spec)


def sigmoid(x):
    return 1.0 / (1.0 + jnp.exp(-x))


def one_less_exp(y):
    series = 1.0 + y / 6.0 * (1.0 + y / 7.0)
    for k in (5.0, 4.0, 3.0, 2.0):
        series = 1.0 + y / k * series
    return jnp.where(y > -0.5, -y * series, 1.0 - jnp.exp(y))


GELU_SCALE = 0.7978845608028654
GELU_CUBE = 0.044715


def gelu(x):
    return 0.5 * x * (1.0 + jnp.tanh(GELU_SCALE * (x + GELU_CUBE * x * x * x)))


def gelu_both(x):
    square = x * x
    bent = jnp.tanh(GELU_SCALE * (x + GELU_CUBE * square * x))
    half = 0.5 * (1.0 + bent)
    slope = half + 0.5 * x * (1.0 - bent * bent) * (
        GELU_SCALE * (1.0 + 3.0 * GELU_CUBE * square)
    )
    return x * half, slope


def rows_of(index, size):
    return pl.ds(pl.multiple_of(index * size, size), size)


def contract(left, right, dims):
    return lax.dot_general(left, right, ((dims[:1], dims[1:]), ((), ())), preferred_element_type=F32)


def scan_rows(rate, out, which, length, base=0, backward=False):
    tile = 8
    width = out.shape[1]
    row = lax.broadcasted_iota(jnp.int32, (tile, width), 0)

    def body(i, carried):
        k = length // tile - 1 - i if backward else i
        ends = []
        for at, s in enumerate(which):
            start = pl.multiple_of(s * length + k * tile, tile)
            rows = pl.ds(start, tile)
            if backward:
                pair = rate[pl.ds(start, 2 * tile), :]
                step = pltpu.roll(pair, 2 * tile - 1, 0)[:tile]
                step = jnp.where((row == tile - 1) & (i == 0), 0.0, step)
            else:
                step = rate[rows, :]
            held = pl.ds(pl.multiple_of(base + start, tile), tile)
            drive = out[held, :]
            for shift in (1, 2, 4):
                turn = tile - shift if backward else shift
                inside = row < tile - shift if backward else row >= shift
                before = jnp.where(inside, pltpu.roll(drive, turn, 0), 0.0)
                drive = drive + step * before
                step = step * jnp.where(inside, pltpu.roll(step, turn, 0), 1.0)
            states = drive + step * carried[at]
            out[held, :] = states
            ends.append(states[0:1] if backward else states[tile - 1 : tile])
        return tuple(ends)

    start = tuple(jnp.zeros((1, width), F32) for _ in which)
    lax.fori_loop(0, length // tile, body, start, unroll=2)


STRIP = 16
PANEL = 640


def gate_blocks(parity, width, block):
    half = block // 2
    shift = parity * half
    blocks = []
    for k in range((width + half) // block):
        low, high = k * block - shift, (k + 1) * block - shift
        blocks.append((k, max(low, 0), min(high, width)))
    return blocks


def front_kernel(
    depth,
    cotangent,
    token_weight,
    gelu_shard,
    input_shard,
    gate_in_shard,
    gate_dec_shard,
    out_shard,
    gate_in_place,
    up_in_place,
    down_in_place,
    taps,
    rate,
    act,
    gain,
    first_gain,
    middle,
    normed_out,
    cot_out,
    normed_two_out,
    gelu_full,
    input_full,
    gate_in_full,
    gate_dec_full,
    out_full,
    gate_full,
    up_full,
    down_full,
    gelu_pre_out,
    input_pre_out,
    window_out,
    gate_in_out,
    gate_dec_out,
    states_out,
    mixed_out,
    gate_pre_out,
    lift_pre_out,
    hidden_out,
    *scratch,
):
    normed, gelu_w, input_w, gate_in_w, gate_dec_w, out_w = scratch[:6]
    gelu_pre, input_pre, conv, window, gate_in, gate_dec, decay, states, mixed, part = scratch[6:16]
    local, send, recv = scratch[16:19]
    line_sems = [scratch[19 + 3 * i : 22 + 3 * i] for i in range(6)]
    rim_send, rim_recv, save_sem = scratch[37:40]
    cot, normed_two, block_two, panel_w, product = scratch[40:45]
    panel_sem, product_sem = scratch[45:47]
    got, ssem, rsem = scratch[47:50]
    normed_block, cot_block, hidden = scratch[50:53]
    gate_shard, up_shard, down_shard, shard_sem = scratch[53:57]
    sources = (gate_in_place, up_in_place, down_in_place)
    shard_loads = [
        pltpu.make_async_copy(source, shard, shard_sem.at[i])
        for i, (source, shard) in enumerate(zip(sources, (gate_shard, up_shard, down_shard)))
    ]
    for copy in shard_loads:
        copy.start()
    d, t = place()
    parity = lax.rem(t, 2)
    even = parity == 0
    odd = parity == 1

    def prepare():
        for s in range(act.shape[0]):
            value = act[s].astype(F32)
            inverse = lax.rsqrt(jnp.mean(value * value, axis=-1, keepdims=True) + EPS)
            normed_block[s] = (value * inverse * first_gain[...][None]).astype(BF16)
            cot_block[s] = (cotangent[s].astype(F32) * token_weight[s]).astype(BF16)

    greet(d, t, depth, meanwhile=prepare)
    seqs, length, model = normed.shape
    tokens = seqs * length
    width = conv.shape[1]
    block = gate_in_w.shape[0]
    half = block // 2
    spans = [pl.ds(s * length, length) for s in range(seqs)]
    firsts = [
        LineGather(normed_block.at[s], normed.at[s], *line_sems[5 * s], d, t, depth)
        for s in range(seqs)
    ]
    cots = [
        LineGather(cot_block.at[s], cot.at[spans[s]], *line_sems[1 + s], d, t, depth)
        for s in range(seqs)
    ]
    twos = [
        LineGather(block_two.at[s], normed_two.at[spans[s]], *line_sems[3 + s], d, t, depth)
        for s in range(seqs)
    ]
    scatters = [LineScatter(part, got, ssem, rsem, d, t, depth, (s,)) for s in range(seqs)]
    pairs = (
        (gelu_shard, gelu_w),
        (input_shard, input_w),
        (gate_in_shard, gate_in_w),
        (gate_dec_shard, gate_dec_w),
        (out_shard, out_w),
        (gate_shard, gate_full),
        (up_shard, up_full),
        (down_shard, down_full),
    )
    gathers = [
        WeightGather(shard, full, local.at[i], send.at[i], recv.at[i], d, t)
        for i, (shard, full) in enumerate(pairs)
    ]
    saves = []

    def save(src, dst):
        copy = pltpu.make_async_copy(src, dst, save_sem.at[len(saves)])
        copy.start()
        saves.append(copy)

    one = [gathers[1], gathers[0], gathers[2], gathers[3]]
    out_g, gate_g, up_g, down_g = gathers[4:]
    even_blocks, odd_blocks = gate_blocks(0, width, block), gate_blocks(1, width, block)

    def rim(s, to, src, dst):
        return pltpu.make_async_remote_copy(
            src_ref=conv.at[spans[s], pl.ds(src, half)],
            dst_ref=window.at[spans[s], pl.ds(dst, half)],
            send_sem=rim_send.at[s],
            recv_sem=rim_recv.at[s],
            device_id=(d, to),
            device_id_type=MESH,
        )

    def convolve(s):
        input_pre[s, 0:8, :] = jnp.zeros((8, width), F32)
        input_pre[s, 8 : 8 + length, :] = contract(normed[s], input_w[...], (1, 0))

        @pl.loop(0, length // STRIP)
        def _(i):
            near = input_pre[s, pl.ds(pl.multiple_of(i * STRIP, STRIP), STRIP + 8), :]
            total = taps[0:1, :] * near[8:]
            for k in range(1, taps.shape[0]):
                total = total + taps[k : k + 1, :] * pltpu.roll(near, k, 0)[8:]
            rows = pl.ds(pl.multiple_of(s * length + i * STRIP, STRIP), STRIP)
            conv[rows, :] = total.astype(BF16)

        @pl.when(even)
        def _():
            rim(s, t + 1, width - half, 0).start()
            window[spans[s], 0:width] = conv[spans[s], :]

        @pl.when(odd)
        def _():
            rim(s, t - 1, 0, width).start()
            window[spans[s], half : half + width] = conv[spans[s], :]

    def gates(s, blocks):
        for k, low, high in blocks:
            near = window[spans[s], k * block : (k + 1) * block]
            gate_in[spans[s], low:high] = contract(near, gate_in_w[:, low:high], (1, 0))
            gate_dec[spans[s], low:high] = contract(near, gate_dec_w[:, low:high], (1, 0))

    def inner_gates(s):
        gelu_pre[spans[s], :] = contract(normed[s], gelu_w[...], (1, 0))

        @pl.when(even)
        def _():
            gates(s, even_blocks[:-1])

        @pl.when(odd)
        def _():
            gates(s, odd_blocks[1:])

    def recur(s):
        @pl.when(even)
        def _():
            rim(s, t + 1, width - half, width).wait_recv()
            gates(s, even_blocks[-1:])

        @pl.when(odd)
        def _():
            rim(s, t - 1, 0, 0).wait_recv()
            gates(s, odd_blocks[:1])

        @pl.loop(0, length // STRIP)
        def _(i):
            start = pl.multiple_of(s * length + i * STRIP, STRIP)
            rows = pl.ds(start, STRIP)
            log = -8.0 * sigmoid(gate_dec[rows, :]) * rate[...][None]
            decay[rows, :] = jnp.exp(log)
            drive = jnp.sqrt(one_less_exp(2.0 * log)) * sigmoid(gate_in[rows, :])
            held = pl.ds(pl.multiple_of(start + 8, 8), STRIP)
            states[held, :] = drive * conv[rows, :].astype(F32)

        scan_rows(decay, states, (s,), length, base=8)

    def mix(s):
        @pl.loop(0, length // STRIP)
        def _(i):
            start = pl.multiple_of(s * length + i * STRIP, STRIP)
            rows, held = pl.ds(start, STRIP), pl.ds(pl.multiple_of(start + 8, 8), STRIP)
            mixed[rows, :] = (gelu(gelu_pre[rows, :]) * states[held, :]).astype(BF16)

        panel = 512

        @pl.loop(0, model // panel)
        def _(i):
            columns = rows_of(i, panel)
            part[s, :, columns] = contract(mixed[spans[s], :], out_w[columns, :], (1, 1)).astype(
                BF16
            )

    def norm_step(s):
        scatters[s].total([middle.at[i] for i in range(seqs)])
        value = middle[s] + act[s].astype(F32)
        middle[s] = value
        inverse = lax.rsqrt(jnp.mean(value * value, axis=-1, keepdims=True) + EPS)
        block_two[s] = (value * inverse * gain[...][None]).astype(BF16)
        twos[s].step(0)

    firsts[0].step(0)
    for g in one:
        g.start()
    firsts[0].step(1)
    firsts[1].step(0)
    for g in one:
        g.relay()
    out_g.start()
    firsts[0].step(2)
    for line in cots:
        line.open(0)
    for g in one:
        g.relay_two()
    firsts[1].step(1)
    for g in one:
        g.relay_last()
    firsts[0].finish()
    for line in cots:
        line.open(1)
    one[0].arrive()
    states[0:8, :] = jnp.zeros((8, width), F32)
    convolve(0)
    out_g.relay()
    for copy in shard_loads:
        copy.wait()
    gate_g.start()
    up_g.start()
    for g in one[1:]:
        g.arrive()
    inner_gates(0)
    out_g.relay_two()
    firsts[1].step(2)
    recur(0)
    out_g.relay_last()
    out_g.arrive()
    mix(0)
    firsts[1].finish()
    scatters[0].start(0, 1)
    for line in cots:
        line.open(2)
    convolve(1)
    scatters[0].start(1)
    inner_gates(1)
    scatters[0].step(1)
    gate_g.relay()
    recur(1)
    scatters[0].step(2)
    mix(1)
    scatters[1].start()
    save(normed, normed_out)
    save(gelu_w, gelu_full)
    save(input_w, input_full)
    save(gate_in_w, gate_in_full)
    save(gate_dec_w, gate_dec_full)
    save(out_w, out_full)
    save(gelu_pre, gelu_pre_out)
    save(input_pre, input_pre_out)
    save(window, window_out)
    save(gate_in, gate_in_out)
    save(gate_dec, gate_dec_out)
    save(states, states_out)
    save(mixed, mixed_out)
    gate_g.relay_two()
    scatters[1].step(1)
    norm_step(0)
    up_g.relay()
    down_g.start()
    scatters[1].step(2)
    up_g.relay_two()
    twos[0].step(1)
    norm_step(1)
    twos[0].step(2)
    gate_g.relay_last()
    twos[1].step(1)
    for line in cots:
        line.step(1)
    twos[1].step(2)
    for line in cots:
        line.step(2)
    up_g.relay_last()
    panels = down_full.shape[1] // PANEL

    kinds = ((gate_full, gate_pre_out), (up_full, lift_pre_out))
    order = [(s, p, i) for s in range(seqs) for p in range(panels) for i in range(2)]

    def load_panel(at):
        _, p, i = order[at]
        columns = pl.ds(p * PANEL, PANEL)
        copy = pltpu.make_async_copy(
            kinds[i][0].at[:, columns], panel_w.at[at % 2], panel_sem.at[at % 2]
        )
        copy.start()
        return copy

    results = [[], []]

    def store(src, out, s, p, i):
        columns = pl.ds(p * PANEL, PANEL)
        copy = pltpu.make_async_copy(src, out.at[spans[s], columns], product_sem.at[3 * s + i])
        copy.start()
        results[s].append(copy)

    def multiply(s, p):
        nonlocal loaded
        while results[s]:
            results[s].pop().wait()
        for i, (_, out) in enumerate(kinds):
            at = (s * panels + p) * 2 + i
            loaded.wait()
            if at + 1 < len(order):
                loaded = load_panel(at + 1)
            product[i, spans[s], :] = contract(normed_two[spans[s], :], panel_w[at % 2], (1, 0))
            store(product.at[i, spans[s]], out, s, p, i)

        @pl.loop(0, length // STRIP)
        def _(k):
            rows = pl.ds(pl.multiple_of(s * length + k * STRIP, STRIP), STRIP)
            hidden[rows, :] = (gelu(product[0, rows, :]) * product[1, rows, :]).astype(BF16)

        store(hidden.at[spans[s]], hidden_out, s, p, 2)

    gate_g.arrive()
    loaded = load_panel(0)
    up_g.arrive()
    twos[0].finish()
    multiply(0, 0)
    down_g.relay()
    multiply(0, 1)
    multiply(0, 2)
    down_g.relay_two()
    twos[1].finish()
    multiply(1, 0)
    multiply(1, 1)
    multiply(1, 2)
    save(normed_two, normed_two_out)
    for line in cots:
        line.finish()
    save(cot, cot_out)
    down_g.relay_last()
    down_g.arrive()

    for s in range(seqs):

        @pl.when(even)
        def _():
            rim(s, t + 1, width - half, 0).wait_send()

        @pl.when(odd)
        def _():
            rim(s, t - 1, 0, width).wait_send()

    for g in gathers:
        g.end()
    for line in firsts + cots + twos + scatters:
        line.end()
    for copy in saves + results[0] + results[1]:
        copy.wait()


def front_phase(cotangent, token_weight, weights, taps, rate, act, gain, first_gain, depth):
    seqs, rows, model = act.shape
    length = rows * depth
    tokens = seqs * length
    n = len(weights)
    block, width = weights[2].shape[0] * 8, weights[0].shape[1]
    units = weights[-1].shape[1]
    wide = block // 2 + width
    wide_rows = (seqs, length, model)
    mixers = [(model, width), (model, width), (block, width), (block, width), (model, width)]
    saved = [
        ((tokens, width), F32),
        ((seqs, length + 8, width), F32),
        ((tokens, wide), BF16),
        ((tokens, width), F32),
        ((tokens, width), F32),
        ((tokens + 8, width), F32),
        ((tokens, width), BF16),
    ]
    outs = [shaped(act.shape, F32, VMEM)]
    outs += [shaped(wide_rows, BF16, ANY)] + [shaped((tokens, model), BF16, ANY)] * 2
    outs += [shaped(shape, BF16, ANY) for shape in mixers]
    outs += [shaped((model, units), BF16, ANY)] * 3
    outs += [shaped(shape, dtype, ANY) for shape, dtype in saved]
    outs += [shaped((tokens, units), F32, ANY)] * 2 + [shaped((tokens, units), BF16, ANY)]
    saved_scratch = saved[:2] + [((tokens, width), BF16)] + saved[2:5] + [((tokens, width), F32)]
    saved_scratch += saved[5:] + [(wide_rows, BF16)]
    scratch = [pltpu.VMEM(wide_rows, BF16)]
    scratch += [pltpu.VMEM(shape, BF16) for shape in mixers]
    scratch += [pltpu.VMEM(shape, dtype) for shape, dtype in saved_scratch]
    scratch += gather_scratch(n) + line_gather_scratch(depth) * 6 + [DMA((seqs,)), DMA((seqs,)), DMA((16,))]
    scratch += [
        pltpu.VMEM((tokens, model), BF16),
        pltpu.VMEM((tokens, model), BF16),
        pltpu.VMEM(act.shape, BF16),
        pltpu.VMEM((2, model, PANEL), BF16),
        pltpu.VMEM((2, tokens, PANEL), F32),
        DMA((2,)),
        DMA((6,)),
    ]
    scratch += line_scatter_scratch(seqs, rows, model, depth)
    scratch += [pltpu.VMEM(act.shape, BF16)] * 2 + [pltpu.VMEM((tokens, PANEL), BF16)]
    scratch += [pltpu.VMEM(w.shape, BF16) for w in weights[-3:]] + [DMA((3,))]
    res = call(
        functools.partial(front_kernel, depth),
        "front_phase",
        0,
        [VMEM] * (n - 1) + [ANY] * 3 + [VMEM] * 5,
        outs,
        scratch,
        (cotangent, token_weight)
        + tuple(weights)
        + (taps, rate, act, gain, first_gain),
    )
    return res[0], res[1:4], res[4:9], res[9:12], res[12:19], res[19:]


def norm_back(value, gain, error):
    inverse = lax.rsqrt(jnp.mean(value * value, axis=-1, keepdims=True) + EPS)
    scaled = error * gain
    mean = jnp.mean(scaled * value, axis=-1, keepdims=True)
    grad = inverse * scaled - value * (inverse * inverse * inverse * mean)
    return grad, jnp.sum(error * value * inverse, axis=0, keepdims=True)


def feed_kernel(
    depth,
    normed_in,
    cot_in,
    gate_in,
    up_in,
    down_in,
    gate_pre_in,
    lift_pre_in,
    hidden_in,
    middle,
    gain,
    cotangent,
    token_weight,
    grad,
    wide,
    gain_grad,
    feed_out,
    lift_rows_out,
    output_first,
    down_out,
    gate_out,
    *refs,
):
    panels = gate_in.shape[1] // PANEL
    outs = [
        out.at[:, pl.ds(p * PANEL, PANEL)] for out in (down_out, gate_out) for p in range(panels)
    ]
    normed, cot, hidden, gate_rows, lift_rows = refs[:5]
    gate_w, up_w, down_w, gate_pre, lift_pre, grad_hidden, acc, part, block, feed_part = refs[5:15]
    got, ssem, rsem = refs[15:18]
    load_sem, weight_sem, save_sem = refs[18:21]
    lines = refs[21:24], refs[24:27]
    feed_got, feed_ssem, feed_rsem = refs[27:30]
    d, t = place()
    greet(d, t, depth)
    seqs = middle.shape[0]
    tokens, model = normed_in.shape
    length = tokens // seqs
    tile = 512
    ring = PanelRing(outs, refs[30:], d, t)
    scatters = [LineScatter(part, got, ssem, rsem, d, t, depth, (s,)) for s in range(seqs)]
    early_feed = LineScatter(feed_part, feed_got, feed_ssem, feed_rsem, d, t, depth, (0,), 0)
    gathers = [
        LineGather(block.at[s], wide.at[s], *lines[s], d, t, depth) for s in range(seqs)
    ]

    def load(i, src, dst):
        copy = pltpu.make_async_copy(src, dst, load_sem.at[i])
        copy.start()
        return copy

    def weight(i, src, dst, p):
        copy = pltpu.make_async_copy(
            src.at[:, pl.ds(p * PANEL, PANEL)], dst, weight_sem.at[i]
        )
        copy.start()
        return copy

    def held_rows(s, p):
        rows, columns = pl.ds(s * length, length), pl.ds(p * PANEL, PANEL)
        q = (s * panels + p) % 2
        return [
            load(2 + q, gate_pre_in.at[rows, columns], gate_pre.at[q]),
            load(4 + q, lift_pre_in.at[rows, columns], lift_pre.at[q]),
        ]

    hidden_load = load(6, hidden_in, hidden)
    cot_load = load(1, cot_in, cot)
    down_loads = [weight(p, down_in, w, p) for p, w in enumerate((gate_w, up_w, down_w))]
    row_loads = held_rows(0, 0)
    normed_load = load(0, normed_in, normed)

    def forward(s, p, more):
        nonlocal down_load, gate_load, up_load, row_loads
        rows = pl.ds(s * length, length)
        columns = pl.ds(p * PANEL, PANEL)
        q = (s * panels + p) % 2
        down_load.wait()
        grad_hidden[...] = contract(cot[rows, :], down_w[...], (1, 0))
        for copy in row_loads:
            copy.wait()
        if more is not None:
            down_load = weight(2, down_in, down_w, more)
            row_loads = held_rows(*((s, more) if more > p else (s + 1, more)))

        @pl.loop(0, length // STRIP)
        def _(i):
            strip = rows_of(i, STRIP)
            held = pl.ds(pl.multiple_of(s * length + i * STRIP, STRIP), STRIP)
            act, slope = gelu_both(gate_pre[q, strip, :])
            lift = lift_pre[q, strip, :]
            came = grad_hidden[strip, :]
            gate_rows[held, columns] = (came * lift * slope).astype(BF16)
            lift_rows[held, columns] = (came * act).astype(BF16)

        gate_load.wait()
        up_load.wait()

        @pl.loop(0, model // tile)
        def _(i):
            out = rows_of(i, tile)
            value = contract(gate_rows[rows, columns], gate_w[out, :], (1, 1))
            value = value + contract(lift_rows[rows, columns], up_w[out, :], (1, 1))
            if p == 0:
                acc[:, out] = value
            elif p < panels - 1:
                acc[:, out] += value
            else:
                part[s, :, out] = (acc[:, out] + value).astype(BF16)

        if more is not None:
            gate_load = weight(0, gate_in, gate_w, more)
            up_load = weight(1, up_in, up_w, more)

    kinds = ((cot, hidden), (normed, gate_rows), (normed, lift_rows))

    def weight_grad(i, out):
        left, right = kinds[i // panels]
        columns = pl.ds(i % panels * PANEL, PANEL)

        @pl.loop(0, model // tile)
        def _(k):
            rows = rows_of(k, tile)
            out[rows, :] = contract(left[:, rows], right[:, columns], (0, 0)).astype(BF16)

    def begin(i):
        panel = ring.panels[i]
        weight_grad(i, panel.grad)
        panel.start()

    def push(i):
        ring.panels[i].first()
        ring.panels[i].second()

    def norm_step(s):
        scatters[s].total([grad.at[i] for i in range(seqs)])
        change, gain_part = norm_back(middle[s], gain[...][None], grad[s])
        change = change + cotangent[s].astype(F32) * token_weight[s]
        grad[s] = change
        block[s] = change.astype(BF16)
        if s == 0:
            gain_grad[...] = gain_part
        else:
            gain_grad[...] += gain_part

    def feed(s, out):
        rows = pl.ds(s * length, length)
        downs = (gate_w, up_w, down_w)

        @pl.loop(0, model // tile)
        def _(i):
            columns = rows_of(i, tile)
            value = contract(hidden[rows, 0:PANEL], downs[0][columns, :], (1, 1))
            for p in range(1, panels):
                units = pl.ds(p * PANEL, PANEL)
                value = value + contract(hidden[rows, units], downs[p][columns, :], (1, 1))
            out[:, columns] = value.astype(BF16)

    saves = []

    def save(i, src, dst):
        copy = pltpu.make_async_copy(src, dst, save_sem.at[i])
        copy.start()
        saves.append(copy)

    hidden_load.wait()
    cot_load.wait()
    begin(0)
    for copy in down_loads:
        copy.wait()
    feed(0, feed_part)
    early_feed.start()
    down_load = weight(2, down_in, down_w, 0)
    gate_load = weight(0, gate_in, gate_w, 0)
    up_load = weight(1, up_in, up_w, 0)
    push(0)
    forward(0, 0, 1)
    begin(1)
    early_feed.step(1)
    forward(0, 1, 2)
    early_feed.step(2)
    ring.panels[0].third()
    push(1)
    forward(0, 2, 0)
    scatters[0].start()
    forward(1, 0, 1)
    scatters[0].step(1)
    ring.panels[0].end()
    ring.panels[1].third()
    begin(2)
    scatters[0].step(2)
    forward(1, 1, 2)
    push(2)
    norm_step(0)
    gathers[0].step(0)
    forward(1, 2, None)
    down_loads = [weight(0, down_in, gate_w, 0), weight(1, down_in, up_w, 1)]
    down_loads.append(weight(2, down_in, down_w, 2))
    scatters[1].start()
    save(2, lift_rows, lift_rows_out)
    gathers[0].step(1)
    ring.panels[1].end()
    ring.panels[2].third()
    normed_load.wait()
    begin(3)
    scatters[1].step(1)
    gathers[0].step(2)
    push(3)
    begin(4)
    scatters[1].step(2)
    ring.panels[2].end()
    ring.panels[3].third()
    for copy in down_loads:
        copy.wait()
    feed(1, cot.at[pl.ds(length, length)])
    save(1, cot.at[pl.ds(length, length)], feed_out)
    push(4)
    norm_step(1)
    gathers[1].step(0)
    ring.panels[3].end()
    begin(5)
    ring.panels[4].third()
    total = acc.at[pl.ds(0, middle.shape[1])]
    early_feed.total([total])
    output_first[...] = (total[...] + middle[0]).astype(BF16)
    gathers[1].step(1)
    push(5)
    ring.panels[4].end()
    gathers[1].step(2)
    ring.panels[5].third()
    for line in gathers:
        line.finish()
    ring.panels[5].end()
    ring.end()
    for copy in saves:
        copy.wait()
    for line in scatters + gathers + [early_feed]:
        line.end()


def feed_phase(normed, cot, weights, held, middle, gain, cotangent, token_weight, depth):
    gate_w, up_w, down_w = weights
    seqs, rows, model = middle.shape
    tokens = normed.shape[0]
    length = tokens // seqs
    wide_rows = (seqs, length, model)
    units = gate_w.shape[1]
    outs = [
        shaped(middle.shape, F32, VMEM),
        shaped(wide_rows, BF16, ANY),
        shaped((1, model), F32, VMEM),
        shaped((length, model), BF16, ANY),
        shaped((tokens, units), BF16, ANY),
        shaped(middle.shape[1:], BF16, VMEM),
    ] + [shaped((model // 8, units), F32, ANY)] * 2
    scratch = [pltpu.VMEM((tokens, model), BF16)] * 2
    scratch += [pltpu.VMEM((tokens, units), BF16)] * 3
    scratch += [pltpu.VMEM((model, PANEL), BF16)] * 3
    scratch += [pltpu.VMEM((2, length, PANEL), F32)] * 2 + [pltpu.VMEM((length, PANEL), F32)]
    scratch += [
        pltpu.VMEM((length, model), F32),
        pltpu.VMEM(wide_rows, BF16),
        pltpu.VMEM(middle.shape, BF16),
        pltpu.VMEM((length, model), BF16),
    ]
    scratch += line_scatter_scratch(seqs, rows, model, depth)
    scratch += [DMA((7,)), DMA((3,)), DMA((3,))]
    scratch += line_gather_scratch(depth) * 2
    scratch += line_scatter_scratch(1, rows, model, depth)
    scratch += ring_scratch(3, model // 8, PANEL)
    return call(
        functools.partial(feed_kernel, depth),
        "feed_phase",
        2,
        [ANY] * 8 + [VMEM] * 4,
        outs,
        scratch,
        (normed, cot, gate_w, up_w, down_w) + tuple(held) + (middle, gain, cotangent, token_weight),
        vmem=63 * 1024 * 1024,
    )


def mixer_back_kernel(
    depth,
    branch_in,
    normed_in,
    out_w_in,
    gelu_pre_in,
    input_pre_in,
    window_in,
    gate_in_in,
    gate_dec_in,
    states_in,
    mixed_in,
    gelu_w_in,
    input_w_in,
    gate_in_w_in,
    gate_dec_w_in,
    normed_two_in,
    lift_rows_in,
    feed_in,
    middle_in,
    taps,
    rate,
    act,
    gain,
    grad_middle,
    mlp_part,
    output_first,
    *refs,
):
    output, input_grad, norm_grad, mlp_grad, rate_grad, taps_grad = refs[:6]
    gate_in_out, gate_dec_out, out_out, gelu_out, input_out, up_out = refs[6:12]
    scratch = refs[12:]
    panels = up_out.shape[1] // PANEL
    ups = [up_out.at[:, pl.ds(p * PANEL, PANEL)] for p in range(panels)]
    branch, weight, input_w = scratch[:3]
    gelu_pre, input_pre, window, gate_in, gate_dec, states, gate_in_w, gate_dec_w = scratch[3:11]
    grad, decay, gelu_grad, grad_in, grad_dec = scratch[11:16]
    input_rows = scratch[-1]
    grad_conv = [decay.at[pl.ds(s * (decay.shape[0] // 2), decay.shape[0] // 2)] for s in range(2)]
    rim_out, rim_in, gate_in_grad, gate_dec_grad, part, sums = scratch[16 : 22]
    panel_sem = scratch[22]
    got, ssem, rsem = scratch[23 : 26]
    rim_send, rim_recv, load_sem, feed_sem = scratch[26 : 30]
    small, small_all, pack, packs, line_pack, line_packs = scratch[30 : 36]
    psend, precv, qsend, qrecv, zsend, zrecv = scratch[36 : 42]
    d, t = place()
    ring = PanelRing([out_out] + ups + [gelu_out, input_out], scratch[42 : 51], d, t)
    feed, lift_rows, feed_got, feed_ssem, feed_rsem = scratch[51 : 56]
    parity = lax.rem(t, 2)
    even = parity == 0
    odd = parity == 1
    greet(d, t, depth, dp_masks=(1, 2, 3, 4, 5, 6, 7), z_all=True)
    seqs, length, model = branch_in.shape
    tokens = seqs * length
    width = gate_in.shape[1]
    block = gate_in_w.shape[0]
    half = block // 2
    even_blocks, odd_blocks = gate_blocks(0, width, block), gate_blocks(1, width, block)
    gate_scatters = make_scatters(
        (gate_in_grad, gate_dec_grad),
        (gate_in_out, gate_dec_out),
        (False, False),
        scratch[56:-1],
        d,
        t,
    )
    feed_line = LineScatter(feed, feed_got, feed_ssem, feed_rsem, d, t, depth, (0,), 0)
    lines = [
        LineScatter(part, got, ssem, rsem, d, t, depth, (s,), s * length) for s in range(seqs)
    ]

    def load(i, src, dst):
        copy = pltpu.make_async_copy(src, dst, load_sem.at[i])
        copy.start()
        return copy

    def load_wide(i, src, dst):
        spans = [pl.ds(s * length, length) for s in range(seqs)]
        return [
            load(i + s, src.at[s] if len(src.shape) == 3 else src.at[rows], dst.at[rows])
            for s, rows in enumerate(spans)
        ]

    early = [load(0, out_w_in, weight)] + load_wide(12, branch_in, branch)
    next_ = [
        load(2, gelu_pre_in, gelu_pre),
        load(3, states_in, states),
        load(4, gate_dec_in, gate_dec),
    ]
    feed_load = pltpu.make_async_copy(feed_in, feed, feed_sem)
    feed_load.start()

    def dp_copies(src, dst, send, recv):
        return [
            pltpu.make_async_remote_copy(
                src_ref=src,
                dst_ref=dst.at[d],
                send_sem=send.at[mask - 1],
                recv_sem=recv.at[mask - 1],
                device_id=(d ^ mask, t),
                device_id_type=MESH,
            )
            for mask in range(1, 8)
        ]

    def weight_grad(left, right, out):
        panel = 512

        @pl.loop(0, model // panel)
        def _(i):
            columns = rows_of(i, panel)
            out[columns, :] = contract(left[:, columns], right[...], (0, 0)).astype(BF16)

    def begin(i, left, right):
        weight_grad(left, right, ring.panels[i].grad)
        ring.panels[i].start()

    def push(i):
        ring.panels[i].first()
        ring.panels[i].second()

    def load_lift(p):
        copy = pltpu.make_async_copy(
            lift_rows_in.at[:, pl.ds(p * PANEL, PANEL)], lift_rows, panel_sem
        )
        copy.start()
        return copy

    mixed_load = load(1, mixed_in, lift_rows)
    two_loads = load_wide(12 + seqs, normed_two_in, part)
    then = [
        load(5, gate_in_in, gate_in),
        load(7, window_in, window),
        load(8, gate_in_w_in, gate_in_w),
        load(9, gate_dec_w_in, gate_dec_w),
        load(10, input_pre_in, input_pre),
        load(11, input_w_in, input_w),
    ]
    for copy in early:
        copy.wait()
    feed_load.wait()
    feed_line.start()
    mixed_load.wait()
    begin(0, branch, lift_rows)
    lift_load = load_lift(0)
    for s in range(seqs):
        rows = pl.ds(s * length, length)
        grad[rows, :] = contract(branch[rows, :], weight[...], (1, 0))
    reload = load(0, gelu_w_in, weight)
    wide_loads = load_wide(12, normed_in, branch)
    push(0)
    for copy in two_loads:
        copy.wait()
    lift_load.wait()
    begin(1, part, lift_rows)
    lift_load = load_lift(1)
    for copy in next_:
        copy.wait()
    spans = [pl.ds(s * length, length) for s in range(seqs)]
    sums[...] = jnp.zeros(sums.shape, F32)

    def fold(value):
        return value[0:8] + value[8:16]

    own_columns = pl.ds(pl.multiple_of(parity * half, half), width)
    first_row = lax.broadcasted_iota(jnp.int32, (STRIP, width), 0) == 0

    def states_back(s):
        @pl.loop(0, length // STRIP)
        def _(i):
            start = pl.multiple_of(s * length + i * STRIP, STRIP)
            rows, held = pl.ds(start, STRIP), pl.ds(pl.multiple_of(start + 8, 8), STRIP)
            act, slope = gelu_both(gelu_pre[rows, :])
            came = grad[rows, :]
            gelu_grad[rows, :] = (came * states[held, :] * slope).astype(BF16)
            grad[rows, :] = came * act
            decay[rows, :] = jnp.exp(-8.0 * sigmoid(gate_dec[rows, :]) * rate[...][None])

        end = (s + 1) * length
        decay[end : end + 8, :] = jnp.zeros((8, width), F32)
        scan_rows(decay, grad, (s,), length, backward=True)

    def drive_back(s):
        @pl.loop(0, length // STRIP)
        def _(i):
            start = pl.multiple_of(s * length + i * STRIP, STRIP)
            rows = pl.ds(start, STRIP)
            earlier = pltpu.roll(states[pl.ds(start, STRIP + 8), :], 1, 0)[8:]
            earlier = jnp.where(first_row & (i == 0), 0.0, earlier)
            came = grad[rows, :]
            open_in = sigmoid(gate_in[rows, :])
            open_dec = sigmoid(gate_dec[rows, :])
            slow = -8.0 * rate[...][None]
            lost = one_less_exp(2.0 * open_dec * slow)
            root = jnp.sqrt(lost)
            value = window[rows, own_columns].astype(F32)
            step = jnp.exp(open_dec * slow)
            through = came * open_in
            grad_log = step * (came * earlier - through * value * step / root)
            sums[0] += fold(grad_log * (-8.0 * open_dec))
            through = through * root
            grad_conv[s][pl.ds(pl.multiple_of(i * STRIP, STRIP), STRIP), :] = through
            grad_in[rows, :] = (through * value * (1.0 - open_in)).astype(BF16)
            grad_dec[rows, :] = (grad_log * slow * open_dec * (1.0 - open_dec)).astype(BF16)

        grad_conv[s][length : length + 8, :] = jnp.zeros((8, width), F32)

    def gates_back(s, k, low, high):
        rows = spans[s]
        return contract(grad_in[rows, low:high], gate_in_w[:, low:high], (1, 1)) + contract(
            grad_dec[rows, low:high], gate_dec_w[:, low:high], (1, 1)
        )

    def add_conv(s, low, high, value):
        grad_conv[s][0:length, low:high] += value

    def rim(s, to):
        return pltpu.make_async_remote_copy(
            src_ref=rim_out.at[spans[s]],
            dst_ref=rim_in.at[spans[s]],
            send_sem=rim_send.at[s],
            recv_sem=rim_recv.at[s],
            device_id=(d, to),
            device_id_type=MESH,
        )

    def rim_start(s):
        @pl.when(even)
        def _():
            value = gates_back(s, *even_blocks[-1])
            rim_out[spans[s], :] = value[:, half:].astype(BF16)
            rim(s, t + 1).start()
            add_conv(s, width - half, width, value[:, :half])

        @pl.when(odd)
        def _():
            value = gates_back(s, *odd_blocks[0])
            rim_out[spans[s], :] = value[:, :half].astype(BF16)
            rim(s, t - 1).start()
            add_conv(s, 0, half, value[:, half:])

    def inner(s):
        @pl.when(even)
        def _():
            for k, low, high in even_blocks[:-1]:
                add_conv(s, low, high, gates_back(s, k, low, high))

        @pl.when(odd)
        def _():
            for k, low, high in odd_blocks[1:]:
                add_conv(s, low, high, gates_back(s, k, low, high))

    def conv_back(s):
        @pl.when(even)
        def _():
            rim(s, t + 1).wait()
            add_conv(s, width - half, width, rim_in[spans[s], :].astype(F32))

        @pl.when(odd)
        def _():
            rim(s, t - 1).wait()
            add_conv(s, 0, half, rim_in[spans[s], :].astype(F32))

        @pl.loop(0, length // STRIP)
        def _(i):
            near = pl.ds(pl.multiple_of(i * STRIP, STRIP), STRIP + 8)
            later = grad_conv[s][near, :]
            before = input_pre[s, near, :]
            here = later[:STRIP]
            value = taps[0:1, :] * here
            sums[1] += fold(here * before[8:])
            for k in range(1, taps.shape[0]):
                value = value + taps[k : k + 1, :] * pltpu.roll(later, STRIP + 8 - k, 0)[:STRIP]
                sums[1 + k] += fold(here * pltpu.roll(before, k, 0)[8:])
            rows = pl.ds(pl.multiple_of(s * length + i * STRIP, STRIP), STRIP)
            input_rows[rows, :] = value.astype(BF16)

    def project_back(s):
        rows, panel = spans[s], 512

        @pl.loop(0, weight.shape[0] // panel)
        def _(i):
            columns = rows_of(i, panel)
            value = contract(gelu_grad[rows, :], weight[columns, :], (1, 1))
            value = value + contract(input_rows[rows, :], input_w[columns, :], (1, 1))
            part[rows, columns] = value.astype(BF16)

    def gate_grads(blocks):
        for k, low, high in blocks:
            near = window[:, k * block : (k + 1) * block]
            gate_in_grad[:, low:high] = contract(near, grad_in[:, low:high], (0, 0)).astype(BF16)
            gate_dec_grad[:, low:high] = contract(near, grad_dec[:, low:high], (0, 0)).astype(BF16)

    states_back(0)
    feed_line.step(1)
    push(1)
    ring.panels[0].third()
    for copy in then:
        copy.wait()
    drive_back(0)
    rim_start(0)
    feed_line.step(2)
    inner(0)
    lift_load.wait()
    begin(2, part, lift_rows)
    lift_load = load_lift(2)
    conv_back(0)
    push(2)
    ring.panels[1].third()
    ring.panels[0].end()
    lift_load.wait()
    begin(3, part, lift_rows)
    reload.wait()
    project_back(0)
    lines[0].start(0, 1)
    states_back(1)
    ring.panels[2].third()
    push(3)
    drive_back(1)
    rim_start(1)
    lines[0].start(1)
    lines[0].step(1)
    inner(1)

    @pl.when(even)
    def _():
        gate_grads(even_blocks)

    @pl.when(odd)
    def _():
        gate_grads(odd_blocks)

    for g in gate_scatters:
        g.start()
    conv_back(1)
    lines[0].step(2)
    project_back(1)
    lines[1].start()
    middle_load = load(0, middle_in.at[1], input_grad.at[1])
    ring.panels[3].third()
    for k in range(sums.shape[0]):
        small[k : k + 1, :] = jnp.sum(sums[k], axis=0, keepdims=True)
    small[sums.shape[0] :, :] = jnp.zeros((8 - sums.shape[0], width), F32)
    small_copies = dp_copies(small, small_all, qsend, qrecv)
    for c in small_copies:
        c.start()
    small_all[d] = small[...]
    for copy in wide_loads:
        copy.wait()
    ring.panels[1].end()
    begin(4, branch, gelu_grad)
    for g in gate_scatters:
        g.first()
        g.second()
    push(4)
    lines[1].step(1)
    ring.panels[2].end()
    begin(5, branch, input_rows)
    ring.panels[4].third()
    lines[1].step(2)
    push(5)
    ring.panels[3].end()
    for g in gate_scatters:
        g.third()
    middle_load.wait()
    feed_line.total([input_grad.at[1]], more=True)
    output[0] = output_first[...]
    output[1] = input_grad[1].astype(BF16)
    quarter = pack.shape[1]
    for i in range(4):
        pack[4 + i : 5 + i, :] = mlp_part[:, i * quarter : (i + 1) * quarter]
    for s in range(seqs):
        lines[s].total([input_grad.at[i] for i in range(seqs)])
        change, gain_part = norm_back(act[s].astype(F32), gain[...][None], input_grad[s])
        input_grad[s] = change + grad_middle[s]
        for i in range(4):
            piece = gain_part[:, i * quarter : (i + 1) * quarter]
            if s == 0:
                pack[i : i + 1, :] = piece
            else:
                pack[i : i + 1, :] += piece
    pack_copies = dp_copies(pack, packs, psend, precv)
    for c in pack_copies:
        c.start()
    ring.panels[5].third()
    ring.panels[4].end()
    for g in gate_scatters:
        g.end()
    packs[d] = pack[...]
    for c in small_copies:
        c.wait_recv()
    sum_ = small_all[0]
    for i in range(1, 8):
        sum_ = sum_ + small_all[i]
    rate_grad[...] = sum_[0]
    taps_grad[...] = sum_[1:5]
    for c in pack_copies:
        c.wait_recv()
    sum_ = packs[0]
    for i in range(1, 8):
        sum_ = sum_ + packs[i]
    line_pack[...] = sum_
    z_copies = [
        pltpu.make_async_remote_copy(
            src_ref=line_pack,
            dst_ref=line_packs.at[t],
            send_sem=zsend.at[step - 1],
            recv_sem=zrecv.at[step - 1],
            device_id=(d, lax.rem(t + step, depth)),
            device_id_type=MESH,
        )
        for step in range(1, depth)
    ]
    for c in z_copies:
        c.start()
    line_packs[t] = sum_
    ring.panels[5].end()
    for c in z_copies:
        c.wait_recv()
    sum_ = line_packs[0]
    for i in range(1, depth):
        sum_ = sum_ + line_packs[i]
    for i in range(4):
        norm_grad[i * quarter : (i + 1) * quarter] = sum_[i]
        mlp_grad[i * quarter : (i + 1) * quarter] = sum_[4 + i]
    for c in small_copies + pack_copies + z_copies:
        c.wait_send()
    ring.end()
    for line in lines + [feed_line]:
        line.end()


def mixer_back_phase(
    branch, normed, saved, weights, normed_two, lift_rows, feed, middle, taps, rate, act, gain,
    grad_middle, mlp_part, output_first, depth,
):
    seqs, length, model = branch.shape
    tokens = seqs * length
    units = lift_rows.shape[1]
    gelu_w, input_w, gate_in_w, gate_dec_w, out_w = weights[:5]
    gelu_pre, input_pre, window, gate_in, gate_dec, states, mixed = saved
    width = out_w.shape[1]
    block = gate_in_w.shape[0]
    half = block // 2
    panel = (model // 8, PANEL)
    gate = (block // 8, width)
    pack = (8, model // 4)
    small = (8, width)
    flat = (tokens, width)
    outs = [
        shaped(act.shape, BF16, VMEM),
        shaped(act.shape, F32, VMEM),
        shaped((model,), F32, VMEM),
        shaped((model,), F32, VMEM),
        shaped((width,), F32, VMEM),
        shaped(taps.shape, F32, VMEM),
        shaped(gate, F32, VMEM),
        shaped(gate, F32, VMEM),
    ]
    outs += [shaped(panel, F32, ANY)] * 3 + [shaped((model // 8, units), F32, ANY)]
    scratch = [pltpu.VMEM((tokens, model), BF16)]
    scratch += [
        pltpu.VMEM(x.shape, x.dtype)
        for x in (
            out_w,
            input_w,
            gelu_pre,
            input_pre,
            window,
            gate_in,
            gate_dec,
            states,
            gate_in_w,
            gate_dec_w,
        )
    ]
    scratch += [pltpu.VMEM(flat, F32), pltpu.VMEM((seqs * (length + 8), width), F32)]
    scratch += [pltpu.VMEM(flat, BF16)] * 3
    scratch += [pltpu.VMEM((tokens, half), BF16)] * 2
    scratch += [pltpu.VMEM(gate_in_w.shape, BF16)] * 2
    scratch += [
        pltpu.VMEM((tokens, model), BF16),
        pltpu.VMEM((1 + taps.shape[0], 8, width), F32),
        DMA,
    ]
    scratch += line_scatter_scratch(seqs, length // depth, model, depth)
    scratch += [DMA((seqs,)), DMA((seqs,)), DMA((12 + 2 * seqs,)), DMA]
    scratch += [
        pltpu.VMEM(small, F32),
        pltpu.VMEM((8,) + small, F32),
        pltpu.VMEM(pack, F32),
        pltpu.VMEM((8,) + pack, F32),
        pltpu.VMEM(pack, F32),
        pltpu.VMEM((depth,) + pack, F32),
    ]
    scratch += [DMA((7,))] * 4 + [DMA((depth - 1,))] * 2
    scratch += ring_scratch(3, *panel)
    scratch += [pltpu.VMEM((length, model), BF16), pltpu.VMEM((tokens, PANEL), BF16)]
    scratch += line_scatter_scratch(1, length // depth, model, depth)
    scratch += scatter_scratch([gate] * 2, (False, False))
    scratch += [pltpu.VMEM(flat, BF16)]
    return call(
        functools.partial(mixer_back_kernel, depth),
        "mixer_back_phase",
        3,
        [ANY] * 18 + [VMEM] * 7,
        outs,
        scratch,
        (
            branch,
            normed,
            out_w,
            gelu_pre,
            input_pre,
            window,
            gate_in,
            gate_dec,
            states,
            mixed,
            gelu_w,
            input_w,
            gate_in_w,
            gate_dec_w,
            normed_two,
            lift_rows,
            feed,
            middle,
            taps,
            rate,
            act,
            gain,
            grad_middle,
            mlp_part,
            output_first,
        ),
        vmem=63 * 1024 * 1024,
    )


def finish_kernel(*refs):
    n = (len(refs) - 2) // 3
    ins, outs, held = refs[:n], refs[n : 2 * n], refs[2 * n : 3 * n]
    load_sem, save_sem = refs[3 * n :]
    loads = [pltpu.make_async_copy(ins[i], held[i], load_sem.at[i]) for i in range(n)]
    saves = [pltpu.make_async_copy(held[i], outs[i], save_sem.at[i]) for i in range(n)]
    for copy in loads:
        copy.start()
    for load, save in zip(loads, saves):
        load.wait()
        save.start()
    for save in saves:
        save.wait()


def finish(arrays):
    n = len(arrays)
    return pl.pallas_call(
        finish_kernel,
        name="finish",
        out_shape=[jax.ShapeDtypeStruct(x.shape, x.dtype) for x in arrays],
        in_specs=[ANY] * n,
        out_specs=[ANY] * n,
        scratch_shapes=[pltpu.VMEM(x.shape, x.dtype) for x in arrays] + [DMA((n,))] * 2,
        compiler_params=pltpu.CompilerParams(vmem_limit_bytes=62 * 1024 * 1024),
    )(*arrays)


def swapped(block, axis):
    count = lax.axis_size(axis)
    return lax.ppermute(block, axis, [(i, i ^ 1) for i in range(count)])


def normalize(value_entries, scale_gain):
    return (
        value_entries
        * lax.rsqrt(jnp.mean(value_entries * value_entries, axis=-1, keepdims=True) + EPS)
        * scale_gain
    )


def causal_conv(value_entries, kernel):
    summed = value_entries * kernel[0]
    for offset in range(1, kernel.shape[0]):
        shifted = jnp.concatenate(
            [jnp.zeros_like(value_entries[:, :offset]), value_entries[:, :-offset]], axis=1
        )
        summed = summed + shifted * kernel[offset]
    return summed


def decay_inputs(input_pre, decay_pre, conv_vals, decay_rate):
    log_decay = -8.0 * jax.nn.sigmoid(decay_pre) * decay_rate
    scaled = jnp.sqrt(-jnp.expm1(2.0 * log_decay))
    return (log_decay, scaled * jax.nn.sigmoid(input_pre) * conv_vals)


def recurrence(rate, drive):
    def join(left, right):
        return left[0] * right[0], left[1] * right[0] + right[1]

    return lax.associative_scan(join, (rate, drive), axis=1)[1]


def dot(spec, left, right):
    return jnp.einsum(spec, left, right, preferred_element_type=F32)


def weight_grad(left, right):
    return dot("pkr,pku->ru", left, right).astype(BF16)


class Fast:
    def __init__(self, depth, taps, rate):
        self.depth, self.taps, self.rate = depth, taps, rate

    def front(self, cotangent, token_weight, weights, act, gain, first_gain):
        middle, rows, self.weights, self.feeds, self.saved, self.held = front_phase(
            cotangent, token_weight, weights, self.taps, self.rate, act, gain, first_gain,
            self.depth,
        )
        self.normed, self.cot, self.normed_two = rows
        return middle

    def back(self, middle, gain, cotangent, token_weight, act, first_gain):
        grad_middle, branch, mlp_part, feed, lift_rows, output, down_grad, gate_grad = feed_phase(
            self.normed_two, self.cot, self.feeds, self.held, middle, gain, cotangent,
            token_weight, self.depth,
        )
        res = mixer_back_phase(
            branch, self.normed, self.saved, self.weights, self.normed_two, lift_rows, feed,
            middle, self.taps, self.rate, act, first_gain, grad_middle, mlp_part,
            output, self.depth,
        )
        output, input_grad, norm_grad, mlp_grad, rate_grad, taps_grad = res[:6]
        gate_in, gate_dec, out_grad, gelu_grad, input_w_grad, up_grad = res[6:]
        results = (
            output, input_grad, norm_grad, mlp_grad, rate_grad, taps_grad, gelu_grad, input_w_grad,
            gate_in, gate_dec, out_grad, gate_grad, up_grad, down_grad,
        )
        results = finish(results)
        return tuple(results[:6]) + (tuple(results[6:]),)


class Plain:
    def __init__(self, depth, taps, rate):
        self.depth, self.taps, self.rate = depth, taps, rate

    @staticmethod
    def wide(block):
        return lax.all_gather(block, "tensor", axis=1, tiled=True)

    @staticmethod
    def narrow(part):
        return lax.psum_scatter(part, "tensor", scatter_dimension=1, tiled=True).astype(F32)

    @staticmethod
    def full(shard):
        return lax.all_gather(shard, "dp", axis=0, tiled=True)

    @staticmethod
    def own(grad):
        return lax.psum_scatter(grad, "dp", scatter_dimension=0, tiled=True).astype(F32)

    def front(self, cotangent, token_weight, weights, act, gain, first_gain):
        cot = (cotangent.astype(F32) * token_weight).astype(BF16)
        normed = normalize(act.astype(F32), first_gain).astype(BF16)
        gelu_w, input_w, gate_in_w, gate_dec_w, out_w = (self.full(w) for w in weights[:5])
        self.feeds = tuple(self.full(w) for w in weights[5:])
        normed_all = self.wide(normed)
        seqs, length, _ = normed_all.shape
        channels = gelu_w.shape[1]
        block = gate_in_w.shape[0]
        half = block // 2
        width = channels + half
        parity = lax.axis_index("tensor") % 2
        gelu_pre = dot("kqg,ga->kqa", normed_all, gelu_w)
        input_pre = dot("kqg,ga->kqa", normed_all, input_w)
        gelu_out, gelu_back = jax.vjp(jax.nn.gelu, gelu_pre)
        conv_out, conv_back = jax.vjp(causal_conv, input_pre, self.taps)
        conv_bf = conv_out.astype(BF16)
        rim = lax.dynamic_slice_in_dim(conv_bf, (1 - parity) * (channels - half), half, 2)
        window = jnp.zeros((seqs, length, width), BF16)
        window = lax.dynamic_update_slice_in_dim(window, conv_bf, parity * half, 2)
        window = lax.dynamic_update_slice_in_dim(
            window, swapped(rim, "tensor"), (1 - parity) * channels, 2
        )
        tiles = window.reshape(seqs, length, width // block, block)
        placed = lax.dynamic_update_slice_in_dim(
            jnp.zeros((2, block, width), BF16), jnp.stack([gate_in_w, gate_dec_w]), parity * half, 2
        ).reshape(2, block, width // block, block)
        gates = dot("slbk,gkbc->gslbc", tiles, placed).reshape(2, seqs, length, width)
        gates = lax.dynamic_slice_in_dim(gates, parity * half, channels, 3)
        (log_decay, drive), gate_back = jax.vjp(
            decay_inputs, gates[0], gates[1], conv_bf.astype(F32), self.rate
        )
        decay = jnp.exp(log_decay)
        states = recurrence(decay, drive)
        mixed = (gelu_out * states).astype(BF16)
        self.kept = (
            normed_all, gelu_w, input_w, out_w, gelu_out, gelu_back, conv_back, tiles, placed,
            gate_back, decay, states, mixed,
        )
        part = dot("xgq,pq->xgp", mixed, out_w).astype(BF16)
        self.cot = self.wide(cot)
        middle = act.astype(F32) + self.narrow(part)
        self.normed_two = self.wide(normalize(middle, gain).astype(BF16))
        return middle

    def back(self, middle, gain, cotangent, token_weight, act, first_gain):
        cot_own = cotangent.astype(F32) * token_weight
        gate_w, up_w, down_w = self.feeds
        normed, cot = self.normed_two, self.cot
        gate_pre = dot("nwo,ob->nwb", normed, gate_w)
        lift_pre = dot("nwo,ob->nwb", normed, up_w)
        gate_act, activ_back = jax.vjp(jax.nn.gelu, gate_pre)
        hidden = (gate_act * lift_pre).astype(BF16)
        grad_hidden = dot("gre,eu->gru", cot, down_w)
        gate_grad = activ_back(grad_hidden * lift_pre)[0].astype(BF16)
        lift_grad = (grad_hidden * gate_act).astype(BF16)
        part = dot("mqa,ya->mqy", gate_grad, gate_w) + dot("mqa,ya->mqy", lift_grad, up_w)
        _, back = jax.vjp(normalize, middle, gain)
        change, gain_grad = back(self.narrow(part.astype(BF16)))
        grad = cot_own + change
        panels = (
            weight_grad(cot, hidden), weight_grad(normed, gate_grad), weight_grad(normed, lift_grad)
        )
        feed = dot("xav,tv->xat", hidden, down_w).astype(BF16)
        output = (middle + self.narrow(feed)).astype(BF16)
        branch = self.wide(grad.astype(BF16))
        (
            normed_all, gelu_w, input_w, out_w, gelu_out, gelu_back, conv_back, tiles, placed,
            gate_back, decay, states, mixed,
        ) = self.kept
        seqs, length, channels = states.shape
        block = tiles.shape[-1]
        half = block // 2
        width = channels + half
        parity = lax.axis_index("tensor") % 2
        grad_mixed = dot("xtz,zm->xtm", branch, out_w)
        gelu_grad = gelu_back(grad_mixed * states)[0].astype(BF16)
        later = jnp.concatenate([decay[:, 1:], jnp.zeros_like(decay[:, :1])], axis=1)
        grad_drive = jnp.flip(
            recurrence(jnp.flip(later, 1), jnp.flip(grad_mixed * gelu_out, 1)), 1
        )
        earlier = jnp.concatenate([jnp.zeros_like(states[:, :1]), states[:, :-1]], axis=1)
        grad_in, grad_dec, grad_conv, grad_rate = gate_back(
            (grad_drive * decay * earlier, grad_drive)
        )
        grads = lax.dynamic_update_slice_in_dim(
            jnp.zeros((2, seqs, length, width), BF16),
            jnp.stack([grad_in, grad_dec]).astype(BF16),
            parity * half,
            3,
        ).reshape(2, seqs, length, width // block, block)
        grad_window = dot("gslbc,gkbc->slbk", grads, placed).reshape(seqs, length, width)
        grad_placed = dot("slbk,gslbc->gkbc", tiles, grads).reshape(2, block, width)
        grad_gates = lax.dynamic_slice_in_dim(grad_placed, parity * half, channels, 2)
        rim = lax.dynamic_slice_in_dim(grad_window, (1 - parity) * channels, half, 2)
        rim = swapped(rim.astype(BF16), "tensor").astype(F32)
        grad_conv = grad_conv + lax.dynamic_slice_in_dim(grad_window, parity * half, channels, 2)
        start = (1 - parity) * (channels - half)
        rim = lax.dynamic_slice_in_dim(grad_conv, start, half, 2) + rim
        grad_conv = lax.dynamic_update_slice_in_dim(grad_conv, rim, start, 2)
        input_rows, grad_taps = conv_back(grad_conv)
        input_rows = input_rows.astype(BF16)
        part = dot("mzf,af->mza", gelu_grad, gelu_w) + dot("mzf,af->mza", input_rows, input_w)
        _, back = jax.vjp(normalize, act.astype(F32), first_gain)
        change, norm_grad = back(self.narrow(part.astype(BF16)))
        gains = lax.psum((norm_grad, gain_grad), ("dp", "tensor"))
        small = lax.psum((grad_rate, grad_taps), "dp")
        parts = (
            weight_grad(normed_all, gelu_grad),
            weight_grad(normed_all, input_rows),
            grad_gates[0].astype(BF16),
            grad_gates[1].astype(BF16),
            weight_grad(branch, mixed),
            panels[1],
            panels[2],
            panels[0],
        )
        own = [self.own(g) for g in parts]
        return (output, grad + change) + gains + small + (tuple(own),)


def shards(
    activations,
    norm_gain,
    gelu_proj,
    input_proj,
    conv_weight,
    gate_input,
    gate_decay,
    decay_rate,
    out_proj,
    mlp_gain,
    feed_gate,
    feed_up,
    feed_down,
    cotangent,
    lengths,
    batch_of,
):
    depth = lax.axis_size("tensor")
    fast = lax.axis_size("dp") == 8 and depth == 4
    run = (Fast if fast else Plain)(depth, conv_weight, decay_rate)
    tensor_index = lax.axis_index("tensor")
    data_index = lax.axis_index("dp")
    seq_count, row_count, _ = activations.shape
    full_length = row_count * depth
    members = (batch_of[:, None] == jnp.arange(MICRO)[None, :]).astype(F32)
    counts = jnp.sum(members * lengths[:, None].astype(F32), axis=0)
    total_seqs = lengths.shape[0]
    per_batch = float(total_seqs * full_length) / (MICRO * counts)
    weight_all = jnp.sum(members * per_batch[None, :], axis=1)
    my_weight = lax.dynamic_slice_in_dim(weight_all, data_index * seq_count, seq_count)
    my_length = lax.dynamic_slice_in_dim(lengths, data_index * seq_count, seq_count)
    places = tensor_index * row_count + jnp.arange(row_count)
    valid_mask = (places[None, :] < my_length[:, None]).astype(F32)
    token_weight = (valid_mask * my_weight[:, None])[:, :, None]

    weights = (
        gelu_proj, input_proj, gate_input, gate_decay, out_proj.T, feed_gate, feed_up, feed_down.T
    )
    middle = run.front(cotangent, token_weight, weights, activations, mlp_gain, norm_gain)
    output, input_grad, norm_grad, mlp_grad, rate_grad, taps_grad, grads = run.back(
        middle, mlp_gain, cotangent, token_weight, activations, norm_gain
    )
    return (
        output,
        input_grad,
        norm_grad,
        grads[0],
        grads[1],
        taps_grad,
        grads[2],
        grads[3],
        rate_grad,
        grads[4].T,
        mlp_grad,
        grads[5],
        grads[6],
        grads[7].T,
    )


def solution(mesh):
    placed = (
        P("dp", "tensor", None),
        P(),
        P("dp", "tensor"),
        P("dp", "tensor"),
        P(None, "tensor"),
        P("dp", "tensor"),
        P("dp", "tensor"),
        P("tensor"),
        P("tensor", "dp"),
        P(),
        P("dp", "tensor"),
        P("dp", "tensor"),
        P("tensor", "dp"),
        P("dp", "tensor", None),
        P(),
        P(),
    )
    return jax.shard_map(
        shards,
        mesh=mesh,
        in_specs=placed,
        out_specs=(
            P("dp", "tensor", None),
            P("dp", "tensor", None),
            P(),
            P("dp", "tensor"),
            P("dp", "tensor"),
            P(None, "tensor"),
            P("dp", "tensor"),
            P("dp", "tensor"),
            P("tensor"),
            P("tensor", "dp"),
            P(),
            P("dp", "tensor"),
            P("dp", "tensor"),
            P("tensor", "dp"),
        ),
        check_vma=False,
    )
```
